32 devices in a mesh: dom: 8 (over z, y), rep: 4 (over x, core).
Axes of the slice: x: 2, y: 2, z: 4, core: 2. Of those that a mesh axis runs over, the one named last changes fastest.
Arguments:
- entities: bfloat16 [2048, 400], P('dom'), may hold values from -2.5 to 2.5, as said below
- relation: float32 [1000, 400], replicated, may hold values from 0.25 to 1.75
- serve_ids: int32 [8, 8, 2], P('dom'), may hold values from 0 to 255
- edge_src: int32 [8, 4, 512], P('dom', 'rep'), may hold values from 0 to 255
- edge_rel: int32 [8, 4, 512], P('dom', 'rep'), may hold values from 0 to 999
- edge_dst: int32 [8, 4, 512], P('dom', 'rep'), may hold values from 0 to 15
- neg_ids: int32 [8, 4, 2, 384], P('dom', 'rep'), may hold values from 0 to 15
- edge_count: int32 [8, 4], P('dom', 'rep'), may hold values from 1 to 512, 1536 in all within a row
Outputs:
- entity_grad: float32 [2048, 400], P('dom', 'rep')
- relation_grad: float32 [1000, 400], replicated
The draws below stay inside these ranges and needn't reach their ends.
Inputs may be any that keep to these rules, and one draw needn't show every extreme that they name: `entities`: entity entries are bounded.
All inputs are finite; a program needn't handle non-finite values. No bound on the sum of `edge_count` on one device may be relied on, other than what follows from the above.
Results may differ from the reference program's by a relative error of at most 0.0021.
The reference program's roundings to bfloat16 on the way count: a program that leaves them out, or rounds other values in their place, can miss the bound.
Values may be sent and summed in bfloat16 or wider, within the bound.
No kernel may reach another device: no remote copies, remote signals or barrier semaphores. Data moves between devices by JAX's collectives and lax.ppermute only.
A program may use at most 64 MiB of HBM per device.

```python
import math
import jax
import jax.numpy as jnp
import numpy as np
from jax import lax

D = 400
NREL = 1000
ENT_DEV = 256
CAP = 2
EDGE_DEV = 512
NEG = 384
WORKERS = 8
REPS = 4
ENTITIES = 2048
GROUPS = 2


def draw_entities(key, part):
    first = jax.random.fold_in(key, 0)
    values = 0.3 * jax.random.truncated_normal(first, -4.0, 4.0, (ENTITIES, D), jnp.float32)
    return values.astype(jnp.bfloat16)


def set_ends(entries, rng, low, top_value):
    spot = [jax.random.randint(jax.random.fold_in(rng, axis), (), 0, length) for axis, length in enumerate(entries.shape)]
    longest = entries.shape.index(max(entries.shape))
    neighbour = spot[:longest] + [(spot[longest] + 1) % entries.shape[longest]] + spot[longest + 1:]
    return entries.at[tuple(spot)].set(low).at[tuple(neighbour)].set(top_value)


def rank_bounds(count, slope):
    weights = [(1 << 20) // math.isqrt(grade ** slope) + 1 for grade in range(1, count + 1)]
    scale = 1 + sum(weights) // (1 << 30)
    return np.cumsum(np.array([max(1, weight // scale) for weight in weights]))


def ranked(stream_key, extent, number_of, slope):
    grid = rank_bounds(number_of, slope)
    lot = jax.random.randint(jax.random.fold_in(stream_key, 1), extent, 0, int(grid[number_of - 1]))
    rank = jnp.searchsorted(jnp.asarray(grid, jnp.int32), lot, side="right")
    return jax.random.permutation(jax.random.fold_in(stream_key, 2), number_of)[rank].astype(jnp.int32)


def length_profile(number_of, total, limit, slope):
    portions = [(1 << 20) // math.isqrt(standing ** slope) + 1 for standing in range(2, number_of + 1)]
    rest, counts = total - limit - (number_of - 1), [1] * (number_of - 1)
    while rest > 0:
        free = [i for i in range(number_of - 1) if counts[i] < limit]
        pool, left = sum([portions[i] for i in free]), rest
        for i in free:
            addition = min(limit - counts[i], max(1, left * portions[i] // pool), rest)
            counts[i] = counts[i] + addition
            rest = rest - addition
    return np.array([limit] + counts)


def uneven(rng, count, total, bound, skew):
    if count == 2:
        one = jax.random.randint(rng, (), max(1, total - bound), min(bound, total - 1) + 1)
        return jnp.stack([one, total - one])
    tallies = jnp.asarray(length_profile(count, total, bound, skew), jnp.int32)
    pairs = (count - 1) // 2
    donor, taker = tallies[1:1 + 2 * pairs:2], tallies[2:2 + 2 * pairs:2]
    room = jnp.minimum(donor - 1, bound - taker)
    shifted = jax.random.randint(jax.random.fold_in(rng, 1), (pairs,), 0, 1 << 20) % (room + 1)
    tallies = tallies.at[1:1 + 2 * pairs:2].set(donor - shifted).at[2:2 + 2 * pairs:2].set(taker + shifted)
    return tallies[jax.random.permutation(jax.random.fold_in(rng, 2), count)]


def setup_inputs(seed: int = 0) -> dict:
    streams_of = jax.random.split(jax.random.key(seed), 9)
    return {
        "entities": draw_entities(jax.random.fold_in(streams_of[8], 71), 0),
        "relation": jnp.clip(jax.random.uniform(streams_of[1], (NREL, D), jnp.float32, 0.25, 1.75), 0.25, 1.75),
        "serve_ids": set_ends(jax.random.randint(streams_of[2], (WORKERS, WORKERS, CAP), 0, ENT_DEV), jax.random.fold_in(streams_of[2], 1), 0, ENT_DEV - 1).astype(jnp.int32),
        "edge_src": set_ends(jax.random.randint(streams_of[3], (WORKERS, REPS, EDGE_DEV), 0, ENT_DEV), jax.random.fold_in(streams_of[3], 1), 0, ENT_DEV - 1).astype(jnp.int32),
        "edge_rel": set_ends(ranked(streams_of[4], (WORKERS, REPS, EDGE_DEV), NREL, 2), jax.random.fold_in(streams_of[4], 3), 0, NREL - 1).astype(jnp.int32),
        "edge_dst": set_ends(jax.random.randint(streams_of[5], (WORKERS, REPS, EDGE_DEV), 0, WORKERS * CAP), jax.random.fold_in(streams_of[5], 1), 0, (WORKERS * CAP) - 1).astype(jnp.int32),
        "neg_ids": set_ends(jax.random.randint(streams_of[6], (WORKERS, REPS, GROUPS, NEG), 0, WORKERS * CAP), jax.random.fold_in(streams_of[6], 1), 0, (WORKERS * CAP) - 1).astype(jnp.int32),
        "edge_count": jax.vmap(lambda own: uneven(own, REPS, 3 * EDGE_DEV, EDGE_DEV, 2))(jax.random.split(streams_of[7], WORKERS)).reshape((WORKERS, REPS)).astype(jnp.int32),
    }


def shard_grads(lhs_block, relation, table, src, rel, dst, neg, count):
    groups = neg.shape[0]
    edges = src.shape[0]
    width = edges // groups
    lhs_rows = lhs_block[src].astype(jnp.float32)
    rel_rows = relation[rel]
    query = (lhs_rows * rel_rows).astype(jnp.bfloat16).reshape(groups, width, -1)
    cands = jnp.concatenate([table[dst].reshape(groups, width, -1), table[neg]], axis=1)
    scores = jnp.einsum("cid,cjd->cij", query.astype(jnp.float32), cands.astype(jnp.float32))
    position = jnp.arange(edges, dtype=jnp.int32).reshape(groups, width)
    live = position < count
    columns = jnp.concatenate([live, jnp.ones((groups, neg.shape[1]), dtype=bool)], axis=1)
    scores = jnp.where(columns[:, None, :], scores, jnp.float32(-1e30))
    top = jnp.max(scores, axis=-1, keepdims=True)
    expo = jnp.exp(scores - top)
    probs = expo / jnp.sum(expo, axis=-1, keepdims=True)
    onehot = (jnp.arange(width + neg.shape[1])[None, :] == jnp.arange(width)[:, None]).astype(jnp.float32)
    grads = ((probs - onehot[None]) * live[:, :, None].astype(jnp.float32)).astype(jnp.bfloat16)
    dquery = jnp.einsum("cij,cjd->cid", grads.astype(jnp.float32), cands.astype(jnp.float32)).reshape(edges, -1)
    dcand = jnp.einsum("cij,cid->cjd", grads.astype(jnp.float32), query.astype(jnp.float32))
    dim = lhs_block.shape[1]
    lhs_grad = jnp.zeros(lhs_block.shape, jnp.float32).at[src].add(dquery * rel_rows)
    rel_grad = jnp.zeros(relation.shape, jnp.float32).at[rel].add(dquery * lhs_rows)
    table_grad = jnp.zeros(table.shape, jnp.float32).at[dst].add(dcand[:, :width].reshape(edges, dim))
    table_grad = table_grad.at[neg.reshape(-1)].add(dcand[:, width:].reshape(-1, dim))
    return lhs_grad, table_grad, rel_grad


def reference(entities, relation, serve_ids, edge_src, edge_rel, edge_dst, neg_ids, edge_count):
    workers = serve_ids.shape[0]
    cap = serve_ids.shape[2]
    dim = entities.shape[1]
    blocks = entities.reshape(workers, -1, dim)
    owners = jnp.arange(workers, dtype=jnp.int32)

    def one_worker(items):
        worker, src, rel, dst, neg, count = items
        picked = serve_ids[:, worker, :]
        table = blocks[owners[:, None], picked].reshape(workers * cap, dim)
        lhs_block = blocks[worker]
        lhs_grad, table_grad, rel_grad = jax.vmap(shard_grads, in_axes=(None, None, None, 0, 0, 0, 0, 0))(lhs_block, relation, table, src, rel, dst, neg, count)
        return jnp.sum(lhs_grad, axis=0), jnp.sum(table_grad, axis=0), jnp.sum(rel_grad, axis=0)

    lhs_all, table_all, rel_all = lax.map(one_worker, (owners, edge_src, edge_rel, edge_dst, neg_ids, edge_count))
    table_all = jnp.transpose(table_all.reshape(workers, workers, cap, dim), (1, 0, 2, 3))

    def own_rows(lhs_grad, served, grads):
        return lhs_grad.at[served.reshape(-1)].add(grads.reshape(-1, dim))

    entity_grad = jax.vmap(own_rows)(lhs_all, serve_ids, table_all).reshape(-1, dim)
    slots = edge_src.shape[0] * edge_src.shape[1] * edge_src.shape[2]
    relation_grad = jnp.sum(rel_all, axis=0) / jnp.float32(slots)
    return entity_grad, relation_grad
```

```python
import functools

import jax
import jax.numpy as jnp
from jax import lax
from jax.experimental import pallas as pl
from jax.experimental.pallas import tpu as pltpu
from jax.sharding import PartitionSpec as P

F32 = jnp.float32
BF16 = jnp.bfloat16
IDX_ROWS = 8
VMEM = pl.BlockSpec(memory_space=pltpu.VMEM)
SMEM = pl.BlockSpec(memory_space=pltpu.SMEM)


def params():
    return pltpu.CompilerParams(vmem_limit_bytes=40 * 1024 * 1024)


def split2(x):
    hi = x.astype(BF16)
    lo = (x - hi.astype(F32)).astype(BF16)
    return hi, lo


def dot(a, b):
    return jnp.dot(a, b, preferred_element_type=F32)


def prep_kernel(serve, count, ent, src, rel, dst, neg, out_rows, out_idx, onehot):
    workers, cap = serve.shape[1], serve.shape[2]
    rows = ent.shape[0]
    groups = neg.shape[2]
    width = neg.shape[3]

    def fill(k, carry):
        spot = lax.broadcasted_iota(jnp.int32, (1, rows), 1)
        picked = serve[0, k // cap, k % cap]
        onehot[pl.ds(k, 1), :] = jnp.where(spot == picked, 1.0, 0.0).astype(F32)
        return carry

    lax.fori_loop(0, workers * cap, fill, 0)
    out_rows[...] = dot(onehot[...].astype(BF16), ent[...]).astype(BF16)
    out_idx[...] = jnp.full(out_idx.shape, count[0, 0], jnp.int32)
    out_idx[0:1, :] = src[0]
    out_idx[1:2, :] = rel[0]
    out_idx[2:3, :] = dst[0]
    for g in range(groups):
        out_idx[3 + g : 4 + g, :width] = neg[0, 0, g : g + 1, :]


def main_kernel(cfg, rep_ref, *refs):
    workers, replicas, cap, groups, width, nrel, pad_rel, block, dim, narrow, total = cfg
    idx_refs = refs[:replicas]
    (ent, relation, table, out_rel, out_lhs) = refs[replicas : replicas + 5]
    (idx_all, idx_col, rel_hi, rel_lo, acc_rel, acc_lhs, acc_tab) = refs[replicas + 5 :]
    edges = idx_all.shape[1]
    rows = ent.shape[0]
    slots = table.shape[0]
    mine = rep_ref[0]
    per = edges // groups

    for i in range(replicas):
        idx_all[i * IDX_ROWS : (i + 1) * IDX_ROWS, :] = idx_refs[i][...]
        idx_col[i] = jnp.transpose(idx_refs[i][...])
    tail = pad_rel - nrel
    if tail:
        rel_hi[nrel:, :] = jnp.zeros((tail, dim), BF16)
        rel_lo[nrel:, :] = jnp.zeros((tail, dim), BF16)
    hi, lo = split2(relation[...])
    rel_hi[:nrel, :] = hi
    rel_lo[:nrel, :] = lo
    acc_rel[...] = jnp.zeros(acc_rel.shape, F32)
    acc_lhs[...] = jnp.zeros(acc_lhs.shape, F32)
    acc_tab[...] = jnp.zeros(acc_tab.shape, F32)

    spot = lax.broadcasted_iota(jnp.int32, (total, edges), 0)
    target = (spot // block) * (block * replicas) + mine * block + spot % block

    def shard(i, carry):
        base = pl.multiple_of(i * IDX_ROWS, IDX_ROWS)
        lanes = idx_all[pl.ds(base, IDX_ROWS), :]
        cols = idx_col[i]
        src_l, rel_l, dst_l = lanes[0:1], lanes[1:2], lanes[2:3]
        count = lanes[IDX_ROWS - 1 : IDX_ROWS]
        src_c, rel_c = cols[:, 0:1], cols[:, 1:2]

        pick = jnp.where(
            lax.broadcasted_iota(jnp.int32, (edges, rows), 1) == src_c, 1.0, 0.0
        ).astype(BF16)
        lhs = dot(pick, ent[...])
        pick = jnp.where(
            lax.broadcasted_iota(jnp.int32, (edges, pad_rel), 1) == rel_c, 1.0, 0.0
        ).astype(BF16)
        rel_rows = dot(pick, rel_hi[...]) + dot(pick, rel_lo[...])
        query = (lhs * rel_rows).astype(BF16)
        scores = lax.dot_general(
            table[...], query, (((1,), (1,)), ((), ())), preferred_element_type=F32
        )
        position = lax.broadcasted_iota(jnp.int32, (1, edges), 1)
        live = jnp.where(position < count, 1.0, 0.0).astype(F32)
        own = jnp.where(
            lax.broadcasted_iota(jnp.int32, (slots, edges), 0) == dst_l, 1.0, 0.0
        ).astype(F32)
        seen = own * live
        parts = []
        for g in range(groups):
            s = scores[:, g * per : (g + 1) * per]
            o = own[:, g * per : (g + 1) * per]
            neg = jnp.where(
                lax.broadcasted_iota(jnp.int32, (slots, width), 0)
                == lanes[3 + g : 4 + g, :width],
                1.0,
                0.0,
            ).astype(F32)
            times = jnp.sum(seen[:, g * per : (g + 1) * per], axis=1, keepdims=True) + jnp.sum(
                neg, axis=1, keepdims=True
            )
            s = jnp.where(times > 0, s, F32(-1e30))
            top = jnp.max(s, axis=0, keepdims=True)
            expo = jnp.exp(s - top)
            norm = jnp.sum(expo * times, axis=0, keepdims=True)
            probs = expo / norm
            other = probs.astype(BF16).astype(F32)
            self_ = (probs - 1.0).astype(BF16).astype(F32)
            grads = (times - o) * other + o * self_
            parts.append(grads * live[:, g * per : (g + 1) * per])
        grads = jnp.concatenate(parts, axis=1)
        g0 = grads.astype(BF16)
        rest = grads - g0.astype(F32)
        g1 = rest.astype(BF16)
        g2 = (rest - g1.astype(F32)).astype(BF16)

        stack = jnp.concatenate([g0, g1, g2], axis=0)
        tables = jnp.concatenate([table[...]] * 3, axis=0)
        dquery = lax.dot_general(
            stack, tables, (((0,), (0,)), ((), ())), preferred_element_type=F32
        )
        acc_tab[:, :dim] += dot(g0, query) + dot(g1, query) + dot(g2, query)
        y0, y1 = split2(dquery * lhs)
        put = jnp.where(target == rel_l, 1.0, 0.0).astype(BF16)
        acc_rel[:, :dim] += dot(put, y0) + dot(put, y1)
        x0, x1 = split2(dquery * rel_rows)
        put = jnp.where(
            lax.broadcasted_iota(jnp.int32, (rows, edges), 0) == src_l, 1.0, 0.0
        ).astype(BF16)
        acc_lhs[:, :dim] += dot(put, x0) + dot(put, x1)
        return carry

    lax.fori_loop(0, replicas, shard, 0)

    lhs_all = acc_lhs[...]
    part = lhs_all[:, :narrow]
    for k in range(1, replicas):
        part = jnp.where(mine == k, lhs_all[:, k * narrow : (k + 1) * narrow], part)
    out_lhs[...] = part
    out_rel[...] = acc_rel[...]
    span = out_rel.shape[1]
    shifted = pltpu.roll(acc_tab[...], dim - mine * narrow, 1)
    lane = lax.broadcasted_iota(jnp.int32, (slots, span), 1)
    shifted = jnp.where((lane >= dim) & (lane < dim + narrow), shifted, 0.0)
    for o in range(workers):
        out_rel[o * block : o * block + cap, :] += shifted[o * cap : (o + 1) * cap, :]


def entity_kernel(dim, serve, lhs, recv, out, rows_ref):
    workers, cap = serve.shape[1], serve.shape[2]
    narrow = out.shape[1]
    out[...] = lhs[...]
    for w in range(workers):
        rows_ref[w * cap : (w + 1) * cap, :] = recv[w, :cap, dim : dim + narrow]

    def add(k, carry):
        picked = serve[0, k // cap, k % cap]
        out[pl.ds(picked, 1), :] += rows_ref[pl.ds(k, 1), :]
        return carry

    lax.fori_loop(0, workers * cap, add, 0)


def shards(entities, relation, serve_ids, edge_src, edge_rel, edge_dst, neg_ids, edge_count):
    workers = lax.axis_size("dom")
    replicas = lax.axis_size("rep")
    rows, dim = entities.shape
    nrel = relation.shape[0]
    cap = serve_ids.shape[2]
    edges = edge_src.shape[2]
    groups, width = neg_ids.shape[2], neg_ids.shape[3]
    slots = workers * cap
    narrow = dim // replicas
    devices = workers * replicas
    block = max(-(-nrel // devices), cap)
    total = workers * block
    pad_rel = -(-nrel // 128) * 128
    span = -(-(dim + narrow) // 128) * 128

    outgoing, idx = pl.pallas_call(
        prep_kernel,
        out_shape=(
            jax.ShapeDtypeStruct((slots, dim), BF16),
            jax.ShapeDtypeStruct((IDX_ROWS, edges), jnp.int32),
        ),
        in_specs=[SMEM, SMEM] + [VMEM] * 5,
        out_specs=(VMEM, VMEM),
        scratch_shapes=[pltpu.VMEM((slots, rows), F32)],
        compiler_params=params(),
        name="prep",
    )(serve_ids, edge_count, entities, edge_src, edge_rel, edge_dst, neg_ids)

    held = [idx]
    for hop in range(1, replicas):
        held.append(
            lax.ppermute(idx, "rep", [(i, (i + hop) % replicas) for i in range(replicas)])
        )
    received = lax.all_to_all(
        outgoing.reshape(workers, cap, dim), "dom", split_axis=0, concat_axis=0, tiled=True
    )
    table = received.reshape(slots, dim)

    cfg = (workers, replicas, cap, groups, width, nrel, pad_rel, block, dim, narrow, total)
    mine = lax.axis_index("rep").astype(jnp.int32).reshape(1)
    rel_part, lhs_part = pl.pallas_call(
        functools.partial(main_kernel, cfg),
        out_shape=(
            jax.ShapeDtypeStruct((total, span), F32),
            jax.ShapeDtypeStruct((rows, narrow), F32),
        ),
        in_specs=[SMEM] + [VMEM] * (replicas + 3),
        out_specs=(VMEM, VMEM),
        scratch_shapes=[
            pltpu.VMEM((replicas * IDX_ROWS, edges), jnp.int32),
            pltpu.VMEM((replicas, edges, IDX_ROWS), jnp.int32),
            pltpu.VMEM((pad_rel, dim), BF16),
            pltpu.VMEM((pad_rel, dim), BF16),
            pltpu.VMEM((total, span), F32),
            pltpu.VMEM((rows, span), F32),
            pltpu.VMEM((slots, span), F32),
        ],
        compiler_params=params(),
        name="edges",
    )(mine, *held, entities, relation, table)

    recv = lax.all_to_all(
        rel_part.reshape(workers, block, span), "dom", split_axis=0, concat_axis=0, tiled=True
    )
    scale = 1.0 / (edges * devices)
    rel_sum = (jnp.sum(recv[:, :, :dim], axis=0) * F32(scale)).astype(BF16)
    gathered = lax.all_gather(rel_sum, ("dom", "rep"), axis=0, tiled=True)
    relation_grad = gathered[:nrel].astype(F32)

    entity_grad = pl.pallas_call(
        functools.partial(entity_kernel, dim),
        out_shape=jax.ShapeDtypeStruct((rows, narrow), F32),
        in_specs=[SMEM, VMEM, VMEM],
        out_specs=VMEM,
        scratch_shapes=[pltpu.VMEM((slots, narrow), F32)],
        compiler_params=params(),
        name="entity",
    )(serve_ids, lhs_part, recv)
    return (entity_grad, relation_grad)


def solution(mesh):
    placed = (
        P("dom", None),
        P(),
        P("dom", None, None),
        P("dom", "rep", None),
        P("dom", "rep", None),
        P("dom", "rep", None),
        P("dom", "rep", None, None),
        P("dom", "rep"),
    )
    return jax.shard_map(
        shards, mesh=mesh, in_specs=placed, out_specs=(P("dom", "rep"), P()), check_vma=False
    )
```

```python
import functools

import jax
import jax.numpy as jnp
from jax import lax
from jax.experimental import pallas as pl
from jax.experimental.pallas import tpu as pltpu
from jax.sharding import PartitionSpec as P

F32 = jnp.float32
BF16 = jnp.bfloat16
IDX_ROWS = 8
LANES = 128
VMEM = pl.BlockSpec(memory_space=pltpu.VMEM)
SMEM = pl.BlockSpec(memory_space=pltpu.SMEM)
HBM = pl.BlockSpec(memory_space=pltpu.HBM)


def params():
    return pltpu.CompilerParams(vmem_limit_bytes=32 * 1024 * 1024)


def up(value, step):
    return -(-value // step) * step


def split2(x):
    hi = x.astype(BF16)
    lo = (x - hi.astype(F32)).astype(BF16)
    return hi, lo


def split3(x):
    hi, rest = x.astype(BF16), x
    rest = rest - hi.astype(F32)
    mid = rest.astype(BF16)
    low = (rest - mid.astype(F32)).astype(BF16)
    return hi, mid, low


def dot(a, b):
    return jnp.dot(a, b, preferred_element_type=F32)


def dot_t(a, b):
    return lax.dot_general(a, b, (((1,), (1,)), ((), ())), preferred_element_type=F32)


def ones_where(flag):
    return jnp.where(flag, 1.0, 0.0).astype(BF16)


def iota(shape, axis):
    return lax.broadcasted_iota(jnp.int32, shape, axis)


def shifted_rows(x, offset, narrow, offsets):
    out = x[offsets[0] : offsets[0] + narrow]
    for other in offsets[1:]:
        out = jnp.where(offset == other, x[other : other + narrow], out)
    return out


def prep_kernel(direct, place, serve, count, ent, src, rel, dst, neg, *refs):
    cap, workers = serve.shape[1], serve.shape[2]
    rows = ent.shape[1]
    groups, width = neg.shape[2], neg.shape[3]
    copies = 7
    out_idx, outs = refs[0], refs[1:-9]
    serve_s, count_s, ent_v, src_v, rel_v, dst_v, neg_v, onehot, sems = refs[-9:]
    moves = [
        pltpu.make_async_copy(a, b, sems.at[n])
        for n, (a, b) in enumerate(
            zip(
                (serve, count, ent, src, rel, dst, neg),
                (serve_s, count_s, ent_v, src_v, rel_v, dst_v, neg_v),
            )
        )
    ]
    for move in moves:
        move.start()
    for move in moves:
        move.wait()
    assert len(moves) == copies
    out_idx[...] = jnp.full(out_idx.shape, count_s[0, 0], jnp.int32)
    out_idx[0:1, :] = src_v[0]
    out_idx[1:2, :] = rel_v[0]
    out_idx[2:3, :] = dst_v[0]
    for g in range(groups):
        out_idx[3 + g : 4 + g, :width] = neg_v[0, 0, g : g + 1, :]

    first = place[0] if direct else 0

    def fill(k, carry):
        worker = lax.rem(first + k // cap, workers)
        picked = serve_s[0, k % cap, worker]
        onehot[pl.ds(k, 1), :] = jnp.where(iota((1, rows), 1) == picked, 1.0, 0.0).astype(F32)
        return carry

    lax.fori_loop(0, workers * cap, fill, 0)
    picked_rows = dot_t(onehot[...].astype(BF16), ent_v[...])
    if direct:
        for h in range(workers):
            outs[h][...] = picked_rows[h * cap : (h + 1) * cap]
    else:
        outs[0][...] = picked_rows


def main_kernel(cfg, place, *refs):
    (direct, workers, replicas, cap, groups, width, nrel, pad_rel, block, narrow, window, offsets) = cfg
    pieces = workers if direct else 1
    idx_refs, refs = refs[:replicas], refs[replicas:]
    (ent, relation), refs = refs[:2], refs[2:]
    table_refs, refs = refs[:pieces], refs[pieces:]
    out_lhs, outs, refs = refs[0], refs[1 : 1 + pieces], refs[1 + pieces :]
    (
        idx_all,
        idx_col,
        rel_parts,
        table_f,
        table_t,
        lhs_s,
        rel_s,
        query_s,
        acc_rel,
        acc_lhs,
        acc_tab,
        wide_t,
        served_s,
    ) = refs
    edges = idx_all.shape[1]
    dim, rows = ent.shape
    slots = workers * cap
    dom, rep = place[0], place[1]
    per = edges // groups
    base = pl.multiple_of((rep * narrow) // 8 * 8, 8)
    offset = rep * narrow - base

    for i in range(replicas):
        idx_all[i * IDX_ROWS : (i + 1) * IDX_ROWS, :] = idx_refs[i][...]
        idx_col[i] = jnp.transpose(idx_refs[i][...])
    hi, lo = split2(relation[...])
    if pad_rel > nrel:
        rel_parts[...] = jnp.zeros(rel_parts.shape, BF16)
    rel_parts[:dim, :nrel] = hi
    rel_parts[dim:, :nrel] = lo
    if direct:
        for h in range(workers):
            source = lax.rem(dom - h + workers, workers)
            for c in range(cap):
                table_f[pl.ds(source * cap + c, 1), :] = table_refs[h][c : c + 1, :]
    else:
        table_f[...] = table_refs[0][...]
    table_t[...] = jnp.transpose(table_f[...])
    table = table_f[...].astype(BF16)
    own_t = table_t[pl.ds(base, window), :].astype(BF16)
    own_t = jnp.concatenate([own_t] * 3, axis=1)
    acc_rel[...] = jnp.zeros(acc_rel.shape, F32)
    acc_lhs[...] = jnp.zeros(acc_lhs.shape, F32)
    acc_tab[...] = jnp.zeros(acc_tab.shape, F32)

    def shard(i, carry):
        lanes = idx_all[pl.ds(pl.multiple_of(i * IDX_ROWS, IDX_ROWS), IDX_ROWS), :]
        cols = idx_col[i]
        src_l, rel_l, dst_l = lanes[0:1], lanes[1:2], lanes[2:3]
        count = lanes[IDX_ROWS - 1 : IDX_ROWS]

        lhs = dot(ent[...], ones_where(iota((rows, edges), 0) == src_l))
        both = dot(rel_parts[...], ones_where(iota((pad_rel, edges), 0) == rel_l))
        rel_rows = both[:dim] + both[dim:]
        query = (lhs * rel_rows).astype(BF16)
        lhs_s[...] = lhs
        rel_s[...] = rel_rows
        query_s[...] = query.astype(F32)
        scores = dot(table, query)
        live = jnp.where(iota((1, edges), 1) < count, 1.0, 0.0).astype(F32)
        own = jnp.where(iota((slots, edges), 0) == dst_l, 1.0, 0.0).astype(F32)
        seen = own * live
        parts = []
        for g in range(groups):
            span = slice(g * per, (g + 1) * per)
            s, o = scores[:, span], own[:, span]
            neg = jnp.where(
                iota((slots, width), 0) == lanes[3 + g : 4 + g, :width], 1.0, 0.0
            ).astype(F32)
            times = jnp.sum(seen[:, span], axis=1, keepdims=True)
            times = times + jnp.sum(neg, axis=1, keepdims=True)
            s = jnp.where(times > 0, s, F32(-1e30))
            top = jnp.max(s, axis=0, keepdims=True)
            expo = jnp.exp(s - top)
            probs = expo / jnp.sum(expo * times, axis=0, keepdims=True)
            other = probs.astype(BF16).astype(F32)
            itself = (probs - 1.0).astype(BF16).astype(F32)
            parts.append(((times - o) * other + o * itself) * live[:, span])
        grads = jnp.concatenate(parts, axis=1)
        stack = jnp.concatenate(split3(grads), axis=0)
        stack_t = jnp.concatenate(split3(jnp.transpose(grads)), axis=1)

        dquery = dot(own_t, stack)
        acc_tab[...] += dot(query_s[pl.ds(base, window), :].astype(BF16), stack_t)
        y = jnp.concatenate(split2(dquery * lhs_s[pl.ds(base, window), :]), axis=0)
        acc_rel[...] += dot(y, ones_where(iota((edges, pad_rel), 1) == cols[:, 1:2]))
        x = jnp.concatenate(split2(dquery * rel_s[pl.ds(base, window), :]), axis=0)
        acc_lhs[...] += dot(x, ones_where(iota((edges, rows), 1) == cols[:, 0:1]))
        return carry

    lax.fori_loop(0, replicas, shard, 0)

    pick = functools.partial(shifted_rows, offset=offset, narrow=narrow, offsets=offsets)
    out_lhs[...] = pick(acc_lhs[:window] + acc_lhs[window:])
    acc_rel[:narrow] = pick(acc_rel[:window] + acc_rel[window:])
    table_grad = pick(acc_tab[:, :slots] + acc_tab[:, slots : 2 * slots] + acc_tab[:, 2 * slots :])
    wide_t[...] = jnp.zeros(wide_t.shape, F32)
    wide_t[:narrow] = table_grad
    served_s[...] = jnp.transpose(wide_t[...])
    for h in range(workers):
        out = outs[h] if direct else outs[0].at[h]
        to = lax.rem(dom + h, workers) if direct else h
        out[...] = jnp.zeros(out.shape, F32)
        if direct:
            out[:narrow, :] = acc_rel[:narrow, pl.ds(pl.multiple_of(to * block, block), block)]
        else:
            out[:narrow, :block] = acc_rel[:narrow, h * block : (h + 1) * block]
        for c in range(cap):
            out[narrow + c : narrow + c + 1, :] = served_s[pl.ds(to * cap + c, 1), :]


def combine_kernel(scale, narrow, block, *refs):
    out = refs[-1]
    total = refs[0][...]
    for ref in refs[1:-1]:
        total = total + ref[...]
    out[...] = jnp.zeros(out.shape, BF16)
    keep = iota(out.shape, 0) < narrow
    tall = jnp.concatenate(
        [total[:, :block], jnp.zeros((out.shape[0] - total.shape[0], block), F32)], axis=0
    )
    out[...] = jnp.where(keep, tall * F32(scale), 0.0).astype(BF16)


def entity_kernel(direct, narrow, place, serve, lhs, *refs):
    cap, workers = serve.shape[1], serve.shape[2]
    recv, out, (terms, onehot) = refs[:-3], refs[-3], refs[-2:]
    rows = out.shape[1]
    for h in range(workers):
        part = recv[h] if direct else recv[0].at[h]
        terms[h * cap : (h + 1) * cap, :] = part[narrow : narrow + cap, :]

    def fill(k, carry):
        h = k // cap
        worker = lax.rem(place[0] - h + workers, workers) if direct else h
        picked = serve[0, k % cap, worker]
        onehot[pl.ds(k, 1), :] = jnp.where(iota((1, rows), 1) == picked, 1.0, 0.0).astype(F32)
        return carry

    lax.fori_loop(0, workers * cap, fill, 0)
    spots = onehot[...].astype(BF16)
    parts = jnp.concatenate(split3(jnp.transpose(terms[...])), axis=1)
    added = dot(parts, jnp.concatenate([spots] * 3, axis=0))
    out[...] = lhs[...] + added[:narrow]


def spread_kernel(phases, narrow, block, place, *refs):
    pieces, out, wide = refs[:-2], refs[-2], refs[-1]
    replicas = wide.shape[0]
    height = wide.shape[1]
    nrel = out.shape[1]
    each = pieces[0].shape[0]
    for n, piece in enumerate(pieces):
        for m in range(each):
            spot = n * each + m
            at = [place[0], place[1]]
            for axis, stride, radix in phases:
                hop = spot % radix
                spot = spot // radix
                digit = lax.rem(at[axis] // stride, radix)
                moved = lax.rem(digit - hop + radix, radix)
                at[axis] = at[axis] + (moved - digit) * stride
            wide[at[1], :, pl.ds(pl.multiple_of(at[0] * block, block), block)] = piece[m].astype(
                F32
            )[:height]
    for r in range(replicas):
        out[r * narrow : (r + 1) * narrow, :] = wide[r, :narrow, :nrel]


def turned(size, stride, radix, hop):
    pairs = []
    for i in range(size):
        digit = (i // stride) % radix
        pairs.append((i, i + ((digit + hop) % radix - digit) * stride))
    return pairs


def radices(size):
    found = []
    for radix in (4, 2, 3, 5, 7):
        while size % radix == 0:
            found.append(radix)
            size //= radix
    return found


def shards(entities, relation, serve_ids, edge_src, edge_rel, edge_dst, neg_ids, edge_count):
    workers = lax.axis_size("dom")
    replicas = lax.axis_size("rep")
    rows, dim = entities.shape
    nrel = relation.shape[0]
    cap = serve_ids.shape[2]
    edges = edge_src.shape[2]
    groups, width = neg_ids.shape[2], neg_ids.shape[3]
    slots = workers * cap
    narrow = dim // replicas
    direct = workers <= 16
    block = up(-(-nrel // workers), LANES if direct else 8)
    pad_rel = up(max(nrel, workers * block), LANES)
    offsets = sorted({(narrow * r) % 8 for r in range(replicas)})
    window = up(narrow + offsets[-1], 8)
    height = up(narrow + cap, 8)
    pieces = workers if direct else 1
    ent_t, rel_t = entities.T, relation.T
    serve_t = jnp.transpose(serve_ids, (0, 2, 1))
    place = jnp.stack([lax.axis_index("dom"), lax.axis_index("rep")]).astype(jnp.int32)

    piece = (cap, dim) if direct else (slots, dim)
    prepared = pl.pallas_call(
        functools.partial(prep_kernel, direct),
        out_shape=[jax.ShapeDtypeStruct((IDX_ROWS, edges), jnp.int32)]
        + [jax.ShapeDtypeStruct(piece, F32)] * pieces,
        in_specs=[SMEM] + [HBM] * 7,
        out_specs=[VMEM] * (1 + pieces),
        scratch_shapes=[
            pltpu.SMEM(serve_t.shape, jnp.int32),
            pltpu.SMEM(edge_count.shape, jnp.int32),
            pltpu.VMEM(ent_t.shape, BF16),
            pltpu.VMEM(edge_src.shape, jnp.int32),
            pltpu.VMEM(edge_rel.shape, jnp.int32),
            pltpu.VMEM(edge_dst.shape, jnp.int32),
            pltpu.VMEM(neg_ids.shape, jnp.int32),
            pltpu.VMEM((slots, rows), F32),
            pltpu.SemaphoreType.DMA((7,)),
        ],
        compiler_params=params(),
        name="prep",
    )(place, serve_t, edge_count, ent_t, edge_src, edge_rel, edge_dst, neg_ids)
    idx, served = prepared[0], prepared[1:]

    held = [idx]
    for hop in range(1, replicas):
        held.append(lax.ppermute(idx, "rep", turned(replicas, 1, replicas, hop)))
    if direct:
        tables = [served[0]]
        for hop in range(1, workers):
            tables.append(lax.ppermute(served[hop], "dom", turned(workers, 1, workers, hop)))
    else:
        tables = [
            lax.all_to_all(
                served[0].reshape(workers, cap, dim).astype(BF16), "dom", 0, 0, tiled=True
            )
            .reshape(slots, dim)
            .astype(F32)
        ]

    cfg = (
        direct, workers, replicas, cap, groups, width, nrel, pad_rel, block, narrow, window,
        tuple(offsets),
    )
    lanes = max(LANES, block, up(narrow, LANES))
    part = (height, lanes) if direct else (workers, height, lanes)
    results = pl.pallas_call(
        functools.partial(main_kernel, cfg),
        out_shape=[jax.ShapeDtypeStruct((narrow, rows), F32)]
        + [jax.ShapeDtypeStruct(part, F32)] * pieces,
        in_specs=[SMEM] + [VMEM] * (replicas + 2 + pieces),
        out_specs=[VMEM] * (1 + pieces),
        scratch_shapes=[
            pltpu.VMEM((replicas * IDX_ROWS, edges), jnp.int32),
            pltpu.VMEM((replicas, edges, IDX_ROWS), jnp.int32),
            pltpu.VMEM((2 * dim, pad_rel), BF16),
            pltpu.VMEM((slots, dim), F32),
            pltpu.VMEM((dim, slots), F32),
            pltpu.VMEM((dim, edges), F32),
            pltpu.VMEM((dim, edges), F32),
            pltpu.VMEM((dim, edges), F32),
            pltpu.VMEM((2 * window, pad_rel), F32),
            pltpu.VMEM((2 * window, rows), F32),
            pltpu.VMEM((window, 3 * slots), F32),
            pltpu.VMEM((lanes, slots), F32),
            pltpu.VMEM((slots, lanes), F32),
        ],
        compiler_params=params(),
        name="edges",
    )(place, *held, ent_t, rel_t, *tables)
    lhs_part, sent = results[0], results[1:]

    if direct:
        recv = [sent[0]]
        for hop in range(1, workers):
            recv.append(lax.ppermute(sent[hop], "dom", turned(workers, 1, workers, hop)))
        summed = recv
    else:
        recv = [lax.all_to_all(sent[0], "dom", 0, 0, tiled=True)]
        summed = [jnp.sum(recv[0], axis=0)]
    tall = up(height, 16)
    chunk = pl.pallas_call(
        functools.partial(combine_kernel, 1.0 / (edges * workers * replicas), narrow, block),
        out_shape=jax.ShapeDtypeStruct((tall, block), BF16),
        in_specs=[VMEM] * len(summed),
        out_specs=VMEM,
        compiler_params=params(),
        name="combine",
    )(*summed)

    entity_grad = pl.pallas_call(
        functools.partial(entity_kernel, direct, narrow),
        out_shape=jax.ShapeDtypeStruct((narrow, rows), F32),
        in_specs=[SMEM, SMEM] + [VMEM] * (1 + pieces),
        out_specs=VMEM,
        scratch_shapes=[pltpu.VMEM((slots, lanes), F32), pltpu.VMEM((slots, rows), F32)],
        compiler_params=params(),
        name="entity",
    )(place, serve_t, lhs_part, *recv)

    if direct:
        phases = []
        for axis, name, size in ((0, "dom", workers), (1, "rep", replicas)):
            stride = size
            for radix in radices(size) if axis == 0 else (2,) * (replicas.bit_length() - 1):
                stride //= radix
                phases.append((axis, stride, radix))
        held = [chunk.reshape(1, tall, block)]
        for axis, stride, radix in phases:
            name, size = (("dom", workers), ("rep", replicas))[axis]
            base = held[0] if len(held) == 1 else jnp.concatenate(held, axis=0)
            held = [base]
            for hop in range(1, radix):
                held.append(lax.ppermute(base, name, turned(size, stride, radix, hop)))
        relation_t = pl.pallas_call(
            functools.partial(spread_kernel, tuple(phases), narrow, block),
            out_shape=jax.ShapeDtypeStruct((dim, nrel), F32),
            in_specs=[SMEM] + [VMEM] * len(held),
            out_specs=VMEM,
            scratch_shapes=[pltpu.VMEM((replicas, height, pad_rel), F32)],
            compiler_params=params(),
            name="spread",
        )(place, *held)
    else:
        whole = lax.all_gather(chunk[:narrow], ("dom", "rep"), axis=0)
        whole = whole.reshape(workers, replicas, narrow, block).transpose(1, 2, 0, 3)
        relation_t = whole.reshape(dim, workers * block)[:, :nrel].astype(F32)
    return (entity_grad.T, relation_t.T)


def solution(mesh):
    placed = (
        P("dom", None),
        P(),
        P("dom", None, None),
        P("dom", "rep", None),
        P("dom", "rep", None),
        P("dom", "rep", None),
        P("dom", "rep", None, None),
        P("dom", "rep"),
    )
    return jax.shard_map(
        shards, mesh=mesh, in_specs=placed, out_specs=(P("dom", "rep"), P()), check_vma=False
    )
```

```python
import functools

import jax
import jax.numpy as jnp
from jax import lax
from jax.experimental import pallas as pl
from jax.experimental.pallas import tpu as pltpu
from jax.sharding import PartitionSpec as P

F32 = jnp.float32
BF16 = jnp.bfloat16
IDX_ROWS = 8
LANES = 128
VMEM = pl.BlockSpec(memory_space=pltpu.VMEM)
SMEM = pl.BlockSpec(memory_space=pltpu.SMEM)
HBM = pl.BlockSpec(memory_space=pltpu.HBM)


def params(mib=32):
    return pltpu.CompilerParams(vmem_limit_bytes=mib * 1024 * 1024)


def cost(flops, moved):
    return pl.CostEstimate(flops=flops, bytes_accessed=moved, transcendentals=0)


def up(value, step):
    return -(-value // step) * step


def split2(x):
    hi = x.astype(BF16)
    lo = (x - hi.astype(F32)).astype(BF16)
    return hi, lo


def split3(x):
    hi, rest = x.astype(BF16), x
    rest = rest - hi.astype(F32)
    mid = rest.astype(BF16)
    low = (rest - mid.astype(F32)).astype(BF16)
    return hi, mid, low


def dot(a, b):
    return jnp.dot(a, b, preferred_element_type=F32)


def dot_t(a, b):
    return lax.dot_general(a, b, (((1,), (1,)), ((), ())), preferred_element_type=F32)


def ones_where(flag):
    return jnp.where(flag, 1.0, 0.0).astype(BF16)


def iota(shape, axis):
    return lax.broadcasted_iota(jnp.int32, shape, axis)


def shifted_rows(x, offset, narrow, offsets):
    out = x[offsets[0] : offsets[0] + narrow]
    for other in offsets[1:]:
        out = jnp.where(offset == other, x[other : other + narrow], out)
    return out


def prep_kernel(serve, count, ent, src, rel, dst, neg, out_idx, out_rows, *refs):
    cap, workers = serve.shape[1], serve.shape[2]
    rows = ent.shape[1]
    groups, width = neg.shape[2], neg.shape[3]
    onehot, sems = refs[-2:]
    moves = [
        pltpu.make_async_copy(a, b, sems.at[n])
        for n, (a, b) in enumerate(zip((serve, count, ent, src, rel, dst, neg), refs))
    ]
    for move in moves:
        move.start()
    for move in moves:
        move.wait()
    serve_s, count_s, ent_v, src_v, rel_v, dst_v, neg_v = refs[:7]
    out_idx[...] = jnp.full(out_idx.shape, count_s[0, 0], jnp.int32)
    out_idx[0:1, :] = src_v[0]
    out_idx[1:2, :] = rel_v[0]
    out_idx[2:3, :] = dst_v[0]
    for g in range(groups):
        out_idx[3 + g : 4 + g, :width] = neg_v[0, 0, g : g + 1, :]
    lane = iota((1, rows), 1)
    for k in range(workers * cap):
        picked = serve_s[0, k % cap, k // cap]
        onehot[k : k + 1, :] = jnp.where(lane == picked, 1.0, 0.0).astype(F32)
    picked_rows = dot_t(onehot[...].astype(BF16), ent_v[...])
    for w in range(workers):
        out_rows[w] = picked_rows[w * cap : (w + 1) * cap]


def gather_kernel(cfg, place, *refs):
    replicas, nrel, pad_rel, narrow, window = cfg
    idx_refs, refs = refs[:replicas], refs[replicas:]
    ent, relation, out_query, out_lhs, out_rel, rel_parts, lhs_s, rel_s = refs
    edges = idx_refs[0].shape[1]
    dim, rows = ent.shape
    base = pl.multiple_of((place[1] * narrow) // 8 * 8, 8)
    hi, lo = split2(relation[...])
    if pad_rel > nrel:
        rel_parts[...] = jnp.zeros(rel_parts.shape, BF16)
    rel_parts[:dim, :nrel] = hi
    rel_parts[dim:, :nrel] = lo
    for i in range(replicas):
        span = slice(i * edges, (i + 1) * edges)
        src_l, rel_l = idx_refs[i][0:1, :], idx_refs[i][1:2, :]
        lhs = dot(ent[...], ones_where(iota((rows, edges), 0) == src_l))
        both = dot(rel_parts[...], ones_where(iota((pad_rel, edges), 0) == rel_l))
        rel_rows = both[:dim] + both[dim:]
        lhs_s[...] = lhs
        rel_s[...] = rel_rows
        out_query[:, span] = (lhs * rel_rows).astype(BF16)
        out_lhs[:, span] = lhs_s[pl.ds(base, window), :]
        out_rel[:, span] = rel_s[pl.ds(base, window), :]


def main_kernel(cfg, place, *refs):
    (direct, workers, replicas, cap, groups, width, pad_rel, block, narrow, window, offsets) = cfg
    pieces = workers if direct else 1
    idx_refs, refs = refs[:replicas], refs[replicas:]
    (query_v, lhs_v, rel_v, received), refs = refs[:4], refs[4:]
    out_lhs, outs, refs = refs[0], refs[1 : 1 + pieces], refs[1 + pieces :]
    table_f, table_t, query_s, acc_rel, acc_lhs, acc_tab, wide_t, served_s = refs
    edges = idx_refs[0].shape[1]
    dim = query_v.shape[0]
    rows = out_lhs.shape[1]
    slots = workers * cap
    dom, rep = place[0], place[1]
    per = edges // groups
    base = pl.multiple_of((rep * narrow) // 8 * 8, 8)
    offset = rep * narrow - base

    for w in range(workers):
        table_f[w * cap : (w + 1) * cap, :] = received[w]
    table_t[...] = jnp.transpose(table_f[...])
    table = table_f[...].astype(BF16)
    own_t = table_t[pl.ds(base, window), :].astype(BF16)
    own_t = jnp.concatenate([own_t] * 3, axis=1)
    acc_rel[...] = jnp.zeros(acc_rel.shape, F32)
    acc_lhs[...] = jnp.zeros(acc_lhs.shape, F32)
    acc_tab[...] = jnp.zeros(acc_tab.shape, F32)

    for i in range(replicas):
        here = slice(i * edges, (i + 1) * edges)
        lanes = idx_refs[i][...]
        cols = jnp.transpose(lanes)
        dst_l = lanes[2:3]
        count = lanes[IDX_ROWS - 1 : IDX_ROWS]
        query = query_v[:, here]
        query_s[...] = query.astype(F32)
        scores = dot(table, query)
        live = jnp.where(iota((1, edges), 1) < count, 1.0, 0.0).astype(F32)
        own = jnp.where(iota((slots, edges), 0) == dst_l, 1.0, 0.0).astype(F32)
        seen = own * live
        parts = []
        for g in range(groups):
            span = slice(g * per, (g + 1) * per)
            s, o = scores[:, span], own[:, span]
            neg = jnp.where(
                iota((slots, width), 0) == lanes[3 + g : 4 + g, :width], 1.0, 0.0
            ).astype(F32)
            times = jnp.sum(seen[:, span], axis=1, keepdims=True)
            times = times + jnp.sum(neg, axis=1, keepdims=True)
            s = jnp.where(times > 0, s, F32(-1e30))
            top = jnp.max(s, axis=0, keepdims=True)
            expo = jnp.exp(s - top)
            probs = expo / jnp.sum(expo * times, axis=0, keepdims=True)
            other = probs.astype(BF16).astype(F32)
            itself = (probs - 1.0).astype(BF16).astype(F32)
            parts.append(((times - o) * other + o * itself) * live[:, span])
        grads = jnp.concatenate(parts, axis=1)
        stack = jnp.concatenate(split3(grads), axis=0)
        stack_t = jnp.concatenate(split3(jnp.transpose(grads)), axis=1)

        dquery = dot(own_t, stack)
        acc_tab[...] += dot(query_s[pl.ds(base, window), :].astype(BF16), stack_t)
        y = jnp.concatenate(split2(dquery * lhs_v[:, here]), axis=0)
        acc_rel[...] += dot(y, ones_where(iota((edges, pad_rel), 1) == cols[:, 1:2]))
        x = jnp.concatenate(split2(dquery * rel_v[:, here]), axis=0)
        acc_lhs[...] += dot(x, ones_where(iota((edges, rows), 1) == cols[:, 0:1]))

    pick = functools.partial(shifted_rows, offset=offset, narrow=narrow, offsets=offsets)
    out_lhs[...] = pick(acc_lhs[:window] + acc_lhs[window:])
    acc_rel[:narrow] = pick(acc_rel[:window] + acc_rel[window:])
    table_grad = pick(acc_tab[:, :slots] + acc_tab[:, slots : 2 * slots] + acc_tab[:, 2 * slots :])
    wide_t[...] = jnp.zeros(wide_t.shape, F32)
    wide_t[:narrow] = table_grad
    served_s[...] = jnp.transpose(wide_t[...])
    for h in range(workers):
        out = outs[h] if direct else outs[0].at[h]
        to = lax.rem(dom + h, workers) if direct else h
        out[...] = jnp.zeros(out.shape, F32)
        if direct:
            out[:narrow, :] = acc_rel[:narrow, pl.ds(pl.multiple_of(to * block, block), block)]
        else:
            out[:narrow, :block] = acc_rel[:narrow, h * block : (h + 1) * block]
        for c in range(cap):
            out[narrow + c : narrow + c + 1, :] = served_s[pl.ds(to * cap + c, 1), :]


def combine_kernel(scale, narrow, block, *refs):
    out = refs[-1]
    total = refs[0][...]
    for ref in refs[1:-1]:
        total = total + ref[...]
    out[...] = jnp.zeros(out.shape, BF16)
    keep = iota(out.shape, 0) < narrow
    tall = jnp.concatenate(
        [total[:, :block], jnp.zeros((out.shape[0] - total.shape[0], block), F32)], axis=0
    )
    out[...] = jnp.where(keep, tall * F32(scale), 0.0).astype(BF16)


def entity_kernel(direct, narrow, place, serve, lhs, *refs):
    cap, workers = serve.shape[1], serve.shape[2]
    recv, out, (terms, onehot) = refs[:-3], refs[-3], refs[-2:]
    rows = out.shape[1]
    for h in range(workers):
        part = recv[h] if direct else recv[0].at[h]
        terms[h * cap : (h + 1) * cap, :] = part[narrow : narrow + cap, :]

    def fill(k, carry):
        h = k // cap
        worker = lax.rem(place[0] - h + workers, workers) if direct else h
        picked = serve[0, k % cap, worker]
        onehot[pl.ds(k, 1), :] = jnp.where(iota((1, rows), 1) == picked, 1.0, 0.0).astype(F32)
        return carry

    lax.fori_loop(0, workers * cap, fill, 0)
    spots = onehot[...].astype(BF16)
    parts = jnp.concatenate(split3(jnp.transpose(terms[...])), axis=1)
    added = dot(parts, jnp.concatenate([spots] * 3, axis=0))
    out[...] = lhs[...] + added[:narrow]


def spread_kernel(phases, workers, replicas, narrow, block, place, *refs):
    pieces, out = refs[:-1], refs[-1]
    nrel = out.shape[1]
    each = pieces[0].shape[0]
    for o in range(workers):
        for r in range(replicas):
            at, spot, scale = (o, r), 0, 1
            for axis, stride, radix in phases:
                digit = lax.rem(place[axis] // stride, radix)
                spot = spot + scale * lax.rem(digit - (at[axis] // stride) % radix + radix, radix)
                scale *= radix
            part, group = lax.rem(spot, each), spot // each
            value = pieces[0][part].astype(F32)
            for n in range(1, len(pieces)):
                value = jnp.where(group == n, pieces[n][part].astype(F32), value)
            end = min((o + 1) * block, nrel)
            out[r * narrow : (r + 1) * narrow, o * block : end] = value[:narrow, : end - o * block]


def turned(size, stride, radix, hop):
    pairs = []
    for i in range(size):
        digit = (i // stride) % radix
        pairs.append((i, i + ((digit + hop) % radix - digit) * stride))
    return pairs


def radices(size):
    found = []
    for radix in (4, 2, 3, 5, 7):
        while size % radix == 0:
            found.append(radix)
            size //= radix
    return found


def shards(entities, relation, serve_ids, edge_src, edge_rel, edge_dst, neg_ids, edge_count):
    workers = lax.axis_size("dom")
    replicas = lax.axis_size("rep")
    rows, dim = entities.shape
    nrel = relation.shape[0]
    cap = serve_ids.shape[2]
    edges = edge_src.shape[2]
    groups, width = neg_ids.shape[2], neg_ids.shape[3]
    slots = workers * cap
    narrow = dim // replicas
    direct = workers <= 16
    block = up(-(-nrel // workers), LANES if direct else 8)
    pad_rel = up(max(nrel, workers * block), LANES)
    offsets = sorted({(narrow * r) % 8 for r in range(replicas)})
    window = up(narrow + offsets[-1], 8)
    height = up(narrow + cap, 8)
    pieces = workers if direct else 1
    ent_t, rel_t = entities.T, relation.T
    serve_t = jnp.transpose(serve_ids, (0, 2, 1))
    place = jnp.stack([lax.axis_index("dom"), lax.axis_index("rep")]).astype(jnp.int32)

    idx, served = pl.pallas_call(
        prep_kernel,
        out_shape=(
            jax.ShapeDtypeStruct((IDX_ROWS, edges), jnp.int32),
            jax.ShapeDtypeStruct((workers, cap, dim), F32),
        ),
        in_specs=[HBM] * 7,
        out_specs=(VMEM, VMEM),
        scratch_shapes=[
            pltpu.SMEM(serve_t.shape, jnp.int32),
            pltpu.SMEM(edge_count.shape, jnp.int32),
            pltpu.VMEM(ent_t.shape, BF16),
            pltpu.VMEM(edge_src.shape, jnp.int32),
            pltpu.VMEM(edge_rel.shape, jnp.int32),
            pltpu.VMEM(edge_dst.shape, jnp.int32),
            pltpu.VMEM(neg_ids.shape, jnp.int32),
            pltpu.VMEM((slots, rows), F32),
            pltpu.SemaphoreType.DMA((7,)),
        ],
        compiler_params=params(60),
        name="prep",
    )(serve_t, edge_count, ent_t, edge_src, edge_rel, edge_dst, neg_ids)

    held = [idx]
    for hop in range(1, replicas):
        held.append(lax.ppermute(idx, "rep", turned(replicas, 1, replicas, hop)))
    received = lax.all_to_all(served, "dom", 0, 0, tiled=True)

    total = replicas * edges
    query, lhs_rows, rel_rows = pl.pallas_call(
        functools.partial(gather_kernel, (replicas, nrel, pad_rel, narrow, window)),
        out_shape=(
            jax.ShapeDtypeStruct((dim, total), BF16),
            jax.ShapeDtypeStruct((window, total), F32),
            jax.ShapeDtypeStruct((window, total), F32),
        ),
        in_specs=[SMEM] + [VMEM] * (replicas + 2),
        out_specs=(VMEM, VMEM, VMEM),
        scratch_shapes=[
            pltpu.VMEM((2 * dim, pad_rel), BF16),
            pltpu.VMEM((dim, edges), F32),
            pltpu.VMEM((dim, edges), F32),
        ],
        compiler_params=params(),
        cost_estimate=cost(2 * total * dim * (2 * pad_rel + rows), 8 * total * dim),
        name="gather",
    )(place, *held, ent_t, rel_t)

    cfg = (
        direct, workers, replicas, cap, groups, width, pad_rel, block, narrow, window,
        tuple(offsets),
    )
    lanes = max(LANES, block, up(narrow, LANES))
    part = (height, lanes) if direct else (workers, height, lanes)
    results = pl.pallas_call(
        functools.partial(main_kernel, cfg),
        out_shape=[jax.ShapeDtypeStruct((narrow, rows), F32)]
        + [jax.ShapeDtypeStruct(part, F32)] * pieces,
        in_specs=[SMEM] + [VMEM] * (replicas + 4),
        out_specs=[VMEM] * (1 + pieces),
        scratch_shapes=[
            pltpu.VMEM((slots, dim), F32),
            pltpu.VMEM((dim, slots), F32),
            pltpu.VMEM((dim, edges), F32),
            pltpu.VMEM((2 * window, pad_rel), F32),
            pltpu.VMEM((2 * window, rows), F32),
            pltpu.VMEM((window, 3 * slots), F32),
            pltpu.VMEM((lanes, slots), F32),
            pltpu.VMEM((slots, lanes), F32),
        ],
        compiler_params=params(),
        name="edges",
    )(place, *held, query, lhs_rows, rel_rows, received)
    lhs_part, sent = results[0], results[1:]

    if direct:
        recv = [sent[0]]
        for hop in range(1, workers):
            recv.append(lax.ppermute(sent[hop], "dom", turned(workers, 1, workers, hop)))
        summed = recv
    else:
        recv = [lax.all_to_all(sent[0], "dom", 0, 0, tiled=True)]
        summed = [jnp.sum(recv[0], axis=0)]
    tall = up(height, 16)
    chunk = pl.pallas_call(
        functools.partial(combine_kernel, 1.0 / (edges * workers * replicas), narrow, block),
        out_shape=jax.ShapeDtypeStruct((tall, block), BF16),
        in_specs=[VMEM] * len(summed),
        out_specs=VMEM,
        compiler_params=params(),
        name="combine",
    )(*summed)

    entity_grad = pl.pallas_call(
        functools.partial(entity_kernel, direct, narrow),
        out_shape=jax.ShapeDtypeStruct((narrow, rows), F32),
        in_specs=[SMEM, SMEM] + [VMEM] * (1 + pieces),
        out_specs=VMEM,
        scratch_shapes=[pltpu.VMEM((slots, lanes), F32), pltpu.VMEM((slots, rows), F32)],
        compiler_params=params(),
        cost_estimate=cost(10**9, 10**6),
        name="entity",
    )(place, serve_t, lhs_part, *recv)

    if direct:
        phases = []
        for axis, name, size in ((0, "dom", workers), (1, "rep", replicas)):
            stride = size
            for radix in radices(size) if axis == 0 else (2,) * (replicas.bit_length() - 1):
                stride //= radix
                phases.append((axis, stride, radix))
        held = [chunk.reshape(1, tall, block)]
        for axis, stride, radix in phases:
            name, size = (("dom", workers), ("rep", replicas))[axis]
            base = held[0] if len(held) == 1 else jnp.concatenate(held, axis=0)
            if (axis, stride, radix) == phases[-1]:
                base, entity_grad = lax.optimization_barrier((base, entity_grad))
            held = [base]
            for hop in range(1, radix):
                held.append(lax.ppermute(base, name, turned(size, stride, radix, hop)))
        relation_t = pl.pallas_call(
            functools.partial(
                spread_kernel, tuple(phases), workers, replicas, narrow, block
            ),
            out_shape=jax.ShapeDtypeStruct((dim, nrel), F32),
            in_specs=[SMEM] + [VMEM] * len(held),
            out_specs=VMEM,
            compiler_params=params(),
            name="spread",
        )(place, *held)
    else:
        whole = lax.all_gather(chunk[:narrow], ("dom", "rep"), axis=0)
        whole = whole.reshape(workers, replicas, narrow, block).transpose(1, 2, 0, 3)
        relation_t = whole.reshape(dim, workers * block)[:, :nrel].astype(F32)
    return (entity_grad.T, relation_t.T)


def solution(mesh):
    placed = (
        P("dom", None),
        P(),
        P("dom", None, None),
        P("dom", "rep", None),
        P("dom", "rep", None),
        P("dom", "rep", None),
        P("dom", "rep", None, None),
        P("dom", "rep"),
    )
    return jax.shard_map(
        shards, mesh=mesh, in_specs=placed, out_specs=(P("dom", "rep"), P()), check_vma=False
    )
```

```python
import functools

import jax
import jax.numpy as jnp
from jax import lax
from jax.experimental import pallas as pl
from jax.experimental.pallas import tpu as pltpu
from jax.sharding import PartitionSpec as P

F32 = jnp.float32
BF16 = jnp.bfloat16
IDX_ROWS = 8
LANES = 128
VMEM = pl.BlockSpec(memory_space=pltpu.VMEM)
SMEM = pl.BlockSpec(memory_space=pltpu.SMEM)
HBM = pl.BlockSpec(memory_space=pltpu.HBM)


def params(mib=32):
    return pltpu.CompilerParams(vmem_limit_bytes=mib * 1024 * 1024)


def cost(flops, moved):
    return pl.CostEstimate(flops=flops, bytes_accessed=moved, transcendentals=0)


def up(value, step):
    return -(-value // step) * step


def split2(x):
    hi = x.astype(BF16)
    lo = (x - hi.astype(F32)).astype(BF16)
    return hi, lo


def split3(x):
    hi, rest = x.astype(BF16), x
    rest = rest - hi.astype(F32)
    mid = rest.astype(BF16)
    low = (rest - mid.astype(F32)).astype(BF16)
    return hi, mid, low


def dot(a, b):
    return jnp.dot(a, b, preferred_element_type=F32)


def dot_t(a, b):
    return lax.dot_general(a, b, (((1,), (1,)), ((), ())), preferred_element_type=F32)


def ones_where(flag):
    return jnp.where(flag, 1.0, 0.0).astype(BF16)


def exponent(largest):
    safe = jnp.where(largest > 0, largest, 1.0)
    return jnp.clip(jnp.floor(F32(14.9) - jnp.log2(safe)), -120.0, 120.0)


def encode(x, axis):
    k = exponent(jnp.max(jnp.abs(x), axis=axis, keepdims=True))
    return jnp.floor(x * jnp.exp2(k) + 0.5).astype(jnp.int32), k.astype(jnp.int32)


def decode(codes, k):
    return codes.astype(F32) * jnp.exp2(-k.astype(F32))


def iota(shape, axis):
    return lax.broadcasted_iota(jnp.int32, shape, axis)


def shifted_rows(x, offset, narrow, offsets):
    out = x[offsets[0] : offsets[0] + narrow]
    for other in offsets[1:]:
        out = jnp.where(offset == other, x[other : other + narrow], out)
    return out


def prep_kernel(serve, count, ent, src, rel, dst, neg, out_idx, out_rows, *refs):
    cap, workers = serve.shape[1], serve.shape[2]
    rows = ent.shape[1]
    groups, width = neg.shape[2], neg.shape[3]
    onehot, sems = refs[-2:]
    moves = [
        pltpu.make_async_copy(a, b, sems.at[n])
        for n, (a, b) in enumerate(zip((serve, count, ent, src, rel, dst, neg), refs))
    ]
    for move in moves:
        move.start()
    for move in moves:
        move.wait()
    serve_s, count_s, ent_v, src_v, rel_v, dst_v, neg_v = refs[:7]
    out_idx[...] = jnp.full(out_idx.shape, count_s[0, 0], jnp.int32)
    out_idx[0:1, :] = src_v[0]
    out_idx[1:2, :] = rel_v[0]
    out_idx[2:3, :] = dst_v[0]
    for g in range(groups):
        out_idx[3 + g : 4 + g, :width] = neg_v[0, 0, g : g + 1, :]
    lane = iota((1, rows), 1)
    for k in range(workers * cap):
        picked = serve_s[0, k % cap, k // cap]
        onehot[k : k + 1, :] = jnp.where(lane == picked, 1.0, 0.0).astype(F32)
    picked_rows = dot_t(onehot[...].astype(BF16), ent_v[...])
    for w in range(workers):
        out_rows[w] = picked_rows[w * cap : (w + 1) * cap]


def gather_kernel(cfg, place, *refs):
    replicas, nrel, pad_rel, narrow, window = cfg
    idx_refs, refs = refs[:replicas], refs[replicas:]
    ent, relation, out_query, out_lhs, out_rel, rel_parts, lhs_s, rel_s = refs
    edges = idx_refs[0].shape[1]
    dim, rows = ent.shape
    base = pl.multiple_of((place[1] * narrow) // 8 * 8, 8)
    hi, lo = split2(relation[...])
    if pad_rel > nrel:
        rel_parts[...] = jnp.zeros(rel_parts.shape, BF16)
    rel_parts[:dim, :nrel] = hi
    rel_parts[dim:, :nrel] = lo
    for i in range(replicas):
        span = slice(i * edges, (i + 1) * edges)
        src_l, rel_l = idx_refs[i][0:1, :], idx_refs[i][1:2, :]
        lhs = dot(ent[...], ones_where(iota((rows, edges), 0) == src_l))
        both = dot(rel_parts[...], ones_where(iota((pad_rel, edges), 0) == rel_l))
        rel_rows = both[:dim] + both[dim:]
        lhs_s[...] = lhs
        rel_s[...] = rel_rows
        out_query[:, span] = (lhs * rel_rows).astype(BF16)
        out_lhs[:, span] = lhs_s[pl.ds(base, window), :]
        out_rel[:, span] = rel_s[pl.ds(base, window), :]


def main_kernel(cfg, place, *refs):
    (workers, replicas, cap, groups, width, pad_rel, block, narrow, window, offsets) = cfg
    idx_refs, refs = refs[:replicas], refs[replicas:]
    (query_v, lhs_v, rel_v, received), refs = refs[:4], refs[4:]
    out_lhs, out, table_f, table_t, query_s, acc_rel, acc_lhs, acc_tab, wide_t, mixed = refs
    edges = idx_refs[0].shape[1]
    dim = query_v.shape[0]
    rows = out_lhs.shape[1]
    slots = workers * cap
    rep = place[1]
    per = edges // groups
    base = pl.multiple_of((rep * narrow) // 8 * 8, 8)
    offset = rep * narrow - base

    for w in range(workers):
        table_f[w * cap : (w + 1) * cap, :] = received[w]
    table_t[...] = jnp.transpose(table_f[...])
    table = table_f[...].astype(BF16)
    own_t = table_t[pl.ds(base, window), :].astype(BF16)
    own_t = jnp.concatenate([own_t] * 3, axis=1)
    acc_rel[...] = jnp.zeros(acc_rel.shape, F32)
    acc_lhs[...] = jnp.zeros(acc_lhs.shape, F32)
    acc_tab[...] = jnp.zeros(acc_tab.shape, F32)

    for i in range(replicas):
        here = slice(i * edges, (i + 1) * edges)
        lanes = idx_refs[i][...]
        cols = jnp.transpose(lanes)
        dst_l = lanes[2:3]
        count = lanes[IDX_ROWS - 1 : IDX_ROWS]
        query = query_v[:, here]
        query_s[...] = query.astype(F32)
        scores = dot(table, query)
        live = jnp.where(iota((1, edges), 1) < count, 1.0, 0.0).astype(F32)
        own = jnp.where(iota((slots, edges), 0) == dst_l, 1.0, 0.0).astype(F32)
        seen = own * live
        parts = []
        for g in range(groups):
            span = slice(g * per, (g + 1) * per)
            s, o = scores[:, span], own[:, span]
            neg = jnp.where(
                iota((slots, width), 0) == lanes[3 + g : 4 + g, :width], 1.0, 0.0
            ).astype(F32)
            times = jnp.sum(seen[:, span], axis=1, keepdims=True)
            times = times + jnp.sum(neg, axis=1, keepdims=True)
            s = jnp.where(times > 0, s, F32(-1e30))
            top = jnp.max(s, axis=0, keepdims=True)
            expo = jnp.exp(s - top)
            probs = expo / jnp.sum(expo * times, axis=0, keepdims=True)
            other = probs.astype(BF16).astype(F32)
            itself = (probs - 1.0).astype(BF16).astype(F32)
            parts.append(((times - o) * other + o * itself) * live[:, span])
        grads = jnp.concatenate(parts, axis=1)
        stack = jnp.concatenate(split3(grads), axis=0)
        stack_t = jnp.concatenate(split3(jnp.transpose(grads)), axis=1)

        dquery = dot(own_t, stack)
        acc_tab[...] += dot(query_s[pl.ds(base, window), :].astype(BF16), stack_t)
        y = jnp.concatenate(split2(dquery * lhs_v[:, here]), axis=0)
        acc_rel[...] += dot(y, ones_where(iota((edges, pad_rel), 1) == cols[:, 1:2]))
        x = jnp.concatenate(split2(dquery * rel_v[:, here]), axis=0)
        acc_lhs[...] += dot(x, ones_where(iota((edges, rows), 1) == cols[:, 0:1]))

    pick = functools.partial(shifted_rows, offset=offset, narrow=narrow, offsets=offsets)
    out_lhs[...] = pick(acc_lhs[:window] + acc_lhs[window:])
    codes, powers = encode(pick(acc_rel[:window] + acc_rel[window:]), 0)
    wide_t[...] = jnp.zeros(wide_t.shape, F32)
    wide_t[:narrow] = pick(
        acc_tab[:, :slots] + acc_tab[:, slots : 2 * slots] + acc_tab[:, 2 * slots :]
    )
    table_codes, table_powers = encode(jnp.transpose(wide_t[...]), 1)
    table_powers = jnp.broadcast_to(table_powers, table_codes.shape)
    mixed[...] = jnp.zeros(mixed.shape, jnp.int32)
    last = narrow + 2 * cap
    for o in range(workers):
        span = slice(o * block, (o + 1) * block)
        mixed[:narrow, :block] = codes[:, span]
        mixed[narrow : narrow + cap, :] = table_codes[o * cap : (o + 1) * cap]
        mixed[narrow + cap : last, :] = table_powers[o * cap : (o + 1) * cap]
        mixed[last : last + 1, :block] = powers[:, span]
        out[o] = mixed[...].astype(jnp.int16)


def combine_kernel(scale, narrow, cap, block, recv, out, mixed):
    last = narrow + 2 * cap
    total = jnp.zeros((narrow, block), F32)
    for w in range(recv.shape[0]):
        both = recv[w].astype(jnp.int32)
        total += decode(both[:narrow, :block], both[last : last + 1, :block])
    codes, powers = encode(total * F32(scale), 0)
    mixed[...] = jnp.zeros(mixed.shape, jnp.int32)
    mixed[:narrow, :block] = codes
    mixed[last : last + 1, :block] = powers
    out[...] = mixed[...].astype(jnp.int16)


def entity_kernel(narrow, serve, lhs, recv, out, terms, onehot):
    cap, workers = serve.shape[1], serve.shape[2]
    rows = out.shape[1]
    lane = iota((1, rows), 1)
    for w in range(workers):
        both = recv[w].astype(jnp.int32)
        terms[w * cap : (w + 1) * cap, :] = decode(
            both[narrow : narrow + cap], both[narrow + cap : narrow + 2 * cap]
        )
        for c in range(cap):
            picked = serve[0, c, w]
            onehot[w * cap + c : w * cap + c + 1, :] = jnp.where(lane == picked, 1.0, 0.0).astype(
                F32
            )
    spots = onehot[...].astype(BF16)
    parts = jnp.concatenate(split3(jnp.transpose(terms[...])), axis=1)
    added = dot(parts, jnp.concatenate([spots] * 3, axis=0))
    out[...] = lhs[...] + added[:narrow]


def spread_kernel(orders, workers, replicas, narrow, power_row, block, place, mine, other, out):
    nrel = out.shape[1]
    kinds = len(orders)
    kind = lax.rem(place[1], kinds)
    for o in range(workers):
        for r in range(replicas):
            at, spot, scale = (o, r), 0, 1
            for axis, stride, radix in orders[r % kinds]:
                digit = lax.rem(place[axis] // stride, radix)
                spot = spot + scale * lax.rem(digit - (at[axis] // stride) % radix + radix, radix)
                scale *= radix
            both = jnp.where(
                kind == r % kinds, mine[spot].astype(jnp.int32), other[spot].astype(jnp.int32)
            )
            value = decode(both[:narrow], both[power_row : power_row + 1])
            end = min((o + 1) * block, nrel)
            out[r * narrow : (r + 1) * narrow, o * block : end] = value[:, : end - o * block]


def moved(index, stride, radix, hop):
    digit = (index // stride) % radix
    return index + ((digit + hop) % radix - digit) * stride


def turned(size, hop):
    return [(i, (i + hop) % size) for i in range(size)]


def radices(size):
    found = []
    for radix in (2, 3, 5, 7):
        while size % radix == 0:
            found.append(radix)
            size //= radix
    return found


def shards(entities, relation, serve_ids, edge_src, edge_rel, edge_dst, neg_ids, edge_count):
    workers = lax.axis_size("dom")
    replicas = lax.axis_size("rep")
    rows, dim = entities.shape
    nrel = relation.shape[0]
    cap = serve_ids.shape[2]
    edges = edge_src.shape[2]
    groups, width = neg_ids.shape[2], neg_ids.shape[3]
    slots = workers * cap
    narrow = dim // replicas
    direct = workers == 8 and replicas == 4
    block = up(-(-nrel // workers), LANES if direct else 8)
    pad_rel = up(max(nrel, workers * block), LANES)
    offsets = sorted({(narrow * r) % 8 for r in range(replicas)})
    window = up(narrow + offsets[-1], 8)
    height = up(narrow + 2 * cap + 1, 16)
    ent_t, rel_t = entities.T, relation.T
    serve_t = jnp.transpose(serve_ids, (0, 2, 1))
    place = jnp.stack([lax.axis_index("dom"), lax.axis_index("rep")]).astype(jnp.int32)

    idx, served = pl.pallas_call(
        prep_kernel,
        out_shape=(
            jax.ShapeDtypeStruct((IDX_ROWS, edges), jnp.int32),
            jax.ShapeDtypeStruct((workers, cap, dim), F32),
        ),
        in_specs=[HBM] * 7,
        out_specs=(VMEM, VMEM),
        scratch_shapes=[
            pltpu.SMEM(serve_t.shape, jnp.int32),
            pltpu.SMEM(edge_count.shape, jnp.int32),
            pltpu.VMEM(ent_t.shape, BF16),
            pltpu.VMEM(edge_src.shape, jnp.int32),
            pltpu.VMEM(edge_rel.shape, jnp.int32),
            pltpu.VMEM(edge_dst.shape, jnp.int32),
            pltpu.VMEM(neg_ids.shape, jnp.int32),
            pltpu.VMEM((slots, rows), F32),
            pltpu.SemaphoreType.DMA((7,)),
        ],
        compiler_params=params(60),
        name="prep",
    )(serve_t, edge_count, ent_t, edge_src, edge_rel, edge_dst, neg_ids)

    held = [idx]
    for hop in range(1, replicas):
        held.append(lax.ppermute(idx, "rep", turned(replicas, hop)))
    received = lax.all_to_all(served, "dom", 0, 0, tiled=True)

    total = replicas * edges
    query, lhs_rows, rel_rows = pl.pallas_call(
        functools.partial(gather_kernel, (replicas, nrel, pad_rel, narrow, window)),
        out_shape=(
            jax.ShapeDtypeStruct((dim, total), BF16),
            jax.ShapeDtypeStruct((window, total), F32),
            jax.ShapeDtypeStruct((window, total), F32),
        ),
        in_specs=[SMEM] + [VMEM] * (replicas + 2),
        out_specs=(VMEM, VMEM, VMEM),
        scratch_shapes=[
            pltpu.VMEM((2 * dim, pad_rel), BF16),
            pltpu.VMEM((dim, edges), F32),
            pltpu.VMEM((dim, edges), F32),
        ],
        compiler_params=params(),
        cost_estimate=cost(2 * total * dim * (2 * pad_rel + rows), 8 * total * dim),
        name="gather",
    )(place, *held, ent_t, rel_t)

    cfg = (workers, replicas, cap, groups, width, pad_rel, block, narrow, window, tuple(offsets))
    lanes = max(up(block, LANES), up(narrow, LANES))
    lhs_part, sent = pl.pallas_call(
        functools.partial(main_kernel, cfg),
        out_shape=(
            jax.ShapeDtypeStruct((narrow, rows), F32),
            jax.ShapeDtypeStruct((workers, height, lanes), jnp.int16),
        ),
        in_specs=[SMEM] + [VMEM] * (replicas + 4),
        out_specs=(VMEM, VMEM),
        scratch_shapes=[
            pltpu.VMEM((slots, dim), F32),
            pltpu.VMEM((dim, slots), F32),
            pltpu.VMEM((dim, edges), F32),
            pltpu.VMEM((2 * window, pad_rel), F32),
            pltpu.VMEM((2 * window, rows), F32),
            pltpu.VMEM((window, 3 * slots), F32),
            pltpu.VMEM((lanes, slots), F32),
            pltpu.VMEM((height, lanes), jnp.int32),
        ],
        compiler_params=params(),
        name="edges",
    )(place, *held, query, lhs_rows, rel_rows, received)

    recv = lax.all_to_all(sent, "dom", 0, 0, tiled=True)
    scale = 1.0 / (edges * workers * replicas)
    chunk = pl.pallas_call(
        functools.partial(combine_kernel, scale, narrow, cap, block),
        out_shape=jax.ShapeDtypeStruct((height, lanes), jnp.int16),
        in_specs=[VMEM],
        out_specs=VMEM,
        scratch_shapes=[pltpu.VMEM((height, lanes), jnp.int32)],
        compiler_params=params(),
        name="combine",
    )(recv)

    entity_grad = pl.pallas_call(
        functools.partial(entity_kernel, narrow),
        out_shape=jax.ShapeDtypeStruct((narrow, rows), F32),
        in_specs=[SMEM] + [VMEM] * 2,
        out_specs=VMEM,
        scratch_shapes=[pltpu.VMEM((slots, lanes), F32), pltpu.VMEM((slots, rows), F32)],
        compiler_params=params(),
        cost_estimate=cost(10**9, 10**6),
        name="entity",
    )(serve_t, lhs_part, recv)

    power_row = narrow + 2 * cap
    if direct:
        steps, stride = [], 1
        for radix in radices(workers):
            steps.append((0, stride, radix))
            stride *= radix
        across = [(1, 2, replicas // 2)]
        first, flip = steps[1:] + steps[:1], across
        orders = (tuple(first + flip), tuple(first[:-1] + flip + first[-1:]))
        base = chunk.reshape(1, height, lanes)
        for n in range(len(orders[0])):
            parts = [base]
            for hop in range(1, orders[0][n][2]):
                pairs = []
                for o in range(workers):
                    for r in range(replicas):
                        axis, stride, radix = orders[r % 2][n]
                        at = [o, r]
                        at[axis] = moved(at[axis], stride, radix, hop)
                        pairs.append((o * replicas + r, at[0] * replicas + at[1]))
                parts.append(lax.ppermute(base, ("dom", "rep"), pairs))
            base = jnp.concatenate(parts, axis=0)
        base, entity_grad = lax.optimization_barrier((base, entity_grad))
        swapped = lax.ppermute(base, "rep", [(i, i ^ 1) for i in range(replicas)])
        relation_t = pl.pallas_call(
            functools.partial(
                spread_kernel, orders, workers, replicas, narrow, power_row, block
            ),
            out_shape=jax.ShapeDtypeStruct((dim, nrel), F32),
            in_specs=[SMEM] + [VMEM] * 2,
            out_specs=VMEM,
            compiler_params=params(),
            name="spread",
        )(place, base, swapped)
    else:
        whole = lax.all_gather(chunk[:, :block], ("dom", "rep"), axis=0)
        whole = decode(whole[:, :narrow], whole[:, power_row : power_row + 1])
        whole = whole.reshape(workers, replicas, narrow, block).transpose(1, 2, 0, 3)
        relation_t = whole.reshape(dim, workers * block)[:, :nrel]
    return (entity_grad.T, relation_t.T)


def solution(mesh):
    placed = (
        P("dom", None),
        P(),
        P("dom", None, None),
        P("dom", "rep", None),
        P("dom", "rep", None),
        P("dom", "rep", None),
        P("dom", "rep", None, None),
        P("dom", "rep"),
    )
    return jax.shard_map(
        shards, mesh=mesh, in_specs=placed, out_specs=(P("dom", "rep"), P()), check_vma=False
    )
```

```python
import functools

import jax
import jax.numpy as jnp
from jax import lax
from jax.experimental import pallas as pl
from jax.experimental.pallas import tpu as pltpu
from jax.sharding import PartitionSpec as P

F32 = jnp.float32
BF16 = jnp.bfloat16
IDX_ROWS = 8
LANES = 128
VMEM = pl.BlockSpec(memory_space=pltpu.VMEM)
SMEM = pl.BlockSpec(memory_space=pltpu.SMEM)
HBM = pl.BlockSpec(memory_space=pltpu.HBM)


def params(mib=32):
    return pltpu.CompilerParams(vmem_limit_bytes=mib * 1024 * 1024)


def cost(flops, moved):
    return pl.CostEstimate(flops=flops, bytes_accessed=moved, transcendentals=0)


def up(value, step):
    return -(-value // step) * step


def split2(x):
    hi = x.astype(BF16)
    lo = (x - hi.astype(F32)).astype(BF16)
    return hi, lo


def split3(x):
    hi, rest = x.astype(BF16), x
    rest = rest - hi.astype(F32)
    mid = rest.astype(BF16)
    low = (rest - mid.astype(F32)).astype(BF16)
    return hi, mid, low


def dot(a, b):
    return jnp.dot(a, b, preferred_element_type=F32)


def dot_t(a, b):
    return lax.dot_general(a, b, (((1,), (1,)), ((), ())), preferred_element_type=F32)


def ones_where(flag):
    return jnp.where(flag, 1.0, 0.0).astype(BF16)


def exponent(largest):
    safe = jnp.where(largest > 0, largest, 1.0)
    return jnp.clip(jnp.floor(F32(14.9) - jnp.log2(safe)), -120.0, 120.0)


def encode(x, axis):
    k = exponent(jnp.max(jnp.abs(x), axis=axis, keepdims=True))
    return jnp.floor(x * jnp.exp2(k) + 0.5).astype(jnp.int32), k.astype(jnp.int32)


def decode(codes, k):
    return codes.astype(F32) * jnp.exp2(-k.astype(F32))


def iota(shape, axis):
    return lax.broadcasted_iota(jnp.int32, shape, axis)


def shifted_rows(x, offset, narrow, offsets):
    out = x[offsets[0] : offsets[0] + narrow]
    for other in offsets[1:]:
        out = jnp.where(offset == other, x[other : other + narrow], out)
    return out


def prep_kernel(serve, count, ent, src, rel, dst, neg, out_idx, out_rows, *refs):
    cap, workers = serve.shape[1], serve.shape[2]
    rows = ent.shape[1]
    groups, width = neg.shape[2], neg.shape[3]
    onehot, sems = refs[-2:]
    moves = [
        pltpu.make_async_copy(a, b, sems.at[n])
        for n, (a, b) in enumerate(zip((serve, count, ent, src, rel, dst, neg), refs))
    ]
    for move in moves:
        move.start()
    for move in moves:
        move.wait()
    serve_s, count_s, ent_v, src_v, rel_v, dst_v, neg_v = refs[:7]
    out_idx[...] = jnp.full(out_idx.shape, count_s[0, 0], jnp.int32)
    out_idx[0:1, :] = src_v[0]
    out_idx[1:2, :] = rel_v[0]
    out_idx[2:3, :] = dst_v[0]
    for g in range(groups):
        out_idx[3 + g : 4 + g, :width] = neg_v[0, 0, g : g + 1, :]
    lane = iota((1, rows), 1)
    for k in range(workers * cap):
        picked = serve_s[0, k % cap, k // cap]
        onehot[k : k + 1, :] = jnp.where(lane == picked, 1.0, 0.0).astype(F32)
    picked_rows = dot_t(onehot[...].astype(BF16), ent_v[...])
    for w in range(workers):
        out_rows[w] = picked_rows[w * cap : (w + 1) * cap]


def gather_kernel(cfg, place, *refs):
    replicas, nrel, pad_rel, narrow, window = cfg
    idx_refs, refs = refs[:replicas], refs[replicas:]
    ent, relation, out_query, out_lhs, out_rel, rel_parts, lhs_s, rel_s = refs
    edges = idx_refs[0].shape[1]
    dim, rows = ent.shape
    base = pl.multiple_of((place[1] * narrow) // 8 * 8, 8)
    hi, lo = split2(relation[...])
    if pad_rel > nrel:
        rel_parts[...] = jnp.zeros(rel_parts.shape, BF16)
    rel_parts[:dim, :nrel] = hi
    rel_parts[dim:, :nrel] = lo
    for i in range(replicas):
        span = slice(i * edges, (i + 1) * edges)
        src_l, rel_l = idx_refs[i][0:1, :], idx_refs[i][1:2, :]
        lhs = dot(ent[...], ones_where(iota((rows, edges), 0) == src_l))
        both = dot(rel_parts[...], ones_where(iota((pad_rel, edges), 0) == rel_l))
        rel_rows = both[:dim] + both[dim:]
        lhs_s[...] = lhs
        rel_s[...] = rel_rows
        out_query[:, span] = (lhs * rel_rows).astype(BF16)
        out_lhs[:, span] = lhs_s[pl.ds(base, window), :]
        out_rel[:, span] = rel_s[pl.ds(base, window), :]


def main_kernel(cfg, place, *refs):
    (direct, workers, replicas, cap, groups, width, pad_rel, block, narrow, window, offsets) = cfg
    idx_refs, refs = refs[:replicas], refs[replicas:]
    (query_v, lhs_v, rel_v, received), refs = refs[:4], refs[4:]
    out_lhs, refs = refs[0], refs[1:]
    (keep, send), refs = (refs[:2], refs[2:]) if direct else ((None, refs[0]), refs[1:])
    table_f, table_t, query_s, acc_rel, acc_lhs, acc_tab, wide_t, mixed = refs[:8]
    codes_s, powers_s, tables_s, table_powers_s = refs[8:]
    edges = idx_refs[0].shape[1]
    dim = query_v.shape[0]
    rows = out_lhs.shape[1]
    slots = workers * cap
    rep = place[1]
    per = edges // groups
    base = pl.multiple_of((rep * narrow) // 8 * 8, 8)
    offset = rep * narrow - base

    for w in range(workers):
        table_f[w * cap : (w + 1) * cap, :] = received[w]
    table_t[...] = jnp.transpose(table_f[...])
    table = table_f[...].astype(BF16)
    own_t = table_t[pl.ds(base, window), :].astype(BF16)
    own_t = jnp.concatenate([own_t] * 3, axis=1)
    acc_rel[...] = jnp.zeros(acc_rel.shape, F32)
    acc_lhs[...] = jnp.zeros(acc_lhs.shape, F32)
    acc_tab[...] = jnp.zeros(acc_tab.shape, F32)

    for i in range(replicas):
        here = slice(i * edges, (i + 1) * edges)
        lanes = idx_refs[i][...]
        cols = jnp.transpose(lanes)
        dst_l = lanes[2:3]
        count = lanes[IDX_ROWS - 1 : IDX_ROWS]
        query = query_v[:, here]
        query_s[...] = query.astype(F32)
        scores = dot(table, query)
        live = jnp.where(iota((1, edges), 1) < count, 1.0, 0.0).astype(F32)
        own = jnp.where(iota((slots, edges), 0) == dst_l, 1.0, 0.0).astype(F32)
        seen = own * live
        parts = []
        for g in range(groups):
            span = slice(g * per, (g + 1) * per)
            s, o = scores[:, span], own[:, span]
            neg = jnp.where(
                iota((slots, width), 0) == lanes[3 + g : 4 + g, :width], 1.0, 0.0
            ).astype(F32)
            times = jnp.sum(seen[:, span], axis=1, keepdims=True)
            times = times + jnp.sum(neg, axis=1, keepdims=True)
            s = jnp.where(times > 0, s, F32(-1e30))
            top = jnp.max(s, axis=0, keepdims=True)
            expo = jnp.exp(s - top)
            probs = expo / jnp.sum(expo * times, axis=0, keepdims=True)
            other = probs.astype(BF16).astype(F32)
            itself = (probs - 1.0).astype(BF16).astype(F32)
            parts.append(((times - o) * other + o * itself) * live[:, span])
        grads = jnp.concatenate(parts, axis=1)
        stack = jnp.concatenate(split3(grads), axis=0)
        stack_t = jnp.concatenate(split3(jnp.transpose(grads)), axis=1)

        dquery = dot(own_t, stack)
        acc_tab[...] += dot(query_s[pl.ds(base, window), :].astype(BF16), stack_t)
        y = jnp.concatenate(split2(dquery * lhs_v[:, here]), axis=0)
        acc_rel[...] += dot(y, ones_where(iota((edges, pad_rel), 1) == cols[:, 1:2]))
        x = jnp.concatenate(split2(dquery * rel_v[:, here]), axis=0)
        acc_lhs[...] += dot(x, ones_where(iota((edges, rows), 1) == cols[:, 0:1]))

    pick = functools.partial(shifted_rows, offset=offset, narrow=narrow, offsets=offsets)
    out_lhs[...] = pick(acc_lhs[:window] + acc_lhs[window:])
    codes, powers = encode(pick(acc_rel[:window] + acc_rel[window:]), 0)
    wide_t[...] = jnp.zeros(wide_t.shape, F32)
    wide_t[:narrow] = pick(
        acc_tab[:, :slots] + acc_tab[:, slots : 2 * slots] + acc_tab[:, 2 * slots :]
    )
    table_codes, table_powers = encode(jnp.transpose(wide_t[...]), 1)
    table_powers = jnp.broadcast_to(table_powers, table_codes.shape)
    mixed[...] = jnp.zeros(mixed.shape, jnp.int32)
    codes_s[...] = codes
    powers_s[...] = powers
    tables_s[...] = table_codes
    table_powers_s[...] = table_powers
    places = rows_of(narrow, cap)
    for h in range(workers):
        if direct:
            turn, z = h // (workers // 2), h % (workers // 2)
            o = z * 2 + lax.rem(place[0] + turn, 2)
            lane = pl.ds(pl.multiple_of(o * block, block), block)
            target = (keep if turn == 0 else send).at[z]
        else:
            o, lane, target = h, slice(h * block, (h + 1) * block), send.at[h]
        mixed[:narrow, :block] = codes_s[:, lane]
        for c in range(cap):
            for ref, row in ((tables_s, places[0]), (table_powers_s, places[2])):
                mixed[row + c : row + c + 1, :] = ref[pl.ds(o * cap + c, 1), :]
        mixed[places[4] : places[4] + 1, :block] = powers_s[0:1, lane]
        target[...] = mixed[...].astype(jnp.int16)


def rows_of(narrow, cap):
    return [narrow + n * cap for n in range(5)]


def pair_kernel(narrow, cap, block, keep, got, out, mixed):
    places = rows_of(narrow, cap)
    mixed[...] = jnp.zeros(mixed.shape, jnp.int32)
    for z in range(keep.shape[0]):
        ours, theirs = keep[z].astype(jnp.int32), got[z].astype(jnp.int32)
        power = slice(places[4], places[4] + 1)
        total = decode(ours[:narrow], ours[power]) + decode(theirs[:narrow], theirs[power])
        mixed[:narrow, :], mixed[power, :] = encode(total, 0)
        for n in (0, 2):
            mixed[places[n] : places[n + 1], :] = ours[places[n] : places[n + 1]]
            mixed[places[n + 1] : places[n + 2], :] = theirs[places[n] : places[n + 1]]
        out[z] = mixed[...].astype(jnp.int16)


def sum_kernel(scale, narrow, cap, block, *refs):
    parts, out, mixed = refs[:-2], refs[-2], refs[-1]
    power = slice(narrow + 4 * cap, narrow + 4 * cap + 1)
    mixed[...] = jnp.zeros(mixed.shape, jnp.int32)
    for z in range(out.shape[0]):
        total = jnp.zeros((narrow, block), F32)
        for part in parts:
            both = part[z].astype(jnp.int32)
            total += decode(both[:narrow, :block], both[power, :block])
        mixed[:narrow, :block], mixed[power, :block] = encode(total * F32(scale), 0)
        out[z] = mixed[...].astype(jnp.int16)


def entity_kernel(direct, narrow, place, serve, lhs, *refs):
    recv, out, terms, onehot = refs[:-3], refs[-3], refs[-2], refs[-1]
    cap, workers = serve.shape[1], serve.shape[2]
    rows = out.shape[1]
    lane = iota((1, rows), 1)
    places = rows_of(narrow, cap)
    for h in range(workers):
        if direct:
            turn, hop = h % 2, h // 2
            z = place[0] // 2
            both = recv[hop][z].astype(jnp.int32)
            far = lax.rem(z - hop + len(recv), len(recv))
            worker = far * 2 + lax.rem(place[0] + turn, 2)
        else:
            turn, both, worker = 0, recv[0][h].astype(jnp.int32), h
        span = slice(h * cap, (h + 1) * cap)
        terms[span, :] = decode(
            both[places[turn] : places[turn + 1]], both[places[turn + 2] : places[turn + 3]]
        )
        for c in range(cap):
            spot = jnp.where(lane == serve[0, c, worker], 1.0, 0.0).astype(F32)
            onehot[h * cap + c : h * cap + c + 1, :] = spot
    spots = onehot[...].astype(BF16)
    parts = jnp.concatenate(split3(jnp.transpose(terms[...])), axis=1)
    added = dot(parts, jnp.concatenate([spots] * 3, axis=0))
    out[...] = lhs[...] + added[:narrow]


def spread_kernel(workers, replicas, narrow, power_row, block, place, mine, other, out):
    nrel = out.shape[1]
    depth = workers // 2
    for o in range(workers):
        for r in range(replicas):
            over_y = lax.rem(place[0] + o, 2)
            over_x = lax.rem(place[1] // 2 + r // 2, 2)
            spot = (over_y + 2 * over_x) * depth + o // 2
            here = lax.rem(place[1], 2) == r % 2
            both = jnp.where(here, mine[spot].astype(jnp.int32), other[spot].astype(jnp.int32))
            value = decode(both[:narrow], both[power_row : power_row + 1])
            end = min((o + 1) * block, nrel)
            out[r * narrow : (r + 1) * narrow, o * block : end] = value[:, : end - o * block]


def turned(size, hop):
    return [(i, (i + hop) % size) for i in range(size)]


def shards(entities, relation, serve_ids, edge_src, edge_rel, edge_dst, neg_ids, edge_count):
    workers = lax.axis_size("dom")
    replicas = lax.axis_size("rep")
    rows, dim = entities.shape
    nrel = relation.shape[0]
    cap = serve_ids.shape[2]
    edges = edge_src.shape[2]
    groups, width = neg_ids.shape[2], neg_ids.shape[3]
    slots = workers * cap
    narrow = dim // replicas
    direct = workers == 8 and replicas == 4
    block = up(-(-nrel // workers), LANES if direct else 8)
    pad_rel = up(max(nrel, workers * block), LANES)
    offsets = sorted({(narrow * r) % 8 for r in range(replicas)})
    window = up(narrow + offsets[-1], 8)
    height = up(narrow + 4 * cap + 1, 16)
    ent_t, rel_t = entities.T, relation.T
    serve_t = jnp.transpose(serve_ids, (0, 2, 1))
    place = jnp.stack([lax.axis_index("dom"), lax.axis_index("rep")]).astype(jnp.int32)

    idx, served = pl.pallas_call(
        prep_kernel,
        out_shape=(
            jax.ShapeDtypeStruct((IDX_ROWS, edges), jnp.int32),
            jax.ShapeDtypeStruct((workers, cap, dim), F32),
        ),
        in_specs=[HBM] * 7,
        out_specs=(VMEM, VMEM),
        scratch_shapes=[
            pltpu.SMEM(serve_t.shape, jnp.int32),
            pltpu.SMEM(edge_count.shape, jnp.int32),
            pltpu.VMEM(ent_t.shape, BF16),
            pltpu.VMEM(edge_src.shape, jnp.int32),
            pltpu.VMEM(edge_rel.shape, jnp.int32),
            pltpu.VMEM(edge_dst.shape, jnp.int32),
            pltpu.VMEM(neg_ids.shape, jnp.int32),
            pltpu.VMEM((slots, rows), F32),
            pltpu.SemaphoreType.DMA((7,)),
        ],
        compiler_params=params(60),
        name="prep",
    )(serve_t, edge_count, ent_t, edge_src, edge_rel, edge_dst, neg_ids)

    held = [idx]
    for hop in range(1, replicas):
        held.append(lax.ppermute(idx, "rep", turned(replicas, hop)))
    received = lax.all_to_all(served, "dom", 0, 0, tiled=True)

    total = replicas * edges
    query, lhs_rows, rel_rows = pl.pallas_call(
        functools.partial(gather_kernel, (replicas, nrel, pad_rel, narrow, window)),
        out_shape=(
            jax.ShapeDtypeStruct((dim, total), BF16),
            jax.ShapeDtypeStruct((window, total), F32),
            jax.ShapeDtypeStruct((window, total), F32),
        ),
        in_specs=[SMEM] + [VMEM] * (replicas + 2),
        out_specs=(VMEM, VMEM, VMEM),
        scratch_shapes=[
            pltpu.VMEM((2 * dim, pad_rel), BF16),
            pltpu.VMEM((dim, edges), F32),
            pltpu.VMEM((dim, edges), F32),
        ],
        compiler_params=params(),
        cost_estimate=cost(2 * total * dim * (2 * pad_rel + rows), 8 * total * dim),
        name="gather",
    )(place, *held, ent_t, rel_t)

    cfg = (
        direct, workers, replicas, cap, groups, width, pad_rel, block, narrow, window,
        tuple(offsets),
    )
    lanes = max(up(block, LANES), up(narrow, LANES))
    half = workers // 2
    outs = [half, half] if direct else [workers]
    sizes = [jax.ShapeDtypeStruct((n, height, lanes), jnp.int16) for n in outs]
    lhs_part, *sent = pl.pallas_call(
        functools.partial(main_kernel, cfg),
        out_shape=[jax.ShapeDtypeStruct((narrow, rows), F32)] + sizes,
        in_specs=[SMEM] + [VMEM] * (replicas + 4),
        out_specs=[VMEM] * (1 + len(sizes)),
        scratch_shapes=[
            pltpu.VMEM((slots, dim), F32),
            pltpu.VMEM((dim, slots), F32),
            pltpu.VMEM((dim, edges), F32),
            pltpu.VMEM((2 * window, pad_rel), F32),
            pltpu.VMEM((2 * window, rows), F32),
            pltpu.VMEM((window, 3 * slots), F32),
            pltpu.VMEM((lanes, slots), F32),
            pltpu.VMEM((height, lanes), jnp.int32),
            pltpu.VMEM((narrow, pad_rel), jnp.int32),
            pltpu.VMEM((1, pad_rel), jnp.int32),
            pltpu.VMEM((slots, lanes), jnp.int32),
            pltpu.VMEM((slots, lanes), jnp.int32),
        ],
        compiler_params=params(),
        name="edges",
    )(place, *held, query, lhs_rows, rel_rows, received)

    def swap(array, over_z=0, over_y=0, over_x=0):
        pairs = []
        for o in range(workers):
            for r in range(replicas):
                z, y, x = (o // 2 + over_z) % half, (o + over_y) % 2, (r // 2 + over_x) % 2
                pairs.append((o * replicas + r, (z * 2 + y) * replicas + x * 2 + r % 2))
        return lax.ppermute(array, ("dom", "rep"), pairs)

    stack = jax.ShapeDtypeStruct((outs[0], height, lanes), jnp.int16)
    mixed = [pltpu.VMEM((height, lanes), jnp.int32)]
    if direct:
        summed = pl.pallas_call(
            functools.partial(pair_kernel, narrow, cap, block),
            out_shape=stack,
            in_specs=[VMEM] * 2,
            out_specs=VMEM,
            scratch_shapes=mixed,
            compiler_params=params(),
            name="pair",
        )(sent[0], swap(sent[1], over_y=1))
        recv = [summed] + [swap(summed, over_z=hop) for hop in range(1, half)]
        parts = recv
    else:
        recv = [lax.all_to_all(sent[0], "dom", 0, 0, tiled=True)]
        parts = [recv[0][w : w + 1] for w in range(workers)]
        stack = jax.ShapeDtypeStruct((1, height, lanes), jnp.int16)
    scale = 1.0 / (edges * workers * replicas)
    chunk = pl.pallas_call(
        functools.partial(sum_kernel, scale, narrow, cap, block),
        out_shape=stack,
        in_specs=[VMEM] * len(parts),
        out_specs=VMEM,
        scratch_shapes=mixed,
        compiler_params=params(),
        name="total",
    )(*parts)

    entity_grad = pl.pallas_call(
        functools.partial(entity_kernel, direct, narrow),
        out_shape=jax.ShapeDtypeStruct((narrow, rows), F32),
        in_specs=[SMEM] * 2 + [VMEM] * (1 + len(recv)),
        out_specs=VMEM,
        scratch_shapes=[pltpu.VMEM((slots, lanes), F32), pltpu.VMEM((slots, rows), F32)],
        compiler_params=params(),
        cost_estimate=cost(10**9, 10**6),
        name="entity",
    )(place, serve_t, lhs_part, *recv)

    power_row = narrow + 4 * cap
    if direct:
        base = jnp.concatenate(
            [chunk, swap(chunk, over_y=1), swap(chunk, over_x=1), swap(chunk, over_y=1, over_x=1)],
            axis=0,
        )
        base, entity_grad = lax.optimization_barrier((base, entity_grad))
        swapped = lax.ppermute(base, "rep", [(i, i ^ 1) for i in range(replicas)])
        relation_t = pl.pallas_call(
            functools.partial(spread_kernel, workers, replicas, narrow, power_row, block),
            out_shape=jax.ShapeDtypeStruct((dim, nrel), F32),
            in_specs=[SMEM] + [VMEM] * 2,
            out_specs=VMEM,
            compiler_params=params(),
            name="spread",
        )(place, base, swapped)
    else:
        whole = lax.all_gather(chunk[0, :, :block], ("dom", "rep"), axis=0)
        whole = decode(whole[:, :narrow], whole[:, power_row : power_row + 1])
        whole = whole.reshape(workers, replicas, narrow, block).transpose(1, 2, 0, 3)
        relation_t = whole.reshape(dim, workers * block)[:, :nrel]
    return (entity_grad.T, relation_t.T)


def solution(mesh):
    placed = (
        P("dom", None),
        P(),
        P("dom", None, None),
        P("dom", "rep", None),
        P("dom", "rep", None),
        P("dom", "rep", None),
        P("dom", "rep", None, None),
        P("dom", "rep"),
    )
    return jax.shard_map(
        shards, mesh=mesh, in_specs=placed, out_specs=(P("dom", "rep"), P()), check_vma=False
    )
```

```python
import functools

import jax
import jax.numpy as jnp
from jax import lax
from jax.experimental import pallas as pl
from jax.experimental.pallas import tpu as pltpu
from jax.sharding import PartitionSpec as P

F32 = jnp.float32
BF16 = jnp.bfloat16
IDX_ROWS = 8
LANES = 128
VMEM = pl.BlockSpec(memory_space=pltpu.VMEM)
SMEM = pl.BlockSpec(memory_space=pltpu.SMEM)
HBM = pl.BlockSpec(memory_space=pltpu.HBM)


def params(mib=32):
    return pltpu.CompilerParams(vmem_limit_bytes=mib * 1024 * 1024)


def cost(flops, moved):
    return pl.CostEstimate(flops=flops, bytes_accessed=moved, transcendentals=0)


def up(value, step):
    return -(-value // step) * step


def split2(x):
    hi = x.astype(BF16)
    lo = (x - hi.astype(F32)).astype(BF16)
    return hi, lo


def split3(x):
    hi, rest = x.astype(BF16), x
    rest = rest - hi.astype(F32)
    mid = rest.astype(BF16)
    low = (rest - mid.astype(F32)).astype(BF16)
    return hi, mid, low


def dot(a, b):
    return jnp.dot(a, b, preferred_element_type=F32)


def dot_t(a, b):
    return lax.dot_general(a, b, (((1,), (1,)), ((), ())), preferred_element_type=F32)


def ones_where(flag):
    return jnp.where(flag, 1.0, 0.0).astype(BF16)


def exponent(largest):
    safe = jnp.where(largest > 0, largest, 1.0)
    return jnp.clip(jnp.floor(F32(14.9) - jnp.log2(safe)), -120.0, 120.0)


def encode(x, axis):
    k = exponent(jnp.max(jnp.abs(x), axis=axis, keepdims=True))
    return jnp.floor(x * jnp.exp2(k) + 0.5).astype(jnp.int32), k.astype(jnp.int32)


def decode(codes, k):
    return codes.astype(F32) * jnp.exp2(-k.astype(F32))


def iota(shape, axis):
    return lax.broadcasted_iota(jnp.int32, shape, axis)


def shifted_rows(x, offset, narrow, offsets):
    out = x[offsets[0] : offsets[0] + narrow]
    for other in offsets[1:]:
        out = jnp.where(offset == other, x[other : other + narrow], out)
    return out


def prep_kernel(direct, place, serve, count, ent, src, rel, dst, neg, out_idx, *refs):
    cap, workers = serve.shape[1], serve.shape[2]
    rows = ent.shape[1]
    groups, width = neg.shape[2], neg.shape[3]
    onehot, sems = refs[-2:]
    scratch, outs = refs[-9:-2], refs[:-9]
    moves = [
        pltpu.make_async_copy(a, b, sems.at[n])
        for n, (a, b) in enumerate(zip((serve, count, ent, src, rel, dst, neg), scratch))
    ]
    for move in moves:
        move.start()
    for move in moves:
        move.wait()
    serve_s, count_s, ent_v, src_v, rel_v, dst_v, neg_v = scratch
    out_idx[...] = jnp.full(out_idx.shape, count_s[0, 0].astype(F32), F32)
    out_idx[0:1, :] = src_v[0].astype(F32)
    out_idx[1:2, :] = rel_v[0].astype(F32)
    out_idx[2:3, :] = dst_v[0].astype(F32)
    for g in range(groups):
        out_idx[3 + g : 4 + g, :width] = neg_v[0, 0, g : g + 1, :].astype(F32)
    lane = iota((1, rows), 1)
    if direct:
        onehot[...] = jnp.zeros(onehot.shape, F32)
    for k in range(len(outs) * cap if direct else workers * cap):
        worker = lax.rem(place[0] + len(outs) * place[1] + k // cap, workers) if direct else k // cap
        spot = jnp.where(lane == serve_s[0, k % cap, worker], 1.0, 0.0).astype(F32)
        onehot[k : k + 1, :] = spot
    picked_rows = dot_t(onehot[...].astype(BF16), ent_v[...])
    if direct:
        for n, out in enumerate(outs):
            out[...] = picked_rows[n * cap : (n + 1) * cap]
    else:
        for w in range(workers):
            outs[0][w] = picked_rows[w * cap : (w + 1) * cap]


def halves_kernel(relation, ent, out_parts, out_ent):
    dim, nrel = relation.shape
    hi, lo = split2(relation[...])
    if out_parts.shape[1] > nrel:
        out_parts[...] = jnp.zeros(out_parts.shape, BF16)
    out_parts[:dim, :nrel] = hi
    out_parts[dim:, :nrel] = lo
    out_ent[...] = ent[...]


def pack_kernel(idx, *refs):
    out = refs[-1]
    out[...] = jnp.zeros(out.shape, F32)
    out[:IDX_ROWS] = idx[...]
    cap, dim = refs[0].shape
    for n, rows in enumerate(refs[:-1]):
        out[IDX_ROWS + n * cap : IDX_ROWS + (n + 1) * cap, :dim] = rows[...]


def main_kernel(cfg, place, *refs):
    (direct, workers, replicas, cap, groups, width, pad_rel, block, narrow, window, offsets) = cfg
    packs, refs = refs[:replicas], refs[replicas:]
    (rel_parts, ent), refs = refs[:2], refs[2:]
    received, refs = (None, refs) if direct else (refs[0], refs[1:])
    out_lhs, refs = refs[0], refs[1:]
    (keep, send), refs = (refs[:2], refs[2:]) if direct else ((None, refs[0]), refs[1:])
    table_f, table_t, lhs_s, rel_s, query_s, acc_rel, acc_lhs, acc_tab, wide_t, mixed = refs[:10]
    codes_s, powers_s, tables_s, table_powers_s = refs[10:]
    edges = packs[0].shape[1]
    dim, rows = ent.shape
    slots = workers * cap
    dom, rep = place[0], place[1]
    per = edges // groups
    base = pl.multiple_of((rep * narrow) // 8 * 8, 8)
    offset = rep * narrow - base

    if direct:
        each = workers // replicas
        for h in range(replicas):
            first = dom - each * lax.rem(rep - h + replicas, replicas) + workers
            for n in range(each):
                owner = lax.rem(first - n, workers)
                for c in range(cap):
                    row = IDX_ROWS + n * cap + c
                    table_f[pl.ds(owner * cap + c, 1), :] = packs[h][row : row + 1, :dim]
    else:
        for w in range(workers):
            table_f[w * cap : (w + 1) * cap, :] = received[w]
    table_t[...] = jnp.transpose(table_f[...])
    table = table_f[...].astype(BF16)
    own_t = table_t[pl.ds(base, window), :].astype(BF16)
    own_t = jnp.concatenate([own_t] * 3, axis=1)
    acc_rel[...] = jnp.zeros(acc_rel.shape, F32)
    acc_lhs[...] = jnp.zeros(acc_lhs.shape, F32)
    acc_tab[...] = jnp.zeros(acc_tab.shape, F32)

    for i in range(replicas):
        lanes = packs[i][:IDX_ROWS].astype(jnp.int32)
        cols = jnp.transpose(lanes)
        src_l, rel_l, dst_l = lanes[0:1], lanes[1:2], lanes[2:3]
        count = lanes[IDX_ROWS - 1 : IDX_ROWS]
        lhs = dot(ent[...], ones_where(iota((rows, edges), 0) == src_l))
        both = dot(rel_parts[...], ones_where(iota((pad_rel, edges), 0) == rel_l))
        rel_rows = both[:dim] + both[dim:]
        query = (lhs * rel_rows).astype(BF16)
        lhs_s[...] = lhs
        rel_s[...] = rel_rows
        query_s[...] = query.astype(F32)
        scores = dot(table, query)
        live = jnp.where(iota((1, edges), 1) < count, 1.0, 0.0).astype(F32)
        own = jnp.where(iota((slots, edges), 0) == dst_l, 1.0, 0.0).astype(F32)
        seen = own * live
        parts = []
        for g in range(groups):
            span = slice(g * per, (g + 1) * per)
            s, o = scores[:, span], own[:, span]
            neg = jnp.where(
                iota((slots, width), 0) == lanes[3 + g : 4 + g, :width], 1.0, 0.0
            ).astype(F32)
            times = jnp.sum(seen[:, span], axis=1, keepdims=True)
            times = times + jnp.sum(neg, axis=1, keepdims=True)
            s = jnp.where(times > 0, s, F32(-1e30))
            top = jnp.max(s, axis=0, keepdims=True)
            expo = jnp.exp(s - top)
            probs = expo / jnp.sum(expo * times, axis=0, keepdims=True)
            other = probs.astype(BF16).astype(F32)
            itself = (probs - 1.0).astype(BF16).astype(F32)
            parts.append(((times - o) * other + o * itself) * live[:, span])
        grads = jnp.concatenate(parts, axis=1)
        stack = jnp.concatenate(split3(grads), axis=0)
        stack_t = jnp.concatenate(split3(jnp.transpose(grads)), axis=1)

        dquery = dot(own_t, stack)
        acc_tab[...] += dot(query_s[pl.ds(base, window), :].astype(BF16), stack_t)
        y = jnp.concatenate(split2(dquery * lhs_s[pl.ds(base, window), :]), axis=0)
        acc_rel[...] += dot(y, ones_where(iota((edges, pad_rel), 1) == cols[:, 1:2]))
        x = jnp.concatenate(split2(dquery * rel_s[pl.ds(base, window), :]), axis=0)
        acc_lhs[...] += dot(x, ones_where(iota((edges, rows), 1) == cols[:, 0:1]))

    pick = functools.partial(shifted_rows, offset=offset, narrow=narrow, offsets=offsets)
    out_lhs[...] = pick(acc_lhs[:window] + acc_lhs[window:])
    codes, powers = encode(pick(acc_rel[:window] + acc_rel[window:]), 0)
    wide_t[...] = jnp.zeros(wide_t.shape, F32)
    wide_t[:narrow] = pick(
        acc_tab[:, :slots] + acc_tab[:, slots : 2 * slots] + acc_tab[:, 2 * slots :]
    )
    table_codes, table_powers = encode(jnp.transpose(wide_t[...]), 1)
    table_powers = jnp.broadcast_to(table_powers, table_codes.shape)
    mixed[...] = jnp.zeros(mixed.shape, jnp.int32)
    codes_s[...] = codes
    powers_s[...] = powers
    tables_s[...] = table_codes
    table_powers_s[...] = table_powers
    places = rows_of(narrow, cap)
    for h in range(workers):
        if direct:
            turn, z = h // (workers // 2), h % (workers // 2)
            o = z * 2 + lax.rem(place[0] + turn, 2)
            lane = pl.ds(pl.multiple_of(o * block, block), block)
            target = (keep if turn == 0 else send).at[z]
        else:
            o, lane, target = h, slice(h * block, (h + 1) * block), send.at[h]
        mixed[:narrow, :block] = codes_s[:, lane]
        for c in range(cap):
            for ref, row in ((tables_s, places[0]), (table_powers_s, places[2])):
                mixed[row + c : row + c + 1, :] = ref[pl.ds(o * cap + c, 1), :]
        mixed[places[4] : places[4] + 1, :block] = powers_s[0:1, lane]
        target[...] = mixed[...].astype(jnp.int16)


def rows_of(narrow, cap):
    return [narrow + n * cap for n in range(5)]


def pair_kernel(narrow, cap, block, keep, got, out, mixed):
    places = rows_of(narrow, cap)
    mixed[...] = jnp.zeros(mixed.shape, jnp.int32)
    for z in range(keep.shape[0]):
        ours, theirs = keep[z].astype(jnp.int32), got[z].astype(jnp.int32)
        power = slice(places[4], places[4] + 1)
        total = decode(ours[:narrow], ours[power]) + decode(theirs[:narrow], theirs[power])
        mixed[:narrow, :], mixed[power, :] = encode(total, 0)
        for n in (0, 2):
            mixed[places[n] : places[n + 1], :] = ours[places[n] : places[n + 1]]
            mixed[places[n + 1] : places[n + 2], :] = theirs[places[n] : places[n + 1]]
        out[z] = mixed[...].astype(jnp.int16)


def sum_kernel(scale, narrow, cap, block, *refs):
    parts, out, mixed = refs[:-2], refs[-2], refs[-1]
    power = slice(narrow + 4 * cap, narrow + 4 * cap + 1)
    mixed[...] = jnp.zeros(mixed.shape, jnp.int32)
    for z in range(out.shape[0]):
        total = jnp.zeros((narrow, block), F32)
        for part in parts:
            both = part[z].astype(jnp.int32)
            total += decode(both[:narrow, :block], both[power, :block])
        mixed[:narrow, :block], mixed[power, :block] = encode(total * F32(scale), 0)
        out[z] = mixed[...].astype(jnp.int16)


def entity_kernel(direct, narrow, place, serve, lhs, *refs):
    recv, out, terms, onehot = refs[:-3], refs[-3], refs[-2], refs[-1]
    cap, workers = serve.shape[1], serve.shape[2]
    rows = out.shape[1]
    lane = iota((1, rows), 1)
    places = rows_of(narrow, cap)
    for h in range(workers):
        if direct:
            turn, hop = h % 2, h // 2
            z = place[0] // 2
            both = recv[hop][z].astype(jnp.int32)
            far = lax.rem(z - hop + len(recv), len(recv))
            worker = far * 2 + lax.rem(place[0] + turn, 2)
        else:
            turn, both, worker = 0, recv[0][h].astype(jnp.int32), h
        span = slice(h * cap, (h + 1) * cap)
        terms[span, :] = decode(
            both[places[turn] : places[turn + 1]], both[places[turn + 2] : places[turn + 3]]
        )
        for c in range(cap):
            spot = jnp.where(lane == serve[0, c, worker], 1.0, 0.0).astype(F32)
            onehot[h * cap + c : h * cap + c + 1, :] = spot
    spots = onehot[...].astype(BF16)
    parts = jnp.concatenate(split3(jnp.transpose(terms[...])), axis=1)
    added = dot(parts, jnp.concatenate([spots] * 3, axis=0))
    out[...] = lhs[...] + added[:narrow]


def spread_kernel(workers, replicas, narrow, power_row, block, place, mine, other, out):
    nrel = out.shape[1]
    depth = workers // 2
    for o in range(workers):
        for r in range(replicas):
            over_y = lax.rem(place[0] + o, 2)
            over_x = lax.rem(place[1] // 2 + r // 2, 2)
            spot = (over_y + 2 * over_x) * depth + o // 2
            here = lax.rem(place[1], 2) == r % 2
            both = jnp.where(here, mine[spot].astype(jnp.int32), other[spot].astype(jnp.int32))
            value = decode(both[:narrow], both[power_row : power_row + 1])
            end = min((o + 1) * block, nrel)
            out[r * narrow : (r + 1) * narrow, o * block : end] = value[:, : end - o * block]


def turned(size, hop):
    return [(i, (i + hop) % size) for i in range(size)]


def shards(entities, relation, serve_ids, edge_src, edge_rel, edge_dst, neg_ids, edge_count):
    workers = lax.axis_size("dom")
    replicas = lax.axis_size("rep")
    rows, dim = entities.shape
    nrel = relation.shape[0]
    cap = serve_ids.shape[2]
    edges = edge_src.shape[2]
    groups, width = neg_ids.shape[2], neg_ids.shape[3]
    slots = workers * cap
    narrow = dim // replicas
    direct = workers == 8 and replicas == 4
    block = up(-(-nrel // workers), LANES if direct else 8)
    pad_rel = up(max(nrel, workers * block), LANES)
    offsets = sorted({(narrow * r) % 8 for r in range(replicas)})
    window = up(narrow + offsets[-1], 8)
    height = up(narrow + 4 * cap + 1, 16)
    ent_t, rel_t = entities.T, relation.T
    serve_t = jnp.transpose(serve_ids, (0, 2, 1))
    place = jnp.stack([lax.axis_index("dom"), lax.axis_index("rep")]).astype(jnp.int32)

    each = workers // replicas
    served = (
        [jax.ShapeDtypeStruct((cap, dim), F32)] * each
        if direct
        else [jax.ShapeDtypeStruct((workers, cap, dim), F32)]
    )
    idx, *served = pl.pallas_call(
        functools.partial(prep_kernel, direct),
        out_shape=[jax.ShapeDtypeStruct((IDX_ROWS, edges), F32)] + served,
        in_specs=[SMEM] + [HBM] * 7,
        out_specs=[VMEM] * (1 + len(served)),
        scratch_shapes=[
            pltpu.SMEM(serve_t.shape, jnp.int32),
            pltpu.SMEM(edge_count.shape, jnp.int32),
            pltpu.VMEM(ent_t.shape, BF16),
            pltpu.VMEM(edge_src.shape, jnp.int32),
            pltpu.VMEM(edge_rel.shape, jnp.int32),
            pltpu.VMEM(edge_dst.shape, jnp.int32),
            pltpu.VMEM(neg_ids.shape, jnp.int32),
            pltpu.VMEM((up(each * cap, 16) if direct else slots, rows), F32),
            pltpu.SemaphoreType.DMA((7,)),
        ],
        compiler_params=params(60),
        name="prep",
    )(place, serve_t, edge_count, ent_t, edge_src, edge_rel, edge_dst, neg_ids)

    rel_late, ent_late, idx = lax.optimization_barrier((rel_t, ent_t, idx))
    rel_parts, ent_late = pl.pallas_call(
        halves_kernel,
        out_shape=(
            jax.ShapeDtypeStruct((2 * dim, pad_rel), BF16),
            jax.ShapeDtypeStruct(ent_t.shape, BF16),
        ),
        in_specs=[VMEM, VMEM],
        out_specs=(VMEM, VMEM),
        compiler_params=params(),
        cost_estimate=cost(10 * dim * nrel, 8 * dim * nrel),
        name="halves",
    )(rel_late, ent_late)

    if direct:
        fetched = []
        for n in range(each):
            pairs = []
            for o in range(workers):
                for r in range(replicas):
                    to = (o + each * r + n) % workers
                    pairs.append((o * replicas + r, to * replicas + r))
            fetched.append(lax.ppermute(served[n], ("dom", "rep"), pairs))
        idx = pl.pallas_call(
            pack_kernel,
            out_shape=jax.ShapeDtypeStruct((up(IDX_ROWS + each * cap, 8), edges), F32),
            in_specs=[VMEM] * (1 + each),
            out_specs=VMEM,
            compiler_params=params(),
            name="pack",
        )(idx, *fetched)
        received = []
    else:
        received = [lax.all_to_all(served[0], "dom", 0, 0, tiled=True)]
    held = [idx]
    for hop in range(1, replicas):
        held.append(lax.ppermute(idx, "rep", turned(replicas, hop)))

    cfg = (
        direct, workers, replicas, cap, groups, width, pad_rel, block, narrow, window,
        tuple(offsets),
    )
    lanes = max(up(block, LANES), up(narrow, LANES))
    half = workers // 2
    outs = [half, half] if direct else [workers]
    sizes = [jax.ShapeDtypeStruct((n, height, lanes), jnp.int16) for n in outs]
    lhs_part, *sent = pl.pallas_call(
        functools.partial(main_kernel, cfg),
        out_shape=[jax.ShapeDtypeStruct((narrow, rows), F32)] + sizes,
        in_specs=[SMEM] + [VMEM] * (replicas + 2 + len(received)),
        out_specs=[VMEM] * (1 + len(sizes)),
        scratch_shapes=[
            pltpu.VMEM((slots, dim), F32),
            pltpu.VMEM((dim, slots), F32),
            pltpu.VMEM((dim, edges), F32),
            pltpu.VMEM((dim, edges), F32),
            pltpu.VMEM((dim, edges), F32),
            pltpu.VMEM((2 * window, pad_rel), F32),
            pltpu.VMEM((2 * window, rows), F32),
            pltpu.VMEM((window, 3 * slots), F32),
            pltpu.VMEM((lanes, slots), F32),
            pltpu.VMEM((height, lanes), jnp.int32),
            pltpu.VMEM((narrow, pad_rel), jnp.int32),
            pltpu.VMEM((1, pad_rel), jnp.int32),
            pltpu.VMEM((slots, lanes), jnp.int32),
            pltpu.VMEM((slots, lanes), jnp.int32),
        ],
        compiler_params=params(),
        name="edges",
    )(place, *held, rel_parts, ent_late, *received)

    def swap(array, over_z=0, over_y=0, over_x=0):
        pairs = []
        for o in range(workers):
            for r in range(replicas):
                z, y, x = (o // 2 + over_z) % half, (o + over_y) % 2, (r // 2 + over_x) % 2
                pairs.append((o * replicas + r, (z * 2 + y) * replicas + x * 2 + r % 2))
        return lax.ppermute(array, ("dom", "rep"), pairs)

    stack = jax.ShapeDtypeStruct((outs[0], height, lanes), jnp.int16)
    mixed = [pltpu.VMEM((height, lanes), jnp.int32)]
    if direct:
        summed = pl.pallas_call(
            functools.partial(pair_kernel, narrow, cap, block),
            out_shape=stack,
            in_specs=[VMEM] * 2,
            out_specs=VMEM,
            scratch_shapes=mixed,
            compiler_params=params(),
            name="pair",
        )(sent[0], swap(sent[1], over_y=1))
        recv = [summed] + [swap(summed, over_z=hop) for hop in range(1, half)]
        parts = recv
    else:
        recv = [lax.all_to_all(sent[0], "dom", 0, 0, tiled=True)]
        parts = [recv[0][w : w + 1] for w in range(workers)]
        stack = jax.ShapeDtypeStruct((1, height, lanes), jnp.int16)
    scale = 1.0 / (edges * workers * replicas)
    chunk = pl.pallas_call(
        functools.partial(sum_kernel, scale, narrow, cap, block),
        out_shape=stack,
        in_specs=[VMEM] * len(parts),
        out_specs=VMEM,
        scratch_shapes=mixed,
        compiler_params=params(),
        name="total",
    )(*parts)

    entity_grad = pl.pallas_call(
        functools.partial(entity_kernel, direct, narrow),
        out_shape=jax.ShapeDtypeStruct((narrow, rows), F32),
        in_specs=[SMEM] * 2 + [VMEM] * (1 + len(recv)),
        out_specs=VMEM,
        scratch_shapes=[pltpu.VMEM((slots, lanes), F32), pltpu.VMEM((slots, rows), F32)],
        compiler_params=params(),
        cost_estimate=cost(10**9, 10**6),
        name="entity",
    )(place, serve_t, lhs_part, *recv)

    power_row = narrow + 4 * cap
    if direct:
        base = jnp.concatenate(
            [chunk, swap(chunk, over_y=1), swap(chunk, over_x=1), swap(chunk, over_y=1, over_x=1)],
            axis=0,
        )
        base, entity_grad = lax.optimization_barrier((base, entity_grad))
        swapped = lax.ppermute(base, "rep", [(i, i ^ 1) for i in range(replicas)])
        relation_t = pl.pallas_call(
            functools.partial(spread_kernel, workers, replicas, narrow, power_row, block),
            out_shape=jax.ShapeDtypeStruct((dim, nrel), F32),
            in_specs=[SMEM] + [VMEM] * 2,
            out_specs=VMEM,
            compiler_params=params(),
            name="spread",
        )(place, base, swapped)
    else:
        whole = lax.all_gather(chunk[0, :, :block], ("dom", "rep"), axis=0)
        whole = decode(whole[:, :narrow], whole[:, power_row : power_row + 1])
        whole = whole.reshape(workers, replicas, narrow, block).transpose(1, 2, 0, 3)
        relation_t = whole.reshape(dim, workers * block)[:, :nrel]
    return (entity_grad.T, relation_t.T)


def solution(mesh):
    placed = (
        P("dom", None),
        P(),
        P("dom", None, None),
        P("dom", "rep", None),
        P("dom", "rep", None),
        P("dom", "rep", None),
        P("dom", "rep", None, None),
        P("dom", "rep"),
    )
    return jax.shard_map(
        shards, mesh=mesh, in_specs=placed, out_specs=(P("dom", "rep"), P()), check_vma=False
    )
```

```python
import functools

import jax
import jax.numpy as jnp
from jax import lax
from jax.experimental import pallas as pl
from jax.experimental.pallas import tpu as pltpu
from jax.sharding import PartitionSpec as P

F32 = jnp.float32
BF16 = jnp.bfloat16
IDX_ROWS = 8
LANES = 128
SOURCES = 4
VMEM = pl.BlockSpec(memory_space=pltpu.VMEM)
SMEM = pl.BlockSpec(memory_space=pltpu.SMEM)
HBM = pl.BlockSpec(memory_space=pltpu.HBM)


def params(mib=32):
    return pltpu.CompilerParams(vmem_limit_bytes=mib * 1024 * 1024)


def cost(flops, moved):
    return pl.CostEstimate(flops=flops, bytes_accessed=moved, transcendentals=0)


def up(value, step):
    return -(-value // step) * step


def split2(x):
    hi = x.astype(BF16)
    lo = (x - hi.astype(F32)).astype(BF16)
    return hi, lo


def split3(x):
    hi, rest = x.astype(BF16), x
    rest = rest - hi.astype(F32)
    mid = rest.astype(BF16)
    low = (rest - mid.astype(F32)).astype(BF16)
    return hi, mid, low


def dot(a, b):
    return jnp.dot(a, b, preferred_element_type=F32)


def dot_t(a, b):
    return lax.dot_general(a, b, (((1,), (1,)), ((), ())), preferred_element_type=F32)


def ones_where(flag):
    return jnp.where(flag, 1.0, 0.0).astype(BF16)


def exponent(largest):
    safe = jnp.where(largest > 0, largest, 1.0)
    return jnp.clip(jnp.floor(F32(14.9) - jnp.log2(safe)), -120.0, 120.0)


def encode(x, axis):
    k = exponent(jnp.max(jnp.abs(x), axis=axis, keepdims=True))
    return jnp.floor(x * jnp.exp2(k) + 0.5).astype(jnp.int32), k.astype(jnp.int32)


def decode(codes, k):
    return codes.astype(F32) * jnp.exp2(-k.astype(F32))


def iota(shape, axis):
    return lax.broadcasted_iota(jnp.int32, shape, axis)


def shifted_rows(x, offset, narrow, offsets):
    out = x[offsets[0] : offsets[0] + narrow]
    for other in offsets[1:]:
        out = jnp.where(offset == other, x[other : other + narrow], out)
    return out


def prep_kernel(serve, count, ent, src, rel, dst, neg, out_idx, out_rows, *refs):
    cap, workers = serve.shape[1], serve.shape[2]
    rows = ent.shape[1]
    groups, width = neg.shape[2], neg.shape[3]
    onehot, sems = refs[-2:]
    moves = [
        pltpu.make_async_copy(a, b, sems.at[n])
        for n, (a, b) in enumerate(zip((serve, count, ent, src, rel, dst, neg), refs))
    ]
    for move in moves:
        move.start()
    for move in moves:
        move.wait()
    serve_s, count_s, ent_v, src_v, rel_v, dst_v, neg_v = refs[:7]
    out_idx[...] = jnp.full(out_idx.shape, count_s[0, 0], jnp.int32)
    out_idx[0:1, :] = src_v[0]
    out_idx[1:2, :] = rel_v[0]
    out_idx[2:3, :] = dst_v[0]
    for g in range(groups):
        out_idx[3 + g : 4 + g, :width] = neg_v[0, 0, g : g + 1, :]
    lane = iota((1, rows), 1)
    for k in range(workers * cap):
        picked = serve_s[0, k % cap, k // cap]
        onehot[k : k + 1, :] = jnp.where(lane == picked, 1.0, 0.0).astype(F32)
    picked_rows = dot_t(onehot[...].astype(BF16), ent_v[...])
    for w in range(workers):
        out_rows[w] = picked_rows[w * cap : (w + 1) * cap]


def gather_kernel(cfg, place, *refs):
    replicas, nrel, pad_rel, narrow, window = cfg
    idx_refs, refs = refs[:replicas], refs[replicas:]
    ent, relation, out_query, out_lhs, out_rel, rel_parts, lhs_s, rel_s = refs
    edges = idx_refs[0].shape[1]
    dim, rows = ent.shape
    base = pl.multiple_of((place[1] * narrow) // 8 * 8, 8)
    hi, lo = split2(relation[...])
    if pad_rel > nrel:
        rel_parts[...] = jnp.zeros(rel_parts.shape, BF16)
    rel_parts[:dim, :nrel] = hi
    rel_parts[dim:, :nrel] = lo
    for i in range(replicas):
        span = slice(i * edges, (i + 1) * edges)
        src_l, rel_l = idx_refs[i][0:1, :], idx_refs[i][1:2, :]
        lhs = dot(ent[...], ones_where(iota((rows, edges), 0) == src_l))
        both = dot(rel_parts[...], ones_where(iota((pad_rel, edges), 0) == rel_l))
        rel_rows = both[:dim] + both[dim:]
        lhs_s[...] = lhs
        rel_s[...] = rel_rows
        out_query[:, span] = (lhs * rel_rows).astype(BF16)
        out_lhs[:, span] = lhs_s[pl.ds(base, window), :]
        out_rel[:, span] = rel_s[pl.ds(base, window), :]


def main_kernel(cfg, place, *refs):
    (direct, workers, replicas, cap, groups, width, pad_rel, block, narrow, window, offsets) = cfg
    idx_refs, refs = refs[:replicas], refs[replicas:]
    (query_v, lhs_v, rel_v, received), refs = refs[:4], refs[4:]
    out_lhs, refs = refs[0], refs[1:]
    outs, refs = (refs[:SOURCES], refs[SOURCES:]) if direct else (refs[:1], refs[1:])
    table_f, table_t, query_s, acc_rel, acc_lhs, acc_tab, wide_t, mixed = refs[:8]
    codes_s, powers_s, tables_s = refs[8:]
    edges = idx_refs[0].shape[1]
    dim = query_v.shape[0]
    rows = out_lhs.shape[1]
    slots = workers * cap
    rep = place[1]
    per = edges // groups
    base = pl.multiple_of((rep * narrow) // 8 * 8, 8)
    offset = rep * narrow - base

    for w in range(workers):
        table_f[w * cap : (w + 1) * cap, :] = received[w]
    table_t[...] = jnp.transpose(table_f[...])
    table = table_f[...].astype(BF16)
    own_t = table_t[pl.ds(base, window), :].astype(BF16)
    own_t = jnp.concatenate([own_t] * 3, axis=1)
    acc_rel[...] = jnp.zeros(acc_rel.shape, F32)
    acc_lhs[...] = jnp.zeros(acc_lhs.shape, F32)
    acc_tab[...] = jnp.zeros(acc_tab.shape, F32)

    for i in range(replicas):
        here = slice(i * edges, (i + 1) * edges)
        lanes = idx_refs[i][...]
        cols = jnp.transpose(lanes)
        dst_l = lanes[2:3]
        count = lanes[IDX_ROWS - 1 : IDX_ROWS]
        query = query_v[:, here]
        query_s[...] = query.astype(F32)
        scores = dot(table, query)
        live = jnp.where(iota((1, edges), 1) < count, 1.0, 0.0).astype(F32)
        own = jnp.where(iota((slots, edges), 0) == dst_l, 1.0, 0.0).astype(F32)
        seen = own * live
        parts = []
        for g in range(groups):
            span = slice(g * per, (g + 1) * per)
            s, o = scores[:, span], own[:, span]
            neg = jnp.where(
                iota((slots, width), 0) == lanes[3 + g : 4 + g, :width], 1.0, 0.0
            ).astype(F32)
            times = jnp.sum(seen[:, span], axis=1, keepdims=True)
            times = times + jnp.sum(neg, axis=1, keepdims=True)
            s = jnp.where(times > 0, s, F32(-1e30))
            top = jnp.max(s, axis=0, keepdims=True)
            expo = jnp.exp(s - top)
            probs = expo / jnp.sum(expo * times, axis=0, keepdims=True)
            other = probs.astype(BF16).astype(F32)
            itself = (probs - 1.0).astype(BF16).astype(F32)
            parts.append(((times - o) * other + o * itself) * live[:, span])
        grads = jnp.concatenate(parts, axis=1)
        stack = jnp.concatenate(split3(grads), axis=0)
        stack_t = jnp.concatenate(split3(jnp.transpose(grads)), axis=1)

        dquery = dot(own_t, stack)
        acc_tab[...] += dot(query_s[pl.ds(base, window), :].astype(BF16), stack_t)
        y = jnp.concatenate(split2(dquery * lhs_v[:, here]), axis=0)
        acc_rel[...] += dot(y, ones_where(iota((edges, pad_rel), 1) == cols[:, 1:2]))
        x = jnp.concatenate(split2(dquery * rel_v[:, here]), axis=0)
        acc_lhs[...] += dot(x, ones_where(iota((edges, rows), 1) == cols[:, 0:1]))

    pick = functools.partial(shifted_rows, offset=offset, narrow=narrow, offsets=offsets)
    out_lhs[...] = pick(acc_lhs[:window] + acc_lhs[window:])
    codes, powers = encode(pick(acc_rel[:window] + acc_rel[window:]), 0)
    wide_t[...] = jnp.zeros(wide_t.shape, F32)
    wide_t[:narrow] = pick(
        acc_tab[:, :slots] + acc_tab[:, slots : 2 * slots] + acc_tab[:, 2 * slots :]
    )
    table_codes, table_powers = encode(jnp.transpose(wide_t[...]), 1)
    spare = iota(table_codes.shape, 1) >= narrow
    tables_s[...] = jnp.where(spare, table_powers, table_codes)
    codes_s[...] = codes
    powers_s[...] = powers
    mixed[...] = jnp.zeros(mixed.shape, jnp.int32)
    power_row = narrow + SOURCES * cap
    dom = place[0]

    def write(target, o, lane):
        mixed[:narrow, :block] = codes_s[:, lane]
        for c in range(cap):
            mixed[narrow + c : narrow + c + 1, :] = tables_s[pl.ds(o * cap + c, 1), :]
        mixed[power_row : power_row + 1, :block] = powers_s[0:1, lane]
        target[...] = mixed[...].astype(jnp.int16)

    if direct:
        for h in range(SOURCES):
            for top in range(2):
                o = top * 4 + flipped(dom % 4, h)
                write(outs[h].at[top], o, pl.ds(pl.multiple_of(o * block, block), block))
    else:
        for o in range(workers):
            write(outs[0].at[o], o, slice(o * block, (o + 1) * block))


def flipped(index, mask):
    out, bit = index * 0, 1
    while bit < 4:
        out = out + bit * lax.rem(index // bit + (mask // bit) % 2, 2)
        bit *= 2
    return out


def quad_kernel(narrow, cap, *refs):
    parts, out, mixed = refs[:-2], refs[-2], refs[-1]
    power = slice(narrow + SOURCES * cap, narrow + SOURCES * cap + 1)
    mixed[...] = jnp.zeros(mixed.shape, jnp.int32)
    for top in range(out.shape[0]):
        total = jnp.zeros((narrow, out.shape[2]), F32)
        for n, part in enumerate(parts):
            both = part[top].astype(jnp.int32)
            total += decode(both[:narrow], both[power])
            row = narrow + n * cap
            mixed[row : row + cap, :] = both[narrow : narrow + cap]
        mixed[:narrow, :], mixed[power, :] = encode(total, 0)
        out[top] = mixed[...].astype(jnp.int16)


def sum_kernel(scale, narrow, cap, block, *refs):
    parts, out, mixed = refs[:-2], refs[-2], refs[-1]
    power = slice(narrow + SOURCES * cap, narrow + SOURCES * cap + 1)
    mixed[...] = jnp.zeros(mixed.shape, jnp.int32)
    for top in range(out.shape[0]):
        total = jnp.zeros((narrow, block), F32)
        for part in parts:
            both = part[top].astype(jnp.int32)
            total += decode(both[:narrow, :block], both[power, :block])
        mixed[:narrow, :block], mixed[power, :block] = encode(total * F32(scale), 0)
        out[top] = mixed[...].astype(jnp.int16)


def entity_kernel(direct, narrow, place, serve, lhs, *refs):
    recv, out, terms, onehot = refs[:-3], refs[-3], refs[-2], refs[-1]
    cap, workers = serve.shape[1], serve.shape[2]
    rows = out.shape[1]
    lane = iota((1, rows), 1)
    for h in range(workers):
        if direct:
            turn, hop = h % SOURCES, h // SOURCES
            mine = place[0] // 4
            both = recv[hop][mine].astype(jnp.int32)
            worker = lax.rem(mine + hop, 2) * 4 + flipped(place[0] % 4, turn)
        else:
            turn, both, worker = 0, recv[0][h].astype(jnp.int32), h
        row = narrow + turn * cap
        both = both[row : row + cap]
        terms[h * cap : (h + 1) * cap, :] = jnp.where(
            iota(both.shape, 1) < narrow, decode(both, both[:, narrow : narrow + 1]), 0.0
        )
        for c in range(cap):
            spot = jnp.where(lane == serve[0, c, worker], 1.0, 0.0).astype(F32)
            onehot[h * cap + c : h * cap + c + 1, :] = spot
    spots = onehot[...].astype(BF16)
    parts = jnp.concatenate(split3(jnp.transpose(terms[...])), axis=1)
    added = dot(parts, jnp.concatenate([spots] * 3, axis=0))
    out[...] = lhs[...] + added[:narrow]


def spread_kernel(workers, replicas, narrow, power_row, block, place, mine, other, out, whole, sems):
    dim, nrel = out.shape
    dom, rep = place[0], place[1]
    here = lax.rem(rep, 2)
    moves, start = [], 0
    for r in range(replicas):
        for o in range(workers):
            over_low = lax.rem(dom // 2 + o // 2, 2)
            over_y = lax.rem(dom + o, 2)
            over_x = lax.rem(rep // 2 + r // 2, 2)
            spot = (over_y + 2 * over_x) * 4 + over_low * 2 + o // 4
            both = jnp.where(
                here == r % 2, mine[spot].astype(jnp.int32), other[spot].astype(jnp.int32)
            )
            value = decode(both[:narrow], both[power_row : power_row + 1])
            end = min((o + 1) * block, nrel)
            whole[r * narrow : (r + 1) * narrow, o * block : end] = value[:, : end - o * block]
        end = (r + 1) * narrow // 8 * 8 if r + 1 < replicas else dim
        band = slice(start, end)
        moves.append(pltpu.make_async_copy(whole.at[band], out.at[band], sems.at[r]))
        moves[-1].start()
        start = end
    for move in moves:
        move.wait()


def turned(size, hop):
    return [(i, (i + hop) % size) for i in range(size)]


def shards(entities, relation, serve_ids, edge_src, edge_rel, edge_dst, neg_ids, edge_count):
    workers = lax.axis_size("dom")
    replicas = lax.axis_size("rep")
    rows, dim = entities.shape
    nrel = relation.shape[0]
    cap = serve_ids.shape[2]
    edges = edge_src.shape[2]
    groups, width = neg_ids.shape[2], neg_ids.shape[3]
    slots = workers * cap
    narrow = dim // replicas
    direct = workers == 8 and replicas == 4
    block = up(-(-nrel // workers), LANES if direct else 8)
    pad_rel = up(max(nrel, workers * block), LANES)
    offsets = sorted({(narrow * r) % 8 for r in range(replicas)})
    window = up(narrow + offsets[-1], 8)
    height = up(narrow + SOURCES * cap + 1, 16)
    ent_t, rel_t = entities.T, relation.T
    serve_t = jnp.transpose(serve_ids, (0, 2, 1))
    place = jnp.stack([lax.axis_index("dom"), lax.axis_index("rep")]).astype(jnp.int32)

    idx, served = pl.pallas_call(
        prep_kernel,
        out_shape=(
            jax.ShapeDtypeStruct((IDX_ROWS, edges), jnp.int32),
            jax.ShapeDtypeStruct((workers, cap, dim), F32),
        ),
        in_specs=[HBM] * 7,
        out_specs=(VMEM, VMEM),
        scratch_shapes=[
            pltpu.SMEM(serve_t.shape, jnp.int32),
            pltpu.SMEM(edge_count.shape, jnp.int32),
            pltpu.VMEM(ent_t.shape, BF16),
            pltpu.VMEM(edge_src.shape, jnp.int32),
            pltpu.VMEM(edge_rel.shape, jnp.int32),
            pltpu.VMEM(edge_dst.shape, jnp.int32),
            pltpu.VMEM(neg_ids.shape, jnp.int32),
            pltpu.VMEM((slots, rows), F32),
            pltpu.SemaphoreType.DMA((7,)),
        ],
        compiler_params=params(60),
        name="prep",
    )(serve_t, edge_count, ent_t, edge_src, edge_rel, edge_dst, neg_ids)

    held = [idx]
    for hop in range(1, replicas):
        held.append(lax.ppermute(idx, "rep", turned(replicas, hop)))
    received = lax.all_to_all(served, "dom", 0, 0, tiled=True)

    total = replicas * edges
    query, lhs_rows, rel_rows = pl.pallas_call(
        functools.partial(gather_kernel, (replicas, nrel, pad_rel, narrow, window)),
        out_shape=(
            jax.ShapeDtypeStruct((dim, total), BF16),
            jax.ShapeDtypeStruct((window, total), F32),
            jax.ShapeDtypeStruct((window, total), F32),
        ),
        in_specs=[SMEM] + [VMEM] * (replicas + 2),
        out_specs=(VMEM, VMEM, VMEM),
        scratch_shapes=[
            pltpu.VMEM((2 * dim, pad_rel), BF16),
            pltpu.VMEM((dim, edges), F32),
            pltpu.VMEM((dim, edges), F32),
        ],
        compiler_params=params(),
        cost_estimate=cost(2 * total * dim * (2 * pad_rel + rows), 8 * total * dim),
        name="gather",
    )(place, *held, ent_t, rel_t)

    cfg = (
        direct, workers, replicas, cap, groups, width, pad_rel, block, narrow, window,
        tuple(offsets),
    )
    lanes = max(up(block, LANES), up(narrow, LANES))
    outs = [2] * SOURCES if direct else [workers]
    sizes = [jax.ShapeDtypeStruct((n, height, lanes), jnp.int16) for n in outs]
    lhs_part, *sent = pl.pallas_call(
        functools.partial(main_kernel, cfg),
        out_shape=[jax.ShapeDtypeStruct((narrow, rows), F32)] + sizes,
        in_specs=[SMEM] + [VMEM] * (replicas + 4),
        out_specs=[VMEM] * (1 + len(sizes)),
        scratch_shapes=[
            pltpu.VMEM((slots, dim), F32),
            pltpu.VMEM((dim, slots), F32),
            pltpu.VMEM((dim, edges), F32),
            pltpu.VMEM((2 * window, pad_rel), F32),
            pltpu.VMEM((2 * window, rows), F32),
            pltpu.VMEM((window, 3 * slots), F32),
            pltpu.VMEM((lanes, slots), F32),
            pltpu.VMEM((height, lanes), jnp.int32),
            pltpu.VMEM((narrow, pad_rel), jnp.int32),
            pltpu.VMEM((1, pad_rel), jnp.int32),
            pltpu.VMEM((slots, lanes), jnp.int32),
        ],
        compiler_params=params(),
        name="edges",
    )(place, *held, query, lhs_rows, rel_rows, received)

    def swap(array, dom_bits=0, rep_bits=0):
        pairs = []
        for o in range(workers):
            for r in range(replicas):
                pairs.append((o * replicas + r, (o ^ dom_bits) * replicas + (r ^ rep_bits)))
        return lax.ppermute(array, ("dom", "rep"), pairs)

    stack = jax.ShapeDtypeStruct((outs[0], height, lanes), jnp.int16)
    mixed = [pltpu.VMEM((height, lanes), jnp.int32)]
    if direct:
        summed = pl.pallas_call(
            functools.partial(quad_kernel, narrow, cap),
            out_shape=stack,
            in_specs=[VMEM] * SOURCES,
            out_specs=VMEM,
            scratch_shapes=mixed,
            compiler_params=params(),
            name="quad",
        )(sent[0], *[swap(sent[n], n) for n in range(1, SOURCES)])
        recv = [summed, swap(summed, 4)]
        parts = recv
    else:
        recv = [lax.all_to_all(sent[0], "dom", 0, 0, tiled=True)]
        parts = [recv[0][w : w + 1] for w in range(workers)]
        stack = jax.ShapeDtypeStruct((1, height, lanes), jnp.int16)
    scale = 1.0 / (edges * workers * replicas)
    chunk = pl.pallas_call(
        functools.partial(sum_kernel, scale, narrow, cap, block),
        out_shape=stack,
        in_specs=[VMEM] * len(parts),
        out_specs=VMEM,
        scratch_shapes=mixed,
        compiler_params=params(),
        name="total",
    )(*parts)

    entity_grad = pl.pallas_call(
        functools.partial(entity_kernel, direct, narrow),
        out_shape=jax.ShapeDtypeStruct((narrow, rows), F32),
        in_specs=[SMEM] * 2 + [VMEM] * (1 + len(recv)),
        out_specs=VMEM,
        scratch_shapes=[pltpu.VMEM((slots, lanes), F32), pltpu.VMEM((slots, rows), F32)],
        compiler_params=params(),
        cost_estimate=cost(10**9, 10**6),
        name="entity",
    )(place, serve_t, lhs_part, *recv)

    power_row = narrow + SOURCES * cap
    if direct:
        base = jnp.concatenate([chunk, swap(chunk, 2)], axis=0)
        base = jnp.concatenate(
            [base, swap(base, 1), swap(base, 0, 2), swap(base, 1, 2)], axis=0
        )
        base, entity_grad = lax.optimization_barrier((base, entity_grad))
        swapped = lax.ppermute(base, "rep", [(i, i ^ 1) for i in range(replicas)])
        relation_t = pl.pallas_call(
            functools.partial(spread_kernel, workers, replicas, narrow, power_row, block),
            out_shape=jax.ShapeDtypeStruct((dim, nrel), F32),
            in_specs=[SMEM] + [VMEM] * 2,
            out_specs=HBM,
            scratch_shapes=[
                pltpu.VMEM((dim, nrel), F32),
                pltpu.SemaphoreType.DMA((replicas,)),
            ],
            compiler_params=params(),
            name="spread",
        )(place, base, swapped)
    else:
        whole = lax.all_gather(chunk[0, :, :block], ("dom", "rep"), axis=0)
        whole = decode(whole[:, :narrow], whole[:, power_row : power_row + 1])
        whole = whole.reshape(workers, replicas, narrow, block).transpose(1, 2, 0, 3)
        relation_t = whole.reshape(dim, workers * block)[:, :nrel]
    return (entity_grad.T, relation_t.T)


def solution(mesh):
    placed = (
        P("dom", None),
        P(),
        P("dom", None, None),
        P("dom", "rep", None),
        P("dom", "rep", None),
        P("dom", "rep", None),
        P("dom", "rep", None, None),
        P("dom", "rep"),
    )
    return jax.shard_map(
        shards, mesh=mesh, in_specs=placed, out_specs=(P("dom", "rep"), P()), check_vma=False
    )
```

```python
import functools

import jax
import jax.numpy as jnp
from jax import lax
from jax.experimental import pallas as pl
from jax.experimental.pallas import tpu as pltpu
from jax.sharding import PartitionSpec as P

F32 = jnp.float32
BF16 = jnp.bfloat16
IDX_ROWS = 8
LANES = 128
SOURCES = 4
VMEM = pl.BlockSpec(memory_space=pltpu.VMEM)
SMEM = pl.BlockSpec(memory_space=pltpu.SMEM)
HBM = pl.BlockSpec(memory_space=pltpu.HBM)


def params(mib=32):
    return pltpu.CompilerParams(vmem_limit_bytes=mib * 1024 * 1024)


def cost(flops, moved):
    return pl.CostEstimate(flops=flops, bytes_accessed=moved, transcendentals=0)


def up(value, step):
    return -(-value // step) * step


def split2(x):
    hi = x.astype(BF16)
    lo = (x - hi.astype(F32)).astype(BF16)
    return hi, lo


def split3(x):
    hi, rest = x.astype(BF16), x
    rest = rest - hi.astype(F32)
    mid = rest.astype(BF16)
    low = (rest - mid.astype(F32)).astype(BF16)
    return hi, mid, low


def dot(a, b):
    return jnp.dot(a, b, preferred_element_type=F32)


def dot_t(a, b):
    return lax.dot_general(a, b, (((1,), (1,)), ((), ())), preferred_element_type=F32)


def ones_where(flag):
    return jnp.where(flag, 1.0, 0.0).astype(BF16)


def exponent(largest):
    safe = jnp.where(largest > 0, largest, 1.0)
    return jnp.clip(jnp.floor(F32(14.9) - jnp.log2(safe)), -120.0, 120.0)


def encode(x, axis):
    k = exponent(jnp.max(jnp.abs(x), axis=axis, keepdims=True))
    return jnp.floor(x * jnp.exp2(k) + 0.5).astype(jnp.int32), k.astype(jnp.int32)


def decode(codes, k):
    return codes.astype(F32) * jnp.exp2(-k.astype(F32))


def iota(shape, axis):
    return lax.broadcasted_iota(jnp.int32, shape, axis)


def shifted_rows(x, offset, narrow, offsets):
    out = x[offsets[0] : offsets[0] + narrow]
    for other in offsets[1:]:
        out = jnp.where(offset == other, x[other : other + narrow], out)
    return out


def prep_kernel(serve, count, ent, src, rel, dst, neg, out_idx, out_rows, *refs):
    cap, workers = serve.shape[1], serve.shape[2]
    rows = ent.shape[1]
    groups, width = neg.shape[2], neg.shape[3]
    onehot, sems = refs[-2:]
    moves = [
        pltpu.make_async_copy(a, b, sems.at[n])
        for n, (a, b) in enumerate(zip((serve, count, ent, src, rel, dst, neg), refs))
    ]
    for move in moves:
        move.start()
    for move in moves:
        move.wait()
    serve_s, count_s, ent_v, src_v, rel_v, dst_v, neg_v = refs[:7]
    out_idx[...] = jnp.full(out_idx.shape, count_s[0, 0], jnp.int32)
    out_idx[0:1, :] = src_v[0]
    out_idx[1:2, :] = rel_v[0]
    out_idx[2:3, :] = dst_v[0]
    for g in range(groups):
        out_idx[3 + g : 4 + g, :width] = neg_v[0, 0, g : g + 1, :]
    lane = iota((1, rows), 1)
    for k in range(workers * cap):
        picked = serve_s[0, k % cap, k // cap]
        onehot[k : k + 1, :] = jnp.where(lane == picked, 1.0, 0.0).astype(F32)
    picked_rows = dot_t(onehot[...].astype(BF16), ent_v[...])
    for w in range(workers):
        out_rows[w] = picked_rows[w * cap : (w + 1) * cap]


def gather_kernel(cfg, place, *refs):
    replicas, nrel, pad_rel, narrow, window = cfg
    idx_refs, refs = refs[:replicas], refs[replicas:]
    ent, relation, out_query, out_lhs, out_rel, rel_parts, lhs_s, rel_s = refs
    edges = idx_refs[0].shape[1]
    dim, rows = ent.shape
    base = pl.multiple_of((place[1] * narrow) // 8 * 8, 8)
    hi, lo = split2(relation[...])
    if pad_rel > nrel:
        rel_parts[...] = jnp.zeros(rel_parts.shape, BF16)
    rel_parts[:dim, :nrel] = hi
    rel_parts[dim:, :nrel] = lo
    for i in range(replicas):
        span = slice(i * edges, (i + 1) * edges)
        src_l, rel_l = idx_refs[i][0:1, :], idx_refs[i][1:2, :]
        lhs = dot(ent[...], ones_where(iota((rows, edges), 0) == src_l))
        both = dot(rel_parts[...], ones_where(iota((pad_rel, edges), 0) == rel_l))
        rel_rows = both[:dim] + both[dim:]
        lhs_s[...] = lhs
        rel_s[...] = rel_rows
        out_query[:, span] = (lhs * rel_rows).astype(BF16)
        out_lhs[:, span] = lhs_s[pl.ds(base, window), :]
        out_rel[:, span] = rel_s[pl.ds(base, window), :]


def main_kernel(cfg, place, *refs):
    (direct, workers, replicas, cap, groups, width, pad_rel, block, narrow, window, offsets) = cfg
    idx_refs, refs = refs[:replicas], refs[replicas:]
    (query_v, lhs_v, rel_v, received), refs = refs[:4], refs[4:]
    out_lhs, refs = refs[0], refs[1:]
    outs, refs = (refs[:SOURCES], refs[SOURCES:]) if direct else (refs[:1], refs[1:])
    table_f, table_t, query_s, acc_rel, acc_lhs, acc_tab, wide_t, mixed = refs[:8]
    codes_s, powers_s, tables_s = refs[8:]
    edges = idx_refs[0].shape[1]
    dim = query_v.shape[0]
    rows = out_lhs.shape[1]
    slots = workers * cap
    rep = place[1]
    per = edges // groups
    base = pl.multiple_of((rep * narrow) // 8 * 8, 8)
    offset = rep * narrow - base

    for w in range(workers):
        table_f[w * cap : (w + 1) * cap, :] = received[w]
    table_t[...] = jnp.transpose(table_f[...])
    table = table_f[...].astype(BF16)
    own_t = table_t[pl.ds(base, window), :].astype(BF16)
    own_t = jnp.concatenate([own_t] * 3, axis=1)
    acc_rel[...] = jnp.zeros(acc_rel.shape, F32)
    acc_lhs[...] = jnp.zeros(acc_lhs.shape, F32)
    acc_tab[...] = jnp.zeros(acc_tab.shape, F32)

    for i in range(replicas):
        here = slice(i * edges, (i + 1) * edges)
        lanes = idx_refs[i][...]
        cols = jnp.transpose(lanes)
        dst_l = lanes[2:3]
        count = lanes[IDX_ROWS - 1 : IDX_ROWS]
        query = query_v[:, here]
        query_s[...] = query.astype(F32)
        scores = dot(table, query)
        live = jnp.where(iota((1, edges), 1) < count, 1.0, 0.0).astype(F32)
        own = jnp.where(iota((slots, edges), 0) == dst_l, 1.0, 0.0).astype(F32)
        seen = own * live
        parts = []
        for g in range(groups):
            span = slice(g * per, (g + 1) * per)
            s, o = scores[:, span], own[:, span]
            neg = jnp.where(
                iota((slots, width), 0) == lanes[3 + g : 4 + g, :width], 1.0, 0.0
            ).astype(F32)
            times = jnp.sum(seen[:, span], axis=1, keepdims=True)
            times = times + jnp.sum(neg, axis=1, keepdims=True)
            s = jnp.where(times > 0, s, F32(-1e30))
            top = jnp.max(s, axis=0, keepdims=True)
            expo = jnp.exp(s - top)
            probs = expo / jnp.sum(expo * times, axis=0, keepdims=True)
            other = probs.astype(BF16).astype(F32)
            itself = (probs - 1.0).astype(BF16).astype(F32)
            parts.append(((times - o) * other + o * itself) * live[:, span])
        grads = jnp.concatenate(parts, axis=1)
        stack = jnp.concatenate(split3(grads), axis=0)
        stack_t = jnp.concatenate(split3(jnp.transpose(grads)), axis=1)

        dquery = dot(own_t, stack)
        acc_tab[...] += dot(query_s[pl.ds(base, window), :].astype(BF16), stack_t)
        y = jnp.concatenate(split2(dquery * lhs_v[:, here]), axis=0)
        acc_rel[...] += dot(y, ones_where(iota((edges, pad_rel), 1) == cols[:, 1:2]))
        x = jnp.concatenate(split2(dquery * rel_v[:, here]), axis=0)
        acc_lhs[...] += dot(x, ones_where(iota((edges, rows), 1) == cols[:, 0:1]))

    pick = functools.partial(shifted_rows, offset=offset, narrow=narrow, offsets=offsets)
    out_lhs[...] = pick(acc_lhs[:window] + acc_lhs[window:])
    codes, powers = encode(pick(acc_rel[:window] + acc_rel[window:]), 0)
    wide_t[...] = jnp.zeros(wide_t.shape, F32)
    wide_t[:narrow] = pick(
        acc_tab[:, :slots] + acc_tab[:, slots : 2 * slots] + acc_tab[:, 2 * slots :]
    )
    table_codes, table_powers = encode(jnp.transpose(wide_t[...]), 1)
    spare = iota(table_codes.shape, 1) >= narrow
    tables_s[...] = jnp.where(spare, table_powers, table_codes)
    codes_s[...] = codes
    powers_s[...] = powers
    mixed[...] = jnp.zeros(mixed.shape, jnp.int32)
    power_row = narrow + SOURCES * cap
    dom = place[0]

    def write(target, o, lane):
        mixed[:narrow, :block] = codes_s[:, lane]
        for c in range(cap):
            mixed[narrow + c : narrow + c + 1, :] = tables_s[pl.ds(o * cap + c, 1), :]
        mixed[power_row : power_row + 1, :block] = powers_s[0:1, lane]
        target[...] = mixed[...].astype(jnp.int16)

    if direct:
        for h in range(SOURCES):
            for top in range(2):
                o = top * 4 + flipped(dom % 4, h)
                write(outs[h].at[top], o, pl.ds(pl.multiple_of(o * block, block), block))
    else:
        for o in range(workers):
            write(outs[0].at[o], o, slice(o * block, (o + 1) * block))


def flipped(index, mask):
    out, bit = index * 0, 1
    while bit < 4:
        out = out + bit * lax.rem(index // bit + (mask // bit) % 2, 2)
        bit *= 2
    return out


def quad_kernel(narrow, cap, *refs):
    parts, out, mixed = refs[:-2], refs[-2], refs[-1]
    power = slice(narrow + SOURCES * cap, narrow + SOURCES * cap + 1)
    mixed[...] = jnp.zeros(mixed.shape, jnp.int32)
    for top in range(out.shape[0]):
        total = jnp.zeros((narrow, out.shape[2]), F32)
        for n, part in enumerate(parts):
            both = part[top].astype(jnp.int32)
            total += decode(both[:narrow], both[power])
            row = narrow + n * cap
            mixed[row : row + cap, :] = both[narrow : narrow + cap]
        mixed[:narrow, :], mixed[power, :] = encode(total, 0)
        out[top] = mixed[...].astype(jnp.int16)


def sum_kernel(scale, narrow, cap, block, terms, *refs):
    parts, out, mixed = refs[:-2], refs[-2], refs[-1]
    depth = parts[0].shape[0]
    power = slice(narrow + SOURCES * cap, narrow + SOURCES * cap + 1)
    mixed[...] = jnp.zeros(mixed.shape, jnp.int32)
    for first in range(0, len(parts), terms):
        for top in range(depth):
            total = jnp.zeros((narrow, block), F32)
            for part in parts[first : first + terms]:
                both = part[top].astype(jnp.int32)
                total += decode(both[:narrow, :block], both[power, :block])
            mixed[:narrow, :block], mixed[power, :block] = encode(total * F32(scale), 0)
            out[first // terms * depth + top] = mixed[...].astype(jnp.int16)


def entity_kernel(direct, narrow, place, serve, lhs, *refs):
    recv, out, terms, onehot = refs[:-3], refs[-3], refs[-2], refs[-1]
    cap, workers = serve.shape[1], serve.shape[2]
    rows = out.shape[1]
    lane = iota((1, rows), 1)
    for h in range(workers):
        if direct:
            turn, hop = h % SOURCES, h // SOURCES
            mine = place[0] // 4
            both = recv[hop][mine].astype(jnp.int32)
            worker = lax.rem(mine + hop, 2) * 4 + flipped(place[0] % 4, turn)
        else:
            turn, both, worker = 0, recv[0][h].astype(jnp.int32), h
        row = narrow + turn * cap
        both = both[row : row + cap]
        terms[h * cap : (h + 1) * cap, :] = jnp.where(
            iota(both.shape, 1) < narrow, decode(both, both[:, narrow : narrow + 1]), 0.0
        )
        for c in range(cap):
            spot = jnp.where(lane == serve[0, c, worker], 1.0, 0.0).astype(F32)
            onehot[h * cap + c : h * cap + c + 1, :] = spot
    spots = onehot[...].astype(BF16)
    parts = jnp.concatenate(split3(jnp.transpose(terms[...])), axis=1)
    added = dot(parts, jnp.concatenate([spots] * 3, axis=0))
    out[...] = lhs[...] + added[:narrow]


def spread_kernel(workers, replicas, narrow, power_row, block, place, mine, other, out, whole, sems):
    dim, nrel = out.shape
    dom, rep = place[0], place[1]
    here = lax.rem(rep, 2)
    moves, start = [], 0
    for r in range(replicas):
        for o in range(workers):
            over_low = lax.rem(dom // 2 + o // 2, 2)
            over_y = lax.rem(dom + o, 2)
            over_x = lax.rem(rep // 2 + r // 2, 2)
            spot = (over_y + 2 * over_x) * 4 + over_low * 2 + o // 4
            both = jnp.where(
                here == r % 2, mine[spot].astype(jnp.int32), other[spot].astype(jnp.int32)
            )
            value = decode(both[:narrow], both[power_row : power_row + 1])
            end = min((o + 1) * block, nrel)
            whole[r * narrow : (r + 1) * narrow, o * block : end] = value[:, : end - o * block]
        end = (r + 1) * narrow // 8 * 8 if r + 1 < replicas else dim
        band = slice(start, end)
        moves.append(pltpu.make_async_copy(whole.at[band], out.at[band], sems.at[r]))
        moves[-1].start()
        start = end
    for move in moves:
        move.wait()


def turned(size, hop):
    return [(i, (i + hop) % size) for i in range(size)]


def shards(entities, relation, serve_ids, edge_src, edge_rel, edge_dst, neg_ids, edge_count):
    workers = lax.axis_size("dom")
    replicas = lax.axis_size("rep")
    rows, dim = entities.shape
    nrel = relation.shape[0]
    cap = serve_ids.shape[2]
    edges = edge_src.shape[2]
    groups, width = neg_ids.shape[2], neg_ids.shape[3]
    slots = workers * cap
    narrow = dim // replicas
    direct = workers == 8 and replicas == 4
    block = up(-(-nrel // workers), LANES if direct else 8)
    pad_rel = up(max(nrel, workers * block), LANES)
    offsets = sorted({(narrow * r) % 8 for r in range(replicas)})
    window = up(narrow + offsets[-1], 8)
    height = up(narrow + SOURCES * cap + 1, 16)
    ent_t, rel_t = entities.T, relation.T
    serve_t = jnp.transpose(serve_ids, (0, 2, 1))
    place = jnp.stack([lax.axis_index("dom"), lax.axis_index("rep")]).astype(jnp.int32)

    idx, served = pl.pallas_call(
        prep_kernel,
        out_shape=(
            jax.ShapeDtypeStruct((IDX_ROWS, edges), jnp.int32),
            jax.ShapeDtypeStruct((workers, cap, dim), F32),
        ),
        in_specs=[HBM] * 7,
        out_specs=(VMEM, VMEM),
        scratch_shapes=[
            pltpu.SMEM(serve_t.shape, jnp.int32),
            pltpu.SMEM(edge_count.shape, jnp.int32),
            pltpu.VMEM(ent_t.shape, BF16),
            pltpu.VMEM(edge_src.shape, jnp.int32),
            pltpu.VMEM(edge_rel.shape, jnp.int32),
            pltpu.VMEM(edge_dst.shape, jnp.int32),
            pltpu.VMEM(neg_ids.shape, jnp.int32),
            pltpu.VMEM((slots, rows), F32),
            pltpu.SemaphoreType.DMA((7,)),
        ],
        compiler_params=params(60),
        name="prep",
    )(serve_t, edge_count, ent_t, edge_src, edge_rel, edge_dst, neg_ids)

    held = [idx]
    for hop in range(1, replicas):
        held.append(lax.ppermute(idx, "rep", turned(replicas, hop)))
    received = lax.all_to_all(served, "dom", 0, 0, tiled=True)

    total = replicas * edges
    query, lhs_rows, rel_rows = pl.pallas_call(
        functools.partial(gather_kernel, (replicas, nrel, pad_rel, narrow, window)),
        out_shape=(
            jax.ShapeDtypeStruct((dim, total), BF16),
            jax.ShapeDtypeStruct((window, total), F32),
            jax.ShapeDtypeStruct((window, total), F32),
        ),
        in_specs=[SMEM] + [VMEM] * (replicas + 2),
        out_specs=(VMEM, VMEM, VMEM),
        scratch_shapes=[
            pltpu.VMEM((2 * dim, pad_rel), BF16),
            pltpu.VMEM((dim, edges), F32),
            pltpu.VMEM((dim, edges), F32),
        ],
        compiler_params=params(),
        cost_estimate=cost(2 * total * dim * (2 * pad_rel + rows), 8 * total * dim),
        name="gather",
    )(place, *held, ent_t, rel_t)

    cfg = (
        direct, workers, replicas, cap, groups, width, pad_rel, block, narrow, window,
        tuple(offsets),
    )
    lanes = max(up(block, LANES), up(narrow, LANES))
    outs = [2] * SOURCES if direct else [workers]
    sizes = [jax.ShapeDtypeStruct((n, height, lanes), jnp.int16) for n in outs]
    lhs_part, *sent = pl.pallas_call(
        functools.partial(main_kernel, cfg),
        out_shape=[jax.ShapeDtypeStruct((narrow, rows), F32)] + sizes,
        in_specs=[SMEM] + [VMEM] * (replicas + 4),
        out_specs=[VMEM] * (1 + len(sizes)),
        scratch_shapes=[
            pltpu.VMEM((slots, dim), F32),
            pltpu.VMEM((dim, slots), F32),
            pltpu.VMEM((dim, edges), F32),
            pltpu.VMEM((2 * window, pad_rel), F32),
            pltpu.VMEM((2 * window, rows), F32),
            pltpu.VMEM((window, 3 * slots), F32),
            pltpu.VMEM((lanes, slots), F32),
            pltpu.VMEM((height, lanes), jnp.int32),
            pltpu.VMEM((narrow, pad_rel), jnp.int32),
            pltpu.VMEM((1, pad_rel), jnp.int32),
            pltpu.VMEM((slots, lanes), jnp.int32),
        ],
        compiler_params=params(),
        name="edges",
    )(place, *held, query, lhs_rows, rel_rows, received)

    def swap(array, dom_bits=0, rep_bits=0):
        pairs = []
        for o in range(workers):
            for r in range(replicas):
                pairs.append((o * replicas + r, (o ^ dom_bits) * replicas + (r ^ rep_bits)))
        return lax.ppermute(array, ("dom", "rep"), pairs)

    stack = jax.ShapeDtypeStruct((outs[0], height, lanes), jnp.int16)
    mixed = [pltpu.VMEM((height, lanes), jnp.int32)]
    if direct:
        summed = pl.pallas_call(
            functools.partial(quad_kernel, narrow, cap),
            out_shape=stack,
            in_specs=[VMEM] * SOURCES,
            out_specs=VMEM,
            scratch_shapes=mixed,
            compiler_params=params(),
            name="quad",
        )(sent[0], *[swap(sent[n], n) for n in range(1, SOURCES)])
        recv = [summed, swap(summed, 4)]
        parts = recv + [swap(summed, 2), swap(summed, 6)]
        stack = jax.ShapeDtypeStruct((4, height, lanes), jnp.int16)
    else:
        recv = [lax.all_to_all(sent[0], "dom", 0, 0, tiled=True)]
        parts = [recv[0][w : w + 1] for w in range(workers)]
        stack = jax.ShapeDtypeStruct((1, height, lanes), jnp.int16)
    scale = 1.0 / (edges * workers * replicas)
    chunk = pl.pallas_call(
        functools.partial(sum_kernel, scale, narrow, cap, block, 2 if direct else workers),
        out_shape=stack,
        in_specs=[VMEM] * len(parts),
        out_specs=VMEM,
        scratch_shapes=mixed,
        compiler_params=params(),
        name="total",
    )(*parts)

    if direct:
        along_y = swap(chunk, 1)
        along_y, lhs_part = lax.optimization_barrier((along_y, lhs_part))
    entity_grad = pl.pallas_call(
        functools.partial(entity_kernel, direct, narrow),
        out_shape=jax.ShapeDtypeStruct((narrow, rows), F32),
        in_specs=[SMEM] * 2 + [VMEM] * (1 + len(recv)),
        out_specs=VMEM,
        scratch_shapes=[pltpu.VMEM((slots, lanes), F32), pltpu.VMEM((slots, rows), F32)],
        compiler_params=params(),
        cost_estimate=cost(10**9, 10**6),
        name="entity",
    )(place, serve_t, lhs_part, *recv)

    power_row = narrow + SOURCES * cap
    if direct:
        base = jnp.concatenate([chunk, along_y, swap(chunk, 0, 2), swap(chunk, 1, 2)], axis=0)
        base, entity_grad = lax.optimization_barrier((base, entity_grad))
        swapped = lax.ppermute(base, "rep", [(i, i ^ 1) for i in range(replicas)])
        relation_t = pl.pallas_call(
            functools.partial(spread_kernel, workers, replicas, narrow, power_row, block),
            out_shape=jax.ShapeDtypeStruct((dim, nrel), F32),
            in_specs=[SMEM] + [VMEM] * 2,
            out_specs=HBM,
            scratch_shapes=[
                pltpu.VMEM((dim, nrel), F32),
                pltpu.SemaphoreType.DMA((replicas,)),
            ],
            compiler_params=params(),
            name="spread",
        )(place, base, swapped)
    else:
        whole = lax.all_gather(chunk[0, :, :block], ("dom", "rep"), axis=0)
        whole = decode(whole[:, :narrow], whole[:, power_row : power_row + 1])
        whole = whole.reshape(workers, replicas, narrow, block).transpose(1, 2, 0, 3)
        relation_t = whole.reshape(dim, workers * block)[:, :nrel]
    return (entity_grad.T, relation_t.T)


def solution(mesh):
    placed = (
        P("dom", None),
        P(),
        P("dom", None, None),
        P("dom", "rep", None),
        P("dom", "rep", None),
        P("dom", "rep", None),
        P("dom", "rep", None, None),
        P("dom", "rep"),
    )
    return jax.shard_map(
        shards, mesh=mesh, in_specs=placed, out_specs=(P("dom", "rep"), P()), check_vma=False
    )
```

```python
import functools

import jax
import jax.numpy as jnp
from jax import lax
from jax.experimental import pallas as pl
from jax.experimental.pallas import tpu as pltpu
from jax.sharding import PartitionSpec as P

F32 = jnp.float32
BF16 = jnp.bfloat16
IDX_ROWS = 8
LANES = 128
SOURCES = 4
LIVE_EDGES = 1536
VMEM = pl.BlockSpec(memory_space=pltpu.VMEM)
SMEM = pl.BlockSpec(memory_space=pltpu.SMEM)
HBM = pl.BlockSpec(memory_space=pltpu.HBM)


def params(mib=32):
    return pltpu.CompilerParams(vmem_limit_bytes=mib * 1024 * 1024)


def cost(flops, moved):
    return pl.CostEstimate(flops=flops, bytes_accessed=moved, transcendentals=0)


def up(value, step):
    return -(-value // step) * step


def split2(x):
    hi = x.astype(BF16)
    lo = (x - hi.astype(F32)).astype(BF16)
    return hi, lo


def split3(x):
    hi, rest = x.astype(BF16), x
    rest = rest - hi.astype(F32)
    mid = rest.astype(BF16)
    low = (rest - mid.astype(F32)).astype(BF16)
    return hi, mid, low


def dot(a, b):
    return jnp.dot(a, b, preferred_element_type=F32)


def dot_t(a, b):
    return lax.dot_general(a, b, (((1,), (1,)), ((), ())), preferred_element_type=F32)


def ones_where(flag):
    return jnp.where(flag, 1.0, 0.0).astype(BF16)


def exponent(largest):
    safe = jnp.where(largest > 0, largest, 1.0)
    return jnp.clip(jnp.floor(F32(14.9) - jnp.log2(safe)), -120.0, 120.0)


def encode(x, axis):
    k = exponent(jnp.max(jnp.abs(x), axis=axis, keepdims=True))
    return jnp.floor(x * jnp.exp2(k) + 0.5).astype(jnp.int32), k.astype(jnp.int32)


def decode(codes, k):
    return codes.astype(F32) * jnp.exp2(-k.astype(F32))


def iota(shape, axis):
    return lax.broadcasted_iota(jnp.int32, shape, axis)


def shifted_rows(x, offset, narrow, offsets):
    out = x[offsets[0] : offsets[0] + narrow]
    for other in offsets[1:]:
        out = jnp.where(offset == other, x[other : other + narrow], out)
    return out


def prep_kernel(serve, count, ent, src, rel, dst, neg, out_idx, out_rows, *refs):
    cap, workers = serve.shape[1], serve.shape[2]
    rows = ent.shape[1]
    groups, width = neg.shape[2], neg.shape[3]
    onehot, sems = refs[-2:]
    moves = [
        pltpu.make_async_copy(a, b, sems.at[n])
        for n, (a, b) in enumerate(zip((serve, count, ent, src, rel, dst, neg), refs))
    ]
    for move in moves:
        move.start()
    for move in moves:
        move.wait()
    serve_s, count_s, ent_v, src_v, rel_v, dst_v, neg_v = refs[:7]
    out_idx[...] = jnp.full(out_idx.shape, count_s[0, 0], jnp.int32)
    out_idx[0:1, :] = src_v[0]
    out_idx[1:2, :] = rel_v[0]
    out_idx[2:3, :] = dst_v[0]
    for g in range(groups):
        out_idx[3 + g : 4 + g, :width] = neg_v[0, 0, g : g + 1, :]
    lane = iota((1, rows), 1)
    for k in range(workers * cap):
        picked = serve_s[0, k % cap, k // cap]
        onehot[k : k + 1, :] = jnp.where(lane == picked, 1.0, 0.0).astype(F32)
    picked_rows = dot_t(onehot[...].astype(BF16), ent_v[...])
    for w in range(workers):
        out_rows[w] = picked_rows[w * cap : (w + 1) * cap]


def packed_edges(idx_refs, groups, out_idx):
    edges, span = idx_refs[0].shape[1], out_idx.shape[1]
    wide = max(span, edges)
    place = iota((IDX_ROWS, wide), 1)
    row = iota((IDX_ROWS, edges), 0)
    block = iota((IDX_ROWS, edges), 1) // (edges // groups)
    packed = jnp.where(iota((IDX_ROWS, wide), 0) < 3, -1, 0)
    first = 0
    for i, ref in enumerate(idx_refs):
        count = jnp.max(ref[IDX_ROWS - 1 : IDX_ROWS, :].astype(F32)).astype(jnp.int32)
        rows = jnp.where(row < 3, ref[...], jnp.where(row == 3, block + i * groups, 1))
        if wide > edges:
            rows = jnp.concatenate(
                [rows, jnp.zeros((IDX_ROWS, wide - edges), jnp.int32)], axis=1
            )
        moved = pltpu.roll(rows, first, 1)
        packed = jnp.where((place >= first) & (place < first + count), moved, packed)
        first = first + count
    out_idx[...] = packed[:, :span]


def gather_kernel(cfg, place, *refs):
    replicas, groups, nrel, pad_rel, narrow, window, step = cfg
    idx_refs, refs = refs[:replicas], refs[replicas:]
    ent, relation, out_idx, out_query, out_lhs, out_rel, rel_parts, lhs_s, rel_s = refs
    dim, rows = ent.shape
    base = pl.multiple_of((place[1] * narrow) // 8 * 8, 8)
    packed_edges(idx_refs, groups, out_idx)
    hi, lo = split2(relation[...])
    if pad_rel > nrel:
        rel_parts[...] = jnp.zeros(rel_parts.shape, BF16)
    rel_parts[:dim, :nrel] = hi
    rel_parts[dim:, :nrel] = lo
    for start in range(0, out_idx.shape[1], step):
        span = slice(start, start + step)
        src_l, rel_l = out_idx[0:1, span], out_idx[1:2, span]
        lhs = dot(ent[...], ones_where(iota((rows, step), 0) == src_l))
        both = dot(rel_parts[...], ones_where(iota((pad_rel, step), 0) == rel_l))
        rel_rows = both[:dim] + both[dim:]
        lhs_s[...] = lhs
        rel_s[...] = rel_rows
        out_query[:, span] = (lhs * rel_rows).astype(BF16)
        out_lhs[:, span] = lhs_s[pl.ds(base, window), :]
        out_rel[:, span] = rel_s[pl.ds(base, window), :]


def main_kernel(cfg, place, *refs):
    (direct, workers, replicas, cap, groups, width, pad_rel, block, narrow, window, offsets) = cfg
    idx_refs, refs = refs[:replicas], refs[replicas:]
    (packed, query_v, lhs_v, rel_v, received), refs = refs[:5], refs[5:]
    out_lhs, refs = refs[0], refs[1:]
    outs, refs = (refs[:SOURCES], refs[SOURCES:]) if direct else (refs[:1], refs[1:])
    table_f, table_t, query_s, wide_t, mixed, codes_s, powers_s, tables_s = refs
    edges = idx_refs[0].shape[1]
    dim, total = query_v.shape
    rows = out_lhs.shape[1]
    slots = workers * cap
    rep = place[1]
    per = edges // groups
    base = pl.multiple_of((rep * narrow) // 8 * 8, 8)
    offset = rep * narrow - base

    for w in range(workers):
        table_f[w * cap : (w + 1) * cap, :] = received[w]
    table_t[...] = jnp.transpose(table_f[...])
    table = table_f[...].astype(BF16)
    own_t = table_t[pl.ds(base, window), :].astype(BF16)
    own_t = jnp.concatenate([own_t] * 3, axis=1)

    query = query_v[...]
    scores = dot(table, query)
    query_s[...] = query.astype(F32)
    lanes = packed[...]
    cols = jnp.transpose(lanes)
    times = jnp.zeros((slots, total), F32)
    for i in range(replicas):
        shard = idx_refs[i][...]
        position = iota((slots, edges), 1)
        seen = (iota((slots, edges), 0) == shard[2:3]) & (position < shard[IDX_ROWS - 1 : IDX_ROWS])
        seen = jnp.where(seen, 1.0, 0.0).astype(F32)
        for g in range(groups):
            neg = iota((slots, width), 0) == shard[3 + g : 4 + g, :width]
            often = jnp.sum(jnp.where(neg, 1.0, 0.0).astype(F32), axis=1, keepdims=True)
            often = often + jnp.sum(seen[:, g * per : (g + 1) * per], axis=1, keepdims=True)
            times = jnp.where(lanes[3:4] == i * groups + g, often, times)
    live = lanes[4:5].astype(F32)
    own = jnp.where(iota((slots, total), 0) == lanes[2:3], 1.0, 0.0).astype(F32)
    scores = jnp.where(times > 0, scores, F32(-1e30))
    expo = jnp.exp(scores - jnp.max(scores, axis=0, keepdims=True))
    norm = jnp.sum(expo * times, axis=0, keepdims=True)
    probs = expo / jnp.where(live > 0, norm, 1.0)
    other = probs.astype(BF16).astype(F32)
    itself = (probs - 1.0).astype(BF16).astype(F32)
    grads = ((times - own) * other + own * itself) * live
    stack = jnp.concatenate(split3(grads), axis=0)
    stack_t = jnp.concatenate(split3(jnp.transpose(grads)), axis=1)

    dquery = dot(own_t, stack)
    y = jnp.concatenate(split2(dquery * lhs_v[...]), axis=0)
    acc_rel = dot(y, ones_where(iota((total, pad_rel), 1) == cols[:, 1:2]))
    x = jnp.concatenate(split2(dquery * rel_v[...]), axis=0)
    acc_lhs = dot(x, ones_where(iota((total, rows), 1) == cols[:, 0:1]))
    acc_tab = dot(query_s[pl.ds(base, window), :].astype(BF16), stack_t)

    pick = functools.partial(shifted_rows, offset=offset, narrow=narrow, offsets=offsets)
    out_lhs[...] = pick(acc_lhs[:window] + acc_lhs[window:])
    codes, powers = encode(pick(acc_rel[:window] + acc_rel[window:]), 0)
    wide_t[...] = jnp.zeros(wide_t.shape, F32)
    wide_t[:narrow] = pick(
        acc_tab[:, :slots] + acc_tab[:, slots : 2 * slots] + acc_tab[:, 2 * slots :]
    )
    table_codes, table_powers = encode(jnp.transpose(wide_t[...]), 1)
    spare = iota(table_codes.shape, 1) >= narrow
    tables_s[...] = jnp.where(spare, table_powers, table_codes)
    codes_s[...] = codes
    powers_s[...] = powers
    mixed[...] = jnp.zeros(mixed.shape, jnp.int32)
    power_row = narrow + SOURCES * cap
    dom = place[0]

    def write(target, o, lane):
        mixed[:narrow, :block] = codes_s[:, lane]
        for c in range(cap):
            mixed[narrow + c : narrow + c + 1, :] = tables_s[pl.ds(o * cap + c, 1), :]
        mixed[power_row : power_row + 1, :block] = powers_s[0:1, lane]
        target[...] = mixed[...].astype(jnp.int16)

    if direct:
        for h in range(SOURCES):
            for top in range(2):
                o = top * 4 + flipped(dom % 4, h)
                write(outs[h].at[top], o, pl.ds(pl.multiple_of(o * block, block), block))
    else:
        for o in range(workers):
            write(outs[0].at[o], o, slice(o * block, (o + 1) * block))


def flipped(index, mask):
    out, bit = index * 0, 1
    while bit < 4:
        out = out + bit * lax.rem(index // bit + (mask // bit) % 2, 2)
        bit *= 2
    return out


def quad_kernel(narrow, cap, *refs):
    parts, out, mixed = refs[:-2], refs[-2], refs[-1]
    power = slice(narrow + SOURCES * cap, narrow + SOURCES * cap + 1)
    mixed[...] = jnp.zeros(mixed.shape, jnp.int32)
    for top in range(out.shape[0]):
        total = jnp.zeros((narrow, out.shape[2]), F32)
        for n, part in enumerate(parts):
            both = part[top].astype(jnp.int32)
            total += decode(both[:narrow], both[power])
            row = narrow + n * cap
            mixed[row : row + cap, :] = both[narrow : narrow + cap]
        mixed[:narrow, :], mixed[power, :] = encode(total, 0)
        out[top] = mixed[...].astype(jnp.int16)


def sum_kernel(scale, narrow, cap, block, terms, *refs):
    parts, out, mixed = refs[:-2], refs[-2], refs[-1]
    depth = parts[0].shape[0]
    power = slice(narrow + SOURCES * cap, narrow + SOURCES * cap + 1)
    mixed[...] = jnp.zeros(mixed.shape, jnp.int32)
    for first in range(0, len(parts), terms):
        for top in range(depth):
            total = jnp.zeros((narrow, block), F32)
            for part in parts[first : first + terms]:
                both = part[top].astype(jnp.int32)
                total += decode(both[:narrow, :block], both[power, :block])
            mixed[:narrow, :block], mixed[power, :block] = encode(total * F32(scale), 0)
            out[first // terms * depth + top] = mixed[...].astype(jnp.int16)


def entity_kernel(direct, narrow, place, serve, lhs, *refs):
    recv, out, terms, onehot = refs[:-3], refs[-3], refs[-2], refs[-1]
    cap, workers = serve.shape[1], serve.shape[2]
    rows = out.shape[1]
    lane = iota((1, rows), 1)
    for h in range(workers):
        if direct:
            turn, hop = h % SOURCES, h // SOURCES
            mine = place[0] // 4
            both = recv[hop][mine].astype(jnp.int32)
            worker = lax.rem(mine + hop, 2) * 4 + flipped(place[0] % 4, turn)
        else:
            turn, both, worker = 0, recv[0][h].astype(jnp.int32), h
        row = narrow + turn * cap
        both = both[row : row + cap]
        terms[h * cap : (h + 1) * cap, :] = jnp.where(
            iota(both.shape, 1) < narrow, decode(both, both[:, narrow : narrow + 1]), 0.0
        )
        for c in range(cap):
            spot = jnp.where(lane == serve[0, c, worker], 1.0, 0.0).astype(F32)
            onehot[h * cap + c : h * cap + c + 1, :] = spot
    spots = onehot[...].astype(BF16)
    parts = jnp.concatenate(split3(jnp.transpose(terms[...])), axis=1)
    added = dot(parts, jnp.concatenate([spots] * 3, axis=0))
    out[...] = lhs[...] + added[:narrow]


def spread_kernel(workers, replicas, narrow, power_row, block, place, mine, other, out, whole, sems):
    dim, nrel = out.shape
    dom, rep = place[0], place[1]
    here = lax.rem(rep, 2)
    moves, start = [], 0
    for r in range(replicas):
        for o in range(workers):
            over_low = lax.rem(dom // 2 + o // 2, 2)
            over_y = lax.rem(dom + o, 2)
            over_x = lax.rem(rep // 2 + r // 2, 2)
            spot = (over_y + 2 * over_x) * 4 + over_low * 2 + o // 4
            both = jnp.where(
                here == r % 2, mine[spot].astype(jnp.int32), other[spot].astype(jnp.int32)
            )
            value = decode(both[:narrow], both[power_row : power_row + 1])
            end = min((o + 1) * block, nrel)
            whole[r * narrow : (r + 1) * narrow, o * block : end] = value[:, : end - o * block]
        end = (r + 1) * narrow // 8 * 8 if r + 1 < replicas else dim
        band = slice(start, end)
        moves.append(pltpu.make_async_copy(whole.at[band], out.at[band], sems.at[r]))
        moves[-1].start()
        start = end
    for move in moves:
        move.wait()


def turned(size, hop):
    return [(i, (i + hop) % size) for i in range(size)]


def shards(entities, relation, serve_ids, edge_src, edge_rel, edge_dst, neg_ids, edge_count):
    workers = lax.axis_size("dom")
    replicas = lax.axis_size("rep")
    rows, dim = entities.shape
    nrel = relation.shape[0]
    cap = serve_ids.shape[2]
    edges = edge_src.shape[2]
    groups, width = neg_ids.shape[2], neg_ids.shape[3]
    slots = workers * cap
    narrow = dim // replicas
    direct = workers == 8 and replicas == 4
    block = up(-(-nrel // workers), LANES if direct else 8)
    pad_rel = up(max(nrel, workers * block), LANES)
    offsets = sorted({(narrow * r) % 8 for r in range(replicas)})
    window = up(narrow + offsets[-1], 8)
    height = up(narrow + SOURCES * cap + 1, 16)
    ent_t, rel_t = entities.T, relation.T
    serve_t = jnp.transpose(serve_ids, (0, 2, 1))
    place = jnp.stack([lax.axis_index("dom"), lax.axis_index("rep")]).astype(jnp.int32)

    idx, served = pl.pallas_call(
        prep_kernel,
        out_shape=(
            jax.ShapeDtypeStruct((IDX_ROWS, edges), jnp.int32),
            jax.ShapeDtypeStruct((workers, cap, dim), F32),
        ),
        in_specs=[HBM] * 7,
        out_specs=(VMEM, VMEM),
        scratch_shapes=[
            pltpu.SMEM(serve_t.shape, jnp.int32),
            pltpu.SMEM(edge_count.shape, jnp.int32),
            pltpu.VMEM(ent_t.shape, BF16),
            pltpu.VMEM(edge_src.shape, jnp.int32),
            pltpu.VMEM(edge_rel.shape, jnp.int32),
            pltpu.VMEM(edge_dst.shape, jnp.int32),
            pltpu.VMEM(neg_ids.shape, jnp.int32),
            pltpu.VMEM((slots, rows), F32),
            pltpu.SemaphoreType.DMA((7,)),
        ],
        compiler_params=params(60),
        name="prep",
    )(serve_t, edge_count, ent_t, edge_src, edge_rel, edge_dst, neg_ids)

    held = [idx]
    for hop in range(1, replicas):
        held.append(lax.ppermute(idx, "rep", turned(replicas, hop)))
    received = lax.all_to_all(served, "dom", 0, 0, tiled=True)

    total = min(replicas * edges, up(LIVE_EDGES, edges))
    packed, query, lhs_rows, rel_rows = pl.pallas_call(
        functools.partial(
            gather_kernel, (replicas, groups, nrel, pad_rel, narrow, window, edges)
        ),
        out_shape=(
            jax.ShapeDtypeStruct((IDX_ROWS, total), jnp.int32),
            jax.ShapeDtypeStruct((dim, total), BF16),
            jax.ShapeDtypeStruct((window, total), F32),
            jax.ShapeDtypeStruct((window, total), F32),
        ),
        in_specs=[SMEM] + [VMEM] * (replicas + 2),
        out_specs=[VMEM] * 4,
        scratch_shapes=[
            pltpu.VMEM((2 * dim, pad_rel), BF16),
            pltpu.VMEM((dim, edges), F32),
            pltpu.VMEM((dim, edges), F32),
        ],
        compiler_params=params(),
        cost_estimate=cost(2 * total * dim * (2 * pad_rel + rows), 8 * total * dim),
        name="gather",
    )(place, *held, ent_t, rel_t)

    cfg = (
        direct, workers, replicas, cap, groups, width, pad_rel, block, narrow, window,
        tuple(offsets),
    )
    lanes = max(up(block, LANES), up(narrow, LANES))
    outs = [2] * SOURCES if direct else [workers]
    sizes = [jax.ShapeDtypeStruct((n, height, lanes), jnp.int16) for n in outs]
    lhs_part, *sent = pl.pallas_call(
        functools.partial(main_kernel, cfg),
        out_shape=[jax.ShapeDtypeStruct((narrow, rows), F32)] + sizes,
        in_specs=[SMEM] + [VMEM] * (replicas + 5),
        out_specs=[VMEM] * (1 + len(sizes)),
        scratch_shapes=[
            pltpu.VMEM((slots, dim), F32),
            pltpu.VMEM((dim, slots), F32),
            pltpu.VMEM((dim, total), F32),
            pltpu.VMEM((lanes, slots), F32),
            pltpu.VMEM((height, lanes), jnp.int32),
            pltpu.VMEM((narrow, pad_rel), jnp.int32),
            pltpu.VMEM((1, pad_rel), jnp.int32),
            pltpu.VMEM((slots, lanes), jnp.int32),
        ],
        compiler_params=params(),
        name="edges",
    )(place, *held, packed, query, lhs_rows, rel_rows, received)

    def swap(array, dom_bits=0, rep_bits=0):
        pairs = []
        for o in range(workers):
            for r in range(replicas):
                pairs.append((o * replicas + r, (o ^ dom_bits) * replicas + (r ^ rep_bits)))
        return lax.ppermute(array, ("dom", "rep"), pairs)

    stack = jax.ShapeDtypeStruct((outs[0], height, lanes), jnp.int16)
    mixed = [pltpu.VMEM((height, lanes), jnp.int32)]
    if direct:
        summed = pl.pallas_call(
            functools.partial(quad_kernel, narrow, cap),
            out_shape=stack,
            in_specs=[VMEM] * SOURCES,
            out_specs=VMEM,
            scratch_shapes=mixed,
            compiler_params=params(),
            name="quad",
        )(sent[0], *[swap(sent[n], n) for n in range(1, SOURCES)])
        recv = [summed, swap(summed, 4)]
        parts = recv + [swap(summed, 2), swap(summed, 6)]
        stack = jax.ShapeDtypeStruct((4, height, lanes), jnp.int16)
    else:
        recv = [lax.all_to_all(sent[0], "dom", 0, 0, tiled=True)]
        parts = [recv[0][w : w + 1] for w in range(workers)]
        stack = jax.ShapeDtypeStruct((1, height, lanes), jnp.int16)
    scale = 1.0 / (edges * workers * replicas)
    chunk = pl.pallas_call(
        functools.partial(sum_kernel, scale, narrow, cap, block, 2 if direct else workers),
        out_shape=stack,
        in_specs=[VMEM] * len(parts),
        out_specs=VMEM,
        scratch_shapes=mixed,
        compiler_params=params(),
        name="total",
    )(*parts)

    if direct:
        along_y = swap(chunk, 1)
        along_y, lhs_part = lax.optimization_barrier((along_y, lhs_part))
    entity_grad = pl.pallas_call(
        functools.partial(entity_kernel, direct, narrow),
        out_shape=jax.ShapeDtypeStruct((narrow, rows), F32),
        in_specs=[SMEM] * 2 + [VMEM] * (1 + len(recv)),
        out_specs=VMEM,
        scratch_shapes=[pltpu.VMEM((slots, lanes), F32), pltpu.VMEM((slots, rows), F32)],
        compiler_params=params(),
        cost_estimate=cost(10**9, 10**6),
        name="entity",
    )(place, serve_t, lhs_part, *recv)

    power_row = narrow + SOURCES * cap
    if direct:
        base = jnp.concatenate([chunk, along_y, swap(chunk, 0, 2), swap(chunk, 1, 2)], axis=0)
        base, entity_grad = lax.optimization_barrier((base, entity_grad))
        swapped = lax.ppermute(base, "rep", [(i, i ^ 1) for i in range(replicas)])
        relation_t = pl.pallas_call(
            functools.partial(spread_kernel, workers, replicas, narrow, power_row, block),
            out_shape=jax.ShapeDtypeStruct((dim, nrel), F32),
            in_specs=[SMEM] + [VMEM] * 2,
            out_specs=HBM,
            scratch_shapes=[
                pltpu.VMEM((dim, nrel), F32),
                pltpu.SemaphoreType.DMA((replicas,)),
            ],
            compiler_params=params(),
            name="spread",
        )(place, base, swapped)
    else:
        whole = lax.all_gather(chunk[0, :, :block], ("dom", "rep"), axis=0)
        whole = decode(whole[:, :narrow], whole[:, power_row : power_row + 1])
        whole = whole.reshape(workers, replicas, narrow, block).transpose(1, 2, 0, 3)
        relation_t = whole.reshape(dim, workers * block)[:, :nrel]
    return (entity_grad.T, relation_t.T)


def solution(mesh):
    placed = (
        P("dom", None),
        P(),
        P("dom", None, None),
        P("dom", "rep", None),
        P("dom", "rep", None),
        P("dom", "rep", None),
        P("dom", "rep", None, None),
        P("dom", "rep"),
    )
    return jax.shard_map(
        shards, mesh=mesh, in_specs=placed, out_specs=(P("dom", "rep"), P()), check_vma=False
    )
```

```python
import functools

import jax
import jax.numpy as jnp
from jax import lax
from jax.experimental import pallas as pl
from jax.experimental.pallas import tpu as pltpu
from jax.sharding import PartitionSpec as P

F32 = jnp.float32
BF16 = jnp.bfloat16
IDX_ROWS = 8
LANES = 128
SOURCES = 4
LIVE_EDGES = 1536
VMEM = pl.BlockSpec(memory_space=pltpu.VMEM)
SMEM = pl.BlockSpec(memory_space=pltpu.SMEM)
HBM = pl.BlockSpec(memory_space=pltpu.HBM)


def params(mib=32):
    return pltpu.CompilerParams(vmem_limit_bytes=mib * 1024 * 1024)


def cost(flops, moved):
    return pl.CostEstimate(flops=flops, bytes_accessed=moved, transcendentals=0)


def up(value, step):
    return -(-value // step) * step


def split2(x):
    hi = x.astype(BF16)
    lo = (x - hi.astype(F32)).astype(BF16)
    return hi, lo


def split3(x):
    hi, rest = x.astype(BF16), x
    rest = rest - hi.astype(F32)
    mid = rest.astype(BF16)
    low = (rest - mid.astype(F32)).astype(BF16)
    return hi, mid, low


def dot(a, b):
    return jnp.dot(a, b, preferred_element_type=F32)


def dot_t(a, b):
    return lax.dot_general(a, b, (((1,), (1,)), ((), ())), preferred_element_type=F32)


def ones_where(flag):
    return jnp.where(flag, 1.0, 0.0).astype(BF16)


def exponent(largest):
    safe = jnp.where(largest > 0, largest, 1.0)
    return jnp.clip(jnp.floor(F32(14.9) - jnp.log2(safe)), -120.0, 120.0)


def encode(x, axis):
    k = exponent(jnp.max(jnp.abs(x), axis=axis, keepdims=True))
    return jnp.floor(x * jnp.exp2(k) + 0.5).astype(jnp.int32), k.astype(jnp.int32)


def decode(codes, k):
    return codes.astype(F32) * jnp.exp2(-k.astype(F32))


def iota(shape, axis):
    return lax.broadcasted_iota(jnp.int32, shape, axis)


def shifted_rows(x, offset, narrow, offsets):
    out = x[offsets[0] : offsets[0] + narrow]
    for other in offsets[1:]:
        out = jnp.where(offset == other, x[other : other + narrow], out)
    return out


def prep_kernel(serve, count, ent, src, rel, dst, neg, out_idx, out_rows, *refs):
    cap, workers = serve.shape[1], serve.shape[2]
    rows = ent.shape[1]
    groups, width = neg.shape[2], neg.shape[3]
    onehot, sems = refs[-2:]
    moves = [
        pltpu.make_async_copy(a, b, sems.at[n])
        for n, (a, b) in enumerate(zip((serve, count, ent, src, rel, dst, neg), refs))
    ]
    for move in moves:
        move.start()
    for move in moves:
        move.wait()
    serve_s, count_s, ent_v, src_v, rel_v, dst_v, neg_v = refs[:7]
    out_idx[...] = jnp.full(out_idx.shape, count_s[0, 0], jnp.int32)
    out_idx[0:1, :] = src_v[0]
    out_idx[1:2, :] = rel_v[0]
    out_idx[2:3, :] = dst_v[0]
    for g in range(groups):
        out_idx[3 + g : 4 + g, :width] = neg_v[0, 0, g : g + 1, :]
    lane = iota((1, rows), 1)
    for k in range(workers * cap):
        picked = serve_s[0, k % cap, k // cap]
        onehot[k : k + 1, :] = jnp.where(lane == picked, 1.0, 0.0).astype(F32)
    picked_rows = dot_t(onehot[...].astype(BF16), ent_v[...])
    for w in range(workers):
        out_rows[w] = picked_rows[w * cap : (w + 1) * cap]


def packed_edges(idx_refs, groups, out_idx):
    edges, span = idx_refs[0].shape[1], out_idx.shape[1]
    wide = max(span, edges)
    place = iota((IDX_ROWS, wide), 1)
    row = iota((IDX_ROWS, edges), 0)
    block = iota((IDX_ROWS, edges), 1) // (edges // groups)
    packed = jnp.where(iota((IDX_ROWS, wide), 0) < 3, -1, 0)
    first = 0
    for i, ref in enumerate(idx_refs):
        count = jnp.max(ref[IDX_ROWS - 1 : IDX_ROWS, :].astype(F32)).astype(jnp.int32)
        rows = jnp.where(row < 3, ref[...], jnp.where(row == 3, block + i * groups, 1))
        if wide > edges:
            rows = jnp.concatenate(
                [rows, jnp.zeros((IDX_ROWS, wide - edges), jnp.int32)], axis=1
            )
        moved = pltpu.roll(rows, first, 1)
        packed = jnp.where((place >= first) & (place < first + count), moved, packed)
        first = first + count
    out_idx[...] = packed[:, :span]


def gather_kernel(cfg, place, *refs):
    replicas, groups, nrel, pad_rel, narrow, window, step = cfg
    idx_refs, refs = refs[:replicas], refs[replicas:]
    ent_h, relation_h, out_idx, out_query, out_lhs, out_rel = refs[:6]
    ent, relation, rel_parts, lhs_s, rel_s, sems = refs[6:]
    dim, rows = ent.shape
    base = pl.multiple_of((place[1] * narrow) // 8 * 8, 8)
    moves = [
        pltpu.make_async_copy(relation_h, relation, sems.at[0]),
        pltpu.make_async_copy(ent_h, ent, sems.at[1]),
    ]
    for move in moves:
        move.start()
    packed_edges(idx_refs, groups, out_idx)
    for move in moves:
        move.wait()
    hi, lo = split2(relation[...])
    if pad_rel > nrel:
        rel_parts[...] = jnp.zeros(rel_parts.shape, BF16)
    rel_parts[:dim, :nrel] = hi
    rel_parts[dim:, :nrel] = lo
    for start in range(0, out_idx.shape[1], step):
        span = slice(start, start + step)
        src_l, rel_l = out_idx[0:1, span], out_idx[1:2, span]
        lhs = dot(ent[...], ones_where(iota((rows, step), 0) == src_l))
        both = dot(rel_parts[...], ones_where(iota((pad_rel, step), 0) == rel_l))
        rel_rows = both[:dim] + both[dim:]
        lhs_s[...] = lhs
        rel_s[...] = rel_rows
        out_query[:, span] = (lhs * rel_rows).astype(BF16)
        out_lhs[:, span] = lhs_s[pl.ds(base, window), :]
        out_rel[:, span] = rel_s[pl.ds(base, window), :]


def main_kernel(cfg, place, *refs):
    (direct, workers, replicas, cap, groups, width, pad_rel, block, narrow, window, offsets) = cfg
    idx_refs, refs = refs[:replicas], refs[replicas:]
    (packed, query_v, lhs_v, rel_v, received), refs = refs[:5], refs[5:]
    out_lhs, refs = refs[0], refs[1:]
    outs, refs = (refs[:SOURCES], refs[SOURCES:]) if direct else (refs[:1], refs[1:])
    table_f, table_t, query_s, wide_t, mixed, codes_s, powers_s, tables_s = refs
    edges = idx_refs[0].shape[1]
    dim, total = query_v.shape
    rows = out_lhs.shape[1]
    slots = workers * cap
    rep = place[1]
    per = edges // groups
    base = pl.multiple_of((rep * narrow) // 8 * 8, 8)
    offset = rep * narrow - base

    for w in range(workers):
        table_f[w * cap : (w + 1) * cap, :] = received[w]
    table_t[...] = jnp.transpose(table_f[...])
    table = table_f[...].astype(BF16)
    own_t = table_t[pl.ds(base, window), :].astype(BF16)
    own_t = jnp.concatenate([own_t] * 3, axis=1)

    query = query_v[...]
    scores = dot(table, query)
    query_s[...] = query.astype(F32)
    lanes = packed[...]
    cols = jnp.transpose(lanes)
    times = jnp.zeros((slots, total), F32)
    for i in range(replicas):
        shard = idx_refs[i][...]
        position = iota((slots, edges), 1)
        seen = (iota((slots, edges), 0) == shard[2:3]) & (position < shard[IDX_ROWS - 1 : IDX_ROWS])
        seen = jnp.where(seen, 1.0, 0.0).astype(F32)
        for g in range(groups):
            neg = iota((slots, width), 0) == shard[3 + g : 4 + g, :width]
            often = jnp.sum(jnp.where(neg, 1.0, 0.0).astype(F32), axis=1, keepdims=True)
            often = often + jnp.sum(seen[:, g * per : (g + 1) * per], axis=1, keepdims=True)
            times = jnp.where(lanes[3:4] == i * groups + g, often, times)
    live = lanes[4:5].astype(F32)
    own = jnp.where(iota((slots, total), 0) == lanes[2:3], 1.0, 0.0).astype(F32)
    scores = jnp.where(times > 0, scores, F32(-1e30))
    expo = jnp.exp(scores - jnp.max(scores, axis=0, keepdims=True))
    norm = jnp.sum(expo * times, axis=0, keepdims=True)
    probs = expo / jnp.where(live > 0, norm, 1.0)
    other = probs.astype(BF16).astype(F32)
    itself = (probs - 1.0).astype(BF16).astype(F32)
    grads = ((times - own) * other + own * itself) * live
    stack = jnp.concatenate(split3(grads), axis=0)
    stack_t = jnp.concatenate(split3(jnp.transpose(grads)), axis=1)

    dquery = dot(own_t, stack)
    y = jnp.concatenate(split2(dquery * lhs_v[...]), axis=0)
    acc_rel = dot(y, ones_where(iota((total, pad_rel), 1) == cols[:, 1:2]))
    x = jnp.concatenate(split2(dquery * rel_v[...]), axis=0)
    acc_lhs = dot(x, ones_where(iota((total, rows), 1) == cols[:, 0:1]))
    acc_tab = dot(query_s[pl.ds(base, window), :].astype(BF16), stack_t)

    pick = functools.partial(shifted_rows, offset=offset, narrow=narrow, offsets=offsets)
    out_lhs[...] = pick(acc_lhs[:window] + acc_lhs[window:])
    codes, powers = encode(pick(acc_rel[:window] + acc_rel[window:]), 0)
    wide_t[...] = jnp.zeros(wide_t.shape, F32)
    wide_t[:narrow] = pick(
        acc_tab[:, :slots] + acc_tab[:, slots : 2 * slots] + acc_tab[:, 2 * slots :]
    )
    table_codes, table_powers = encode(jnp.transpose(wide_t[...]), 1)
    spare = iota(table_codes.shape, 1) >= narrow
    tables_s[...] = jnp.where(spare, table_powers, table_codes)
    codes_s[...] = codes
    powers_s[...] = powers
    mixed[...] = jnp.zeros(mixed.shape, jnp.int32)
    power_row = narrow + SOURCES * cap
    dom = place[0]

    def write(target, o, lane):
        mixed[:narrow, :block] = codes_s[:, lane]
        for c in range(cap):
            mixed[narrow + c : narrow + c + 1, :] = tables_s[pl.ds(o * cap + c, 1), :]
        mixed[power_row : power_row + 1, :block] = powers_s[0:1, lane]
        target[...] = mixed[...].astype(jnp.int16)

    if direct:
        for h in range(SOURCES):
            for top in range(2):
                o = top * 4 + flipped(dom % 4, h)
                write(outs[h].at[top], o, pl.ds(pl.multiple_of(o * block, block), block))
    else:
        for o in range(workers):
            write(outs[0].at[o], o, slice(o * block, (o + 1) * block))


def flipped(index, mask):
    out, bit = index * 0, 1
    while bit < 4:
        out = out + bit * lax.rem(index // bit + (mask // bit) % 2, 2)
        bit *= 2
    return out


def quad_kernel(narrow, cap, *refs):
    parts, out, mixed = refs[:-2], refs[-2], refs[-1]
    power = slice(narrow + SOURCES * cap, narrow + SOURCES * cap + 1)
    mixed[...] = jnp.zeros(mixed.shape, jnp.int32)
    for top in range(out.shape[0]):
        total = jnp.zeros((narrow, out.shape[2]), F32)
        for n, part in enumerate(parts):
            both = part[top].astype(jnp.int32)
            total += decode(both[:narrow], both[power])
            row = narrow + n * cap
            mixed[row : row + cap, :] = both[narrow : narrow + cap]
        mixed[:narrow, :], mixed[power, :] = encode(total, 0)
        out[top] = mixed[...].astype(jnp.int16)


def sum_kernel(scale, narrow, cap, block, terms, *refs):
    parts, out, mixed = refs[:-2], refs[-2], refs[-1]
    depth = parts[0].shape[0]
    power = slice(narrow + SOURCES * cap, narrow + SOURCES * cap + 1)
    mixed[...] = jnp.zeros(mixed.shape, jnp.int32)
    for first in range(0, len(parts), terms):
        for top in range(depth):
            total = jnp.zeros((narrow, block), F32)
            for part in parts[first : first + terms]:
                both = part[top].astype(jnp.int32)
                total += decode(both[:narrow, :block], both[power, :block])
            mixed[:narrow, :block], mixed[power, :block] = encode(total * F32(scale), 0)
            out[first // terms * depth + top] = mixed[...].astype(jnp.int16)


def entity_kernel(direct, narrow, place, serve, lhs, *refs):
    recv, out, terms, onehot = refs[:-3], refs[-3], refs[-2], refs[-1]
    cap, workers = serve.shape[1], serve.shape[2]
    rows = out.shape[1]
    lane = iota((1, rows), 1)
    for h in range(workers):
        if direct:
            turn, hop = h % SOURCES, h // SOURCES
            mine = place[0] // 4
            both = recv[hop][mine].astype(jnp.int32)
            worker = lax.rem(mine + hop, 2) * 4 + flipped(place[0] % 4, turn)
        else:
            turn, both, worker = 0, recv[0][h].astype(jnp.int32), h
        row = narrow + turn * cap
        both = both[row : row + cap]
        terms[h * cap : (h + 1) * cap, :] = jnp.where(
            iota(both.shape, 1) < narrow, decode(both, both[:, narrow : narrow + 1]), 0.0
        )
        for c in range(cap):
            spot = jnp.where(lane == serve[0, c, worker], 1.0, 0.0).astype(F32)
            onehot[h * cap + c : h * cap + c + 1, :] = spot
    spots = onehot[...].astype(BF16)
    parts = jnp.concatenate(split3(jnp.transpose(terms[...])), axis=1)
    added = dot(parts, jnp.concatenate([spots] * 3, axis=0))
    out[...] = lhs[...] + added[:narrow]


def spread_kernel(workers, replicas, narrow, power_row, block, place, mine, other, out, whole, sems):
    dim, nrel = out.shape
    dom, rep = place[0], place[1]
    here = lax.rem(rep, 2)
    moves, start = [], 0
    for r in range(replicas):
        for o in range(workers):
            over_low = lax.rem(dom // 2 + o // 2, 2)
            over_y = lax.rem(dom + o, 2)
            over_x = lax.rem(rep // 2 + r // 2, 2)
            spot = (over_y + 2 * over_x) * 4 + over_low * 2 + o // 4
            both = jnp.where(
                here == r % 2, mine[spot].astype(jnp.int32), other[spot].astype(jnp.int32)
            )
            value = decode(both[:narrow], both[power_row : power_row + 1])
            end = min((o + 1) * block, nrel)
            whole[r * narrow : (r + 1) * narrow, o * block : end] = value[:, : end - o * block]
        end = (r + 1) * narrow // 8 * 8 if r + 1 < replicas else dim
        band = slice(start, end)
        moves.append(pltpu.make_async_copy(whole.at[band], out.at[band], sems.at[r]))
        moves[-1].start()
        start = end
    for move in moves:
        move.wait()


def turned(size, hop):
    return [(i, (i + hop) % size) for i in range(size)]


def shards(entities, relation, serve_ids, edge_src, edge_rel, edge_dst, neg_ids, edge_count):
    workers = lax.axis_size("dom")
    replicas = lax.axis_size("rep")
    rows, dim = entities.shape
    nrel = relation.shape[0]
    cap = serve_ids.shape[2]
    edges = edge_src.shape[2]
    groups, width = neg_ids.shape[2], neg_ids.shape[3]
    slots = workers * cap
    narrow = dim // replicas
    direct = workers == 8 and replicas == 4
    block = up(-(-nrel // workers), LANES if direct else 8)
    pad_rel = up(max(nrel, workers * block), LANES)
    offsets = sorted({(narrow * r) % 8 for r in range(replicas)})
    window = up(narrow + offsets[-1], 8)
    height = up(narrow + SOURCES * cap + 1, 16)
    ent_t, rel_t = entities.T, relation.T
    serve_t = jnp.transpose(serve_ids, (0, 2, 1))
    place = jnp.stack([lax.axis_index("dom"), lax.axis_index("rep")]).astype(jnp.int32)

    idx, served = pl.pallas_call(
        prep_kernel,
        out_shape=(
            jax.ShapeDtypeStruct((IDX_ROWS, edges), jnp.int32),
            jax.ShapeDtypeStruct((workers, cap, dim), F32),
        ),
        in_specs=[HBM] * 7,
        out_specs=(VMEM, VMEM),
        scratch_shapes=[
            pltpu.SMEM(serve_t.shape, jnp.int32),
            pltpu.SMEM(edge_count.shape, jnp.int32),
            pltpu.VMEM(ent_t.shape, BF16),
            pltpu.VMEM(edge_src.shape, jnp.int32),
            pltpu.VMEM(edge_rel.shape, jnp.int32),
            pltpu.VMEM(edge_dst.shape, jnp.int32),
            pltpu.VMEM(neg_ids.shape, jnp.int32),
            pltpu.VMEM((slots, rows), F32),
            pltpu.SemaphoreType.DMA((7,)),
        ],
        compiler_params=params(60),
        name="prep",
    )(serve_t, edge_count, ent_t, edge_src, edge_rel, edge_dst, neg_ids)

    held = [idx]
    for hop in range(1, replicas):
        held.append(lax.ppermute(idx, "rep", turned(replicas, hop)))
    received = lax.all_to_all(served, "dom", 0, 0, tiled=True)

    total = min(replicas * edges, up(LIVE_EDGES, edges))
    packed, query, lhs_rows, rel_rows = pl.pallas_call(
        functools.partial(
            gather_kernel, (replicas, groups, nrel, pad_rel, narrow, window, edges)
        ),
        out_shape=(
            jax.ShapeDtypeStruct((IDX_ROWS, total), jnp.int32),
            jax.ShapeDtypeStruct((dim, total), BF16),
            jax.ShapeDtypeStruct((window, total), F32),
            jax.ShapeDtypeStruct((window, total), F32),
        ),
        in_specs=[SMEM] + [VMEM] * replicas + [HBM] * 2,
        out_specs=[VMEM] * 4,
        scratch_shapes=[
            pltpu.VMEM(ent_t.shape, BF16),
            pltpu.VMEM(rel_t.shape, F32),
            pltpu.VMEM((2 * dim, pad_rel), BF16),
            pltpu.VMEM((dim, edges), F32),
            pltpu.VMEM((dim, edges), F32),
            pltpu.SemaphoreType.DMA((2,)),
        ],
        compiler_params=params(57),
        cost_estimate=cost(2 * total * dim * (2 * pad_rel + rows), 8 * total * dim),
        name="gather",
    )(place, *held, ent_t, rel_t)

    cfg = (
        direct, workers, replicas, cap, groups, width, pad_rel, block, narrow, window,
        tuple(offsets),
    )
    lanes = max(up(block, LANES), up(narrow, LANES))
    outs = [2] * SOURCES if direct else [workers]
    sizes = [jax.ShapeDtypeStruct((n, height, lanes), jnp.int16) for n in outs]
    lhs_part, *sent = pl.pallas_call(
        functools.partial(main_kernel, cfg),
        out_shape=[jax.ShapeDtypeStruct((narrow, rows), F32)] + sizes,
        in_specs=[SMEM] + [VMEM] * (replicas + 5),
        out_specs=[VMEM] * (1 + len(sizes)),
        scratch_shapes=[
            pltpu.VMEM((slots, dim), F32),
            pltpu.VMEM((dim, slots), F32),
            pltpu.VMEM((dim, total), F32),
            pltpu.VMEM((lanes, slots), F32),
            pltpu.VMEM((height, lanes), jnp.int32),
            pltpu.VMEM((narrow, pad_rel), jnp.int32),
            pltpu.VMEM((1, pad_rel), jnp.int32),
            pltpu.VMEM((slots, lanes), jnp.int32),
        ],
        compiler_params=params(),
        name="edges",
    )(place, *held, packed, query, lhs_rows, rel_rows, received)

    def swap(array, dom_bits=0, rep_bits=0):
        pairs = []
        for o in range(workers):
            for r in range(replicas):
                pairs.append((o * replicas + r, (o ^ dom_bits) * replicas + (r ^ rep_bits)))
        return lax.ppermute(array, ("dom", "rep"), pairs)

    stack = jax.ShapeDtypeStruct((outs[0], height, lanes), jnp.int16)
    mixed = [pltpu.VMEM((height, lanes), jnp.int32)]
    if direct:
        got = {n: swap(sent[n], n) for n in reversed(range(1, SOURCES))}
        summed = pl.pallas_call(
            functools.partial(quad_kernel, narrow, cap),
            out_shape=stack,
            in_specs=[VMEM] * SOURCES,
            out_specs=VMEM,
            scratch_shapes=mixed,
            compiler_params=params(),
            name="quad",
        )(sent[0], *[got[n] for n in range(1, SOURCES)])
        recv = [summed, swap(summed, 4)]
        parts = recv + [swap(summed, 2), swap(summed, 6)]
        stack = jax.ShapeDtypeStruct((4, height, lanes), jnp.int16)
    else:
        recv = [lax.all_to_all(sent[0], "dom", 0, 0, tiled=True)]
        parts = [recv[0][w : w + 1] for w in range(workers)]
        stack = jax.ShapeDtypeStruct((1, height, lanes), jnp.int16)
    scale = 1.0 / (edges * workers * replicas)
    chunk = pl.pallas_call(
        functools.partial(sum_kernel, scale, narrow, cap, block, 2 if direct else workers),
        out_shape=stack,
        in_specs=[VMEM] * len(parts),
        out_specs=VMEM,
        scratch_shapes=mixed,
        compiler_params=params(),
        name="total",
    )(*parts)

    if direct:
        base = jnp.concatenate(
            [chunk, swap(chunk, 1), swap(chunk, 0, 2), swap(chunk, 1, 2)], axis=0
        )
        base, lhs_part = lax.optimization_barrier((base, lhs_part))
    entity_grad = pl.pallas_call(
        functools.partial(entity_kernel, direct, narrow),
        out_shape=jax.ShapeDtypeStruct((narrow, rows), F32),
        in_specs=[SMEM] * 2 + [VMEM] * (1 + len(recv)),
        out_specs=VMEM,
        scratch_shapes=[pltpu.VMEM((slots, lanes), F32), pltpu.VMEM((slots, rows), F32)],
        compiler_params=params(),
        cost_estimate=cost(10**9, 10**6),
        name="entity",
    )(place, serve_t, lhs_part, *recv)

    power_row = narrow + SOURCES * cap
    if direct:
        swapped = lax.ppermute(base, "rep", [(i, i ^ 1) for i in range(replicas)])
        swapped, entity_grad = lax.optimization_barrier((swapped, entity_grad))
        relation_t = pl.pallas_call(
            functools.partial(spread_kernel, workers, replicas, narrow, power_row, block),
            out_shape=jax.ShapeDtypeStruct((dim, nrel), F32),
            in_specs=[SMEM] + [VMEM] * 2,
            out_specs=HBM,
            scratch_shapes=[
                pltpu.VMEM((dim, nrel), F32),
                pltpu.SemaphoreType.DMA((replicas,)),
            ],
            compiler_params=params(),
            name="spread",
        )(place, base, swapped)
    else:
        whole = lax.all_gather(chunk[0, :, :block], ("dom", "rep"), axis=0)
        whole = decode(whole[:, :narrow], whole[:, power_row : power_row + 1])
        whole = whole.reshape(workers, replicas, narrow, block).transpose(1, 2, 0, 3)
        relation_t = whole.reshape(dim, workers * block)[:, :nrel]
    return (entity_grad.T, relation_t.T)


def solution(mesh):
    placed = (
        P("dom", None),
        P(),
        P("dom", None, None),
        P("dom", "rep", None),
        P("dom", "rep", None),
        P("dom", "rep", None),
        P("dom", "rep", None, None),
        P("dom", "rep"),
    )
    return jax.shard_map(
        shards, mesh=mesh, in_specs=placed, out_specs=(P("dom", "rep"), P()), check_vma=False
    )
```

```python
import functools

import jax
import jax.numpy as jnp
from jax import lax
from jax.experimental import pallas as pl
from jax.experimental.pallas import tpu as pltpu
from jax.sharding import PartitionSpec as P

F32 = jnp.float32
BF16 = jnp.bfloat16
IDX_ROWS = 8
LANES = 128
SOURCES = 4
LIVE_EDGES = 1536
VMEM = pl.BlockSpec(memory_space=pltpu.VMEM)
SMEM = pl.BlockSpec(memory_space=pltpu.SMEM)
HBM = pl.BlockSpec(memory_space=pltpu.HBM)


def params(mib=32):
    return pltpu.CompilerParams(vmem_limit_bytes=mib * 1024 * 1024)


def cost(flops, moved):
    return pl.CostEstimate(flops=flops, bytes_accessed=moved, transcendentals=0)


def up(value, step):
    return -(-value // step) * step


def split2(x):
    hi = x.astype(BF16)
    lo = (x - hi.astype(F32)).astype(BF16)
    return hi, lo


def split3(x):
    hi, rest = x.astype(BF16), x
    rest = rest - hi.astype(F32)
    mid = rest.astype(BF16)
    low = (rest - mid.astype(F32)).astype(BF16)
    return hi, mid, low


def dot(a, b):
    return jnp.dot(a, b, preferred_element_type=F32)


def dot_t(a, b):
    return lax.dot_general(a, b, (((1,), (1,)), ((), ())), preferred_element_type=F32)


def ones_where(flag):
    return jnp.where(flag, 1.0, 0.0).astype(BF16)


def exponent(largest):
    safe = jnp.where(largest > 0, largest, 1.0)
    return jnp.clip(jnp.floor(F32(14.9) - jnp.log2(safe)), -120.0, 120.0)


def encode(x, axis):
    k = exponent(jnp.max(jnp.abs(x), axis=axis, keepdims=True))
    return jnp.floor(x * jnp.exp2(k) + 0.5).astype(jnp.int32), k.astype(jnp.int32)


def decode(codes, k):
    return codes.astype(F32) * jnp.exp2(-k.astype(F32))


def iota(shape, axis):
    return lax.broadcasted_iota(jnp.int32, shape, axis)


def shifted_rows(x, offset, narrow, offsets):
    out = x[offsets[0] : offsets[0] + narrow]
    for other in offsets[1:]:
        out = jnp.where(offset == other, x[other : other + narrow], out)
    return out


def prep_kernel(serve, count, ent, src, rel, dst, neg, out_idx, out_rows, *refs):
    cap, workers = serve.shape[1], serve.shape[2]
    rows = ent.shape[1]
    groups, width = neg.shape[2], neg.shape[3]
    onehot, sems = refs[-2:]
    moves = [
        pltpu.make_async_copy(a, b, sems.at[n])
        for n, (a, b) in enumerate(zip((serve, count, ent, src, rel, dst, neg), refs))
    ]
    for move in moves:
        move.start()
    for move in moves:
        move.wait()
    serve_s, count_s, ent_v, src_v, rel_v, dst_v, neg_v = refs[:7]
    out_idx[...] = jnp.full(out_idx.shape, count_s[0, 0], jnp.int32)
    out_idx[0:1, :] = src_v[0]
    out_idx[1:2, :] = rel_v[0]
    out_idx[2:3, :] = dst_v[0]
    for g in range(groups):
        out_idx[3 + g : 4 + g, :width] = neg_v[0, 0, g : g + 1, :]
    lane = iota((1, rows), 1)
    for k in range(workers * cap):
        picked = serve_s[0, k % cap, k // cap]
        onehot[k : k + 1, :] = jnp.where(lane == picked, 1.0, 0.0).astype(F32)
    picked_rows = dot_t(onehot[...].astype(BF16), ent_v[...])
    for w in range(workers):
        out_rows[w] = picked_rows[w * cap : (w + 1) * cap]


def packed_edges(idx_refs, groups, out_idx):
    edges, span = idx_refs[0].shape[1], out_idx.shape[1]
    wide = max(span, edges)
    place = iota((IDX_ROWS, wide), 1)
    row = iota((IDX_ROWS, edges), 0)
    block = iota((IDX_ROWS, edges), 1) // (edges // groups)
    packed = jnp.where(iota((IDX_ROWS, wide), 0) < 3, -1, 0)
    first = 0
    for i, ref in enumerate(idx_refs):
        count = jnp.max(ref[IDX_ROWS - 1 : IDX_ROWS, :].astype(F32)).astype(jnp.int32)
        rows = jnp.where(row < 3, ref[...], jnp.where(row == 3, block + i * groups, 1))
        if wide > edges:
            rows = jnp.concatenate(
                [rows, jnp.zeros((IDX_ROWS, wide - edges), jnp.int32)], axis=1
            )
        moved = pltpu.roll(rows, first, 1)
        packed = jnp.where((place >= first) & (place < first + count), moved, packed)
        first = first + count
    out_idx[...] = packed[:, :span]


def gather_kernel(cfg, place, *refs):
    replicas, groups, nrel, pad_rel, narrow, window, step = cfg
    idx_refs, refs = refs[:replicas], refs[replicas:]
    ent, relation, out_idx, out_query, out_lhs, out_rel, rel_parts, lhs_s, rel_s = refs
    dim, rows = ent.shape
    base = pl.multiple_of((place[1] * narrow) // 8 * 8, 8)
    packed_edges(idx_refs, groups, out_idx)
    hi, lo = split2(relation[...])
    if pad_rel > nrel:
        rel_parts[...] = jnp.zeros(rel_parts.shape, BF16)
    rel_parts[:dim, :nrel] = hi
    rel_parts[dim:, :nrel] = lo
    for start in range(0, out_idx.shape[1], step):
        span = slice(start, start + step)
        src_l, rel_l = out_idx[0:1, span], out_idx[1:2, span]
        lhs = dot(ent[...], ones_where(iota((rows, step), 0) == src_l))
        both = dot(rel_parts[...], ones_where(iota((pad_rel, step), 0) == rel_l))
        rel_rows = both[:dim] + both[dim:]
        lhs_s[...] = lhs
        rel_s[...] = rel_rows
        out_query[:, span] = (lhs * rel_rows).astype(BF16)
        out_lhs[:, span] = lhs_s[pl.ds(base, window), :]
        out_rel[:, span] = rel_s[pl.ds(base, window), :]


def main_kernel(cfg, place, *refs):
    (direct, workers, replicas, cap, groups, width, pad_rel, block, narrow, window, offsets) = cfg
    idx_refs, refs = refs[:replicas], refs[replicas:]
    (packed, query_v, lhs_v, rel_v, received), refs = refs[:5], refs[5:]
    out_lhs, refs = refs[0], refs[1:]
    out, refs = refs[0], refs[1:]
    table_f, table_t, query_s, wide_t, mixed, codes_s, powers_s, tables_s = refs
    edges = idx_refs[0].shape[1]
    dim, total = query_v.shape
    rows = out_lhs.shape[1]
    slots = workers * cap
    rep = place[1]
    per = edges // groups
    base = pl.multiple_of((rep * narrow) // 8 * 8, 8)
    offset = rep * narrow - base

    for w in range(workers):
        table_f[w * cap : (w + 1) * cap, :] = received[w]
    table_t[...] = jnp.transpose(table_f[...])
    table = table_f[...].astype(BF16)
    own_t = table_t[pl.ds(base, window), :].astype(BF16)
    own_t = jnp.concatenate([own_t] * 3, axis=1)

    query = query_v[...]
    scores = dot(table, query)
    query_s[...] = query.astype(F32)
    lanes = packed[...]
    cols = jnp.transpose(lanes)
    times = jnp.zeros((slots, total), F32)
    for i in range(replicas):
        shard = idx_refs[i][...]
        position = iota((slots, edges), 1)
        seen = (iota((slots, edges), 0) == shard[2:3]) & (position < shard[IDX_ROWS - 1 : IDX_ROWS])
        seen = jnp.where(seen, 1.0, 0.0).astype(F32)
        for g in range(groups):
            neg = iota((slots, width), 0) == shard[3 + g : 4 + g, :width]
            often = jnp.sum(jnp.where(neg, 1.0, 0.0).astype(F32), axis=1, keepdims=True)
            often = often + jnp.sum(seen[:, g * per : (g + 1) * per], axis=1, keepdims=True)
            times = jnp.where(lanes[3:4] == i * groups + g, often, times)
    live = lanes[4:5].astype(F32)
    own = jnp.where(iota((slots, total), 0) == lanes[2:3], 1.0, 0.0).astype(F32)
    scores = jnp.where(times > 0, scores, F32(-1e30))
    expo = jnp.exp(scores - jnp.max(scores, axis=0, keepdims=True))
    norm = jnp.sum(expo * times, axis=0, keepdims=True)
    probs = expo / jnp.where(live > 0, norm, 1.0)
    other = probs.astype(BF16).astype(F32)
    itself = (probs - 1.0).astype(BF16).astype(F32)
    grads = ((times - own) * other + own * itself) * live
    stack = jnp.concatenate(split3(grads), axis=0)
    stack_t = jnp.concatenate(split3(jnp.transpose(grads)), axis=1)

    dquery = dot(own_t, stack)
    y = jnp.concatenate(split2(dquery * lhs_v[...]), axis=0)
    acc_rel = dot(y, ones_where(iota((total, pad_rel), 1) == cols[:, 1:2]))
    x = jnp.concatenate(split2(dquery * rel_v[...]), axis=0)
    acc_lhs = dot(x, ones_where(iota((total, rows), 1) == cols[:, 0:1]))
    acc_tab = dot(query_s[pl.ds(base, window), :].astype(BF16), stack_t)

    pick = functools.partial(shifted_rows, offset=offset, narrow=narrow, offsets=offsets)
    out_lhs[...] = pick(acc_lhs[:window] + acc_lhs[window:])
    codes, powers = encode(pick(acc_rel[:window] + acc_rel[window:]), 0)
    wide_t[...] = jnp.zeros(wide_t.shape, F32)
    wide_t[:narrow] = pick(
        acc_tab[:, :slots] + acc_tab[:, slots : 2 * slots] + acc_tab[:, 2 * slots :]
    )
    table_codes, table_powers = encode(jnp.transpose(wide_t[...]), 1)
    spare = iota(table_codes.shape, 1) >= narrow
    tables_s[...] = jnp.where(spare, table_powers, table_codes)
    codes_s[...] = codes
    powers_s[...] = powers
    mixed[...] = jnp.zeros(mixed.shape, jnp.int32)
    power_row = narrow + SOURCES * cap
    dom = place[0]

    def write(target, o, lane):
        mixed[:narrow, :block] = codes_s[:, lane]
        for c in range(cap):
            mixed[narrow + c : narrow + c + 1, :] = tables_s[pl.ds(o * cap + c, 1), :]
        mixed[power_row : power_row + 1, :block] = powers_s[0:1, lane]
        target[...] = mixed[...].astype(jnp.int16)

    if direct:
        for low in range(SOURCES):
            for top in range(2):
                o = top * SOURCES + low
                write(out.at[low, top], o, slice(o * block, (o + 1) * block))
    else:
        for o in range(workers):
            write(out.at[o, 0], o, slice(o * block, (o + 1) * block))


def quad_kernel(narrow, cap, *refs):
    parts, out, mixed = refs
    power = slice(narrow + SOURCES * cap, narrow + SOURCES * cap + 1)
    mixed[...] = jnp.zeros(mixed.shape, jnp.int32)
    for top in range(out.shape[0]):
        total = jnp.zeros((narrow, out.shape[2]), F32)
        for n in range(SOURCES):
            both = parts[n, top].astype(jnp.int32)
            total += decode(both[:narrow], both[power])
            row = narrow + n * cap
            mixed[row : row + cap, :] = both[narrow : narrow + cap]
        mixed[:narrow, :], mixed[power, :] = encode(total, 0)
        out[top] = mixed[...].astype(jnp.int16)


def sum_kernel(scale, narrow, cap, block, recv, out, mixed):
    sources, depth = recv.shape[:2]
    pairs = out.shape[0] // depth
    power = slice(narrow + SOURCES * cap, narrow + SOURCES * cap + 1)
    mixed[...] = jnp.zeros(mixed.shape, jnp.int32)
    for first in range(pairs):
        for top in range(depth):
            total = jnp.zeros((narrow, block), F32)
            for n in range(first, sources, pairs):
                both = recv[n, top].astype(jnp.int32)
                total += decode(both[:narrow, :block], both[power, :block])
            mixed[:narrow, :block], mixed[power, :block] = encode(total * F32(scale), 0)
            out[first * depth + top] = mixed[...].astype(jnp.int16)


def entity_kernel(direct, narrow, place, serve, lhs, recv, out, terms, onehot):
    cap, workers = serve.shape[1], serve.shape[2]
    rows = out.shape[1]
    lane = iota((1, rows), 1)
    for h in range(workers):
        if direct:
            turn, low = h % SOURCES, lax.rem(place[0] // 2, 2)
            both = recv[h // SOURCES * 2 + low, place[0] // SOURCES].astype(jnp.int32)
        else:
            turn, both = 0, recv[h, 0].astype(jnp.int32)
        row = narrow + turn * cap
        both = both[row : row + cap]
        terms[h * cap : (h + 1) * cap, :] = jnp.where(
            iota(both.shape, 1) < narrow, decode(both, both[:, narrow : narrow + 1]), 0.0
        )
        for c in range(cap):
            spot = jnp.where(lane == serve[0, c, h], 1.0, 0.0).astype(F32)
            onehot[h * cap + c : h * cap + c + 1, :] = spot
    spots = onehot[...].astype(BF16)
    parts = jnp.concatenate(split3(jnp.transpose(terms[...])), axis=1)
    added = dot(parts, jnp.concatenate([spots] * 3, axis=0))
    out[...] = lhs[...] + added[:narrow]


def spread_kernel(workers, replicas, narrow, power_row, block, place, mine, other, out, whole, sems):
    dim, nrel = out.shape
    dom, rep = place[0], place[1]
    here = lax.rem(rep, 2)
    moves, start = [], 0
    for r in range(replicas):
        for o in range(workers):
            over_y = lax.rem(dom + o, 2)
            over_x = lax.rem(rep // 2 + r // 2, 2)
            spot = (over_y + 2 * over_x) * 4 + o // 2 % 2 * 2 + o // 4
            both = jnp.where(
                here == r % 2, mine[spot].astype(jnp.int32), other[spot].astype(jnp.int32)
            )
            value = decode(both[:narrow], both[power_row : power_row + 1])
            end = min((o + 1) * block, nrel)
            whole[r * narrow : (r + 1) * narrow, o * block : end] = value[:, : end - o * block]
        end = (r + 1) * narrow // 8 * 8 if r + 1 < replicas else dim
        band = slice(start, end)
        moves.append(pltpu.make_async_copy(whole.at[band], out.at[band], sems.at[r]))
        moves[-1].start()
        start = end
    for move in moves:
        move.wait()


def turned(size, hop):
    return [(i, (i + hop) % size) for i in range(size)]


def shards(entities, relation, serve_ids, edge_src, edge_rel, edge_dst, neg_ids, edge_count):
    workers = lax.axis_size("dom")
    replicas = lax.axis_size("rep")
    rows, dim = entities.shape
    nrel = relation.shape[0]
    cap = serve_ids.shape[2]
    edges = edge_src.shape[2]
    groups, width = neg_ids.shape[2], neg_ids.shape[3]
    slots = workers * cap
    narrow = dim // replicas
    direct = workers == 8 and replicas == 4
    block = up(-(-nrel // workers), LANES if direct else 8)
    pad_rel = up(max(nrel, workers * block), LANES)
    offsets = sorted({(narrow * r) % 8 for r in range(replicas)})
    window = up(narrow + offsets[-1], 8)
    height = up(narrow + SOURCES * cap + 1, 16)
    ent_t, rel_t = entities.T, relation.T
    serve_t = jnp.transpose(serve_ids, (0, 2, 1))
    place = jnp.stack([lax.axis_index("dom"), lax.axis_index("rep")]).astype(jnp.int32)

    idx, served = pl.pallas_call(
        prep_kernel,
        out_shape=(
            jax.ShapeDtypeStruct((IDX_ROWS, edges), jnp.int32),
            jax.ShapeDtypeStruct((workers, cap, dim), F32),
        ),
        in_specs=[HBM] * 7,
        out_specs=(VMEM, VMEM),
        scratch_shapes=[
            pltpu.SMEM(serve_t.shape, jnp.int32),
            pltpu.SMEM(edge_count.shape, jnp.int32),
            pltpu.VMEM(ent_t.shape, BF16),
            pltpu.VMEM(edge_src.shape, jnp.int32),
            pltpu.VMEM(edge_rel.shape, jnp.int32),
            pltpu.VMEM(edge_dst.shape, jnp.int32),
            pltpu.VMEM(neg_ids.shape, jnp.int32),
            pltpu.VMEM((slots, rows), F32),
            pltpu.SemaphoreType.DMA((7,)),
        ],
        compiler_params=params(60),
        name="prep",
    )(serve_t, edge_count, ent_t, edge_src, edge_rel, edge_dst, neg_ids)

    held = [idx]
    for hop in range(1, replicas):
        held.append(lax.ppermute(idx, "rep", turned(replicas, hop)))
    received = lax.all_to_all(served, "dom", 0, 0, tiled=True)

    total = min(replicas * edges, up(LIVE_EDGES, edges))
    packed, query, lhs_rows, rel_rows = pl.pallas_call(
        functools.partial(
            gather_kernel, (replicas, groups, nrel, pad_rel, narrow, window, edges)
        ),
        out_shape=(
            jax.ShapeDtypeStruct((IDX_ROWS, total), jnp.int32),
            jax.ShapeDtypeStruct((dim, total), BF16),
            jax.ShapeDtypeStruct((window, total), F32),
            jax.ShapeDtypeStruct((window, total), F32),
        ),
        in_specs=[SMEM] + [VMEM] * (replicas + 2),
        out_specs=[VMEM] * 4,
        scratch_shapes=[
            pltpu.VMEM((2 * dim, pad_rel), BF16),
            pltpu.VMEM((dim, edges), F32),
            pltpu.VMEM((dim, edges), F32),
        ],
        compiler_params=params(),
        cost_estimate=cost(2 * total * dim * (2 * pad_rel + rows), 8 * total * dim),
        name="gather",
    )(place, *held, ent_t, rel_t)

    cfg = (
        direct, workers, replicas, cap, groups, width, pad_rel, block, narrow, window,
        tuple(offsets),
    )
    lanes = max(up(block, LANES), up(narrow, LANES))
    leading = (SOURCES, 2) if direct else (workers, 1)
    lhs_part, sent = pl.pallas_call(
        functools.partial(main_kernel, cfg),
        out_shape=(
            jax.ShapeDtypeStruct((narrow, rows), F32),
            jax.ShapeDtypeStruct(leading + (height, lanes), jnp.int16),
        ),
        in_specs=[SMEM] + [VMEM] * (replicas + 5),
        out_specs=(VMEM, VMEM),
        scratch_shapes=[
            pltpu.VMEM((slots, dim), F32),
            pltpu.VMEM((dim, slots), F32),
            pltpu.VMEM((dim, total), F32),
            pltpu.VMEM((lanes, slots), F32),
            pltpu.VMEM((height, lanes), jnp.int32),
            pltpu.VMEM((narrow, pad_rel), jnp.int32),
            pltpu.VMEM((1, pad_rel), jnp.int32),
            pltpu.VMEM((slots, lanes), jnp.int32),
        ],
        compiler_params=params(),
        name="edges",
    )(place, *held, packed, query, lhs_rows, rel_rows, received)

    def swap(array, dom_bits=0, rep_bits=0):
        pairs = []
        for o in range(workers):
            for r in range(replicas):
                pairs.append((o * replicas + r, (o ^ dom_bits) * replicas + (r ^ rep_bits)))
        return lax.ppermute(array, ("dom", "rep"), pairs)

    mixed = [pltpu.VMEM((height, lanes), jnp.int32)]
    if direct:
        low_groups = [list(range(n, n + SOURCES)) for n in range(0, workers, SOURCES)]
        got = lax.all_to_all(sent, "dom", 0, 0, axis_index_groups=low_groups, tiled=True)
        summed = pl.pallas_call(
            functools.partial(quad_kernel, narrow, cap),
            out_shape=jax.ShapeDtypeStruct(leading[1:] + (height, lanes), jnp.int16),
            in_specs=[VMEM],
            out_specs=VMEM,
            scratch_shapes=mixed,
            compiler_params=params(),
            name="quad",
        )(got)
        columns = [list(range(n, workers, 2)) for n in range(2)]
        recv = lax.all_gather(summed, "dom", axis_index_groups=columns)
        stack = (4, height, lanes)
    else:
        recv = lax.all_to_all(sent, "dom", 0, 0, tiled=True)
        stack = (1, height, lanes)
    scale = 1.0 / (edges * workers * replicas)
    chunk = pl.pallas_call(
        functools.partial(sum_kernel, scale, narrow, cap, block),
        out_shape=jax.ShapeDtypeStruct(stack, jnp.int16),
        in_specs=[VMEM],
        out_specs=VMEM,
        scratch_shapes=mixed,
        compiler_params=params(),
        name="total",
    )(recv)

    if direct:
        base = jnp.concatenate(
            [chunk, swap(chunk, 1), swap(chunk, 0, 2), swap(chunk, 1, 2)], axis=0
        )
        base, lhs_part = lax.optimization_barrier((base, lhs_part))
    entity_grad = pl.pallas_call(
        functools.partial(entity_kernel, direct, narrow),
        out_shape=jax.ShapeDtypeStruct((narrow, rows), F32),
        in_specs=[SMEM] * 2 + [VMEM] * 2,
        out_specs=VMEM,
        scratch_shapes=[pltpu.VMEM((slots, lanes), F32), pltpu.VMEM((slots, rows), F32)],
        compiler_params=params(),
        cost_estimate=cost(10**9, 10**6),
        name="entity",
    )(place, serve_t, lhs_part, recv)

    power_row = narrow + SOURCES * cap
    if direct:
        swapped = lax.ppermute(base, "rep", [(i, i ^ 1) for i in range(replicas)])
        swapped, entity_grad = lax.optimization_barrier((swapped, entity_grad))
        relation_t = pl.pallas_call(
            functools.partial(spread_kernel, workers, replicas, narrow, power_row, block),
            out_shape=jax.ShapeDtypeStruct((dim, nrel), F32),
            in_specs=[SMEM] + [VMEM] * 2,
            out_specs=HBM,
            scratch_shapes=[
                pltpu.VMEM((dim, nrel), F32),
                pltpu.SemaphoreType.DMA((replicas,)),
            ],
            compiler_params=params(),
            name="spread",
        )(place, base, swapped)
    else:
        whole = lax.all_gather(chunk[0, :, :block], ("dom", "rep"), axis=0)
        whole = decode(whole[:, :narrow], whole[:, power_row : power_row + 1])
        whole = whole.reshape(workers, replicas, narrow, block).transpose(1, 2, 0, 3)
        relation_t = whole.reshape(dim, workers * block)[:, :nrel]
    return (entity_grad.T, relation_t.T)


def solution(mesh):
    placed = (
        P("dom", None),
        P(),
        P("dom", None, None),
        P("dom", "rep", None),
        P("dom", "rep", None),
        P("dom", "rep", None),
        P("dom", "rep", None, None),
        P("dom", "rep"),
    )
    return jax.shard_map(
        shards, mesh=mesh, in_specs=placed, out_specs=(P("dom", "rep"), P()), check_vma=False
    )
```

```python
import functools

import jax
import jax.numpy as jnp
from jax import lax
from jax.experimental import pallas as pl
from jax.experimental.pallas import tpu as pltpu
from jax.sharding import PartitionSpec as P

F32 = jnp.float32
BF16 = jnp.bfloat16
IDX_ROWS = 8
LANES = 128
SOURCES = 4
LIVE_EDGES = 1536
VMEM = pl.BlockSpec(memory_space=pltpu.VMEM)
SMEM = pl.BlockSpec(memory_space=pltpu.SMEM)
HBM = pl.BlockSpec(memory_space=pltpu.HBM)


def params(mib=32):
    return pltpu.CompilerParams(vmem_limit_bytes=mib * 1024 * 1024)


def cost(flops, moved):
    return pl.CostEstimate(flops=flops, bytes_accessed=moved, transcendentals=0)


def up(value, step):
    return -(-value // step) * step


def split2(x):
    hi = x.astype(BF16)
    lo = (x - hi.astype(F32)).astype(BF16)
    return hi, lo


def split3(x):
    hi, rest = x.astype(BF16), x
    rest = rest - hi.astype(F32)
    mid = rest.astype(BF16)
    low = (rest - mid.astype(F32)).astype(BF16)
    return hi, mid, low


def dot(a, b):
    return jnp.dot(a, b, preferred_element_type=F32)


def dot_t(a, b):
    return lax.dot_general(a, b, (((1,), (1,)), ((), ())), preferred_element_type=F32)


def ones_where(flag):
    return jnp.where(flag, 1.0, 0.0).astype(BF16)


def exponent(largest):
    safe = jnp.where(largest > 0, largest, 1.0)
    return jnp.clip(jnp.floor(F32(14.9) - jnp.log2(safe)), -120.0, 120.0)


def encode(x, axis):
    k = exponent(jnp.max(jnp.abs(x), axis=axis, keepdims=True))
    return jnp.floor(x * jnp.exp2(k) + 0.5).astype(jnp.int32), k.astype(jnp.int32)


def decode(codes, k):
    return codes.astype(F32) * jnp.exp2(-k.astype(F32))


def iota(shape, axis):
    return lax.broadcasted_iota(jnp.int32, shape, axis)


def shifted_rows(x, offset, narrow, offsets):
    out = x[offsets[0] : offsets[0] + narrow]
    for other in offsets[1:]:
        out = jnp.where(offset == other, x[other : other + narrow], out)
    return out


def prep_kernel(serve, count, ent, src, rel, dst, neg, out_idx, out_rows, *refs):
    cap, workers = serve.shape[1], serve.shape[2]
    rows = ent.shape[1]
    groups, width = neg.shape[2], neg.shape[3]
    onehot, sems = refs[-2:]
    moves = [
        pltpu.make_async_copy(a, b, sems.at[n])
        for n, (a, b) in enumerate(zip((serve, count, ent, src, rel, dst, neg), refs))
    ]
    for move in moves:
        move.start()
    for move in moves:
        move.wait()
    serve_s, count_s, ent_v, src_v, rel_v, dst_v, neg_v = refs[:7]
    out_idx[...] = jnp.full(out_idx.shape, count_s[0, 0], jnp.int32)
    out_idx[0:1, :] = src_v[0]
    out_idx[1:2, :] = rel_v[0]
    out_idx[2:3, :] = dst_v[0]
    for g in range(groups):
        out_idx[3 + g : 4 + g, :width] = neg_v[0, 0, g : g + 1, :]
    lane = iota((1, rows), 1)
    for k in range(workers * cap):
        picked = serve_s[0, k % cap, k // cap]
        onehot[k : k + 1, :] = jnp.where(lane == picked, 1.0, 0.0).astype(F32)
    picked_rows = dot_t(onehot[...].astype(BF16), ent_v[...])
    for w in range(workers):
        out_rows[w] = picked_rows[w * cap : (w + 1) * cap]


def packed_edges(idx_refs, groups, out_idx):
    edges, span = idx_refs[0].shape[1], out_idx.shape[1]
    wide = max(span, edges)
    place = iota((IDX_ROWS, wide), 1)
    row = iota((IDX_ROWS, edges), 0)
    block = iota((IDX_ROWS, edges), 1) // (edges // groups)
    packed = jnp.where(iota((IDX_ROWS, wide), 0) < 3, -1, 0)
    first = 0
    for i, ref in enumerate(idx_refs):
        count = jnp.max(ref[IDX_ROWS - 1 : IDX_ROWS, :].astype(F32)).astype(jnp.int32)
        rows = jnp.where(row < 3, ref[...], jnp.where(row == 3, block + i * groups, 1))
        if wide > edges:
            rows = jnp.concatenate(
                [rows, jnp.zeros((IDX_ROWS, wide - edges), jnp.int32)], axis=1
            )
        moved = pltpu.roll(rows, first, 1)
        packed = jnp.where((place >= first) & (place < first + count), moved, packed)
        first = first + count
    out_idx[...] = packed[:, :span]


def gather_kernel(cfg, place, *refs):
    replicas, groups, nrel, pad_rel, narrow, window, step = cfg
    idx_refs, refs = refs[:replicas], refs[replicas:]
    ent, relation, out_idx, out_query, out_lhs, out_rel, rel_parts, lhs_s, rel_s = refs
    dim, rows = ent.shape
    base = pl.multiple_of((place[1] * narrow) // 8 * 8, 8)
    packed_edges(idx_refs, groups, out_idx)
    hi, lo = split2(relation[...])
    if pad_rel > nrel:
        rel_parts[...] = jnp.zeros(rel_parts.shape, BF16)
    rel_parts[:dim, :nrel] = hi
    rel_parts[dim:, :nrel] = lo
    for start in range(0, out_idx.shape[1], step):
        span = slice(start, start + step)
        src_l, rel_l = out_idx[0:1, span], out_idx[1:2, span]
        lhs = dot(ent[...], ones_where(iota((rows, step), 0) == src_l))
        both = dot(rel_parts[...], ones_where(iota((pad_rel, step), 0) == rel_l))
        rel_rows = both[:dim] + both[dim:]
        lhs_s[...] = lhs
        rel_s[...] = rel_rows
        out_query[:, span] = (lhs * rel_rows).astype(BF16)
        out_lhs[:, span] = lhs_s[pl.ds(base, window), :]
        out_rel[:, span] = rel_s[pl.ds(base, window), :]


def main_kernel(cfg, place, *refs):
    (direct, workers, replicas, cap, groups, width, pad_rel, block, narrow, window, offsets) = cfg
    idx_refs, refs = refs[:replicas], refs[replicas:]
    (packed, query_v, lhs_v, rel_v, received), refs = refs[:5], refs[5:]
    out_lhs, refs = refs[0], refs[1:]
    outs, refs = (refs[:SOURCES], refs[SOURCES:]) if direct else (refs[:1], refs[1:])
    table_f, table_t, query_s, wide_t, mixed, codes_s, powers_s, tables_s = refs
    edges = idx_refs[0].shape[1]
    dim, total = query_v.shape
    rows = out_lhs.shape[1]
    slots = workers * cap
    rep = place[1]
    per = edges // groups
    base = pl.multiple_of((rep * narrow) // 8 * 8, 8)
    offset = rep * narrow - base

    for w in range(workers):
        table_f[w * cap : (w + 1) * cap, :] = received[w]
    table_t[...] = jnp.transpose(table_f[...])
    table = table_f[...].astype(BF16)
    own_t = table_t[pl.ds(base, window), :].astype(BF16)
    own_t = jnp.concatenate([own_t] * 3, axis=1)

    query = query_v[...]
    scores = dot(table, query)
    query_s[...] = query.astype(F32)
    lanes = packed[...]
    cols = jnp.transpose(lanes)
    times = jnp.zeros((slots, total), F32)
    for i in range(replicas):
        shard = idx_refs[i][...]
        position = iota((slots, edges), 1)
        seen = (iota((slots, edges), 0) == shard[2:3]) & (position < shard[IDX_ROWS - 1 : IDX_ROWS])
        seen = jnp.where(seen, 1.0, 0.0).astype(F32)
        for g in range(groups):
            neg = iota((slots, width), 0) == shard[3 + g : 4 + g, :width]
            often = jnp.sum(jnp.where(neg, 1.0, 0.0).astype(F32), axis=1, keepdims=True)
            often = often + jnp.sum(seen[:, g * per : (g + 1) * per], axis=1, keepdims=True)
            times = jnp.where(lanes[3:4] == i * groups + g, often, times)
    live = lanes[4:5].astype(F32)
    own = jnp.where(iota((slots, total), 0) == lanes[2:3], 1.0, 0.0).astype(F32)
    scores = jnp.where(times > 0, scores, F32(-1e30))
    expo = jnp.exp(scores - jnp.max(scores, axis=0, keepdims=True))
    norm = jnp.sum(expo * times, axis=0, keepdims=True)
    probs = expo / jnp.where(live > 0, norm, 1.0)
    other = probs.astype(BF16).astype(F32)
    itself = (probs - 1.0).astype(BF16).astype(F32)
    grads = ((times - own) * other + own * itself) * live
    stack = jnp.concatenate(split3(grads), axis=0)
    stack_t = jnp.concatenate(split3(jnp.transpose(grads)), axis=1)

    dquery = dot(own_t, stack)
    y = jnp.concatenate(split2(dquery * lhs_v[...]), axis=0)
    acc_rel = dot(y, ones_where(iota((total, pad_rel), 1) == cols[:, 1:2]))
    x = jnp.concatenate(split2(dquery * rel_v[...]), axis=0)
    acc_lhs = dot(x, ones_where(iota((total, rows), 1) == cols[:, 0:1]))
    acc_tab = dot(query_s[pl.ds(base, window), :].astype(BF16), stack_t)

    pick = functools.partial(shifted_rows, offset=offset, narrow=narrow, offsets=offsets)
    out_lhs[...] = pick(acc_lhs[:window] + acc_lhs[window:])
    codes, powers = encode(pick(acc_rel[:window] + acc_rel[window:]), 0)
    wide_t[...] = jnp.zeros(wide_t.shape, F32)
    wide_t[:narrow] = pick(
        acc_tab[:, :slots] + acc_tab[:, slots : 2 * slots] + acc_tab[:, 2 * slots :]
    )
    table_codes, table_powers = encode(jnp.transpose(wide_t[...]), 1)
    spare = iota(table_codes.shape, 1) >= narrow
    tables_s[...] = jnp.where(spare, table_powers, table_codes)
    codes_s[...] = codes
    powers_s[...] = powers
    mixed[...] = jnp.zeros(mixed.shape, jnp.int32)
    power_row = narrow + SOURCES * cap
    dom = place[0]

    def write(target, o, lane):
        mixed[:narrow, :block] = codes_s[:, lane]
        for c in range(cap):
            mixed[narrow + c : narrow + c + 1, :] = tables_s[pl.ds(o * cap + c, 1), :]
        mixed[power_row : power_row + 1, :block] = powers_s[0:1, lane]
        target[...] = mixed[...].astype(jnp.int16)

    if direct:
        for h in range(SOURCES):
            for top in range(2):
                o = top * 4 + flipped(dom % 4, h)
                write(outs[h].at[top], o, pl.ds(pl.multiple_of(o * block, block), block))
    else:
        for o in range(workers):
            write(outs[0].at[o], o, slice(o * block, (o + 1) * block))


def flipped(index, mask):
    out, bit = index * 0, 1
    while bit < 4:
        out = out + bit * lax.rem(index // bit + (mask // bit) % 2, 2)
        bit *= 2
    return out


def quad_kernel(narrow, cap, *refs):
    parts, out, mixed = refs[:-2], refs[-2], refs[-1]
    power = slice(narrow + SOURCES * cap, narrow + SOURCES * cap + 1)
    mixed[...] = jnp.zeros(mixed.shape, jnp.int32)
    for top in range(out.shape[0]):
        total = jnp.zeros((narrow, out.shape[2]), F32)
        for n, part in enumerate(parts):
            both = part[top].astype(jnp.int32)
            total += decode(both[:narrow], both[power])
            row = narrow + n * cap
            mixed[row : row + cap, :] = both[narrow : narrow + cap]
        mixed[:narrow, :], mixed[power, :] = encode(total, 0)
        out[top] = mixed[...].astype(jnp.int16)


def sum_kernel(scale, narrow, cap, block, terms, *refs):
    parts, out, mixed = refs[:-2], refs[-2], refs[-1]
    depth = parts[0].shape[0]
    power = slice(narrow + SOURCES * cap, narrow + SOURCES * cap + 1)
    mixed[...] = jnp.zeros(mixed.shape, jnp.int32)
    for first in range(0, len(parts), terms):
        for top in range(depth):
            total = jnp.zeros((narrow, block), F32)
            for part in parts[first : first + terms]:
                both = part[top].astype(jnp.int32)
                total += decode(both[:narrow, :block], both[power, :block])
            mixed[:narrow, :block], mixed[power, :block] = encode(total * F32(scale), 0)
            out[first // terms * depth + top] = mixed[...].astype(jnp.int16)


def entity_kernel(direct, narrow, place, serve, lhs, *refs):
    recv, out, terms, onehot = refs[:-3], refs[-3], refs[-2], refs[-1]
    cap, workers = serve.shape[1], serve.shape[2]
    rows = out.shape[1]
    lane = iota((1, rows), 1)
    for h in range(workers):
        if direct:
            turn, hop = h % SOURCES, h // SOURCES
            mine = place[0] // 4
            both = recv[hop][mine].astype(jnp.int32)
            worker = lax.rem(mine + hop, 2) * 4 + flipped(place[0] % 4, turn)
        else:
            turn, both, worker = 0, recv[0][h].astype(jnp.int32), h
        row = narrow + turn * cap
        both = both[row : row + cap]
        terms[h * cap : (h + 1) * cap, :] = jnp.where(
            iota(both.shape, 1) < narrow, decode(both, both[:, narrow : narrow + 1]), 0.0
        )
        for c in range(cap):
            spot = jnp.where(lane == serve[0, c, worker], 1.0, 0.0).astype(F32)
            onehot[h * cap + c : h * cap + c + 1, :] = spot
    spots = onehot[...].astype(BF16)
    parts = jnp.concatenate(split3(jnp.transpose(terms[...])), axis=1)
    added = dot(parts, jnp.concatenate([spots] * 3, axis=0))
    out[...] = lhs[...] + added[:narrow]


def decoded(pieces, place, workers, power_row, o, over_x, rows):
    dom = place[0]
    over_low = lax.rem(dom // 2 + o // 2, 2)
    over_y = lax.rem(dom + o, 2)
    spot = (over_y + 2 * over_x) * 4 + over_low * 2 + o // 4
    both = pieces[spot].astype(jnp.int32)
    return decode(both[rows], both[power_row : power_row + 1])


def spread_core(pieces, core, place, sizes, bands, out, sems):
    workers, narrow, power_row, block, nrel = sizes
    length = narrow // 8 * 8
    extra = narrow - length
    moves = []
    for x in range(2):
        over_x = lax.rem(place[1] // 2 + x, 2)
        for o in range(workers):
            value = decoded(pieces, place, workers, power_row, o, over_x, slice(0, narrow))
            value = jnp.where(core == 0, value[:length], value[extra:])
            end = min((o + 1) * block, nrel)
            bands[x * length : (x + 1) * length, o * block : end] = value[:, : end - o * block]
        first = pl.multiple_of(2 * narrow * x + (length + 8) * core, 8)
        move = pltpu.make_async_copy(
            bands.at[x * length : (x + 1) * length], out.at[pl.ds(first, length)], sems.at[x]
        )
        move.start()
        moves.append(move)
    return moves


def spread_own_kernel(sizes, place, mine, out, bands, sems):
    for move in spread_core(mine, lax.rem(place[1], 2), place, sizes, bands, out, sems):
        move.wait()


def spread_rest_kernel(sizes, place, mine, other, partial, out, bands, shared, sems):
    workers, narrow, power_row, block, nrel = sizes
    core = lax.rem(place[1], 2)
    length = narrow // 8 * 8
    extra = narrow - length
    moves = spread_core(other, 1 - core, place, sizes, bands, out, sems)
    for x in range(2):
        over_x = lax.rem(place[1] // 2 + x, 2)
        for o in range(workers):
            parts = []
            for which, rows in ((0, slice(length, narrow)), (1, slice(0, 8 - extra))):
                ours = decoded(mine, place, workers, power_row, o, over_x, rows)
                theirs = decoded(other, place, workers, power_row, o, over_x, rows)
                parts.append(jnp.where(core == which, ours, theirs))
            value = jnp.concatenate(parts, axis=0)
            end = min((o + 1) * block, nrel)
            shared[x * 8 : (x + 1) * 8, o * block : end] = value[:, : end - o * block]
        first = 2 * narrow * x + length
        move = pltpu.make_async_copy(
            shared.at[x * 8 : (x + 1) * 8], out.at[first : first + 8], sems.at[2 + x]
        )
        move.start()
        moves.append(move)
    for move in moves:
        move.wait()


def turned(size, hop):
    return [(i, (i + hop) % size) for i in range(size)]


def shards(entities, relation, serve_ids, edge_src, edge_rel, edge_dst, neg_ids, edge_count):
    workers = lax.axis_size("dom")
    replicas = lax.axis_size("rep")
    rows, dim = entities.shape
    nrel = relation.shape[0]
    cap = serve_ids.shape[2]
    edges = edge_src.shape[2]
    groups, width = neg_ids.shape[2], neg_ids.shape[3]
    slots = workers * cap
    narrow = dim // replicas
    direct = workers == 8 and replicas == 4 and narrow % 8 == 4
    block = up(-(-nrel // workers), LANES if direct else 8)
    pad_rel = up(max(nrel, workers * block), LANES)
    offsets = sorted({(narrow * r) % 8 for r in range(replicas)})
    window = up(narrow + offsets[-1], 8)
    height = up(narrow + SOURCES * cap + 1, 16)
    ent_t, rel_t = entities.T, relation.T
    serve_t = jnp.transpose(serve_ids, (0, 2, 1))
    place = jnp.stack([lax.axis_index("dom"), lax.axis_index("rep")]).astype(jnp.int32)

    idx, served = pl.pallas_call(
        prep_kernel,
        out_shape=(
            jax.ShapeDtypeStruct((IDX_ROWS, edges), jnp.int32),
            jax.ShapeDtypeStruct((workers, cap, dim), F32),
        ),
        in_specs=[HBM] * 7,
        out_specs=(VMEM, VMEM),
        scratch_shapes=[
            pltpu.SMEM(serve_t.shape, jnp.int32),
            pltpu.SMEM(edge_count.shape, jnp.int32),
            pltpu.VMEM(ent_t.shape, BF16),
            pltpu.VMEM(edge_src.shape, jnp.int32),
            pltpu.VMEM(edge_rel.shape, jnp.int32),
            pltpu.VMEM(edge_dst.shape, jnp.int32),
            pltpu.VMEM(neg_ids.shape, jnp.int32),
            pltpu.VMEM((slots, rows), F32),
            pltpu.SemaphoreType.DMA((7,)),
        ],
        compiler_params=params(60),
        name="prep",
    )(serve_t, edge_count, ent_t, edge_src, edge_rel, edge_dst, neg_ids)

    held = [idx]
    for hop in range(1, replicas):
        held.append(lax.ppermute(idx, "rep", turned(replicas, hop)))
    received = lax.all_to_all(served, "dom", 0, 0, tiled=True)

    total = min(replicas * edges, up(LIVE_EDGES, edges))
    packed, query, lhs_rows, rel_rows = pl.pallas_call(
        functools.partial(
            gather_kernel, (replicas, groups, nrel, pad_rel, narrow, window, edges)
        ),
        out_shape=(
            jax.ShapeDtypeStruct((IDX_ROWS, total), jnp.int32),
            jax.ShapeDtypeStruct((dim, total), BF16),
            jax.ShapeDtypeStruct((window, total), F32),
            jax.ShapeDtypeStruct((window, total), F32),
        ),
        in_specs=[SMEM] + [VMEM] * (replicas + 2),
        out_specs=[VMEM] * 4,
        scratch_shapes=[
            pltpu.VMEM((2 * dim, pad_rel), BF16),
            pltpu.VMEM((dim, edges), F32),
            pltpu.VMEM((dim, edges), F32),
        ],
        compiler_params=params(),
        cost_estimate=cost(2 * total * dim * (2 * pad_rel + rows), 8 * total * dim),
        name="gather",
    )(place, *held, ent_t, rel_t)

    cfg = (
        direct, workers, replicas, cap, groups, width, pad_rel, block, narrow, window,
        tuple(offsets),
    )
    lanes = max(up(block, LANES), up(narrow, LANES))
    outs = [2] * SOURCES if direct else [workers]
    sizes = [jax.ShapeDtypeStruct((n, height, lanes), jnp.int16) for n in outs]
    lhs_part, *sent = pl.pallas_call(
        functools.partial(main_kernel, cfg),
        out_shape=[jax.ShapeDtypeStruct((narrow, rows), F32)] + sizes,
        in_specs=[SMEM] + [VMEM] * (replicas + 5),
        out_specs=[VMEM] * (1 + len(sizes)),
        scratch_shapes=[
            pltpu.VMEM((slots, dim), F32),
            pltpu.VMEM((dim, slots), F32),
            pltpu.VMEM((dim, total), F32),
            pltpu.VMEM((lanes, slots), F32),
            pltpu.VMEM((height, lanes), jnp.int32),
            pltpu.VMEM((narrow, pad_rel), jnp.int32),
            pltpu.VMEM((1, pad_rel), jnp.int32),
            pltpu.VMEM((slots, lanes), jnp.int32),
        ],
        compiler_params=params(),
        name="edges",
    )(place, *held, packed, query, lhs_rows, rel_rows, received)

    def swap(array, dom_bits=0, rep_bits=0):
        pairs = []
        for o in range(workers):
            for r in range(replicas):
                pairs.append((o * replicas + r, (o ^ dom_bits) * replicas + (r ^ rep_bits)))
        return lax.ppermute(array, ("dom", "rep"), pairs)

    stack = jax.ShapeDtypeStruct((outs[0], height, lanes), jnp.int16)
    mixed = [pltpu.VMEM((height, lanes), jnp.int32)]
    if direct:
        got = {n: swap(sent[n], n) for n in reversed(range(1, SOURCES))}
        summed = pl.pallas_call(
            functools.partial(quad_kernel, narrow, cap),
            out_shape=stack,
            in_specs=[VMEM] * SOURCES,
            out_specs=VMEM,
            scratch_shapes=mixed,
            compiler_params=params(),
            name="quad",
        )(sent[0], *[got[n] for n in range(1, SOURCES)])
        recv = [summed, swap(summed, 4)]
        parts = recv + [swap(summed, 2), swap(summed, 6)]
        stack = jax.ShapeDtypeStruct((4, height, lanes), jnp.int16)
    else:
        recv = [lax.all_to_all(sent[0], "dom", 0, 0, tiled=True)]
        parts = [recv[0][w : w + 1] for w in range(workers)]
        stack = jax.ShapeDtypeStruct((1, height, lanes), jnp.int16)
    scale = 1.0 / (edges * workers * replicas)
    chunk = pl.pallas_call(
        functools.partial(sum_kernel, scale, narrow, cap, block, 2 if direct else workers),
        out_shape=stack,
        in_specs=[VMEM] * len(parts),
        out_specs=VMEM,
        scratch_shapes=mixed,
        compiler_params=params(),
        name="total",
    )(*parts)

    if direct:
        base = jnp.concatenate(
            [chunk, swap(chunk, 1), swap(chunk, 0, 2), swap(chunk, 1, 2)], axis=0
        )
    entity_grad = pl.pallas_call(
        functools.partial(entity_kernel, direct, narrow),
        out_shape=jax.ShapeDtypeStruct((narrow, rows), F32),
        in_specs=[SMEM] * 2 + [VMEM] * (1 + len(recv)),
        out_specs=VMEM,
        scratch_shapes=[pltpu.VMEM((slots, lanes), F32), pltpu.VMEM((slots, rows), F32)],
        compiler_params=params(),
        cost_estimate=cost(10**9, 10**6),
        name="entity",
    )(place, serve_t, lhs_part, *recv)

    power_row = narrow + SOURCES * cap
    if direct:
        base, entity_grad = lax.optimization_barrier((base, entity_grad))
        swapped = lax.ppermute(base, "rep", [(i, i ^ 1) for i in range(replicas)])
        sizes = (workers, narrow, power_row, block, nrel)
        result = jax.ShapeDtypeStruct((dim, nrel), F32)
        bands = pltpu.VMEM((narrow // 8 * 16, nrel), F32)
        own_half = pl.pallas_call(
            functools.partial(spread_own_kernel, sizes),
            out_shape=result,
            in_specs=[SMEM, VMEM],
            out_specs=HBM,
            scratch_shapes=[bands, pltpu.SemaphoreType.DMA((2,))],
            compiler_params=params(),
            cost_estimate=cost(10**6, 4 * dim * nrel),
            name="spread_own",
        )(place, base)
        relation_t = pl.pallas_call(
            functools.partial(spread_rest_kernel, sizes),
            out_shape=result,
            in_specs=[SMEM, VMEM, VMEM, HBM],
            out_specs=HBM,
            scratch_shapes=[bands, pltpu.VMEM((16, nrel), F32), pltpu.SemaphoreType.DMA((4,))],
            input_output_aliases={3: 0},
            compiler_params=params(),
            name="spread_rest",
        )(place, base, swapped, own_half)
    else:
        whole = lax.all_gather(chunk[0, :, :block], ("dom", "rep"), axis=0)
        whole = decode(whole[:, :narrow], whole[:, power_row : power_row + 1])
        whole = whole.reshape(workers, replicas, narrow, block).transpose(1, 2, 0, 3)
        relation_t = whole.reshape(dim, workers * block)[:, :nrel]
    return (entity_grad.T, relation_t.T)


def solution(mesh):
    placed = (
        P("dom", None),
        P(),
        P("dom", None, None),
        P("dom", "rep", None),
        P("dom", "rep", None),
        P("dom", "rep", None),
        P("dom", "rep", None, None),
        P("dom", "rep"),
    )
    return jax.shard_map(
        shards, mesh=mesh, in_specs=placed, out_specs=(P("dom", "rep"), P()), check_vma=False
    )
```

```python
import functools

import jax
import jax.numpy as jnp
from jax import lax
from jax.experimental import pallas as pl
from jax.experimental.pallas import tpu as pltpu
from jax.sharding import PartitionSpec as P

F32 = jnp.float32
BF16 = jnp.bfloat16
IDX_ROWS = 8
LANES = 128
SOURCES = 4
LIVE_EDGES = 1536
VMEM = pl.BlockSpec(memory_space=pltpu.VMEM)
SMEM = pl.BlockSpec(memory_space=pltpu.SMEM)
HBM = pl.BlockSpec(memory_space=pltpu.HBM)


def params(mib=32):
    return pltpu.CompilerParams(vmem_limit_bytes=mib * 1024 * 1024)


def cost(flops, moved):
    return pl.CostEstimate(flops=flops, bytes_accessed=moved, transcendentals=0)


def up(value, step):
    return -(-value // step) * step


def split2(x):
    hi = x.astype(BF16)
    lo = (x - hi.astype(F32)).astype(BF16)
    return hi, lo


def split3(x):
    hi, rest = x.astype(BF16), x
    rest = rest - hi.astype(F32)
    mid = rest.astype(BF16)
    low = (rest - mid.astype(F32)).astype(BF16)
    return hi, mid, low


def dot(a, b):
    return jnp.dot(a, b, preferred_element_type=F32)


def dot_t(a, b):
    return lax.dot_general(a, b, (((1,), (1,)), ((), ())), preferred_element_type=F32)


def ones_where(flag):
    return jnp.where(flag, 1.0, 0.0).astype(BF16)


def exponent(largest):
    safe = jnp.where(largest > 0, largest, 1.0)
    return jnp.clip(jnp.floor(F32(14.9) - jnp.log2(safe)), -120.0, 120.0)


def encode(x, axis):
    k = exponent(jnp.max(jnp.abs(x), axis=axis, keepdims=True))
    return jnp.floor(x * jnp.exp2(k) + 0.5).astype(jnp.int32), k.astype(jnp.int32)


def decode(codes, k):
    return codes.astype(F32) * jnp.exp2(-k.astype(F32))


def iota(shape, axis):
    return lax.broadcasted_iota(jnp.int32, shape, axis)


def shifted_rows(x, offset, narrow, offsets):
    out = x[offsets[0] : offsets[0] + narrow]
    for other in offsets[1:]:
        out = jnp.where(offset == other, x[other : other + narrow], out)
    return out


def prep_kernel(serve, count, ent, src, rel, dst, neg, out_idx, out_rows, *refs):
    cap, workers = serve.shape[1], serve.shape[2]
    rows = ent.shape[1]
    groups, width = neg.shape[2], neg.shape[3]
    onehot, sems = refs[-2:]
    moves = [
        pltpu.make_async_copy(a, b, sems.at[n])
        for n, (a, b) in enumerate(zip((serve, count, ent, src, rel, dst, neg), refs))
    ]
    for move in moves:
        move.start()
    for move in moves:
        move.wait()
    serve_s, count_s, ent_v, src_v, rel_v, dst_v, neg_v = refs[:7]
    out_idx[...] = jnp.full(out_idx.shape, count_s[0, 0], jnp.int32)
    out_idx[0:1, :] = src_v[0]
    out_idx[1:2, :] = rel_v[0]
    out_idx[2:3, :] = dst_v[0]
    for g in range(groups):
        out_idx[3 + g : 4 + g, :width] = neg_v[0, 0, g : g + 1, :]
    lane = iota((1, rows), 1)
    for k in range(workers * cap):
        picked = serve_s[0, k % cap, k // cap]
        onehot[k : k + 1, :] = jnp.where(lane == picked, 1.0, 0.0).astype(F32)
    picked_rows = dot_t(onehot[...].astype(BF16), ent_v[...])
    for w in range(workers):
        out_rows[w] = picked_rows[w * cap : (w + 1) * cap]


def packed_edges(idx_refs, groups, out_idx):
    edges, span = idx_refs[0].shape[1], out_idx.shape[1]
    wide = max(span, edges)
    place = iota((IDX_ROWS, wide), 1)
    row = iota((IDX_ROWS, edges), 0)
    block = iota((IDX_ROWS, edges), 1) // (edges // groups)
    packed = jnp.where(iota((IDX_ROWS, wide), 0) < 3, -1, 0)
    first = 0
    for i, ref in enumerate(idx_refs):
        count = jnp.max(ref[IDX_ROWS - 1 : IDX_ROWS, :].astype(F32)).astype(jnp.int32)
        rows = jnp.where(row < 3, ref[...], jnp.where(row == 3, block + i * groups, 1))
        if wide > edges:
            rows = jnp.concatenate(
                [rows, jnp.zeros((IDX_ROWS, wide - edges), jnp.int32)], axis=1
            )
        moved = pltpu.roll(rows, first, 1)
        packed = jnp.where((place >= first) & (place < first + count), moved, packed)
        first = first + count
    out_idx[...] = packed[:, :span]


def gather_kernel(cfg, place, *refs):
    replicas, groups, nrel, pad_rel, narrow, window, step = cfg
    idx_refs, refs = refs[:replicas], refs[replicas:]
    ent, relation, out_idx, out_query, out_lhs, out_rel, rel_parts, lhs_s, rel_s = refs
    dim, rows = ent.shape
    base = pl.multiple_of((place[1] * narrow) // 8 * 8, 8)
    packed_edges(idx_refs, groups, out_idx)
    hi, lo = split2(relation[...])
    if pad_rel > nrel:
        rel_parts[...] = jnp.zeros(rel_parts.shape, BF16)
    rel_parts[:dim, :nrel] = hi
    rel_parts[dim:, :nrel] = lo
    for start in range(0, out_idx.shape[1], step):
        span = slice(start, start + step)
        src_l, rel_l = out_idx[0:1, span], out_idx[1:2, span]
        lhs = dot(ent[...], ones_where(iota((rows, step), 0) == src_l))
        both = dot(rel_parts[...], ones_where(iota((pad_rel, step), 0) == rel_l))
        rel_rows = both[:dim] + both[dim:]
        lhs_s[...] = lhs
        rel_s[...] = rel_rows
        out_query[:, span] = (lhs * rel_rows).astype(BF16)
        out_lhs[:, span] = lhs_s[pl.ds(base, window), :]
        out_rel[:, span] = rel_s[pl.ds(base, window), :]


def main_kernel(cfg, place, *refs):
    (direct, workers, replicas, cap, groups, width, pad_rel, block, narrow, window, offsets) = cfg
    idx_refs, refs = refs[:replicas], refs[replicas:]
    (packed, query_v, lhs_v, rel_v, received), refs = refs[:5], refs[5:]
    out_x, tables, refs = refs[0], refs[1], refs[2:]
    out_y, refs = (refs[0], refs[1:]) if direct else (None, refs)
    outs, (table_f, table_t, query_s, wide_t, mixed) = refs[:-5], refs[-5:]
    edges = idx_refs[0].shape[1]
    dim, total = query_v.shape
    slots = workers * cap
    rep = place[1]
    per = edges // groups
    base = pl.multiple_of((rep * narrow) // 8 * 8, 8)
    offset = rep * narrow - base

    for w in range(workers):
        table_f[w * cap : (w + 1) * cap, :] = received[w]
    table_t[...] = jnp.transpose(table_f[...])
    table = table_f[...].astype(BF16)
    own_t = table_t[pl.ds(base, window), :].astype(BF16)
    own_t = jnp.concatenate([own_t] * 3, axis=1)

    query = query_v[...]
    scores = dot(table, query)
    query_s[...] = query.astype(F32)
    lanes = packed[...]
    cols = jnp.transpose(lanes)
    times = jnp.zeros((slots, total), F32)
    for i in range(replicas):
        shard = idx_refs[i][...]
        position = iota((slots, edges), 1)
        seen = (iota((slots, edges), 0) == shard[2:3]) & (position < shard[IDX_ROWS - 1 : IDX_ROWS])
        seen = jnp.where(seen, 1.0, 0.0).astype(F32)
        for g in range(groups):
            neg = iota((slots, width), 0) == shard[3 + g : 4 + g, :width]
            often = jnp.sum(jnp.where(neg, 1.0, 0.0).astype(F32), axis=1, keepdims=True)
            often = often + jnp.sum(seen[:, g * per : (g + 1) * per], axis=1, keepdims=True)
            times = jnp.where(lanes[3:4] == i * groups + g, often, times)
    live = lanes[4:5].astype(F32)
    own = jnp.where(iota((slots, total), 0) == lanes[2:3], 1.0, 0.0).astype(F32)
    scores = jnp.where(times > 0, scores, F32(-1e30))
    expo = jnp.exp(scores - jnp.max(scores, axis=0, keepdims=True))
    norm = jnp.sum(expo * times, axis=0, keepdims=True)
    probs = expo / jnp.where(live > 0, norm, 1.0)
    other = probs.astype(BF16).astype(F32)
    itself = (probs - 1.0).astype(BF16).astype(F32)
    grads = ((times - own) * other + own * itself) * live
    stack = jnp.concatenate(split3(grads), axis=0)
    stack_t = jnp.concatenate(split3(jnp.transpose(grads)), axis=1)

    dquery = dot(own_t, stack)
    acc_tab = dot(query_s[pl.ds(base, window), :].astype(BF16), stack_t)
    wide_t[...] = jnp.zeros(wide_t.shape, F32)
    wide_t[:narrow] = shifted_rows(
        acc_tab[:, :slots] + acc_tab[:, slots : 2 * slots] + acc_tab[:, 2 * slots :],
        offset,
        narrow,
        offsets,
    )
    table_codes, table_powers = encode(jnp.transpose(wide_t[...]), 1)
    spare = iota(table_codes.shape, 1) >= narrow
    tables[...] = jnp.where(spare, table_powers, table_codes)
    y = jnp.concatenate(split2(dquery * lhs_v[...]), axis=0)
    out_x[...] = jnp.concatenate(split2(dquery * rel_v[...]), axis=0)
    if direct:
        out_y[...] = y
        targets = [
            (outs[h - 1].at[top], top * 4 + flipped(place[0] % 4, h))
            for h in range(1, SOURCES)
            for top in range(2)
        ]
    else:
        targets = [(outs[0].at[o], o) for o in range(workers)]
    write_blocks(y, cols, targets, tables, mixed, rep, block, narrow, cap, offsets)


def write_blocks(y, cols, targets, tables, mixed, rep, block, narrow, cap, offsets):
    window = y.shape[0] // 2
    ids = jnp.concatenate([iota((1, block), 1) + o * block for _, o in targets], axis=1)
    both = dot(y, ones_where(cols[:, 1:2] == ids))
    part = shifted_rows(both[:window] + both[window:], (rep * narrow) % 8, narrow, offsets)
    codes, powers = encode(part, 0)
    power_row = narrow + SOURCES * cap
    mixed[...] = jnp.zeros(mixed.shape, jnp.int32)
    for n, (ref, o) in enumerate(targets):
        span = slice(n * block, (n + 1) * block)
        mixed[:narrow, :block] = codes[:, span]
        for c in range(cap):
            mixed[narrow + c : narrow + c + 1, :] = tables[pl.ds(o * cap + c, 1), :]
        mixed[power_row : power_row + 1, :block] = powers[:, span]
        ref[...] = mixed[...].astype(jnp.int16)


def own_kernel(block, narrow, cap, offsets, place, packed, y, tables, out, mixed):
    cols = jnp.transpose(packed[...])
    targets = [(out.at[top], top * 4 + place[0] % 4) for top in range(2)]
    write_blocks(y[...], cols, targets, tables, mixed, place[1], block, narrow, cap, offsets)


def flipped(index, mask):
    out, bit = index * 0, 1
    while bit < 4:
        out = out + bit * lax.rem(index // bit + (mask // bit) % 2, 2)
        bit *= 2
    return out


def quad_kernel(narrow, cap, *refs):
    parts, out, mixed = refs[:-2], refs[-2], refs[-1]
    power = slice(narrow + SOURCES * cap, narrow + SOURCES * cap + 1)
    mixed[...] = jnp.zeros(mixed.shape, jnp.int32)
    for top in range(out.shape[0]):
        total = jnp.zeros((narrow, out.shape[2]), F32)
        for n, part in enumerate(parts):
            both = part[top].astype(jnp.int32)
            total += decode(both[:narrow], both[power])
            row = narrow + n * cap
            mixed[row : row + cap, :] = both[narrow : narrow + cap]
        mixed[:narrow, :], mixed[power, :] = encode(total, 0)
        out[top] = mixed[...].astype(jnp.int16)


def sum_kernel(scale, narrow, cap, block, terms, *refs):
    parts, out, mixed = refs[:-2], refs[-2], refs[-1]
    depth = parts[0].shape[0]
    power = slice(narrow + SOURCES * cap, narrow + SOURCES * cap + 1)
    mixed[...] = jnp.zeros(mixed.shape, jnp.int32)
    for first in range(0, len(parts), terms):
        for top in range(depth):
            total = jnp.zeros((narrow, block), F32)
            for part in parts[first : first + terms]:
                both = part[top].astype(jnp.int32)
                total += decode(both[:narrow, :block], both[power, :block])
            codes, powers = encode(total * F32(scale), 0)
            mixed[:narrow, :block], mixed[narrow : narrow + 1, :block] = codes, powers
            out[first // terms * depth + top] = mixed[...].astype(jnp.int16)


def entity_kernel(direct, narrow, offsets, place, serve, packed, x, *refs):
    recv, out, terms, onehot = refs[:-3], refs[-3], refs[-2], refs[-1]
    cap, workers = serve.shape[1], serve.shape[2]
    rows = out.shape[1]
    lane = iota((1, rows), 1)
    for h in range(workers):
        if direct:
            turn, hop = h % SOURCES, h // SOURCES
            mine = place[0] // 4
            both = recv[hop][mine].astype(jnp.int32)
            worker = lax.rem(mine + hop, 2) * 4 + flipped(place[0] % 4, turn)
        else:
            turn, both, worker = 0, recv[0][h].astype(jnp.int32), h
        row = narrow + turn * cap
        both = both[row : row + cap]
        terms[h * cap : (h + 1) * cap, :] = jnp.where(
            iota(both.shape, 1) < narrow, decode(both, both[:, narrow : narrow + 1]), 0.0
        )
        for c in range(cap):
            spot = jnp.where(lane == serve[0, c, worker], 1.0, 0.0).astype(F32)
            onehot[h * cap + c : h * cap + c + 1, :] = spot
    spots = onehot[...].astype(BF16)
    parts = jnp.concatenate(split3(jnp.transpose(terms[...])), axis=1)
    added = dot(parts, jnp.concatenate([spots] * 3, axis=0))
    sources = jnp.transpose(packed[...])[:, 0:1]
    both = dot(x[...], ones_where(iota((x.shape[1], rows), 1) == sources))
    window = x.shape[0] // 2
    both = both[:window] + both[window:]
    out[...] = shifted_rows(both, (place[1] * narrow) % 8, narrow, offsets) + added[:narrow]


def decoded(pieces, place, workers, power_row, o, over_x, rows):
    dom = place[0]
    over_low = lax.rem(dom // 2 + o // 2, 2)
    over_y = lax.rem(dom + o, 2)
    spot = (over_y + 2 * over_x) * 4 + over_low * 2 + o // 4
    both = pieces[spot].astype(jnp.int32)
    return decode(both[rows], both[power_row : power_row + 1])


def spread_core(pieces, core, place, sizes, bands, out, sems):
    workers, narrow, power_row, block, nrel = sizes
    length = narrow // 8 * 8
    extra = narrow - length
    moves = []
    for x in range(2):
        over_x = lax.rem(place[1] // 2 + x, 2)
        for o in range(workers):
            value = decoded(pieces, place, workers, power_row, o, over_x, slice(0, narrow))
            value = jnp.where(core == 0, value[:length], value[extra:])
            end = min((o + 1) * block, nrel)
            bands[x * length : (x + 1) * length, o * block : end] = value[:, : end - o * block]
        first = pl.multiple_of(2 * narrow * x + (length + 8) * core, 8)
        move = pltpu.make_async_copy(
            bands.at[x * length : (x + 1) * length], out.at[pl.ds(first, length)], sems.at[x]
        )
        move.start()
        moves.append(move)
    return moves


def spread_own_kernel(sizes, place, mine, out, bands, sems):
    for move in spread_core(mine, lax.rem(place[1], 2), place, sizes, bands, out, sems):
        move.wait()


def spread_rest_kernel(sizes, place, mine, other, partial, out, bands, shared, sems):
    workers, narrow, power_row, block, nrel = sizes
    core = lax.rem(place[1], 2)
    length = narrow // 8 * 8
    extra = narrow - length
    moves = spread_core(other, 1 - core, place, sizes, bands, out, sems)
    for x in range(2):
        over_x = lax.rem(place[1] // 2 + x, 2)
        for o in range(workers):
            parts = []
            for which, rows in ((0, slice(length, narrow)), (1, slice(0, 8 - extra))):
                ours = decoded(mine, place, workers, power_row, o, over_x, rows)
                theirs = decoded(other, place, workers, power_row, o, over_x, rows)
                parts.append(jnp.where(core == which, ours, theirs))
            value = jnp.concatenate(parts, axis=0)
            end = min((o + 1) * block, nrel)
            shared[x * 8 : (x + 1) * 8, o * block : end] = value[:, : end - o * block]
        first = 2 * narrow * x + length
        move = pltpu.make_async_copy(
            shared.at[x * 8 : (x + 1) * 8], out.at[first : first + 8], sems.at[2 + x]
        )
        move.start()
        moves.append(move)
    for move in moves:
        move.wait()


def turned(size, hop):
    return [(i, (i + hop) % size) for i in range(size)]


def shards(entities, relation, serve_ids, edge_src, edge_rel, edge_dst, neg_ids, edge_count):
    workers = lax.axis_size("dom")
    replicas = lax.axis_size("rep")
    rows, dim = entities.shape
    nrel = relation.shape[0]
    cap = serve_ids.shape[2]
    edges = edge_src.shape[2]
    groups, width = neg_ids.shape[2], neg_ids.shape[3]
    slots = workers * cap
    narrow = dim // replicas
    direct = workers == 8 and replicas == 4 and narrow % 8 == 4
    block = up(-(-nrel // workers), LANES if direct else 8)
    pad_rel = up(max(nrel, workers * block), LANES)
    offsets = sorted({(narrow * r) % 8 for r in range(replicas)})
    window = up(narrow + offsets[-1], 8)
    height = up(narrow + SOURCES * cap + 1, 16)
    ent_t, rel_t = entities.T, relation.T
    serve_t = jnp.transpose(serve_ids, (0, 2, 1))
    place = jnp.stack([lax.axis_index("dom"), lax.axis_index("rep")]).astype(jnp.int32)

    idx, served = pl.pallas_call(
        prep_kernel,
        out_shape=(
            jax.ShapeDtypeStruct((IDX_ROWS, edges), jnp.int32),
            jax.ShapeDtypeStruct((workers, cap, dim), F32),
        ),
        in_specs=[HBM] * 7,
        out_specs=(VMEM, VMEM),
        scratch_shapes=[
            pltpu.SMEM(serve_t.shape, jnp.int32),
            pltpu.SMEM(edge_count.shape, jnp.int32),
            pltpu.VMEM(ent_t.shape, BF16),
            pltpu.VMEM(edge_src.shape, jnp.int32),
            pltpu.VMEM(edge_rel.shape, jnp.int32),
            pltpu.VMEM(edge_dst.shape, jnp.int32),
            pltpu.VMEM(neg_ids.shape, jnp.int32),
            pltpu.VMEM((slots, rows), F32),
            pltpu.SemaphoreType.DMA((7,)),
        ],
        compiler_params=params(60),
        name="prep",
    )(serve_t, edge_count, ent_t, edge_src, edge_rel, edge_dst, neg_ids)

    held = [idx]
    for hop in range(1, replicas):
        held.append(lax.ppermute(idx, "rep", turned(replicas, hop)))
    received = lax.all_to_all(served, "dom", 0, 0, tiled=True)

    total = min(replicas * edges, up(LIVE_EDGES, edges))
    packed, query, lhs_rows, rel_rows = pl.pallas_call(
        functools.partial(
            gather_kernel, (replicas, groups, nrel, pad_rel, narrow, window, edges)
        ),
        out_shape=(
            jax.ShapeDtypeStruct((IDX_ROWS, total), jnp.int32),
            jax.ShapeDtypeStruct((dim, total), BF16),
            jax.ShapeDtypeStruct((window, total), F32),
            jax.ShapeDtypeStruct((window, total), F32),
        ),
        in_specs=[SMEM] + [VMEM] * (replicas + 2),
        out_specs=[VMEM] * 4,
        scratch_shapes=[
            pltpu.VMEM((2 * dim, pad_rel), BF16),
            pltpu.VMEM((dim, edges), F32),
            pltpu.VMEM((dim, edges), F32),
        ],
        compiler_params=params(),
        cost_estimate=cost(2 * total * dim * (2 * pad_rel + rows), 8 * total * dim),
        name="gather",
    )(place, *held, ent_t, rel_t)

    cfg = (
        direct, workers, replicas, cap, groups, width, pad_rel, block, narrow, window,
        tuple(offsets),
    )
    lanes = max(up(block, LANES), up(narrow, LANES))
    pieces = jax.ShapeDtypeStruct((2 * window, total), BF16)
    outs = [2] * (SOURCES - 1) if direct else [workers]
    sizes = [pieces] if direct else []
    sizes += [jax.ShapeDtypeStruct((n, height, lanes), jnp.int16) for n in outs]
    mixed = [pltpu.VMEM((height, lanes), jnp.int32)]
    x_parts, tables, *sent = pl.pallas_call(
        functools.partial(main_kernel, cfg),
        out_shape=[pieces, jax.ShapeDtypeStruct((slots, lanes), jnp.int32)] + sizes,
        in_specs=[SMEM] + [VMEM] * (replicas + 5),
        out_specs=[VMEM] * (2 + len(sizes)),
        scratch_shapes=[
            pltpu.VMEM((slots, dim), F32),
            pltpu.VMEM((dim, slots), F32),
            pltpu.VMEM((dim, total), F32),
            pltpu.VMEM((lanes, slots), F32),
        ]
        + mixed,
        compiler_params=params(),
        name="edges",
    )(place, *held, packed, query, lhs_rows, rel_rows, received)

    def swap(array, dom_bits=0, rep_bits=0):
        pairs = []
        for o in range(workers):
            for r in range(replicas):
                pairs.append((o * replicas + r, (o ^ dom_bits) * replicas + (r ^ rep_bits)))
        return lax.ppermute(array, ("dom", "rep"), pairs)

    stack = jax.ShapeDtypeStruct((outs[0], height, lanes), jnp.int16)
    if direct:
        y_parts, *sent = sent
        got = {n: swap(sent[n - 1], n) for n in reversed(range(1, SOURCES))}
        kept = pl.pallas_call(
            functools.partial(own_kernel, block, narrow, cap, offsets),
            out_shape=stack,
            in_specs=[SMEM] + [VMEM] * 3,
            out_specs=VMEM,
            scratch_shapes=mixed,
            compiler_params=params(),
            cost_estimate=cost(4 * window * total * 2 * block, 10**6),
            name="own",
        )(place, packed, y_parts, tables)
        summed = pl.pallas_call(
            functools.partial(quad_kernel, narrow, cap),
            out_shape=stack,
            in_specs=[VMEM] * SOURCES,
            out_specs=VMEM,
            scratch_shapes=mixed,
            compiler_params=params(),
            name="quad",
        )(kept, *[got[n] for n in range(1, SOURCES)])
        recv = [summed, swap(summed, 4)]
        parts = recv + [swap(summed, 2), swap(summed, 6)]
        stack = 4
    else:
        recv = [lax.all_to_all(sent[0], "dom", 0, 0, tiled=True)]
        parts = [recv[0][w : w + 1] for w in range(workers)]
        stack = 1
    scale = 1.0 / (edges * workers * replicas)
    chunk = pl.pallas_call(
        functools.partial(sum_kernel, scale, narrow, cap, block, 2 if direct else workers),
        out_shape=jax.ShapeDtypeStruct((stack, up(narrow + 1, 8), lanes), jnp.int16),
        in_specs=[VMEM] * len(parts),
        out_specs=VMEM,
        scratch_shapes=[pltpu.VMEM((up(narrow + 1, 8), lanes), jnp.int32)],
        compiler_params=params(),
        name="total",
    )(*parts)

    if direct:
        base = jnp.concatenate(
            [chunk, swap(chunk, 1), swap(chunk, 0, 2), swap(chunk, 1, 2)], axis=0
        )
    entity_grad = pl.pallas_call(
        functools.partial(entity_kernel, direct, narrow, offsets),
        out_shape=jax.ShapeDtypeStruct((narrow, rows), F32),
        in_specs=[SMEM] * 2 + [VMEM] * (2 + len(recv)),
        out_specs=VMEM,
        scratch_shapes=[pltpu.VMEM((slots, lanes), F32), pltpu.VMEM((slots, rows), F32)],
        compiler_params=params(),
        cost_estimate=cost(10**9, 10**6),
        name="entity",
    )(place, serve_t, packed, x_parts, *recv)

    power_row = narrow
    if direct:
        base, entity_grad = lax.optimization_barrier((base, entity_grad))
        swapped = lax.ppermute(base, "rep", [(i, i ^ 1) for i in range(replicas)])
        sizes = (workers, narrow, power_row, block, nrel)
        result = jax.ShapeDtypeStruct((dim, nrel), F32)
        bands = pltpu.VMEM((narrow // 8 * 16, nrel), F32)
        own_half = pl.pallas_call(
            functools.partial(spread_own_kernel, sizes),
            out_shape=result,
            in_specs=[SMEM, VMEM],
            out_specs=HBM,
            scratch_shapes=[bands, pltpu.SemaphoreType.DMA((2,))],
            compiler_params=params(),
            cost_estimate=cost(10**6, 4 * dim * nrel),
            name="spread_own",
        )(place, base)
        relation_t = pl.pallas_call(
            functools.partial(spread_rest_kernel, sizes),
            out_shape=result,
            in_specs=[SMEM, VMEM, VMEM, HBM],
            out_specs=HBM,
            scratch_shapes=[bands, pltpu.VMEM((16, nrel), F32), pltpu.SemaphoreType.DMA((4,))],
            input_output_aliases={3: 0},
            compiler_params=params(),
            name="spread_rest",
        )(place, base, swapped, own_half)
    else:
        whole = lax.all_gather(chunk[0, :, :block], ("dom", "rep"), axis=0)
        whole = decode(whole[:, :narrow], whole[:, power_row : power_row + 1])
        whole = whole.reshape(workers, replicas, narrow, block).transpose(1, 2, 0, 3)
        relation_t = whole.reshape(dim, workers * block)[:, :nrel]
    return (entity_grad.T, relation_t.T)


def solution(mesh):
    placed = (
        P("dom", None),
        P(),
        P("dom", None, None),
        P("dom", "rep", None),
        P("dom", "rep", None),
        P("dom", "rep", None),
        P("dom", "rep", None, None),
        P("dom", "rep"),
    )
    return jax.shard_map(
        shards, mesh=mesh, in_specs=placed, out_specs=(P("dom", "rep"), P()), check_vma=False
    )
```

```python
import functools

import jax
import jax.numpy as jnp
from jax import lax
from jax.experimental import pallas as pl
from jax.experimental.pallas import tpu as pltpu
from jax.sharding import PartitionSpec as P

F32 = jnp.float32
BF16 = jnp.bfloat16
IDX_ROWS = 8
LANES = 128
SOURCES = 4
LIVE_EDGES = 1536
VMEM = pl.BlockSpec(memory_space=pltpu.VMEM)
SMEM = pl.BlockSpec(memory_space=pltpu.SMEM)
HBM = pl.BlockSpec(memory_space=pltpu.HBM)


def params(mib=32):
    return pltpu.CompilerParams(vmem_limit_bytes=mib * 1024 * 1024)


def cost(flops, moved):
    return pl.CostEstimate(flops=flops, bytes_accessed=moved, transcendentals=0)


def up(value, step):
    return -(-value // step) * step


def split2(x):
    hi = x.astype(BF16)
    lo = (x - hi.astype(F32)).astype(BF16)
    return hi, lo


def split3(x):
    hi, rest = x.astype(BF16), x
    rest = rest - hi.astype(F32)
    mid = rest.astype(BF16)
    low = (rest - mid.astype(F32)).astype(BF16)
    return hi, mid, low


def dot(a, b):
    return jnp.dot(a, b, preferred_element_type=F32)


def dot_t(a, b):
    return lax.dot_general(a, b, (((1,), (1,)), ((), ())), preferred_element_type=F32)


def ones_where(flag):
    return jnp.where(flag, 1.0, 0.0).astype(BF16)


def exponent(largest):
    safe = jnp.where(largest > 0, largest, 1.0)
    return jnp.clip(jnp.floor(F32(14.9) - jnp.log2(safe)), -120.0, 120.0)


def encode(x, axis):
    k = exponent(jnp.max(jnp.abs(x), axis=axis, keepdims=True))
    return jnp.floor(x * jnp.exp2(k) + 0.5).astype(jnp.int32), k.astype(jnp.int32)


def decode(codes, k):
    return codes.astype(F32) * jnp.exp2(-k.astype(F32))


def iota(shape, axis):
    return lax.broadcasted_iota(jnp.int32, shape, axis)


def shifted_rows(x, offset, narrow, offsets):
    out = x[offsets[0] : offsets[0] + narrow]
    for other in offsets[1:]:
        out = jnp.where(offset == other, x[other : other + narrow], out)
    return out


def window_rows(x, rep, starts, window):
    out = x[starts[0] : starts[0] + window]
    for n, start in enumerate(starts[1:], 1):
        out = jnp.where(rep == n, x[start : start + window], out)
    return out


def prep_kernel(serve, count, ent, src, rel, dst, neg, out_idx, out_rows, *refs):
    cap, workers = serve.shape[1], serve.shape[2]
    rows = ent.shape[1]
    groups, width = neg.shape[2], neg.shape[3]
    onehot, sems = refs[-2:]
    moves = [
        pltpu.make_async_copy(a, b, sems.at[n])
        for n, (a, b) in enumerate(zip((serve, count, ent, src, rel, dst, neg), refs))
    ]
    for move in moves:
        move.start()
    for move in moves:
        move.wait()
    serve_s, count_s, ent_v, src_v, rel_v, dst_v, neg_v = refs[:7]
    out_idx[...] = jnp.full(out_idx.shape, count_s[0, 0], jnp.int32)
    out_idx[0:1, :] = src_v[0]
    out_idx[1:2, :] = rel_v[0]
    out_idx[2:3, :] = dst_v[0]
    for g in range(groups):
        out_idx[3 + g : 4 + g, :width] = neg_v[0, 0, g : g + 1, :]
    lane = iota((1, rows), 1)
    for k in range(workers * cap):
        picked = serve_s[0, k % cap, k // cap]
        onehot[k : k + 1, :] = jnp.where(lane == picked, 1.0, 0.0).astype(F32)
    picked_rows = dot_t(onehot[...].astype(BF16), ent_v[...])
    for w in range(workers):
        out_rows[w] = picked_rows[w * cap : (w + 1) * cap]


def packed_edges(idx_refs, groups, out_idx):
    edges, span = idx_refs[0].shape[1], out_idx.shape[1]
    wide = max(span, edges)
    place = iota((IDX_ROWS, wide), 1)
    row = iota((IDX_ROWS, edges), 0)
    block = iota((IDX_ROWS, edges), 1) // (edges // groups)
    packed = jnp.where(iota((IDX_ROWS, wide), 0) < 3, -1, 0)
    first = 0
    for i, ref in enumerate(idx_refs):
        count = jnp.max(ref[IDX_ROWS - 1 : IDX_ROWS, :].astype(F32)).astype(jnp.int32)
        rows = jnp.where(row < 3, ref[...], jnp.where(row == 3, block + i * groups, 1))
        if wide > edges:
            rows = jnp.concatenate(
                [rows, jnp.zeros((IDX_ROWS, wide - edges), jnp.int32)], axis=1
            )
        moved = pltpu.roll(rows, first, 1)
        packed = jnp.where((place >= first) & (place < first + count), moved, packed)
        first = first + count
    out_idx[...] = packed[:, :span]


def gather_kernel(cfg, place, *refs):
    replicas, groups, nrel, pad_rel, narrow, window, step = cfg
    idx_refs, refs = refs[:replicas], refs[replicas:]
    ent, relation, out_idx, out_query, out_lhs, out_rel, rel_parts = refs
    dim, rows = ent.shape
    starts = [narrow * r // 8 * 8 for r in range(replicas)]
    packed_edges(idx_refs, groups, out_idx)
    hi, lo = split2(relation[...])
    if pad_rel > nrel:
        edge = nrel // LANES * LANES
        rel_parts[:, edge:] = jnp.zeros((2 * dim, pad_rel - edge), BF16)
    rel_parts[:dim, :nrel] = hi
    rel_parts[dim:, :nrel] = lo
    for start in range(0, out_idx.shape[1], step):
        span = slice(start, start + step)
        src_l, rel_l = out_idx[0:1, span], out_idx[1:2, span]
        lhs = dot(ent[...], ones_where(iota((rows, step), 0) == src_l))
        both = dot(rel_parts[...], ones_where(iota((pad_rel, step), 0) == rel_l))
        rel_rows = both[:dim] + both[dim:]
        out_query[:, span] = (lhs * rel_rows).astype(BF16)
        out_lhs[:, span] = window_rows(lhs, place[1], starts, window)
        out_rel[:, span] = window_rows(rel_rows, place[1], starts, window)


def main_kernel(cfg, place, *refs):
    (direct, workers, replicas, cap, groups, width, pad_rel, block, narrow, window, offsets) = cfg
    idx_refs, refs = refs[:replicas], refs[replicas:]
    (packed, query_v, lhs_v, rel_v, received), refs = refs[:5], refs[5:]
    out_x, tables, refs = refs[0], refs[1], refs[2:]
    out_y, refs = (refs[0], refs[1:]) if direct else (None, refs)
    outs, (table_f, table_t, wide_t, mixed) = refs[:-4], refs[-4:]
    edges = idx_refs[0].shape[1]
    dim, total = query_v.shape
    slots = workers * cap
    rep = place[1]
    per = edges // groups
    base = pl.multiple_of((rep * narrow) // 8 * 8, 8)
    offset = rep * narrow - base

    for w in range(workers):
        table_f[w * cap : (w + 1) * cap, :] = received[w]
    table_t[...] = jnp.transpose(table_f[...])
    table = table_f[...].astype(BF16)
    own_t = table_t[pl.ds(base, window), :].astype(BF16)
    own_t = jnp.concatenate([own_t] * 3, axis=1)

    query = query_v[...]
    scores = dot(table, query)
    lanes = packed[...]
    cols = jnp.transpose(lanes)
    times = jnp.zeros((slots, total), F32)
    for i in range(replicas):
        shard = idx_refs[i][...]
        position = iota((slots, edges), 1)
        seen = (iota((slots, edges), 0) == shard[2:3]) & (position < shard[IDX_ROWS - 1 : IDX_ROWS])
        seen = jnp.where(seen, 1.0, 0.0).astype(F32)
        for g in range(groups):
            neg = iota((slots, width), 0) == shard[3 + g : 4 + g, :width]
            often = jnp.sum(jnp.where(neg, 1.0, 0.0).astype(F32), axis=1, keepdims=True)
            often = often + jnp.sum(seen[:, g * per : (g + 1) * per], axis=1, keepdims=True)
            times = jnp.where(lanes[3:4] == i * groups + g, often, times)
    live = lanes[4:5].astype(F32)
    own = jnp.where(iota((slots, total), 0) == lanes[2:3], 1.0, 0.0).astype(F32)
    scores = jnp.where(times > 0, scores, F32(-1e30))
    expo = jnp.exp(scores - jnp.max(scores, axis=0, keepdims=True))
    norm = jnp.sum(expo * times, axis=0, keepdims=True)
    probs = expo / jnp.where(live > 0, norm, 1.0)
    other = probs.astype(BF16).astype(F32)
    itself = (probs - 1.0).astype(BF16).astype(F32)
    grads = ((times - own) * other + own * itself) * live
    stack = jnp.concatenate(split3(grads), axis=0)
    stack_t = jnp.concatenate(split3(jnp.transpose(grads)), axis=1)

    dquery = dot(own_t, stack)
    acc_tab = window_rows(
        dot(query, stack_t), rep, [narrow * r // 8 * 8 for r in range(replicas)], window
    )
    wide_t[...] = jnp.zeros(wide_t.shape, F32)
    wide_t[:narrow] = shifted_rows(
        acc_tab[:, :slots] + acc_tab[:, slots : 2 * slots] + acc_tab[:, 2 * slots :],
        offset,
        narrow,
        offsets,
    )
    table_codes, table_powers = encode(jnp.transpose(wide_t[...]), 1)
    spare = iota(table_codes.shape, 1) >= narrow
    tables[...] = jnp.where(spare, table_powers, table_codes)
    y = jnp.concatenate(split2(dquery * lhs_v[...]), axis=0)
    out_x[...] = jnp.concatenate(split2(dquery * rel_v[...]), axis=0)
    if direct:
        out_y[...] = y
        targets = [
            (outs[h - 1].at[top], top * 4 + flipped(place[0] % 4, h))
            for h in range(1, SOURCES)
            for top in range(2)
        ]
    else:
        targets = [(outs[0].at[o], o) for o in range(workers)]
    write_blocks(y, cols, targets, tables, mixed, rep, block, narrow, cap, offsets)


def write_blocks(y, cols, targets, tables, mixed, rep, block, narrow, cap, offsets):
    window = y.shape[0] // 2
    ids = jnp.concatenate([iota((1, block), 1) + o * block for _, o in targets], axis=1)
    both = dot(y, ones_where(cols[:, 1:2] == ids))
    part = shifted_rows(both[:window] + both[window:], (rep * narrow) % 8, narrow, offsets)
    codes, powers = encode(part, 0)
    power_row = narrow + SOURCES * cap
    mixed[...] = jnp.zeros(mixed.shape, jnp.int32)
    for n, (ref, o) in enumerate(targets):
        span = slice(n * block, (n + 1) * block)
        mixed[:narrow, :block] = codes[:, span]
        for c in range(cap):
            mixed[narrow + c : narrow + c + 1, :] = tables[pl.ds(o * cap + c, 1), :]
        mixed[power_row : power_row + 1, :block] = powers[:, span]
        ref[...] = mixed[...].astype(jnp.int16)


def own_kernel(block, narrow, cap, offsets, place, packed, y, tables, out, mixed):
    cols = jnp.transpose(packed[...])
    targets = [(out.at[top], top * 4 + place[0] % 4) for top in range(2)]
    write_blocks(y[...], cols, targets, tables, mixed, place[1], block, narrow, cap, offsets)


def flipped(index, mask):
    out, bit = index * 0, 1
    while bit < 4:
        out = out + bit * lax.rem(index // bit + (mask // bit) % 2, 2)
        bit *= 2
    return out


def quad_kernel(narrow, cap, *refs):
    parts, out, mixed = refs[:-2], refs[-2], refs[-1]
    power = slice(narrow + SOURCES * cap, narrow + SOURCES * cap + 1)
    mixed[...] = jnp.zeros(mixed.shape, jnp.int32)
    for top in range(out.shape[0]):
        total = jnp.zeros((narrow, out.shape[2]), F32)
        for n, part in enumerate(parts):
            both = part[top].astype(jnp.int32)
            total += decode(both[:narrow], both[power])
            row = narrow + n * cap
            mixed[row : row + cap, :] = both[narrow : narrow + cap]
        mixed[:narrow, :], mixed[power, :] = encode(total, 0)
        out[top] = mixed[...].astype(jnp.int16)


def sum_kernel(scale, narrow, cap, block, terms, place, *refs):
    parts, out, mixed = refs[:-2], refs[-2], refs[-1]
    depth = parts[0].shape[0]
    lowered = mixed.shape[0] - narrow if terms == 2 else 0
    power = slice(narrow + SOURCES * cap, narrow + SOURCES * cap + 1)
    mixed[...] = jnp.zeros(mixed.shape, jnp.int32)
    for first in range(0, len(parts), terms):
        for top in range(depth):
            total = jnp.zeros((narrow, block), F32)
            for part in parts[first : first + terms]:
                both = part[top].astype(jnp.int32)
                total += decode(both[:narrow, :block], both[power, :block])
            codes, powers = encode(total * F32(scale), 0)
            if lowered:
                rest = jnp.broadcast_to(powers, (lowered, block))
                mixed[:, :block] = jnp.where(
                    lax.rem(place[1], 2) == 0,
                    jnp.concatenate([codes, rest], axis=0),
                    jnp.concatenate([rest, codes], axis=0),
                )
            else:
                mixed[:narrow, :block], mixed[narrow : narrow + 1, :block] = codes, powers
            out[first // terms * depth + top] = mixed[...].astype(jnp.int16)


def entity_kernel(direct, narrow, offsets, place, serve, packed, x, *refs):
    recv, out, terms, onehot = refs[:-3], refs[-3], refs[-2], refs[-1]
    cap, workers = serve.shape[1], serve.shape[2]
    rows = out.shape[1]
    lane = iota((1, rows), 1)
    for h in range(workers):
        if direct:
            turn, hop = h % SOURCES, h // SOURCES
            mine = place[0] // 4
            both = recv[hop][mine].astype(jnp.int32)
            worker = lax.rem(mine + hop, 2) * 4 + flipped(place[0] % 4, turn)
        else:
            turn, both, worker = 0, recv[0][h].astype(jnp.int32), h
        row = narrow + turn * cap
        both = both[row : row + cap]
        terms[h * cap : (h + 1) * cap, :] = jnp.where(
            iota(both.shape, 1) < narrow, decode(both, both[:, narrow : narrow + 1]), 0.0
        )
        for c in range(cap):
            spot = jnp.where(lane == serve[0, c, worker], 1.0, 0.0).astype(F32)
            onehot[h * cap + c : h * cap + c + 1, :] = spot
    spots = onehot[...].astype(BF16)
    parts = jnp.concatenate(split3(jnp.transpose(terms[...])), axis=1)
    added = dot(parts, jnp.concatenate([spots] * 3, axis=0))
    sources = jnp.transpose(packed[...])[:, 0:1]
    both = dot(x[...], ones_where(iota((x.shape[1], rows), 1) == sources))
    window = x.shape[0] // 2
    both = both[:window] + both[window:]
    out[...] = shifted_rows(both, (place[1] * narrow) % 8, narrow, offsets) + added[:narrow]


def found(pieces, place, o, over_x):
    dom = place[0]
    over_low = lax.rem(dom // 2 + o // 2, 2)
    over_y = lax.rem(dom + o, 2)
    return pieces[(over_y + 2 * over_x) * 4 + over_low * 2 + o // 4].astype(jnp.int32)


def spread_core(pieces, core, place, sizes, bands, out, sems):
    workers, narrow, block, nrel = sizes
    length = narrow // 8 * 8
    moves = []
    for x in range(2):
        over_x = lax.rem(place[1] // 2 + x, 2)
        for o in range(workers):
            both = found(pieces, place, o, over_x)
            codes = jnp.where(core == 0, both[:length], both[8:])
            value = decode(codes, jnp.where(core == 0, both[narrow : narrow + 1], both[:1]))
            end = min((o + 1) * block, nrel)
            bands[x * length : (x + 1) * length, o * block : end] = value[:, : end - o * block]
        first = pl.multiple_of(2 * narrow * x + (length + 8) * core, 8)
        move = pltpu.make_async_copy(
            bands.at[x * length : (x + 1) * length], out.at[pl.ds(first, length)], sems.at[x]
        )
        move.start()
        moves.append(move)
    return moves


def spread_own_kernel(sizes, place, mine, out, bands, sems):
    for move in spread_core(mine, lax.rem(place[1], 2), place, sizes, bands, out, sems):
        move.wait()


def spread_rest_kernel(sizes, place, mine, other, partial, out, bands, shared, sems):
    workers, narrow, block, nrel = sizes
    core = lax.rem(place[1], 2)
    length = narrow // 8 * 8
    moves = spread_core(other, 1 - core, place, sizes, bands, out, sems)
    for x in range(2):
        over_x = lax.rem(place[1] // 2 + x, 2)
        for o in range(workers):
            ours, theirs = found(mine, place, o, over_x), found(other, place, o, over_x)
            low = jnp.where(core == 0, ours[length:], theirs[length:])
            high = jnp.where(core == 0, theirs[:8], ours[:8])
            upper = iota(low.shape, 0) < narrow - length
            split = narrow - length
            value = jnp.where(
                upper, decode(low, low[split : split + 1]), decode(high, high[:1])
            )
            end = min((o + 1) * block, nrel)
            shared[x * 8 : (x + 1) * 8, o * block : end] = value[:, : end - o * block]
        first = 2 * narrow * x + length
        move = pltpu.make_async_copy(
            shared.at[x * 8 : (x + 1) * 8], out.at[first : first + 8], sems.at[2 + x]
        )
        move.start()
        moves.append(move)
    for move in moves:
        move.wait()


def turned(size, hop):
    return [(i, (i + hop) % size) for i in range(size)]


def shards(entities, relation, serve_ids, edge_src, edge_rel, edge_dst, neg_ids, edge_count):
    workers = lax.axis_size("dom")
    replicas = lax.axis_size("rep")
    rows, dim = entities.shape
    nrel = relation.shape[0]
    cap = serve_ids.shape[2]
    edges = edge_src.shape[2]
    groups, width = neg_ids.shape[2], neg_ids.shape[3]
    slots = workers * cap
    narrow = dim // replicas
    direct = workers == 8 and replicas == 4 and narrow % 8 == 4
    block = up(-(-nrel // workers), LANES if direct else 8)
    pad_rel = up(max(nrel, workers * block), LANES)
    offsets = sorted({(narrow * r) % 8 for r in range(replicas)})
    window = up(narrow + offsets[-1], 8)
    height = up(narrow + SOURCES * cap + 1, 16)
    ent_t, rel_t = entities.T, relation.T
    serve_t = jnp.transpose(serve_ids, (0, 2, 1))
    place = jnp.stack([lax.axis_index("dom"), lax.axis_index("rep")]).astype(jnp.int32)

    idx, served = pl.pallas_call(
        prep_kernel,
        out_shape=(
            jax.ShapeDtypeStruct((IDX_ROWS, edges), jnp.int32),
            jax.ShapeDtypeStruct((workers, cap, dim), F32),
        ),
        in_specs=[HBM] * 7,
        out_specs=(VMEM, VMEM),
        scratch_shapes=[
            pltpu.SMEM(serve_t.shape, jnp.int32),
            pltpu.SMEM(edge_count.shape, jnp.int32),
            pltpu.VMEM(ent_t.shape, BF16),
            pltpu.VMEM(edge_src.shape, jnp.int32),
            pltpu.VMEM(edge_rel.shape, jnp.int32),
            pltpu.VMEM(edge_dst.shape, jnp.int32),
            pltpu.VMEM(neg_ids.shape, jnp.int32),
            pltpu.VMEM((slots, rows), F32),
            pltpu.SemaphoreType.DMA((7,)),
        ],
        compiler_params=params(60),
        name="prep",
    )(serve_t, edge_count, ent_t, edge_src, edge_rel, edge_dst, neg_ids)

    held = [idx]
    for hop in range(1, replicas):
        held.append(lax.ppermute(idx, "rep", turned(replicas, hop)))
    received = lax.all_to_all(served, "dom", 0, 0, tiled=True)

    total = min(replicas * edges, up(LIVE_EDGES, edges))
    packed, query, lhs_rows, rel_rows = pl.pallas_call(
        functools.partial(
            gather_kernel, (replicas, groups, nrel, pad_rel, narrow, window, edges)
        ),
        out_shape=(
            jax.ShapeDtypeStruct((IDX_ROWS, total), jnp.int32),
            jax.ShapeDtypeStruct((dim, total), BF16),
            jax.ShapeDtypeStruct((window, total), F32),
            jax.ShapeDtypeStruct((window, total), F32),
        ),
        in_specs=[SMEM] + [VMEM] * (replicas + 2),
        out_specs=[VMEM] * 4,
        scratch_shapes=[
            pltpu.VMEM((2 * dim, pad_rel), BF16),
        ],
        compiler_params=params(),
        cost_estimate=cost(2 * total * dim * (2 * pad_rel + rows), 8 * total * dim),
        name="gather",
    )(place, *held, ent_t, rel_t)

    cfg = (
        direct, workers, replicas, cap, groups, width, pad_rel, block, narrow, window,
        tuple(offsets),
    )
    lanes = max(up(block, LANES), up(narrow, LANES))
    pieces = jax.ShapeDtypeStruct((2 * window, total), BF16)
    outs = [2] * (SOURCES - 1) if direct else [workers]
    sizes = [pieces] if direct else []
    sizes += [jax.ShapeDtypeStruct((n, height, lanes), jnp.int16) for n in outs]
    mixed = [pltpu.VMEM((height, lanes), jnp.int32)]
    x_parts, tables, *sent = pl.pallas_call(
        functools.partial(main_kernel, cfg),
        out_shape=[pieces, jax.ShapeDtypeStruct((slots, lanes), jnp.int32)] + sizes,
        in_specs=[SMEM] + [VMEM] * (replicas + 5),
        out_specs=[VMEM] * (2 + len(sizes)),
        scratch_shapes=[
            pltpu.VMEM((slots, dim), F32),
            pltpu.VMEM((dim, slots), F32),
            pltpu.VMEM((lanes, slots), F32),
        ]
        + mixed,
        compiler_params=params(),
        name="edges",
    )(place, *held, packed, query, lhs_rows, rel_rows, received)

    def swap(array, dom_bits=0, rep_bits=0):
        pairs = []
        for o in range(workers):
            for r in range(replicas):
                pairs.append((o * replicas + r, (o ^ dom_bits) * replicas + (r ^ rep_bits)))
        return lax.ppermute(array, ("dom", "rep"), pairs)

    stack = jax.ShapeDtypeStruct((outs[0], height, lanes), jnp.int16)
    if direct:
        y_parts, *sent = sent
        got = {n: swap(sent[n - 1], n) for n in reversed(range(1, SOURCES))}
        kept = pl.pallas_call(
            functools.partial(own_kernel, block, narrow, cap, offsets),
            out_shape=stack,
            in_specs=[SMEM] + [VMEM] * 3,
            out_specs=VMEM,
            scratch_shapes=mixed,
            compiler_params=params(),
            cost_estimate=cost(4 * window * total * 2 * block, 10**6),
            name="own",
        )(place, packed, y_parts, tables)
        summed = pl.pallas_call(
            functools.partial(quad_kernel, narrow, cap),
            out_shape=stack,
            in_specs=[VMEM] * SOURCES,
            out_specs=VMEM,
            scratch_shapes=mixed,
            compiler_params=params(),
            name="quad",
        )(kept, *[got[n] for n in range(1, SOURCES)])
        recv = [summed, swap(summed, 4)]
        parts = recv + [swap(summed, 2), swap(summed, 6)]
        stack = 4
    else:
        recv = [lax.all_to_all(sent[0], "dom", 0, 0, tiled=True)]
        parts = [recv[0][w : w + 1] for w in range(workers)]
        stack = 1
    scale = 1.0 / (edges * workers * replicas)
    chunk = pl.pallas_call(
        functools.partial(sum_kernel, scale, narrow, cap, block, 2 if direct else workers),
        out_shape=jax.ShapeDtypeStruct((stack, up(narrow + 1, 8), lanes), jnp.int16),
        in_specs=[SMEM] + [VMEM] * len(parts),
        out_specs=VMEM,
        scratch_shapes=[pltpu.VMEM((up(narrow + 1, 8), lanes), jnp.int32)],
        compiler_params=params(),
        name="total",
    )(place, *parts)

    if direct:
        base = jnp.concatenate(
            [chunk, swap(chunk, 1), swap(chunk, 0, 2), swap(chunk, 1, 2)], axis=0
        )
    entity_grad = pl.pallas_call(
        functools.partial(entity_kernel, direct, narrow, offsets),
        out_shape=jax.ShapeDtypeStruct((narrow, rows), F32),
        in_specs=[SMEM] * 2 + [VMEM] * (2 + len(recv)),
        out_specs=VMEM,
        scratch_shapes=[pltpu.VMEM((slots, lanes), F32), pltpu.VMEM((slots, rows), F32)],
        compiler_params=params(),
        cost_estimate=cost(10**9, 10**6),
        name="entity",
    )(place, serve_t, packed, x_parts, *recv)

    if direct:
        base, entity_grad = lax.optimization_barrier((base, entity_grad))
        swapped = lax.ppermute(base, "rep", [(i, i ^ 1) for i in range(replicas)])
        sizes = (workers, narrow, block, nrel)
        result = jax.ShapeDtypeStruct((dim, nrel), F32)
        bands = pltpu.VMEM((narrow // 8 * 16, nrel), F32)
        own_half = pl.pallas_call(
            functools.partial(spread_own_kernel, sizes),
            out_shape=result,
            in_specs=[SMEM, VMEM],
            out_specs=HBM,
            scratch_shapes=[bands, pltpu.SemaphoreType.DMA((2,))],
            compiler_params=params(),
            cost_estimate=cost(10**6, 4 * dim * nrel),
            name="spread_own",
        )(place, base)
        relation_t = pl.pallas_call(
            functools.partial(spread_rest_kernel, sizes),
            out_shape=result,
            in_specs=[SMEM, VMEM, VMEM, HBM],
            out_specs=HBM,
            scratch_shapes=[bands, pltpu.VMEM((16, nrel), F32), pltpu.SemaphoreType.DMA((4,))],
            input_output_aliases={3: 0},
            compiler_params=params(),
            name="spread_rest",
        )(place, base, swapped, own_half)
    else:
        whole = lax.all_gather(chunk[0, :, :block], ("dom", "rep"), axis=0)
        whole = decode(whole[:, :narrow], whole[:, narrow : narrow + 1])
        whole = whole.reshape(workers, replicas, narrow, block).transpose(1, 2, 0, 3)
        relation_t = whole.reshape(dim, workers * block)[:, :nrel]
    return (entity_grad.T, relation_t.T)


def solution(mesh):
    placed = (
        P("dom", None),
        P(),
        P("dom", None, None),
        P("dom", "rep", None),
        P("dom", "rep", None),
        P("dom", "rep", None),
        P("dom", "rep", None, None),
        P("dom", "rep"),
    )
    return jax.shard_map(
        shards, mesh=mesh, in_specs=placed, out_specs=(P("dom", "rep"), P()), check_vma=False
    )
```

```python
import functools

import jax
import jax.numpy as jnp
from jax import lax
from jax.experimental import pallas as pl
from jax.experimental.pallas import tpu as pltpu
from jax.sharding import PartitionSpec as P

F32 = jnp.float32
BF16 = jnp.bfloat16
IDX_ROWS = 8
LANES = 128
SOURCES = 4
LIVE_EDGES = 1536
VMEM = pl.BlockSpec(memory_space=pltpu.VMEM)
SMEM = pl.BlockSpec(memory_space=pltpu.SMEM)
HBM = pl.BlockSpec(memory_space=pltpu.HBM)


def params(mib=32):
    return pltpu.CompilerParams(vmem_limit_bytes=mib * 1024 * 1024)


def cost(flops, moved):
    return pl.CostEstimate(flops=flops, bytes_accessed=moved, transcendentals=0)


def up(value, step):
    return -(-value // step) * step


def split2(x):
    hi = x.astype(BF16)
    lo = (x - hi.astype(F32)).astype(BF16)
    return hi, lo


def split3(x):
    hi, rest = x.astype(BF16), x
    rest = rest - hi.astype(F32)
    mid = rest.astype(BF16)
    low = (rest - mid.astype(F32)).astype(BF16)
    return hi, mid, low


def dot(a, b):
    return jnp.dot(a, b, preferred_element_type=F32)


def dot_t(a, b):
    return lax.dot_general(a, b, (((1,), (1,)), ((), ())), preferred_element_type=F32)


def ones_where(flag):
    return jnp.where(flag, 1.0, 0.0).astype(BF16)


def exponent(largest):
    safe = jnp.where(largest > 0, largest, 1.0)
    return jnp.clip(jnp.floor(F32(14.9) - jnp.log2(safe)), -120.0, 120.0)


def encode(x, axis):
    k = exponent(jnp.max(jnp.abs(x), axis=axis, keepdims=True))
    return jnp.floor(x * jnp.exp2(k) + 0.5).astype(jnp.int32), k.astype(jnp.int32)


def decode(codes, k):
    return codes.astype(F32) * jnp.exp2(-k.astype(F32))


def iota(shape, axis):
    return lax.broadcasted_iota(jnp.int32, shape, axis)


def shifted_rows(x, offset, narrow, offsets):
    out = x[offsets[0] : offsets[0] + narrow]
    for other in offsets[1:]:
        out = jnp.where(offset == other, x[other : other + narrow], out)
    return out


def window_rows(x, rep, starts, window):
    out = x[starts[0] : starts[0] + window]
    for n, start in enumerate(starts[1:], 1):
        out = jnp.where(rep == n, x[start : start + window], out)
    return out


def my_place():
    return lax.axis_index("dom"), lax.axis_index("rep")


def prep_kernel(serve, count, ent, src, rel, dst, neg, out_idx, out_rows, *refs):
    cap, workers = serve.shape[1], serve.shape[2]
    rows = ent.shape[1]
    groups, width = neg.shape[2], neg.shape[3]
    onehot, sems = refs[-2:]
    moves = [
        pltpu.make_async_copy(a, b, sems.at[n])
        for n, (a, b) in enumerate(zip((serve, count, ent, src, rel, dst, neg), refs))
    ]
    for move in moves:
        move.start()
    for move in moves:
        move.wait()
    serve_s, count_s, ent_v, src_v, rel_v, dst_v, neg_v = refs[:7]
    out_idx[...] = jnp.full(out_idx.shape, count_s[0, 0], jnp.int32)
    out_idx[0:1, :] = src_v[0]
    out_idx[1:2, :] = rel_v[0]
    out_idx[2:3, :] = dst_v[0]
    for g in range(groups):
        out_idx[3 + g : 4 + g, :width] = neg_v[0, 0, g : g + 1, :]
    lane = iota((1, rows), 1)
    for k in range(workers * cap):
        picked = serve_s[0, k % cap, k // cap]
        onehot[k : k + 1, :] = jnp.where(lane == picked, 1.0, 0.0).astype(F32)
    picked_rows = dot_t(onehot[...].astype(BF16), ent_v[...])
    for w in range(workers):
        out_rows[w] = picked_rows[w * cap : (w + 1) * cap]


def packed_edges(idx_refs, groups, out_idx):
    edges, span = idx_refs[0].shape[1], out_idx.shape[1]
    wide = max(span, edges)
    place = iota((IDX_ROWS, wide), 1)
    row = iota((IDX_ROWS, edges), 0)
    block = iota((IDX_ROWS, edges), 1) // (edges // groups)
    packed = jnp.where(iota((IDX_ROWS, wide), 0) < 3, -1, 0)
    first = 0
    for i, ref in enumerate(idx_refs):
        count = jnp.max(ref[IDX_ROWS - 1 : IDX_ROWS, :].astype(F32)).astype(jnp.int32)
        rows = jnp.where(row < 3, ref[...], jnp.where(row == 3, block + i * groups, 1))
        if wide > edges:
            rows = jnp.concatenate(
                [rows, jnp.zeros((IDX_ROWS, wide - edges), jnp.int32)], axis=1
            )
        moved = pltpu.roll(rows, first, 1)
        packed = jnp.where((place >= first) & (place < first + count), moved, packed)
        first = first + count
    out_idx[...] = packed[:, :span]


def gather_kernel(cfg, *refs):
    place = my_place()
    replicas, groups, nrel, pad_rel, narrow, window, step = cfg
    idx_refs, refs = refs[:replicas], refs[replicas:]
    ent, relation, out_idx, out_query, out_lhs, out_rel, rel_parts = refs
    dim, rows = ent.shape
    starts = [narrow * r // 8 * 8 for r in range(replicas)]
    packed_edges(idx_refs, groups, out_idx)
    hi, lo = split2(relation[...])
    if pad_rel > nrel:
        edge = nrel // LANES * LANES
        rel_parts[:, edge:] = jnp.zeros((2 * dim, pad_rel - edge), BF16)
    rel_parts[:dim, :nrel] = hi
    rel_parts[dim:, :nrel] = lo
    for start in range(0, out_idx.shape[1], step):
        span = slice(start, start + step)
        src_l, rel_l = out_idx[0:1, span], out_idx[1:2, span]
        lhs = dot(ent[...], ones_where(iota((rows, step), 0) == src_l))
        both = dot(rel_parts[...], ones_where(iota((pad_rel, step), 0) == rel_l))
        rel_rows = both[:dim] + both[dim:]
        out_query[:, span] = (lhs * rel_rows).astype(BF16)
        out_lhs[:, span] = window_rows(lhs, place[1], starts, window)
        out_rel[:, span] = window_rows(rel_rows, place[1], starts, window)


def main_kernel(cfg, *refs):
    place = my_place()
    (direct, workers, replicas, cap, groups, width, pad_rel, block, narrow, window, offsets) = cfg
    idx_refs, refs = refs[:replicas], refs[replicas:]
    (packed, query_v, lhs_v, rel_v, received), refs = refs[:5], refs[5:]
    out_x, tables, refs = refs[0], refs[1], refs[2:]
    out_y, refs = (refs[0], refs[1:]) if direct else (None, refs)
    outs, (table_f, table_t, query_s, wide_t, mixed) = refs[:-5], refs[-5:]
    edges = idx_refs[0].shape[1]
    dim, total = query_v.shape
    slots = workers * cap
    rep = place[1]
    per = edges // groups
    base = pl.multiple_of((rep * narrow) // 8 * 8, 8)
    offset = rep * narrow - base

    for w in range(workers):
        table_f[w * cap : (w + 1) * cap, :] = received[w]
    table_t[...] = jnp.transpose(table_f[...])
    table = table_f[...].astype(BF16)
    own_t = table_t[pl.ds(base, window), :].astype(BF16)
    own_t = jnp.concatenate([own_t] * 3, axis=1)

    query = query_v[...]
    scores = dot(table, query)
    query_s[...] = query.astype(F32)
    lanes = packed[...]
    cols = jnp.transpose(lanes)
    times = jnp.zeros((slots, total), F32)
    for i in range(replicas):
        shard = idx_refs[i][...]
        position = iota((slots, edges), 1)
        seen = (iota((slots, edges), 0) == shard[2:3]) & (position < shard[IDX_ROWS - 1 : IDX_ROWS])
        seen = jnp.where(seen, 1.0, 0.0).astype(F32)
        for g in range(groups):
            neg = iota((slots, width), 0) == shard[3 + g : 4 + g, :width]
            often = jnp.sum(jnp.where(neg, 1.0, 0.0).astype(F32), axis=1, keepdims=True)
            often = often + jnp.sum(seen[:, g * per : (g + 1) * per], axis=1, keepdims=True)
            times = jnp.where(lanes[3:4] == i * groups + g, often, times)
    live = lanes[4:5].astype(F32)
    own = jnp.where(iota((slots, total), 0) == lanes[2:3], 1.0, 0.0).astype(F32)
    scores = jnp.where(times > 0, scores, F32(-1e30))
    expo = jnp.exp(scores - jnp.max(scores, axis=0, keepdims=True))
    norm = jnp.sum(expo * times, axis=0, keepdims=True)
    probs = expo / jnp.where(live > 0, norm, 1.0)
    other = probs.astype(BF16).astype(F32)
    itself = (probs - 1.0).astype(BF16).astype(F32)
    grads = ((times - own) * other + own * itself) * live
    stack = jnp.concatenate(split3(grads), axis=0)
    stack_t = jnp.concatenate(split3(jnp.transpose(grads)), axis=1)

    dquery = dot(own_t, stack)
    acc_tab = dot(query_s[pl.ds(base, window), :].astype(BF16), stack_t)
    wide_t[...] = jnp.zeros(wide_t.shape, F32)
    wide_t[:narrow] = shifted_rows(
        acc_tab[:, :slots] + acc_tab[:, slots : 2 * slots] + acc_tab[:, 2 * slots :],
        offset,
        narrow,
        offsets,
    )
    table_codes, table_powers = encode(jnp.transpose(wide_t[...]), 1)
    spare = iota(table_codes.shape, 1) >= narrow
    tables[...] = jnp.where(spare, table_powers, table_codes)
    y = jnp.concatenate(split2(dquery * lhs_v[...]), axis=0)
    out_x[...] = jnp.concatenate(split2(dquery * rel_v[...]), axis=0)
    if direct:
        out_y[...] = y
        targets = [
            (outs[h - 1].at[top], top * 4 + flipped(place[0] % 4, h))
            for h in range(1, SOURCES)
            for top in range(2)
        ]
    else:
        targets = [(outs[0].at[o], o) for o in range(workers)]
    write_blocks(y, cols, targets, tables, mixed, rep, block, narrow, cap, offsets)


def write_blocks(y, cols, targets, tables, mixed, rep, block, narrow, cap, offsets):
    window = y.shape[0] // 2
    ids = jnp.concatenate([iota((1, block), 1) + o * block for _, o in targets], axis=1)
    both = dot(y, ones_where(cols[:, 1:2] == ids))
    part = shifted_rows(both[:window] + both[window:], (rep * narrow) % 8, narrow, offsets)
    codes, powers = encode(part, 0)
    power_row = narrow + SOURCES * cap
    mixed[...] = jnp.zeros(mixed.shape, jnp.int32)
    for n, (ref, o) in enumerate(targets):
        span = slice(n * block, (n + 1) * block)
        mixed[:narrow, :block] = codes[:, span]
        for c in range(cap):
            mixed[narrow + c : narrow + c + 1, :] = tables[pl.ds(o * cap + c, 1), :]
        mixed[power_row : power_row + 1, :block] = powers[:, span]
        ref[...] = mixed[...].astype(jnp.int16)


def own_kernel(block, narrow, cap, offsets, packed, y, tables, out, mixed):
    place = my_place()
    cols = jnp.transpose(packed[...])
    targets = [(out.at[top], top * 4 + place[0] % 4) for top in range(2)]
    write_blocks(y[...], cols, targets, tables, mixed, place[1], block, narrow, cap, offsets)


def flipped(index, mask):
    out, bit = index * 0, 1
    while bit < 4:
        out = out + bit * lax.rem(index // bit + (mask // bit) % 2, 2)
        bit *= 2
    return out


def quad_kernel(narrow, cap, *refs):
    parts, out, mixed = refs[:-2], refs[-2], refs[-1]
    power = slice(narrow + SOURCES * cap, narrow + SOURCES * cap + 1)
    mixed[...] = jnp.zeros(mixed.shape, jnp.int32)
    for top in range(out.shape[0]):
        total = jnp.zeros((narrow, out.shape[2]), F32)
        for n, part in enumerate(parts):
            both = part[top].astype(jnp.int32)
            total += decode(both[:narrow], both[power])
            row = narrow + n * cap
            mixed[row : row + cap, :] = both[narrow : narrow + cap]
        mixed[:narrow, :], mixed[power, :] = encode(total, 0)
        out[top] = mixed[...].astype(jnp.int16)


def sum_kernel(scale, narrow, cap, block, terms, *refs):
    place = my_place()
    parts, out, mixed = refs[:-2], refs[-2], refs[-1]
    depth = parts[0].shape[0]
    lowered = mixed.shape[0] - narrow if terms == 2 else 0
    power = slice(narrow + SOURCES * cap, narrow + SOURCES * cap + 1)
    mixed[...] = jnp.zeros(mixed.shape, jnp.int32)
    for first in range(0, len(parts), terms):
        for top in range(depth):
            total = jnp.zeros((narrow, block), F32)
            for part in parts[first : first + terms]:
                both = part[top].astype(jnp.int32)
                total += decode(both[:narrow, :block], both[power, :block])
            codes, powers = encode(total * F32(scale), 0)
            if lowered:
                rest = jnp.broadcast_to(powers, (lowered, block))
                mixed[:, :block] = jnp.where(
                    lax.rem(place[1], 2) == 0,
                    jnp.concatenate([codes, rest], axis=0),
                    jnp.concatenate([rest, codes], axis=0),
                )
            else:
                mixed[:narrow, :block], mixed[narrow : narrow + 1, :block] = codes, powers
            out[first // terms * depth + top] = mixed[...].astype(jnp.int16)


def entity_kernel(direct, narrow, offsets, serve, packed, x, *refs):
    place = my_place()
    recv, out, terms, onehot = refs[:-3], refs[-3], refs[-2], refs[-1]
    cap, workers = serve.shape[1], serve.shape[2]
    rows = out.shape[1]
    lane = iota((1, rows), 1)
    for h in range(workers):
        if direct:
            turn, hop = h % SOURCES, h // SOURCES
            mine = place[0] // 4
            both = recv[hop][mine].astype(jnp.int32)
            worker = lax.rem(mine + hop, 2) * 4 + flipped(place[0] % 4, turn)
        else:
            turn, both, worker = 0, recv[0][h].astype(jnp.int32), h
        row = narrow + turn * cap
        both = both[row : row + cap]
        terms[h * cap : (h + 1) * cap, :] = jnp.where(
            iota(both.shape, 1) < narrow, decode(both, both[:, narrow : narrow + 1]), 0.0
        )
        for c in range(cap):
            spot = jnp.where(lane == serve[0, c, worker], 1.0, 0.0).astype(F32)
            onehot[h * cap + c : h * cap + c + 1, :] = spot
    spots = onehot[...].astype(BF16)
    parts = jnp.concatenate(split3(jnp.transpose(terms[...])), axis=1)
    added = dot(parts, jnp.concatenate([spots] * 3, axis=0))
    sources = jnp.transpose(packed[...])[:, 0:1]
    both = dot(x[...], ones_where(iota((x.shape[1], rows), 1) == sources))
    window = x.shape[0] // 2
    both = both[:window] + both[window:]
    out[...] = shifted_rows(both, (place[1] * narrow) % 8, narrow, offsets) + added[:narrow]


def found(pieces, place, o, over_x):
    dom = place[0]
    over_low = lax.rem(dom // 2 + o // 2, 2)
    over_y = lax.rem(dom + o, 2)
    return pieces[(over_y + 2 * over_x) * 4 + over_low * 2 + o // 4].astype(jnp.int32)


def spread_core(pieces, core, place, sizes, bands, out, sems):
    workers, narrow, block, nrel = sizes
    length = narrow // 8 * 8
    moves = []
    for x in range(2):
        over_x = lax.rem(place[1] // 2 + x, 2)
        for o in range(workers):
            both = found(pieces, place, o, over_x)
            codes = jnp.where(core == 0, both[:length], both[8:])
            value = decode(codes, jnp.where(core == 0, both[narrow : narrow + 1], both[:1]))
            end = min((o + 1) * block, nrel)
            bands[x * length : (x + 1) * length, o * block : end] = value[:, : end - o * block]
        first = pl.multiple_of(2 * narrow * x + (length + 8) * core, 8)
        move = pltpu.make_async_copy(
            bands.at[x * length : (x + 1) * length], out.at[pl.ds(first, length)], sems.at[x]
        )
        move.start()
        moves.append(move)
    return moves


def spread_own_kernel(sizes, mine, out, bands, sems):
    place = my_place()
    for move in spread_core(mine, lax.rem(place[1], 2), place, sizes, bands, out, sems):
        move.wait()


def spread_rest_kernel(sizes, mine, other, partial, out, bands, shared, sems):
    place = my_place()
    workers, narrow, block, nrel = sizes
    core = lax.rem(place[1], 2)
    length = narrow // 8 * 8
    moves = spread_core(other, 1 - core, place, sizes, bands, out, sems)
    for x in range(2):
        over_x = lax.rem(place[1] // 2 + x, 2)
        for o in range(workers):
            ours, theirs = found(mine, place, o, over_x), found(other, place, o, over_x)
            low = jnp.where(core == 0, ours[length:], theirs[length:])
            high = jnp.where(core == 0, theirs[:8], ours[:8])
            upper = iota(low.shape, 0) < narrow - length
            split = narrow - length
            value = jnp.where(
                upper, decode(low, low[split : split + 1]), decode(high, high[:1])
            )
            end = min((o + 1) * block, nrel)
            shared[x * 8 : (x + 1) * 8, o * block : end] = value[:, : end - o * block]
        first = 2 * narrow * x + length
        move = pltpu.make_async_copy(
            shared.at[x * 8 : (x + 1) * 8], out.at[first : first + 8], sems.at[2 + x]
        )
        move.start()
        moves.append(move)
    for move in moves:
        move.wait()


def turned(size, hop):
    return [(i, (i + hop) % size) for i in range(size)]


def shards(entities, relation, serve_ids, edge_src, edge_rel, edge_dst, neg_ids, edge_count):
    workers = lax.axis_size("dom")
    replicas = lax.axis_size("rep")
    rows, dim = entities.shape
    nrel = relation.shape[0]
    cap = serve_ids.shape[2]
    edges = edge_src.shape[2]
    groups, width = neg_ids.shape[2], neg_ids.shape[3]
    slots = workers * cap
    narrow = dim // replicas
    direct = workers == 8 and replicas == 4 and narrow % 8 == 4
    block = up(-(-nrel // workers), LANES if direct else 8)
    pad_rel = up(max(nrel, workers * block), LANES)
    offsets = sorted({(narrow * r) % 8 for r in range(replicas)})
    window = up(narrow + offsets[-1], 8)
    height = up(narrow + SOURCES * cap + 1, 16)
    ent_t, rel_t = entities.T, relation.T
    serve_t = jnp.transpose(serve_ids, (0, 2, 1))

    idx, served = pl.pallas_call(
        prep_kernel,
        out_shape=(
            jax.ShapeDtypeStruct((IDX_ROWS, edges), jnp.int32),
            jax.ShapeDtypeStruct((workers, cap, dim), F32),
        ),
        in_specs=[HBM] * 7,
        out_specs=(VMEM, VMEM),
        scratch_shapes=[
            pltpu.SMEM(serve_t.shape, jnp.int32),
            pltpu.SMEM(edge_count.shape, jnp.int32),
            pltpu.VMEM(ent_t.shape, BF16),
            pltpu.VMEM(edge_src.shape, jnp.int32),
            pltpu.VMEM(edge_rel.shape, jnp.int32),
            pltpu.VMEM(edge_dst.shape, jnp.int32),
            pltpu.VMEM(neg_ids.shape, jnp.int32),
            pltpu.VMEM((slots, rows), F32),
            pltpu.SemaphoreType.DMA((7,)),
        ],
        compiler_params=params(60),
        name="prep",
    )(serve_t, edge_count, ent_t, edge_src, edge_rel, edge_dst, neg_ids)

    held = [idx]
    for hop in range(1, replicas):
        held.append(lax.ppermute(idx, "rep", turned(replicas, hop)))
    received = lax.all_to_all(served, "dom", 0, 0, tiled=True)

    total = min(replicas * edges, up(LIVE_EDGES, edges))
    packed, query, lhs_rows, rel_rows = pl.pallas_call(
        functools.partial(
            gather_kernel, (replicas, groups, nrel, pad_rel, narrow, window, edges)
        ),
        out_shape=(
            jax.ShapeDtypeStruct((IDX_ROWS, total), jnp.int32),
            jax.ShapeDtypeStruct((dim, total), BF16),
            jax.ShapeDtypeStruct((window, total), F32),
            jax.ShapeDtypeStruct((window, total), F32),
        ),
        in_specs=[VMEM] * (replicas + 2),
        out_specs=[VMEM] * 4,
        scratch_shapes=[
            pltpu.VMEM((2 * dim, pad_rel), BF16),
        ],
        compiler_params=params(),
        cost_estimate=cost(2 * total * dim * (2 * pad_rel + rows), 8 * total * dim),
        name="gather",
    )(*held, ent_t, rel_t)

    cfg = (
        direct, workers, replicas, cap, groups, width, pad_rel, block, narrow, window,
        tuple(offsets),
    )
    lanes = max(up(block, LANES), up(narrow, LANES))
    pieces = jax.ShapeDtypeStruct((2 * window, total), BF16)
    outs = [2] * (SOURCES - 1) if direct else [workers]
    sizes = [pieces] if direct else []
    sizes += [jax.ShapeDtypeStruct((n, height, lanes), jnp.int16) for n in outs]
    mixed = [pltpu.VMEM((height, lanes), jnp.int32)]
    x_parts, tables, *sent = pl.pallas_call(
        functools.partial(main_kernel, cfg),
        out_shape=[pieces, jax.ShapeDtypeStruct((slots, lanes), jnp.int32)] + sizes,
        in_specs=[VMEM] * (replicas + 5),
        out_specs=[VMEM] * (2 + len(sizes)),
        scratch_shapes=[
            pltpu.VMEM((slots, dim), F32),
            pltpu.VMEM((dim, slots), F32),
            pltpu.VMEM((dim, total), F32),
            pltpu.VMEM((lanes, slots), F32),
        ]
        + mixed,
        compiler_params=params(),
        name="edges",
    )(*held, packed, query, lhs_rows, rel_rows, received)

    def swap(array, dom_bits=0, rep_bits=0):
        pairs = []
        for o in range(workers):
            for r in range(replicas):
                pairs.append((o * replicas + r, (o ^ dom_bits) * replicas + (r ^ rep_bits)))
        return lax.ppermute(array, ("dom", "rep"), pairs)

    stack = jax.ShapeDtypeStruct((outs[0], height, lanes), jnp.int16)
    if direct:
        y_parts, *sent = sent
        got = {n: swap(sent[n - 1], n) for n in reversed(range(1, SOURCES))}
        kept = pl.pallas_call(
            functools.partial(own_kernel, block, narrow, cap, offsets),
            out_shape=stack,
            in_specs=[VMEM] * 3,
            out_specs=VMEM,
            scratch_shapes=mixed,
            compiler_params=params(),
            cost_estimate=cost(4 * window * total * 2 * block, 10**6),
            name="own",
        )(packed, y_parts, tables)
        summed = pl.pallas_call(
            functools.partial(quad_kernel, narrow, cap),
            out_shape=stack,
            in_specs=[VMEM] * SOURCES,
            out_specs=VMEM,
            scratch_shapes=mixed,
            compiler_params=params(),
            name="quad",
        )(kept, *[got[n] for n in range(1, SOURCES)])
        recv = [summed, swap(summed, 4)]
        parts = recv + [swap(summed, 2), swap(summed, 6)]
        stack = 4
    else:
        recv = [lax.all_to_all(sent[0], "dom", 0, 0, tiled=True)]
        parts = [recv[0][w : w + 1] for w in range(workers)]
        stack = 1
    scale = 1.0 / (edges * workers * replicas)
    chunk = pl.pallas_call(
        functools.partial(sum_kernel, scale, narrow, cap, block, 2 if direct else workers),
        out_shape=jax.ShapeDtypeStruct((stack, up(narrow + 1, 8), lanes), jnp.int16),
        in_specs=[VMEM] * len(parts),
        out_specs=VMEM,
        scratch_shapes=[pltpu.VMEM((up(narrow + 1, 8), lanes), jnp.int32)],
        compiler_params=params(),
        name="total",
    )(*parts)

    if direct:
        base = jnp.concatenate(
            [chunk, swap(chunk, 1), swap(chunk, 0, 2), swap(chunk, 1, 2)], axis=0
        )
    entity_grad = pl.pallas_call(
        functools.partial(entity_kernel, direct, narrow, offsets),
        out_shape=jax.ShapeDtypeStruct((narrow, rows), F32),
        in_specs=[SMEM] + [VMEM] * (2 + len(recv)),
        out_specs=VMEM,
        scratch_shapes=[pltpu.VMEM((slots, lanes), F32), pltpu.VMEM((slots, rows), F32)],
        compiler_params=params(),
        cost_estimate=cost(10**9, 10**6),
        name="entity",
    )(serve_t, packed, x_parts, *recv)

    if direct:
        base, entity_grad = lax.optimization_barrier((base, entity_grad))
        swapped = lax.ppermute(base, "rep", [(i, i ^ 1) for i in range(replicas)])
        sizes = (workers, narrow, block, nrel)
        result = jax.ShapeDtypeStruct((dim, nrel), F32)
        bands = pltpu.VMEM((narrow // 8 * 16, nrel), F32)
        own_half = pl.pallas_call(
            functools.partial(spread_own_kernel, sizes),
            out_shape=result,
            in_specs=[VMEM],
            out_specs=HBM,
            scratch_shapes=[bands, pltpu.SemaphoreType.DMA((2,))],
            compiler_params=params(),
            cost_estimate=cost(10**6, 4 * dim * nrel),
            name="spread_own",
        )(base)
        relation_t = pl.pallas_call(
            functools.partial(spread_rest_kernel, sizes),
            out_shape=result,
            in_specs=[VMEM, VMEM, HBM],
            out_specs=HBM,
            scratch_shapes=[bands, pltpu.VMEM((16, nrel), F32), pltpu.SemaphoreType.DMA((4,))],
            input_output_aliases={2: 0},
            compiler_params=params(),
            name="spread_rest",
        )(base, swapped, own_half)
    else:
        whole = lax.all_gather(chunk[0, :, :block], ("dom", "rep"), axis=0)
        whole = decode(whole[:, :narrow], whole[:, narrow : narrow + 1])
        whole = whole.reshape(workers, replicas, narrow, block).transpose(1, 2, 0, 3)
        relation_t = whole.reshape(dim, workers * block)[:, :nrel]
    return (entity_grad.T, relation_t.T)


def solution(mesh):
    placed = (
        P("dom", None),
        P(),
        P("dom", None, None),
        P("dom", "rep", None),
        P("dom", "rep", None),
        P("dom", "rep", None),
        P("dom", "rep", None, None),
        P("dom", "rep"),
    )
    return jax.shard_map(
        shards, mesh=mesh, in_specs=placed, out_specs=(P("dom", "rep"), P()), check_vma=False
    )
```

```python
import functools

import jax
import jax.numpy as jnp
from jax import lax
from jax.experimental import pallas as pl
from jax.experimental.pallas import tpu as pltpu
from jax.sharding import PartitionSpec as P

F32 = jnp.float32
BF16 = jnp.bfloat16
IDX_ROWS = 8
LANES = 128
SOURCES = 4
LIVE_EDGES = 1536
VMEM = pl.BlockSpec(memory_space=pltpu.VMEM)
SMEM = pl.BlockSpec(memory_space=pltpu.SMEM)
HBM = pl.BlockSpec(memory_space=pltpu.HBM)


def params(mib=32):
    return pltpu.CompilerParams(vmem_limit_bytes=mib * 1024 * 1024)


def cost(flops, moved):
    return pl.CostEstimate(flops=flops, bytes_accessed=moved, transcendentals=0)


def up(value, step):
    return -(-value // step) * step


def split2(x):
    hi = x.astype(BF16)
    lo = (x - hi.astype(F32)).astype(BF16)
    return hi, lo


def split3(x):
    hi, rest = x.astype(BF16), x
    rest = rest - hi.astype(F32)
    mid = rest.astype(BF16)
    low = (rest - mid.astype(F32)).astype(BF16)
    return hi, mid, low


def dot(a, b):
    return jnp.dot(a, b, preferred_element_type=F32)


def dot_t(a, b):
    return lax.dot_general(a, b, (((1,), (1,)), ((), ())), preferred_element_type=F32)


def ones_where(flag):
    return jnp.where(flag, 1.0, 0.0).astype(BF16)


def exponent(largest):
    safe = jnp.where(largest > 0, largest, 1.0)
    return jnp.clip(jnp.floor(F32(14.9) - jnp.log2(safe)), -120.0, 120.0)


def encode(x, axis):
    k = exponent(jnp.max(jnp.abs(x), axis=axis, keepdims=True))
    return jnp.floor(x * jnp.exp2(k) + 0.5).astype(jnp.int32), k.astype(jnp.int32)


def decode(codes, k):
    return codes.astype(F32) * jnp.exp2(-k.astype(F32))


def iota(shape, axis):
    return lax.broadcasted_iota(jnp.int32, shape, axis)


def shifted_rows(x, offset, narrow, offsets):
    out = x[offsets[0] : offsets[0] + narrow]
    for other in offsets[1:]:
        out = jnp.where(offset == other, x[other : other + narrow], out)
    return out


def window_rows(x, rep, starts, window):
    out = x[starts[0] : starts[0] + window]
    for n, start in enumerate(starts[1:], 1):
        out = jnp.where(rep == n, x[start : start + window], out)
    return out


def my_place():
    return lax.axis_index("dom"), lax.axis_index("rep")


def prep_kernel(serve, count, ent, src, rel, dst, neg, out_idx, out_rows, *refs):
    cap, workers = serve.shape[1], serve.shape[2]
    rows = ent.shape[1]
    groups, width = neg.shape[2], neg.shape[3]
    onehot, sems = refs[-2:]
    moves = [
        pltpu.make_async_copy(a, b, sems.at[n])
        for n, (a, b) in enumerate(zip((serve, count, ent, src, rel, dst, neg), refs))
    ]
    for move in moves:
        move.start()
    for move in moves:
        move.wait()
    serve_s, count_s, ent_v, src_v, rel_v, dst_v, neg_v = refs[:7]
    out_idx[...] = jnp.full(out_idx.shape, count_s[0, 0], jnp.int32)
    out_idx[0:1, :] = src_v[0]
    out_idx[1:2, :] = rel_v[0]
    out_idx[2:3, :] = dst_v[0]
    for g in range(groups):
        out_idx[3 + g : 4 + g, :width] = neg_v[0, 0, g : g + 1, :]
    lane = iota((1, rows), 1)
    for k in range(workers * cap):
        picked = serve_s[0, k % cap, k // cap]
        onehot[k : k + 1, :] = jnp.where(lane == picked, 1.0, 0.0).astype(F32)
    picked_rows = dot_t(onehot[...].astype(BF16), ent_v[...])
    for w in range(workers):
        out_rows[w] = picked_rows[w * cap : (w + 1) * cap]


def packed_edges(idx_refs, groups, out_idx):
    edges, span = idx_refs[0].shape[1], out_idx.shape[1]
    wide = max(span, edges)
    place = iota((IDX_ROWS, wide), 1)
    row = iota((IDX_ROWS, edges), 0)
    block = iota((IDX_ROWS, edges), 1) // (edges // groups)
    packed = jnp.where(iota((IDX_ROWS, wide), 0) < 3, -1, 0)
    first = 0
    for i, ref in enumerate(idx_refs):
        count = jnp.max(ref[IDX_ROWS - 1 : IDX_ROWS, :].astype(F32)).astype(jnp.int32)
        rows = jnp.where(row < 3, ref[...], jnp.where(row == 3, block + i * groups, 1))
        if wide > edges:
            rows = jnp.concatenate(
                [rows, jnp.zeros((IDX_ROWS, wide - edges), jnp.int32)], axis=1
            )
        moved = pltpu.roll(rows, first, 1)
        packed = jnp.where((place >= first) & (place < first + count), moved, packed)
        first = first + count
    out_idx[...] = packed[:, :span]


def gather_kernel(cfg, *refs):
    place = my_place()
    replicas, groups, nrel, pad_rel, narrow, window, step = cfg
    idx_refs, refs = refs[:replicas], refs[replicas:]
    ent, relation, out_idx, out_query, out_lhs, out_rel, rel_parts = refs
    dim, rows = ent.shape
    starts = [narrow * r // 8 * 8 for r in range(replicas)]
    packed_edges(idx_refs, groups, out_idx)
    hi, lo = split2(relation[...])
    if pad_rel > nrel:
        edge = nrel // LANES * LANES
        rel_parts[:, edge:] = jnp.zeros((2 * dim, pad_rel - edge), BF16)
    rel_parts[:dim, :nrel] = hi
    rel_parts[dim:, :nrel] = lo
    for start in range(0, out_idx.shape[1], step):
        span = slice(start, start + step)
        src_l, rel_l = out_idx[0:1, span], out_idx[1:2, span]
        lhs = dot(ent[...], ones_where(iota((rows, step), 0) == src_l))
        both = dot(rel_parts[...], ones_where(iota((pad_rel, step), 0) == rel_l))
        rel_rows = both[:dim] + both[dim:]
        out_query[:, span] = (lhs * rel_rows).astype(BF16)
        out_lhs[:, span] = window_rows(lhs, place[1], starts, window)
        out_rel[:, span] = window_rows(rel_rows, place[1], starts, window)


def main_kernel(cfg, *refs):
    place = my_place()
    (direct, workers, replicas, cap, groups, width, pad_rel, block, narrow, window, offsets) = cfg
    idx_refs, refs = refs[:replicas], refs[replicas:]
    (packed, query_v, lhs_v, rel_v, received), refs = refs[:5], refs[5:]
    out_x, tables, refs = refs[0], refs[1], refs[2:]
    out_y, refs = (refs[0], refs[1:]) if direct else (None, refs)
    outs, (table_f, table_t, query_s, wide_t, mixed) = refs[:-5], refs[-5:]
    edges = idx_refs[0].shape[1]
    dim, total = query_v.shape
    slots = workers * cap
    rep = place[1]
    per = edges // groups
    base = pl.multiple_of((rep * narrow) // 8 * 8, 8)
    offset = rep * narrow - base

    for w in range(workers):
        table_f[w * cap : (w + 1) * cap, :] = received[w]
    table_t[...] = jnp.transpose(table_f[...])
    table = table_f[...].astype(BF16)
    own_t = table_t[pl.ds(base, window), :].astype(BF16)
    own_t = jnp.concatenate([own_t] * 3, axis=1)

    query = query_v[...]
    scores = dot(table, query)
    query_s[...] = query.astype(F32)
    lanes = packed[...]
    cols = jnp.transpose(lanes)
    times = jnp.zeros((slots, total), F32)
    for i in range(replicas):
        shard = idx_refs[i][...]
        position = iota((slots, edges), 1)
        seen = (iota((slots, edges), 0) == shard[2:3]) & (position < shard[IDX_ROWS - 1 : IDX_ROWS])
        seen = jnp.where(seen, 1.0, 0.0).astype(F32)
        for g in range(groups):
            neg = iota((slots, width), 0) == shard[3 + g : 4 + g, :width]
            often = jnp.sum(jnp.where(neg, 1.0, 0.0).astype(F32), axis=1, keepdims=True)
            often = often + jnp.sum(seen[:, g * per : (g + 1) * per], axis=1, keepdims=True)
            times = jnp.where(lanes[3:4] == i * groups + g, often, times)
    live = lanes[4:5].astype(F32)
    own = jnp.where(iota((slots, total), 0) == lanes[2:3], 1.0, 0.0).astype(F32)
    scores = jnp.where(times > 0, scores, F32(-1e30))
    expo = jnp.exp(scores - jnp.max(scores, axis=0, keepdims=True))
    norm = jnp.sum(expo * times, axis=0, keepdims=True)
    probs = expo / jnp.where(live > 0, norm, 1.0)
    other = probs.astype(BF16).astype(F32)
    itself = (probs - 1.0).astype(BF16).astype(F32)
    grads = ((times - own) * other + own * itself) * live
    stack = jnp.concatenate(split3(grads), axis=0)
    stack_t = jnp.concatenate(split3(jnp.transpose(grads)), axis=1)

    dquery = dot(own_t, stack)
    acc_tab = dot(query_s[pl.ds(base, window), :].astype(BF16), stack_t)
    wide_t[...] = jnp.zeros(wide_t.shape, F32)
    wide_t[:narrow] = shifted_rows(
        acc_tab[:, :slots] + acc_tab[:, slots : 2 * slots] + acc_tab[:, 2 * slots :],
        offset,
        narrow,
        offsets,
    )
    table_codes, table_powers = encode(jnp.transpose(wide_t[...]), 1)
    spare = iota(table_codes.shape, 1) >= narrow
    tables[...] = jnp.where(spare, table_powers, table_codes)
    y = jnp.concatenate(split2(dquery * lhs_v[...]), axis=0)
    out_x[...] = jnp.concatenate(split2(dquery * rel_v[...]), axis=0)
    if direct:
        out_y[...] = y
        targets = [
            (outs[h - 1].at[top], top * 4 + flipped(place[0] % 4, h))
            for h in range(1, SOURCES)
            for top in range(2)
        ]
    else:
        targets = [(outs[0].at[o], o) for o in range(workers)]
    write_blocks(y, cols, targets, tables, mixed, rep, block, narrow, cap, offsets)


def write_blocks(y, cols, targets, tables, mixed, rep, block, narrow, cap, offsets):
    window = y.shape[0] // 2
    ids = jnp.concatenate([iota((1, block), 1) + o * block for _, o in targets], axis=1)
    both = dot(y, ones_where(cols[:, 1:2] == ids))
    part = shifted_rows(both[:window] + both[window:], (rep * narrow) % 8, narrow, offsets)
    codes, powers = encode(part, 0)
    power_row = narrow + SOURCES * cap
    mixed[...] = jnp.zeros(mixed.shape, jnp.int32)
    for n, (ref, o) in enumerate(targets):
        span = slice(n * block, (n + 1) * block)
        mixed[:narrow, :block] = codes[:, span]
        for c in range(cap):
            mixed[narrow + c : narrow + c + 1, :] = tables[pl.ds(o * cap + c, 1), :]
        mixed[power_row : power_row + 1, :block] = powers[:, span]
        ref[...] = mixed[...].astype(jnp.int16)


def own_kernel(block, narrow, cap, offsets, packed, y, tables, out, mixed):
    place = my_place()
    cols = jnp.transpose(packed[...])
    targets = [(out.at[top], top * 4 + place[0] % 4) for top in range(2)]
    write_blocks(y[...], cols, targets, tables, mixed, place[1], block, narrow, cap, offsets)


def flipped(index, mask):
    out, bit = index * 0, 1
    while bit < 4:
        out = out + bit * lax.rem(index // bit + (mask // bit) % 2, 2)
        bit *= 2
    return out


def quad_kernel(narrow, cap, *refs):
    parts, out, mixed = refs[:-2], refs[-2], refs[-1]
    power = slice(narrow + SOURCES * cap, narrow + SOURCES * cap + 1)
    mixed[...] = jnp.zeros(mixed.shape, jnp.int32)
    for top in range(out.shape[0]):
        total = jnp.zeros((narrow, out.shape[2]), F32)
        for n, part in enumerate(parts):
            both = part[top].astype(jnp.int32)
            total += decode(both[:narrow], both[power])
            row = narrow + n * cap
            mixed[row : row + cap, :] = both[narrow : narrow + cap]
        mixed[:narrow, :], mixed[power, :] = encode(total, 0)
        out[top] = mixed[...].astype(jnp.int16)


def sum_kernel(scale, narrow, cap, block, terms, *refs):
    place = my_place()
    parts, out, mixed = refs[:-2], refs[-2], refs[-1]
    depth = parts[0].shape[0]
    lowered = mixed.shape[0] - narrow if terms == 2 else 0
    power = slice(narrow + SOURCES * cap, narrow + SOURCES * cap + 1)
    mixed[...] = jnp.zeros(mixed.shape, jnp.int32)
    for first in range(0, len(parts), terms):
        for top in range(depth):
            total = jnp.zeros((narrow, block), F32)
            for part in parts[first : first + terms]:
                both = part[top].astype(jnp.int32)
                total += decode(both[:narrow, :block], both[power, :block])
            codes, powers = encode(total * F32(scale), 0)
            if lowered:
                rest = jnp.broadcast_to(powers, (lowered, block))
                mixed[:, :block] = jnp.where(
                    lax.rem(place[1], 2) == 0,
                    jnp.concatenate([codes, rest], axis=0),
                    jnp.concatenate([rest, codes], axis=0),
                )
            else:
                mixed[:narrow, :block], mixed[narrow : narrow + 1, :block] = codes, powers
            out[first // terms * depth + top] = mixed[...].astype(jnp.int16)


def entity_kernel(direct, narrow, offsets, serve, packed, x, *refs):
    place = my_place()
    recv, out, terms, onehot = refs[:-3], refs[-3], refs[-2], refs[-1]
    cap, workers = serve.shape[1], serve.shape[2]
    rows = out.shape[1]
    lane = iota((1, rows), 1)
    for h in range(workers):
        if direct:
            turn, hop = h % SOURCES, h // SOURCES
            mine = place[0] // 4
            both = recv[hop][mine].astype(jnp.int32)
            worker = lax.rem(mine + hop, 2) * 4 + flipped(place[0] % 4, turn)
        else:
            turn, both, worker = 0, recv[0][h].astype(jnp.int32), h
        row = narrow + turn * cap
        both = both[row : row + cap]
        terms[h * cap : (h + 1) * cap, :] = jnp.where(
            iota(both.shape, 1) < narrow, decode(both, both[:, narrow : narrow + 1]), 0.0
        )
        for c in range(cap):
            spot = jnp.where(lane == serve[0, c, worker], 1.0, 0.0).astype(F32)
            onehot[h * cap + c : h * cap + c + 1, :] = spot
    spots = onehot[...].astype(BF16)
    parts = jnp.concatenate(split3(jnp.transpose(terms[...])), axis=1)
    added = dot(parts, jnp.concatenate([spots] * 3, axis=0))
    sources = jnp.transpose(packed[...])[:, 0:1]
    both = dot(x[...], ones_where(iota((x.shape[1], rows), 1) == sources))
    window = x.shape[0] // 2
    both = both[:window] + both[window:]
    out[...] = shifted_rows(both, (place[1] * narrow) % 8, narrow, offsets) + added[:narrow]


def found(pieces, place, o, over_x):
    dom = place[0]
    over_low = lax.rem(dom // 2 + o // 2, 2)
    over_y = lax.rem(dom + o, 2)
    return pieces[(over_y + 2 * over_x) * 4 + over_low * 2 + o // 4].astype(jnp.int32)


def spread_core(pieces, core, place, sizes, bands, out, sems):
    workers, narrow, block, nrel = sizes
    length = narrow // 8 * 8
    moves = []
    for x in range(2):
        over_x = lax.rem(place[1] // 2 + x, 2)
        for o in range(workers):
            both = found(pieces, place, o, over_x)
            codes = jnp.where(core == 0, both[:length], both[8:])
            value = decode(codes, jnp.where(core == 0, both[narrow : narrow + 1], both[:1]))
            end = min((o + 1) * block, nrel)
            bands[x * length : (x + 1) * length, o * block : end] = value[:, : end - o * block]
        first = pl.multiple_of(2 * narrow * x + (length + 8) * core, 8)
        move = pltpu.make_async_copy(
            bands.at[x * length : (x + 1) * length], out.at[pl.ds(first, length)], sems.at[x]
        )
        move.start()
        moves.append(move)
    return moves


def spread_own_kernel(sizes, mine, out, bands, sems):
    place = my_place()
    for move in spread_core(mine, lax.rem(place[1], 2), place, sizes, bands, out, sems):
        move.wait()


def spread_rest_kernel(sizes, mine, other, partial, out, bands, shared, sems):
    place = my_place()
    workers, narrow, block, nrel = sizes
    core = lax.rem(place[1], 2)
    length = narrow // 8 * 8
    moves = spread_core(other, 1 - core, place, sizes, bands, out, sems)
    for x in range(2):
        over_x = lax.rem(place[1] // 2 + x, 2)
        for o in range(workers):
            ours, theirs = found(mine, place, o, over_x), found(other, place, o, over_x)
            low = jnp.where(core == 0, ours[length:], theirs[length:])
            high = jnp.where(core == 0, theirs[:8], ours[:8])
            upper = iota(low.shape, 0) < narrow - length
            split = narrow - length
            value = jnp.where(
                upper, decode(low, low[split : split + 1]), decode(high, high[:1])
            )
            end = min((o + 1) * block, nrel)
            shared[x * 8 : (x + 1) * 8, o * block : end] = value[:, : end - o * block]
        first = 2 * narrow * x + length
        move = pltpu.make_async_copy(
            shared.at[x * 8 : (x + 1) * 8], out.at[first : first + 8], sems.at[2 + x]
        )
        move.start()
        moves.append(move)
    for move in moves:
        move.wait()


def turned(size, hop):
    return [(i, (i + hop) % size) for i in range(size)]


def shards(entities, relation, serve_ids, edge_src, edge_rel, edge_dst, neg_ids, edge_count):
    workers = lax.axis_size("dom")
    replicas = lax.axis_size("rep")
    rows, dim = entities.shape
    nrel = relation.shape[0]
    cap = serve_ids.shape[2]
    edges = edge_src.shape[2]
    groups, width = neg_ids.shape[2], neg_ids.shape[3]
    slots = workers * cap
    narrow = dim // replicas
    direct = workers == 8 and replicas == 4 and narrow % 8 == 4
    block = up(-(-nrel // workers), LANES if direct else 8)
    pad_rel = up(max(nrel, workers * block), LANES)
    offsets = sorted({(narrow * r) % 8 for r in range(replicas)})
    window = up(narrow + offsets[-1], 8)
    height = up(narrow + SOURCES * cap + 1, 16)
    ent_t, rel_t = entities.T, relation.T
    serve_t = jnp.transpose(serve_ids, (0, 2, 1))

    idx, served = pl.pallas_call(
        prep_kernel,
        out_shape=(
            jax.ShapeDtypeStruct((IDX_ROWS, edges), jnp.int32),
            jax.ShapeDtypeStruct((workers, cap, dim), F32),
        ),
        in_specs=[HBM] * 7,
        out_specs=(VMEM, VMEM),
        scratch_shapes=[
            pltpu.SMEM(serve_t.shape, jnp.int32),
            pltpu.SMEM(edge_count.shape, jnp.int32),
            pltpu.VMEM(ent_t.shape, BF16),
            pltpu.VMEM(edge_src.shape, jnp.int32),
            pltpu.VMEM(edge_rel.shape, jnp.int32),
            pltpu.VMEM(edge_dst.shape, jnp.int32),
            pltpu.VMEM(neg_ids.shape, jnp.int32),
            pltpu.VMEM((slots, rows), F32),
            pltpu.SemaphoreType.DMA((7,)),
        ],
        compiler_params=params(60),
        name="prep",
    )(serve_t, edge_count, ent_t, edge_src, edge_rel, edge_dst, neg_ids)

    held = [idx]
    for hop in range(1, replicas):
        held.append(lax.ppermute(idx, "rep", turned(replicas, hop)))
    received = lax.all_to_all(served, "dom", 0, 0, tiled=True)

    total = min(replicas * edges, up(LIVE_EDGES, edges))
    packed, query, lhs_rows, rel_rows = pl.pallas_call(
        functools.partial(
            gather_kernel, (replicas, groups, nrel, pad_rel, narrow, window, edges)
        ),
        out_shape=(
            jax.ShapeDtypeStruct((IDX_ROWS, total), jnp.int32),
            jax.ShapeDtypeStruct((dim, total), BF16),
            jax.ShapeDtypeStruct((window, total), F32),
            jax.ShapeDtypeStruct((window, total), F32),
        ),
        in_specs=[VMEM] * (replicas + 2),
        out_specs=[VMEM] * 4,
        scratch_shapes=[
            pltpu.VMEM((2 * dim, pad_rel), BF16),
        ],
        compiler_params=params(),
        cost_estimate=cost(2 * total * dim * (2 * pad_rel + rows), 8 * total * dim),
        name="gather",
    )(*held, ent_t, rel_t)

    cfg = (
        direct, workers, replicas, cap, groups, width, pad_rel, block, narrow, window,
        tuple(offsets),
    )
    lanes = max(up(block, LANES), up(narrow, LANES))
    pieces = jax.ShapeDtypeStruct((2 * window, total), BF16)
    outs = [2] * (SOURCES - 1) if direct else [workers]
    sizes = [pieces] if direct else []
    sizes += [jax.ShapeDtypeStruct((n, height, lanes), jnp.int16) for n in outs]
    mixed = [pltpu.VMEM((height, lanes), jnp.int32)]
    x_parts, tables, *sent = pl.pallas_call(
        functools.partial(main_kernel, cfg),
        out_shape=[pieces, jax.ShapeDtypeStruct((slots, lanes), jnp.int32)] + sizes,
        in_specs=[VMEM] * (replicas + 5),
        out_specs=[VMEM] * (2 + len(sizes)),
        scratch_shapes=[
            pltpu.VMEM((slots, dim), F32),
            pltpu.VMEM((dim, slots), F32),
            pltpu.VMEM((dim, total), F32),
            pltpu.VMEM((lanes, slots), F32),
        ]
        + mixed,
        compiler_params=params(),
        name="edges",
    )(*held, packed, query, lhs_rows, rel_rows, received)

    def swap(array, dom_bits=0, rep_bits=0):
        pairs = []
        for o in range(workers):
            for r in range(replicas):
                pairs.append((o * replicas + r, (o ^ dom_bits) * replicas + (r ^ rep_bits)))
        return lax.ppermute(array, ("dom", "rep"), pairs)

    stack = jax.ShapeDtypeStruct((outs[0], height, lanes), jnp.int16)
    if direct:
        y_parts, *sent = sent
        got = {n: swap(sent[n - 1], n) for n in reversed(range(1, SOURCES))}
        kept = pl.pallas_call(
            functools.partial(own_kernel, block, narrow, cap, offsets),
            out_shape=stack,
            in_specs=[VMEM] * 3,
            out_specs=VMEM,
            scratch_shapes=mixed,
            compiler_params=params(),
            cost_estimate=cost(4 * window * total * 2 * block, 10**6),
            name="own",
        )(packed, y_parts, tables)
        summed = pl.pallas_call(
            functools.partial(quad_kernel, narrow, cap),
            out_shape=stack,
            in_specs=[VMEM] * SOURCES,
            out_specs=VMEM,
            scratch_shapes=mixed,
            compiler_params=params(),
            name="quad",
        )(kept, *[got[n] for n in range(1, SOURCES)])
        near = swap(summed, 2)
        recv = [summed, swap(summed, 4)]
        parts = recv + [near, swap(summed, 6)]
        stack = 4
    else:
        recv = [lax.all_to_all(sent[0], "dom", 0, 0, tiled=True)]
        parts = [recv[0][w : w + 1] for w in range(workers)]
        stack = 1
    scale = 1.0 / (edges * workers * replicas)
    chunk = pl.pallas_call(
        functools.partial(sum_kernel, scale, narrow, cap, block, 2 if direct else workers),
        out_shape=jax.ShapeDtypeStruct((stack, up(narrow + 1, 8), lanes), jnp.int16),
        in_specs=[VMEM] * len(parts),
        out_specs=VMEM,
        scratch_shapes=[pltpu.VMEM((up(narrow + 1, 8), lanes), jnp.int32)],
        compiler_params=params(),
        name="total",
    )(*parts)

    if direct:
        base = jnp.concatenate(
            [chunk, swap(chunk, 1), swap(chunk, 0, 2), swap(chunk, 1, 2)], axis=0
        )
    entity_grad = pl.pallas_call(
        functools.partial(entity_kernel, direct, narrow, offsets),
        out_shape=jax.ShapeDtypeStruct((narrow, rows), F32),
        in_specs=[SMEM] + [VMEM] * (2 + len(recv)),
        out_specs=VMEM,
        scratch_shapes=[pltpu.VMEM((slots, lanes), F32), pltpu.VMEM((slots, rows), F32)],
        compiler_params=params(),
        cost_estimate=cost(10**9, 10**6),
        name="entity",
    )(serve_t, packed, x_parts, *recv)

    if direct:
        base, entity_grad = lax.optimization_barrier((base, entity_grad))
        swapped = lax.ppermute(base, "rep", [(i, i ^ 1) for i in range(replicas)])
        sizes = (workers, narrow, block, nrel)
        result = jax.ShapeDtypeStruct((dim, nrel), F32)
        bands = pltpu.VMEM((narrow // 8 * 16, nrel), F32)
        own_half = pl.pallas_call(
            functools.partial(spread_own_kernel, sizes),
            out_shape=result,
            in_specs=[VMEM],
            out_specs=HBM,
            scratch_shapes=[bands, pltpu.SemaphoreType.DMA((2,))],
            compiler_params=params(),
            cost_estimate=cost(10**6, 4 * dim * nrel),
            name="spread_own",
        )(base)
        relation_t = pl.pallas_call(
            functools.partial(spread_rest_kernel, sizes),
            out_shape=result,
            in_specs=[VMEM, VMEM, HBM],
            out_specs=HBM,
            scratch_shapes=[bands, pltpu.VMEM((16, nrel), F32), pltpu.SemaphoreType.DMA((4,))],
            input_output_aliases={2: 0},
            compiler_params=params(),
            name="spread_rest",
        )(base, swapped, own_half)
    else:
        whole = lax.all_gather(chunk[0, :, :block], ("dom", "rep"), axis=0)
        whole = decode(whole[:, :narrow], whole[:, narrow : narrow + 1])
        whole = whole.reshape(workers, replicas, narrow, block).transpose(1, 2, 0, 3)
        relation_t = whole.reshape(dim, workers * block)[:, :nrel]
    return (entity_grad.T, relation_t.T)


def solution(mesh):
    placed = (
        P("dom", None),
        P(),
        P("dom", None, None),
        P("dom", "rep", None),
        P("dom", "rep", None),
        P("dom", "rep", None),
        P("dom", "rep", None, None),
        P("dom", "rep"),
    )
    return jax.shard_map(
        shards, mesh=mesh, in_specs=placed, out_specs=(P("dom", "rep"), P()), check_vma=False
    )
```

```python
import functools

import jax
import jax.numpy as jnp
from jax import lax
from jax.experimental import pallas as pl
from jax.experimental.pallas import tpu as pltpu
from jax.sharding import PartitionSpec as P

F32 = jnp.float32
BF16 = jnp.bfloat16
IDX_ROWS = 8
LANES = 128
SOURCES = 4
LIVE_EDGES = 1536
VMEM = pl.BlockSpec(memory_space=pltpu.VMEM)
SMEM = pl.BlockSpec(memory_space=pltpu.SMEM)
HBM = pl.BlockSpec(memory_space=pltpu.HBM)


def params(mib=32):
    return pltpu.CompilerParams(vmem_limit_bytes=mib * 1024 * 1024)


def cost(flops, moved):
    return pl.CostEstimate(flops=flops, bytes_accessed=moved, transcendentals=0)


def up(value, step):
    return -(-value // step) * step


def split2(x):
    hi = x.astype(BF16)
    lo = (x - hi.astype(F32)).astype(BF16)
    return hi, lo


def split3(x):
    hi, rest = x.astype(BF16), x
    rest = rest - hi.astype(F32)
    mid = rest.astype(BF16)
    low = (rest - mid.astype(F32)).astype(BF16)
    return hi, mid, low


def dot(a, b):
    return jnp.dot(a, b, preferred_element_type=F32)


def dot_t(a, b):
    return lax.dot_general(a, b, (((1,), (1,)), ((), ())), preferred_element_type=F32)


def ones_where(flag):
    return jnp.where(flag, 1.0, 0.0).astype(BF16)


def exponent(largest):
    safe = jnp.where(largest > 0, largest, 1.0)
    return jnp.clip(jnp.floor(F32(14.9) - jnp.log2(safe)), -120.0, 120.0)


def encode(x, axis):
    k = exponent(jnp.max(jnp.abs(x), axis=axis, keepdims=True))
    return jnp.floor(x * jnp.exp2(k) + 0.5).astype(jnp.int32), k.astype(jnp.int32)


def decode(codes, k):
    return codes.astype(F32) * jnp.exp2(-k.astype(F32))


def iota(shape, axis):
    return lax.broadcasted_iota(jnp.int32, shape, axis)


def shifted_rows(x, offset, narrow, offsets):
    out = x[offsets[0] : offsets[0] + narrow]
    for other in offsets[1:]:
        out = jnp.where(offset == other, x[other : other + narrow], out)
    return out


def window_rows(x, rep, starts, window):
    out = x[starts[0] : starts[0] + window]
    for n, start in enumerate(starts[1:], 1):
        out = jnp.where(rep == n, x[start : start + window], out)
    return out


def my_place():
    return lax.axis_index("dom"), lax.axis_index("rep")


def prep_kernel(serve, count, ent, src, rel, dst, neg, out_idx, out_rows, *refs):
    cap, workers = serve.shape[1], serve.shape[2]
    rows = ent.shape[1]
    groups, width = neg.shape[2], neg.shape[3]
    onehot, sems = refs[-2:]
    moves = [
        pltpu.make_async_copy(a, b, sems.at[n])
        for n, (a, b) in enumerate(zip((serve, count, ent, src, rel, dst, neg), refs))
    ]
    for move in moves:
        move.start()
    for move in moves:
        move.wait()
    serve_s, count_s, ent_v, src_v, rel_v, dst_v, neg_v = refs[:7]
    out_idx[...] = jnp.full(out_idx.shape, count_s[0, 0], jnp.int32)
    out_idx[0:1, :] = src_v[0]
    out_idx[1:2, :] = rel_v[0]
    out_idx[2:3, :] = dst_v[0]
    for g in range(groups):
        out_idx[3 + g : 4 + g, :width] = neg_v[0, 0, g : g + 1, :]
    lane = iota((1, rows), 1)
    for k in range(workers * cap):
        picked = serve_s[0, k % cap, k // cap]
        onehot[k : k + 1, :] = jnp.where(lane == picked, 1.0, 0.0).astype(F32)
    picked_rows = dot_t(onehot[...].astype(BF16), ent_v[...])
    for w in range(workers):
        out_rows[w] = picked_rows[w * cap : (w + 1) * cap]


def packed_edges(idx_refs, groups, out_idx):
    edges, span = idx_refs[0].shape[1], out_idx.shape[1]
    wide = max(span, edges)
    place = iota((IDX_ROWS, wide), 1)
    row = iota((IDX_ROWS, edges), 0)
    block = iota((IDX_ROWS, edges), 1) // (edges // groups)
    packed = jnp.where(iota((IDX_ROWS, wide), 0) < 3, -1, 0)
    first = 0
    for i, ref in enumerate(idx_refs):
        count = jnp.max(ref[IDX_ROWS - 1 : IDX_ROWS, :].astype(F32)).astype(jnp.int32)
        rows = jnp.where(row < 3, ref[...], jnp.where(row == 3, block + i * groups, 1))
        if wide > edges:
            rows = jnp.concatenate(
                [rows, jnp.zeros((IDX_ROWS, wide - edges), jnp.int32)], axis=1
            )
        moved = pltpu.roll(rows, first, 1)
        packed = jnp.where((place >= first) & (place < first + count), moved, packed)
        first = first + count
    out_idx[...] = packed[:, :span]


def gather_kernel(cfg, *refs):
    place = my_place()
    replicas, groups, nrel, pad_rel, narrow, window, step = cfg
    idx_refs, refs = refs[:replicas], refs[replicas:]
    ent, relation, out_idx, out_query, out_lhs, out_rel, rel_parts = refs
    dim, rows = ent.shape
    starts = [narrow * r // 8 * 8 for r in range(replicas)]
    packed_edges(idx_refs, groups, out_idx)
    hi, lo = split2(relation[...])
    if pad_rel > nrel:
        edge = nrel // LANES * LANES
        rel_parts[:, edge:] = jnp.zeros((2 * dim, pad_rel - edge), BF16)
    rel_parts[:dim, :nrel] = hi
    rel_parts[dim:, :nrel] = lo
    for start in range(0, out_idx.shape[1], step):
        span = slice(start, start + step)
        src_l, rel_l = out_idx[0:1, span], out_idx[1:2, span]
        lhs = dot(ent[...], ones_where(iota((rows, step), 0) == src_l))
        both = dot(rel_parts[...], ones_where(iota((pad_rel, step), 0) == rel_l))
        rel_rows = both[:dim] + both[dim:]
        out_query[:, span] = (lhs * rel_rows).astype(BF16)
        out_lhs[:, span] = window_rows(lhs, place[1], starts, window)
        out_rel[:, span] = window_rows(rel_rows, place[1], starts, window)


def main_kernel(cfg, *refs):
    place = my_place()
    (direct, workers, replicas, cap, groups, width, pad_rel, block, narrow, window, offsets) = cfg
    idx_refs, refs = refs[:replicas], refs[replicas:]
    (packed, query_v, lhs_v, rel_v, received), refs = refs[:5], refs[5:]
    out_x, tables, refs = refs[0], refs[1], refs[2:]
    out_y, refs = (refs[0], refs[1:]) if direct else (None, refs)
    outs, (table_f, table_t, query_s, wide_t, mixed) = refs[:-5], refs[-5:]
    edges = idx_refs[0].shape[1]
    dim, total = query_v.shape
    slots = workers * cap
    rep = place[1]
    per = edges // groups
    base = pl.multiple_of((rep * narrow) // 8 * 8, 8)
    offset = rep * narrow - base

    for w in range(workers):
        table_f[w * cap : (w + 1) * cap, :] = received[w]
    table_t[...] = jnp.transpose(table_f[...])
    table = table_f[...].astype(BF16)
    own_t = table_t[pl.ds(base, window), :].astype(BF16)
    own_t = jnp.concatenate([own_t] * 3, axis=1)

    query = query_v[...]
    scores = dot(table, query)
    query_s[...] = query.astype(F32)
    lanes = packed[...]
    cols = jnp.transpose(lanes)
    times = jnp.zeros((slots, total), F32)
    for i in range(replicas):
        shard = idx_refs[i][...]
        position = iota((slots, edges), 1)
        seen = (iota((slots, edges), 0) == shard[2:3]) & (position < shard[IDX_ROWS - 1 : IDX_ROWS])
        seen = jnp.where(seen, 1.0, 0.0).astype(F32)
        for g in range(groups):
            neg = iota((slots, width), 0) == shard[3 + g : 4 + g, :width]
            often = jnp.sum(jnp.where(neg, 1.0, 0.0).astype(F32), axis=1, keepdims=True)
            often = often + jnp.sum(seen[:, g * per : (g + 1) * per], axis=1, keepdims=True)
            times = jnp.where(lanes[3:4] == i * groups + g, often, times)
    live = lanes[4:5].astype(F32)
    own = jnp.where(iota((slots, total), 0) == lanes[2:3], 1.0, 0.0).astype(F32)
    scores = jnp.where(times > 0, scores, F32(-1e30))
    expo = jnp.exp(scores - jnp.max(scores, axis=0, keepdims=True))
    norm = jnp.sum(expo * times, axis=0, keepdims=True)
    probs = expo / jnp.where(live > 0, norm, 1.0)
    other = probs.astype(BF16).astype(F32)
    itself = (probs - 1.0).astype(BF16).astype(F32)
    grads = ((times - own) * other + own * itself) * live
    stack = jnp.concatenate(split3(grads), axis=0)
    stack_t = jnp.concatenate(split3(jnp.transpose(grads)), axis=1)

    dquery = dot(own_t, stack)
    acc_tab = dot(query_s[pl.ds(base, window), :].astype(BF16), stack_t)
    wide_t[...] = jnp.zeros(wide_t.shape, F32)
    wide_t[:narrow] = shifted_rows(
        acc_tab[:, :slots] + acc_tab[:, slots : 2 * slots] + acc_tab[:, 2 * slots :],
        offset,
        narrow,
        offsets,
    )
    table_codes, table_powers = encode(jnp.transpose(wide_t[...]), 1)
    spare = iota(table_codes.shape, 1) >= narrow
    tables[...] = jnp.where(spare, table_powers, table_codes)
    y = jnp.concatenate(split2(dquery * lhs_v[...]), axis=0)
    out_x[...] = jnp.concatenate(split2(dquery * rel_v[...]), axis=0)
    if direct:
        out_y[...] = y
        targets = [
            (outs[h - 1].at[top], top * 4 + flipped(place[0] % 4, h))
            for h in range(1, SOURCES)
            for top in range(2)
        ]
    else:
        targets = [(outs[0].at[o], o) for o in range(workers)]
    write_blocks(y, cols, targets, tables, mixed, rep, block, narrow, cap, offsets)


def write_blocks(y, cols, targets, tables, mixed, rep, block, narrow, cap, offsets):
    window = y.shape[0] // 2
    ids = jnp.concatenate([iota((1, block), 1) + o * block for _, o in targets], axis=1)
    both = dot(y, ones_where(cols[:, 1:2] == ids))
    part = shifted_rows(both[:window] + both[window:], (rep * narrow) % 8, narrow, offsets)
    codes, powers = encode(part, 0)
    power_row = narrow + SOURCES * cap
    mixed[...] = jnp.zeros(mixed.shape, jnp.int32)
    for n, (ref, o) in enumerate(targets):
        span = slice(n * block, (n + 1) * block)
        mixed[:narrow, :block] = codes[:, span]
        for c in range(cap):
            mixed[narrow + c : narrow + c + 1, :] = tables[pl.ds(o * cap + c, 1), :]
        mixed[power_row : power_row + 1, :block] = powers[:, span]
        ref[...] = mixed[...].astype(jnp.int16)


def own_kernel(block, narrow, cap, offsets, packed, y, tables, out, mixed):
    place = my_place()
    cols = jnp.transpose(packed[...])
    targets = [(out.at[top], top * 4 + place[0] % 4) for top in range(2)]
    write_blocks(y[...], cols, targets, tables, mixed, place[1], block, narrow, cap, offsets)


def flipped(index, mask):
    out, bit = index * 0, 1
    while bit < 4:
        out = out + bit * lax.rem(index // bit + (mask // bit) % 2, 2)
        bit *= 2
    return out


def quad_kernel(narrow, cap, *refs):
    parts, out, mixed = refs[:-2], refs[-2], refs[-1]
    power = slice(narrow + SOURCES * cap, narrow + SOURCES * cap + 1)
    mixed[...] = jnp.zeros(mixed.shape, jnp.int32)
    for top in range(out.shape[0]):
        total = jnp.zeros((narrow, out.shape[2]), F32)
        for n, part in enumerate(parts):
            both = part[top].astype(jnp.int32)
            total += decode(both[:narrow], both[power])
            row = narrow + n * cap
            mixed[row : row + cap, :] = both[narrow : narrow + cap]
        mixed[:narrow, :], mixed[power, :] = encode(total, 0)
        out[top] = mixed[...].astype(jnp.int16)


def sum_kernel(scale, narrow, cap, block, terms, *refs):
    place = my_place()
    parts, out, mixed = refs[:-2], refs[-2], refs[-1]
    depth = parts[0].shape[0]
    lowered = mixed.shape[0] - narrow if terms == 2 else 0
    power = slice(narrow + SOURCES * cap, narrow + SOURCES * cap + 1)
    mixed[...] = jnp.zeros(mixed.shape, jnp.int32)
    for first in range(0, len(parts), terms):
        for top in range(depth):
            total = jnp.zeros((narrow, block), F32)
            for part in parts[first : first + terms]:
                both = part[top].astype(jnp.int32)
                total += decode(both[:narrow, :block], both[power, :block])
            codes, powers = encode(total * F32(scale), 0)
            if lowered:
                rest = jnp.broadcast_to(powers, (lowered, block))
                mixed[:, :block] = jnp.where(
                    lax.rem(place[1], 2) == 0,
                    jnp.concatenate([codes, rest], axis=0),
                    jnp.concatenate([rest, codes], axis=0),
                )
            else:
                mixed[:narrow, :block], mixed[narrow : narrow + 1, :block] = codes, powers
            out[first // terms * depth + top] = mixed[...].astype(jnp.int16)


def entity_kernel(direct, narrow, offsets, serve, packed, x, *refs):
    place = my_place()
    recv, out, terms, onehot = refs[:-3], refs[-3], refs[-2], refs[-1]
    cap, workers = serve.shape[1], serve.shape[2]
    rows = out.shape[1]
    lane = iota((1, rows), 1)
    for h in range(workers):
        if direct:
            turn, hop = h % SOURCES, h // SOURCES
            mine = place[0] // 4
            both = recv[hop][mine].astype(jnp.int32)
            worker = lax.rem(mine + hop, 2) * 4 + flipped(place[0] % 4, turn)
        else:
            turn, both, worker = 0, recv[0][h].astype(jnp.int32), h
        row = narrow + turn * cap
        both = both[row : row + cap]
        terms[h * cap : (h + 1) * cap, :] = jnp.where(
            iota(both.shape, 1) < narrow, decode(both, both[:, narrow : narrow + 1]), 0.0
        )
        for c in range(cap):
            spot = jnp.where(lane == serve[0, c, worker], 1.0, 0.0).astype(F32)
            onehot[h * cap + c : h * cap + c + 1, :] = spot
    spots = onehot[...].astype(BF16)
    parts = jnp.concatenate(split3(jnp.transpose(terms[...])), axis=1)
    added = dot(parts, jnp.concatenate([spots] * 3, axis=0))
    sources = jnp.transpose(packed[...])[:, 0:1]
    both = dot(x[...], ones_where(iota((x.shape[1], rows), 1) == sources))
    window = x.shape[0] // 2
    both = both[:window] + both[window:]
    out[...] = shifted_rows(both, (place[1] * narrow) % 8, narrow, offsets) + added[:narrow]


def found(pieces, place, o, over_x):
    dom = place[0]
    over_low = lax.rem(dom // 2 + o // 2, 2)
    over_y = lax.rem(dom + o, 2)
    return pieces[(over_y + 2 * over_x) * 4 + over_low * 2 + o // 4].astype(jnp.int32)


def spread_core(pieces, core, place, sizes, bands, out, sems):
    workers, narrow, block, nrel = sizes
    length = narrow // 8 * 8
    moves = []
    for x in range(2):
        over_x = lax.rem(place[1] // 2 + x, 2)
        for o in range(workers):
            both = found(pieces, place, o, over_x)
            codes = jnp.where(core == 0, both[:length], both[8:])
            value = decode(codes, jnp.where(core == 0, both[narrow : narrow + 1], both[:1]))
            end = min((o + 1) * block, nrel)
            bands[x * length : (x + 1) * length, o * block : end] = value[:, : end - o * block]
        first = pl.multiple_of(2 * narrow * x + (length + 8) * core, 8)
        move = pltpu.make_async_copy(
            bands.at[x * length : (x + 1) * length], out.at[pl.ds(first, length)], sems.at[x]
        )
        move.start()
        moves.append(move)
    return moves


def spread_own_kernel(sizes, mine, out, bands, sems):
    place = my_place()
    for move in spread_core(mine, lax.rem(place[1], 2), place, sizes, bands, out, sems):
        move.wait()


def spread_rest_kernel(sizes, mine, other, partial, out, bands, shared, sems):
    place = my_place()
    workers, narrow, block, nrel = sizes
    core = lax.rem(place[1], 2)
    length = narrow // 8 * 8
    moves = spread_core(other, 1 - core, place, sizes, bands, out, sems)
    for x in range(2):
        over_x = lax.rem(place[1] // 2 + x, 2)
        for o in range(workers):
            ours, theirs = found(mine, place, o, over_x), found(other, place, o, over_x)
            low = jnp.where(core == 0, ours[length:], theirs[length:])
            high = jnp.where(core == 0, theirs[:8], ours[:8])
            upper = iota(low.shape, 0) < narrow - length
            split = narrow - length
            value = jnp.where(
                upper, decode(low, low[split : split + 1]), decode(high, high[:1])
            )
            end = min((o + 1) * block, nrel)
            shared[x * 8 : (x + 1) * 8, o * block : end] = value[:, : end - o * block]
        first = 2 * narrow * x + length
        move = pltpu.make_async_copy(
            shared.at[x * 8 : (x + 1) * 8], out.at[first : first + 8], sems.at[2 + x]
        )
        move.start()
        moves.append(move)
    for move in moves:
        move.wait()


def turned(size, hop):
    return [(i, (i + hop) % size) for i in range(size)]


def shards(entities, relation, serve_ids, edge_src, edge_rel, edge_dst, neg_ids, edge_count):
    workers = lax.axis_size("dom")
    replicas = lax.axis_size("rep")
    rows, dim = entities.shape
    nrel = relation.shape[0]
    cap = serve_ids.shape[2]
    edges = edge_src.shape[2]
    groups, width = neg_ids.shape[2], neg_ids.shape[3]
    slots = workers * cap
    narrow = dim // replicas
    direct = workers == 8 and replicas == 4 and narrow % 8 == 4
    block = up(-(-nrel // workers), LANES if direct else 8)
    pad_rel = up(max(nrel, workers * block), LANES)
    offsets = sorted({(narrow * r) % 8 for r in range(replicas)})
    window = up(narrow + offsets[-1], 8)
    height = up(narrow + SOURCES * cap + 1, 16)
    ent_t, rel_t = entities.T, relation.T
    serve_t = jnp.transpose(serve_ids, (0, 2, 1))

    idx, served = pl.pallas_call(
        prep_kernel,
        out_shape=(
            jax.ShapeDtypeStruct((IDX_ROWS, edges), jnp.int32),
            jax.ShapeDtypeStruct((workers, cap, dim), F32),
        ),
        in_specs=[HBM] * 7,
        out_specs=(VMEM, VMEM),
        scratch_shapes=[
            pltpu.SMEM(serve_t.shape, jnp.int32),
            pltpu.SMEM(edge_count.shape, jnp.int32),
            pltpu.VMEM(ent_t.shape, BF16),
            pltpu.VMEM(edge_src.shape, jnp.int32),
            pltpu.VMEM(edge_rel.shape, jnp.int32),
            pltpu.VMEM(edge_dst.shape, jnp.int32),
            pltpu.VMEM(neg_ids.shape, jnp.int32),
            pltpu.VMEM((slots, rows), F32),
            pltpu.SemaphoreType.DMA((7,)),
        ],
        compiler_params=params(60),
        name="prep",
    )(serve_t, edge_count, ent_t, edge_src, edge_rel, edge_dst, neg_ids)

    held = [idx]
    for hop in range(1, replicas):
        held.append(lax.ppermute(idx, "rep", turned(replicas, hop)))
    received = lax.all_to_all(served, "dom", 0, 0, tiled=True)

    total = min(replicas * edges, up(LIVE_EDGES, edges))
    packed, query, lhs_rows, rel_rows = pl.pallas_call(
        functools.partial(
            gather_kernel, (replicas, groups, nrel, pad_rel, narrow, window, edges)
        ),
        out_shape=(
            jax.ShapeDtypeStruct((IDX_ROWS, total), jnp.int32),
            jax.ShapeDtypeStruct((dim, total), BF16),
            jax.ShapeDtypeStruct((window, total), F32),
            jax.ShapeDtypeStruct((window, total), F32),
        ),
        in_specs=[VMEM] * (replicas + 2),
        out_specs=[VMEM] * 4,
        scratch_shapes=[
            pltpu.VMEM((2 * dim, pad_rel), BF16),
        ],
        compiler_params=params(),
        cost_estimate=cost(2 * total * dim * (2 * pad_rel + rows), 8 * total * dim),
        name="gather",
    )(*held, ent_t, rel_t)

    cfg = (
        direct, workers, replicas, cap, groups, width, pad_rel, block, narrow, window,
        tuple(offsets),
    )
    lanes = max(up(block, LANES), up(narrow, LANES))
    pieces = jax.ShapeDtypeStruct((2 * window, total), BF16)
    outs = [2] * (SOURCES - 1) if direct else [workers]
    sizes = [pieces] if direct else []
    sizes += [jax.ShapeDtypeStruct((n, height, lanes), jnp.int16) for n in outs]
    mixed = [pltpu.VMEM((height, lanes), jnp.int32)]
    x_parts, tables, *sent = pl.pallas_call(
        functools.partial(main_kernel, cfg),
        out_shape=[pieces, jax.ShapeDtypeStruct((slots, lanes), jnp.int32)] + sizes,
        in_specs=[VMEM] * (replicas + 5),
        out_specs=[VMEM] * (2 + len(sizes)),
        scratch_shapes=[
            pltpu.VMEM((slots, dim), F32),
            pltpu.VMEM((dim, slots), F32),
            pltpu.VMEM((dim, total), F32),
            pltpu.VMEM((lanes, slots), F32),
        ]
        + mixed,
        compiler_params=params(),
        name="edges",
    )(*held, packed, query, lhs_rows, rel_rows, received)

    def swap(array, dom_bits=0, rep_bits=0):
        pairs = []
        for o in range(workers):
            for r in range(replicas):
                pairs.append((o * replicas + r, (o ^ dom_bits) * replicas + (r ^ rep_bits)))
        return lax.ppermute(array, ("dom", "rep"), pairs)

    stack = jax.ShapeDtypeStruct((outs[0], height, lanes), jnp.int16)
    if direct:
        y_parts, *sent = sent
        got = {n: swap(sent[n - 1], n) for n in reversed(range(1, SOURCES))}
        kept = pl.pallas_call(
            functools.partial(own_kernel, block, narrow, cap, offsets),
            out_shape=stack,
            in_specs=[VMEM] * 3,
            out_specs=VMEM,
            scratch_shapes=mixed,
            compiler_params=params(),
            cost_estimate=cost(4 * window * total * 2 * block, 10**6),
            name="own",
        )(packed, y_parts, tables)
        summed = pl.pallas_call(
            functools.partial(quad_kernel, narrow, cap),
            out_shape=stack,
            in_specs=[VMEM] * SOURCES,
            out_specs=VMEM,
            scratch_shapes=mixed,
            compiler_params=params(),
            name="quad",
        )(kept, *[got[n] for n in range(1, SOURCES)])
        recv = [summed, swap(summed, 4)]
        parts = recv + [swap(summed, 2), swap(summed, 6)]
        stack = 4
    else:
        recv = [lax.all_to_all(sent[0], "dom", 0, 0, tiled=True)]
        parts = [recv[0][w : w + 1] for w in range(workers)]
        stack = 1
    scale = 1.0 / (edges * workers * replicas)
    chunk = pl.pallas_call(
        functools.partial(sum_kernel, scale, narrow, cap, block, 2 if direct else workers),
        out_shape=jax.ShapeDtypeStruct((stack, up(narrow + 1, 8), lanes), jnp.int16),
        in_specs=[VMEM] * len(parts),
        out_specs=VMEM,
        scratch_shapes=[pltpu.VMEM((up(narrow + 1, 8), lanes), jnp.int32)],
        compiler_params=params(),
        name="total",
    )(*parts)

    if direct:
        sibling = swap(chunk, 0, 1)
        rest = jnp.concatenate([swap(chunk, 1), swap(chunk, 0, 2), swap(chunk, 1, 2)], axis=0)
    entity_grad = pl.pallas_call(
        functools.partial(entity_kernel, direct, narrow, offsets),
        out_shape=jax.ShapeDtypeStruct((narrow, rows), F32),
        in_specs=[SMEM] + [VMEM] * (2 + len(recv)),
        out_specs=VMEM,
        scratch_shapes=[pltpu.VMEM((slots, lanes), F32), pltpu.VMEM((slots, rows), F32)],
        compiler_params=params(),
        cost_estimate=cost(10**9, 10**6),
        name="entity",
    )(serve_t, packed, x_parts, *recv)

    if direct:
        rest, entity_grad = lax.optimization_barrier((rest, entity_grad))
        base = jnp.concatenate([chunk, rest], axis=0)
        swapped = jnp.concatenate([sibling, swap(rest, 0, 1)], axis=0)
        sizes = (workers, narrow, block, nrel)
        result = jax.ShapeDtypeStruct((dim, nrel), F32)
        bands = pltpu.VMEM((narrow // 8 * 16, nrel), F32)
        own_half = pl.pallas_call(
            functools.partial(spread_own_kernel, sizes),
            out_shape=result,
            in_specs=[VMEM],
            out_specs=HBM,
            scratch_shapes=[bands, pltpu.SemaphoreType.DMA((2,))],
            compiler_params=params(),
            cost_estimate=cost(10**6, 4 * dim * nrel),
            name="spread_own",
        )(base)
        relation_t = pl.pallas_call(
            functools.partial(spread_rest_kernel, sizes),
            out_shape=result,
            in_specs=[VMEM, VMEM, HBM],
            out_specs=HBM,
            scratch_shapes=[bands, pltpu.VMEM((16, nrel), F32), pltpu.SemaphoreType.DMA((4,))],
            input_output_aliases={2: 0},
            compiler_params=params(),
            name="spread_rest",
        )(base, swapped, own_half)
    else:
        whole = lax.all_gather(chunk[0, :, :block], ("dom", "rep"), axis=0)
        whole = decode(whole[:, :narrow], whole[:, narrow : narrow + 1])
        whole = whole.reshape(workers, replicas, narrow, block).transpose(1, 2, 0, 3)
        relation_t = whole.reshape(dim, workers * block)[:, :nrel]
    return (entity_grad.T, relation_t.T)


def solution(mesh):
    placed = (
        P("dom", None),
        P(),
        P("dom", None, None),
        P("dom", "rep", None),
        P("dom", "rep", None),
        P("dom", "rep", None),
        P("dom", "rep", None, None),
        P("dom", "rep"),
    )
    return jax.shard_map(
        shards, mesh=mesh, in_specs=placed, out_specs=(P("dom", "rep"), P()), check_vma=False
    )
```

```python
import functools

import jax
import jax.numpy as jnp
from jax import lax
from jax.experimental import pallas as pl
from jax.experimental.pallas import tpu as pltpu
from jax.sharding import PartitionSpec as P

F32 = jnp.float32
BF16 = jnp.bfloat16
IDX_ROWS = 8
LANES = 128
SOURCES = 4
LIVE_EDGES = 1536
VMEM = pl.BlockSpec(memory_space=pltpu.VMEM)
SMEM = pl.BlockSpec(memory_space=pltpu.SMEM)
HBM = pl.BlockSpec(memory_space=pltpu.HBM)


def params(mib=32):
    return pltpu.CompilerParams(vmem_limit_bytes=mib * 1024 * 1024)


def cost(flops, moved):
    return pl.CostEstimate(flops=flops, bytes_accessed=moved, transcendentals=0)


def up(value, step):
    return -(-value // step) * step


def split2(x):
    hi = x.astype(BF16)
    lo = (x - hi.astype(F32)).astype(BF16)
    return hi, lo


def split3(x):
    hi, rest = x.astype(BF16), x
    rest = rest - hi.astype(F32)
    mid = rest.astype(BF16)
    low = (rest - mid.astype(F32)).astype(BF16)
    return hi, mid, low


def dot(a, b):
    return jnp.dot(a, b, preferred_element_type=F32)


def dot_t(a, b):
    return lax.dot_general(a, b, (((1,), (1,)), ((), ())), preferred_element_type=F32)


def ones_where(flag):
    return jnp.where(flag, 1.0, 0.0).astype(BF16)


def exponent(largest):
    safe = jnp.where(largest > 0, largest, 1.0)
    return jnp.clip(jnp.floor(F32(14.9) - jnp.log2(safe)), -120.0, 120.0)


def encode(x, axis):
    k = exponent(jnp.max(jnp.abs(x), axis=axis, keepdims=True))
    return jnp.floor(x * jnp.exp2(k) + 0.5).astype(jnp.int32), k.astype(jnp.int32)


def decode(codes, k):
    return codes.astype(F32) * jnp.exp2(-k.astype(F32))


def iota(shape, axis):
    return lax.broadcasted_iota(jnp.int32, shape, axis)


def shifted_rows(x, offset, narrow, offsets):
    out = x[offsets[0] : offsets[0] + narrow]
    for other in offsets[1:]:
        out = jnp.where(offset == other, x[other : other + narrow], out)
    return out


def window_rows(x, rep, starts, window):
    out = x[starts[0] : starts[0] + window]
    for n, start in enumerate(starts[1:], 1):
        out = jnp.where(rep == n, x[start : start + window], out)
    return out


def my_place():
    return lax.axis_index("dom"), lax.axis_index("rep")


def prep_kernel(serve, count, ent, src, rel, dst, neg, out_idx, out_rows, *refs):
    cap, workers = serve.shape[1], serve.shape[2]
    rows = ent.shape[1]
    groups, width = neg.shape[2], neg.shape[3]
    onehot, sems = refs[-2:]
    moves = [
        pltpu.make_async_copy(a, b, sems.at[n])
        for n, (a, b) in enumerate(zip((serve, count, ent, src, rel, dst, neg), refs))
    ]
    for move in moves:
        move.start()
    for move in moves:
        move.wait()
    serve_s, count_s, ent_v, src_v, rel_v, dst_v, neg_v = refs[:7]
    out_idx[...] = jnp.full(out_idx.shape, count_s[0, 0], jnp.int32)
    out_idx[0:1, :] = src_v[0]
    out_idx[1:2, :] = rel_v[0]
    out_idx[2:3, :] = dst_v[0]
    for g in range(groups):
        out_idx[3 + g : 4 + g, :width] = neg_v[0, 0, g : g + 1, :]
    lane = iota((1, rows), 1)
    for k in range(workers * cap):
        picked = serve_s[0, k % cap, k // cap]
        onehot[k : k + 1, :] = jnp.where(lane == picked, 1.0, 0.0).astype(F32)
    picked_rows = dot_t(onehot[...].astype(BF16), ent_v[...])
    for w in range(workers):
        out_rows[w] = picked_rows[w * cap : (w + 1) * cap]


def packed_edges(idx_refs, groups, out_idx):
    edges, span = idx_refs[0].shape[1], out_idx.shape[1]
    wide = max(span, edges)
    place = iota((IDX_ROWS, wide), 1)
    row = iota((IDX_ROWS, edges), 0)
    block = iota((IDX_ROWS, edges), 1) // (edges // groups)
    packed = jnp.where(iota((IDX_ROWS, wide), 0) < 3, -1, 0)
    first = 0
    for i, ref in enumerate(idx_refs):
        count = jnp.max(ref[IDX_ROWS - 1 : IDX_ROWS, :].astype(F32)).astype(jnp.int32)
        rows = jnp.where(row < 3, ref[...], jnp.where(row == 3, block + i * groups, 1))
        if wide > edges:
            rows = jnp.concatenate(
                [rows, jnp.zeros((IDX_ROWS, wide - edges), jnp.int32)], axis=1
            )
        moved = pltpu.roll(rows, first, 1)
        packed = jnp.where((place >= first) & (place < first + count), moved, packed)
        first = first + count
    out_idx[...] = packed[:, :span]


def gather_kernel(cfg, *refs):
    place = my_place()
    replicas, groups, nrel, pad_rel, narrow, window, step = cfg
    idx_refs, refs = refs[:replicas], refs[replicas:]
    ent, relation, out_idx, out_query, out_lhs, out_rel, rel_parts = refs
    dim, rows = ent.shape
    starts = [narrow * r // 8 * 8 for r in range(replicas)]
    packed_edges(idx_refs, groups, out_idx)
    hi, lo = split2(relation[...])
    if pad_rel > nrel:
        edge = nrel // LANES * LANES
        rel_parts[:, edge:] = jnp.zeros((2 * dim, pad_rel - edge), BF16)
    rel_parts[:dim, :nrel] = hi
    rel_parts[dim:, :nrel] = lo
    for start in range(0, out_idx.shape[1], step):
        span = slice(start, start + step)
        src_l, rel_l = out_idx[0:1, span], out_idx[1:2, span]
        lhs = dot(ent[...], ones_where(iota((rows, step), 0) == src_l))
        both = dot(rel_parts[...], ones_where(iota((pad_rel, step), 0) == rel_l))
        rel_rows = both[:dim] + both[dim:]
        out_query[:, span] = (lhs * rel_rows).astype(BF16)
        out_lhs[:, span] = window_rows(lhs, place[1], starts, window)
        out_rel[:, span] = window_rows(rel_rows, place[1], starts, window)


def main_kernel(cfg, *refs):
    place = my_place()
    (direct, workers, replicas, cap, groups, width, pad_rel, block, narrow, window, offsets) = cfg
    idx_refs, refs = refs[:replicas], refs[replicas:]
    (packed, query_v, lhs_v, rel_v, received), refs = refs[:5], refs[5:]
    out_x, tables, refs = refs[0], refs[1], refs[2:]
    out_y, refs = (refs[0], refs[1:]) if direct else (None, refs)
    outs, (table_f, table_t, query_s, wide_t, mixed) = refs[:-5], refs[-5:]
    edges = idx_refs[0].shape[1]
    dim, total = query_v.shape
    slots = workers * cap
    rep = place[1]
    per = edges // groups
    base = pl.multiple_of((rep * narrow) // 8 * 8, 8)
    offset = rep * narrow - base

    for w in range(workers):
        table_f[w * cap : (w + 1) * cap, :] = received[w]
    table_t[...] = jnp.transpose(table_f[...])
    table = table_f[...].astype(BF16)
    own_t = table_t[pl.ds(base, window), :].astype(BF16)
    own_t = jnp.concatenate([own_t] * 3, axis=1)

    query = query_v[...]
    scores = dot(table, query)
    query_s[...] = query.astype(F32)
    lanes = packed[...]
    cols = jnp.transpose(lanes)
    times = jnp.zeros((slots, total), F32)
    for i in range(replicas):
        shard = idx_refs[i][...]
        position = iota((slots, edges), 1)
        seen = (iota((slots, edges), 0) == shard[2:3]) & (position < shard[IDX_ROWS - 1 : IDX_ROWS])
        seen = jnp.where(seen, 1.0, 0.0).astype(F32)
        for g in range(groups):
            neg = iota((slots, width), 0) == shard[3 + g : 4 + g, :width]
            often = jnp.sum(jnp.where(neg, 1.0, 0.0).astype(F32), axis=1, keepdims=True)
            often = often + jnp.sum(seen[:, g * per : (g + 1) * per], axis=1, keepdims=True)
            times = jnp.where(lanes[3:4] == i * groups + g, often, times)
    live = lanes[4:5].astype(F32)
    own = jnp.where(iota((slots, total), 0) == lanes[2:3], 1.0, 0.0).astype(F32)
    scores = jnp.where(times > 0, scores, F32(-1e30))
    expo = jnp.exp(scores - jnp.max(scores, axis=0, keepdims=True))
    norm = jnp.sum(expo * times, axis=0, keepdims=True)
    probs = expo / jnp.where(live > 0, norm, 1.0)
    other = probs.astype(BF16).astype(F32)
    itself = (probs - 1.0).astype(BF16).astype(F32)
    grads = ((times - own) * other + own * itself) * live
    stack = jnp.concatenate(split3(grads), axis=0)
    stack_t = jnp.concatenate(split3(jnp.transpose(grads)), axis=1)

    dquery = dot(own_t, stack)
    acc_tab = dot(query_s[pl.ds(base, window), :].astype(BF16), stack_t)
    wide_t[...] = jnp.zeros(wide_t.shape, F32)
    wide_t[:narrow] = shifted_rows(
        acc_tab[:, :slots] + acc_tab[:, slots : 2 * slots] + acc_tab[:, 2 * slots :],
        offset,
        narrow,
        offsets,
    )
    table_codes, table_powers = encode(jnp.transpose(wide_t[...]), 1)
    spare = iota(table_codes.shape, 1) >= narrow
    tables[...] = jnp.where(spare, table_powers, table_codes)
    y = jnp.concatenate(split2(dquery * lhs_v[...]), axis=0)
    out_x[...] = jnp.concatenate(split2(dquery * rel_v[...]), axis=0)
    if direct:
        out_y[...] = y
        targets = [
            (outs[h - 1].at[top], top * 4 + flipped(place[0] % 4, h))
            for h in range(1, SOURCES)
            for top in range(2)
        ]
    else:
        targets = [(outs[0].at[o], o) for o in range(workers)]
    write_blocks(y, cols, targets, tables, mixed, rep, block, narrow, cap, offsets)


def write_blocks(y, cols, targets, tables, mixed, rep, block, narrow, cap, offsets):
    window = y.shape[0] // 2
    ids = jnp.concatenate([iota((1, block), 1) + o * block for _, o in targets], axis=1)
    both = dot(y, ones_where(cols[:, 1:2] == ids))
    part = shifted_rows(both[:window] + both[window:], (rep * narrow) % 8, narrow, offsets)
    codes, powers = encode(part, 0)
    power_row = narrow + SOURCES * cap
    mixed[...] = jnp.zeros(mixed.shape, jnp.int32)
    for n, (ref, o) in enumerate(targets):
        span = slice(n * block, (n + 1) * block)
        mixed[:narrow, :block] = codes[:, span]
        for c in range(cap):
            mixed[narrow + c : narrow + c + 1, :] = tables[pl.ds(o * cap + c, 1), :]
        mixed[power_row : power_row + 1, :block] = powers[:, span]
        ref[...] = mixed[...].astype(jnp.int16)


def own_kernel(block, narrow, cap, offsets, packed, y, tables, out, mixed):
    place = my_place()
    cols = jnp.transpose(packed[...])
    targets = [(out.at[top], top * 4 + place[0] % 4) for top in range(2)]
    write_blocks(y[...], cols, targets, tables, mixed, place[1], block, narrow, cap, offsets)


def flipped(index, mask):
    out, bit = index * 0, 1
    while bit < 4:
        out = out + bit * lax.rem(index // bit + (mask // bit) % 2, 2)
        bit *= 2
    return out


def quad_kernel(narrow, cap, *refs):
    parts, out, mixed = refs[:-2], refs[-2], refs[-1]
    power = slice(narrow + SOURCES * cap, narrow + SOURCES * cap + 1)
    mixed[...] = jnp.zeros(mixed.shape, jnp.int32)
    for top in range(out.shape[0]):
        total = jnp.zeros((narrow, out.shape[2]), F32)
        for n, part in enumerate(parts):
            both = part[top].astype(jnp.int32)
            total += decode(both[:narrow], both[power])
            row = narrow + n * cap
            mixed[row : row + cap, :] = both[narrow : narrow + cap]
        mixed[:narrow, :], mixed[power, :] = encode(total, 0)
        out[top] = mixed[...].astype(jnp.int16)


def sum_kernel(scale, narrow, cap, block, terms, *refs):
    place = my_place()
    parts, out, mixed = refs[:-2], refs[-2], refs[-1]
    depth = parts[0].shape[0]
    lowered = mixed.shape[0] - narrow if terms == 2 else 0
    power = slice(narrow + SOURCES * cap, narrow + SOURCES * cap + 1)
    mixed[...] = jnp.zeros(mixed.shape, jnp.int32)
    for first in range(0, len(parts), terms):
        for top in range(depth):
            total = jnp.zeros((narrow, block), F32)
            for part in parts[first : first + terms]:
                both = part[top].astype(jnp.int32)
                total += decode(both[:narrow, :block], both[power, :block])
            codes, powers = encode(total * F32(scale), 0)
            if lowered:
                rest = jnp.broadcast_to(powers, (lowered, block))
                mixed[:, :block] = jnp.where(
                    lax.rem(place[1], 2) == 0,
                    jnp.concatenate([codes, rest], axis=0),
                    jnp.concatenate([rest, codes], axis=0),
                )
            else:
                mixed[:narrow, :block], mixed[narrow : narrow + 1, :block] = codes, powers
            out[first // terms * depth + top] = mixed[...].astype(jnp.int16)


def entity_kernel(direct, narrow, offsets, serve, packed, x, *refs):
    place = my_place()
    recv, out, terms, onehot = refs[:-3], refs[-3], refs[-2], refs[-1]
    cap, workers = serve.shape[1], serve.shape[2]
    rows = out.shape[1]
    lane = iota((1, rows), 1)
    for h in range(workers):
        if direct:
            turn, hop = h % SOURCES, h // SOURCES
            mine = place[0] // 4
            both = recv[hop][mine].astype(jnp.int32)
            worker = lax.rem(mine + hop, 2) * 4 + flipped(place[0] % 4, turn)
        else:
            turn, both, worker = 0, recv[0][h].astype(jnp.int32), h
        row = narrow + turn * cap
        both = both[row : row + cap]
        terms[h * cap : (h + 1) * cap, :] = jnp.where(
            iota(both.shape, 1) < narrow, decode(both, both[:, narrow : narrow + 1]), 0.0
        )
        for c in range(cap):
            spot = jnp.where(lane == serve[0, c, worker], 1.0, 0.0).astype(F32)
            onehot[h * cap + c : h * cap + c + 1, :] = spot
    spots = onehot[...].astype(BF16)
    parts = jnp.concatenate(split3(jnp.transpose(terms[...])), axis=1)
    added = dot(parts, jnp.concatenate([spots] * 3, axis=0))
    sources = jnp.transpose(packed[...])[:, 0:1]
    both = dot(x[...], ones_where(iota((x.shape[1], rows), 1) == sources))
    window = x.shape[0] // 2
    both = both[:window] + both[window:]
    out[...] = shifted_rows(both, (place[1] * narrow) % 8, narrow, offsets) + added[:narrow]


def found(pieces, place, o, over_x):
    dom = place[0]
    over_low = lax.rem(dom // 2 + o // 2, 2)
    over_y = lax.rem(dom + o, 2)
    return pieces[(over_y + 2 * over_x) * 4 + over_low * 2 + o // 4].astype(jnp.int32)


def spread_core(pieces, core, place, sizes, bands, out, sems):
    workers, narrow, block, nrel = sizes
    length = narrow // 8 * 8
    moves = []
    for x in range(2):
        over_x = lax.rem(place[1] // 2 + x, 2)
        for o in range(workers):
            both = found(pieces, place, o, over_x)
            codes = jnp.where(core == 0, both[:length], both[8:])
            value = decode(codes, jnp.where(core == 0, both[narrow : narrow + 1], both[:1]))
            end = min((o + 1) * block, nrel)
            bands[x * length : (x + 1) * length, o * block : end] = value[:, : end - o * block]
        first = pl.multiple_of(2 * narrow * x + (length + 8) * core, 8)
        move = pltpu.make_async_copy(
            bands.at[x * length : (x + 1) * length], out.at[pl.ds(first, length)], sems.at[x]
        )
        move.start()
        moves.append(move)
    return moves


def spread_own_kernel(sizes, mine, out, bands, sems):
    place = my_place()
    for move in spread_core(mine, lax.rem(place[1], 2), place, sizes, bands, out, sems):
        move.wait()


def spread_rest_kernel(sizes, mine, other, partial, out, bands, shared, sems):
    place = my_place()
    workers, narrow, block, nrel = sizes
    core = lax.rem(place[1], 2)
    length = narrow // 8 * 8
    moves = spread_core(other, 1 - core, place, sizes, bands, out, sems)
    for x in range(2):
        over_x = lax.rem(place[1] // 2 + x, 2)
        for o in range(workers):
            ours, theirs = found(mine, place, o, over_x), found(other, place, o, over_x)
            low = jnp.where(core == 0, ours[length:], theirs[length:])
            high = jnp.where(core == 0, theirs[:8], ours[:8])
            upper = iota(low.shape, 0) < narrow - length
            split = narrow - length
            value = jnp.where(
                upper, decode(low, low[split : split + 1]), decode(high, high[:1])
            )
            end = min((o + 1) * block, nrel)
            shared[x * 8 : (x + 1) * 8, o * block : end] = value[:, : end - o * block]
        first = 2 * narrow * x + length
        move = pltpu.make_async_copy(
            shared.at[x * 8 : (x + 1) * 8], out.at[first : first + 8], sems.at[2 + x]
        )
        move.start()
        moves.append(move)
    for move in moves:
        move.wait()


def turned(size, hop):
    return [(i, (i + hop) % size) for i in range(size)]


def shards(entities, relation, serve_ids, edge_src, edge_rel, edge_dst, neg_ids, edge_count):
    workers = lax.axis_size("dom")
    replicas = lax.axis_size("rep")
    rows, dim = entities.shape
    nrel = relation.shape[0]
    cap = serve_ids.shape[2]
    edges = edge_src.shape[2]
    groups, width = neg_ids.shape[2], neg_ids.shape[3]
    slots = workers * cap
    narrow = dim // replicas
    direct = workers == 8 and replicas == 4 and narrow % 8 == 4
    block = up(-(-nrel // workers), LANES if direct else 8)
    pad_rel = up(max(nrel, workers * block), LANES)
    offsets = sorted({(narrow * r) % 8 for r in range(replicas)})
    window = up(narrow + offsets[-1], 8)
    height = up(narrow + SOURCES * cap + 1, 16)
    ent_t, rel_t = entities.T, relation.T
    serve_t = jnp.transpose(serve_ids, (0, 2, 1))

    idx, served = pl.pallas_call(
        prep_kernel,
        out_shape=(
            jax.ShapeDtypeStruct((IDX_ROWS, edges), jnp.int32),
            jax.ShapeDtypeStruct((workers, cap, dim), F32),
        ),
        in_specs=[HBM] * 7,
        out_specs=(VMEM, VMEM),
        scratch_shapes=[
            pltpu.SMEM(serve_t.shape, jnp.int32),
            pltpu.SMEM(edge_count.shape, jnp.int32),
            pltpu.VMEM(ent_t.shape, BF16),
            pltpu.VMEM(edge_src.shape, jnp.int32),
            pltpu.VMEM(edge_rel.shape, jnp.int32),
            pltpu.VMEM(edge_dst.shape, jnp.int32),
            pltpu.VMEM(neg_ids.shape, jnp.int32),
            pltpu.VMEM((slots, rows), F32),
            pltpu.SemaphoreType.DMA((7,)),
        ],
        compiler_params=params(60),
        name="prep",
    )(serve_t, edge_count, ent_t, edge_src, edge_rel, edge_dst, neg_ids)

    received = lax.all_to_all(served, "dom", 0, 0, tiled=True)
    held = [idx]
    for hop in range(1, replicas):
        held.append(lax.ppermute(idx, "rep", turned(replicas, hop)))

    total = min(replicas * edges, up(LIVE_EDGES, edges))
    packed, query, lhs_rows, rel_rows = pl.pallas_call(
        functools.partial(
            gather_kernel, (replicas, groups, nrel, pad_rel, narrow, window, edges)
        ),
        out_shape=(
            jax.ShapeDtypeStruct((IDX_ROWS, total), jnp.int32),
            jax.ShapeDtypeStruct((dim, total), BF16),
            jax.ShapeDtypeStruct((window, total), F32),
            jax.ShapeDtypeStruct((window, total), F32),
        ),
        in_specs=[VMEM] * (replicas + 2),
        out_specs=[VMEM] * 4,
        scratch_shapes=[
            pltpu.VMEM((2 * dim, pad_rel), BF16),
        ],
        compiler_params=params(),
        cost_estimate=cost(2 * total * dim * (2 * pad_rel + rows), 8 * total * dim),
        name="gather",
    )(*held, ent_t, rel_t)

    cfg = (
        direct, workers, replicas, cap, groups, width, pad_rel, block, narrow, window,
        tuple(offsets),
    )
    lanes = max(up(block, LANES), up(narrow, LANES))
    pieces = jax.ShapeDtypeStruct((2 * window, total), BF16)
    outs = [2] * (SOURCES - 1) if direct else [workers]
    sizes = [pieces] if direct else []
    sizes += [jax.ShapeDtypeStruct((n, height, lanes), jnp.int16) for n in outs]
    mixed = [pltpu.VMEM((height, lanes), jnp.int32)]
    x_parts, tables, *sent = pl.pallas_call(
        functools.partial(main_kernel, cfg),
        out_shape=[pieces, jax.ShapeDtypeStruct((slots, lanes), jnp.int32)] + sizes,
        in_specs=[VMEM] * (replicas + 5),
        out_specs=[VMEM] * (2 + len(sizes)),
        scratch_shapes=[
            pltpu.VMEM((slots, dim), F32),
            pltpu.VMEM((dim, slots), F32),
            pltpu.VMEM((dim, total), F32),
            pltpu.VMEM((lanes, slots), F32),
        ]
        + mixed,
        compiler_params=params(),
        name="edges",
    )(*held, packed, query, lhs_rows, rel_rows, received)

    def swap(array, dom_bits=0, rep_bits=0):
        pairs = []
        for o in range(workers):
            for r in range(replicas):
                pairs.append((o * replicas + r, (o ^ dom_bits) * replicas + (r ^ rep_bits)))
        return lax.ppermute(array, ("dom", "rep"), pairs)

    stack = jax.ShapeDtypeStruct((outs[0], height, lanes), jnp.int16)
    if direct:
        y_parts, *sent = sent
        got = {n: swap(sent[n - 1], n) for n in reversed(range(1, SOURCES))}
        kept = pl.pallas_call(
            functools.partial(own_kernel, block, narrow, cap, offsets),
            out_shape=stack,
            in_specs=[VMEM] * 3,
            out_specs=VMEM,
            scratch_shapes=mixed,
            compiler_params=params(),
            cost_estimate=cost(4 * window * total * 2 * block, 10**6),
            name="own",
        )(packed, y_parts, tables)
        summed = pl.pallas_call(
            functools.partial(quad_kernel, narrow, cap),
            out_shape=stack,
            in_specs=[VMEM] * SOURCES,
            out_specs=VMEM,
            scratch_shapes=mixed,
            compiler_params=params(),
            name="quad",
        )(kept, *[got[n] for n in range(1, SOURCES)])
        recv = [summed, swap(summed, 4)]
        parts = recv + [swap(summed, 2), swap(summed, 6)]
        stack = 4
    else:
        recv = [lax.all_to_all(sent[0], "dom", 0, 0, tiled=True)]
        parts = [recv[0][w : w + 1] for w in range(workers)]
        stack = 1
    scale = 1.0 / (edges * workers * replicas)
    chunk = pl.pallas_call(
        functools.partial(sum_kernel, scale, narrow, cap, block, 2 if direct else workers),
        out_shape=jax.ShapeDtypeStruct((stack, up(narrow + 1, 8), lanes), jnp.int16),
        in_specs=[VMEM] * len(parts),
        out_specs=VMEM,
        scratch_shapes=[pltpu.VMEM((up(narrow + 1, 8), lanes), jnp.int32)],
        compiler_params=params(),
        name="total",
    )(*parts)

    if direct:
        sibling = swap(chunk, 0, 1)
        rest = jnp.concatenate([swap(chunk, 1), swap(chunk, 0, 2), swap(chunk, 1, 2)], axis=0)
    entity_grad = pl.pallas_call(
        functools.partial(entity_kernel, direct, narrow, offsets),
        out_shape=jax.ShapeDtypeStruct((narrow, rows), F32),
        in_specs=[SMEM] + [VMEM] * (2 + len(recv)),
        out_specs=VMEM,
        scratch_shapes=[pltpu.VMEM((slots, lanes), F32), pltpu.VMEM((slots, rows), F32)],
        compiler_params=params(),
        cost_estimate=cost(10**9, 10**6),
        name="entity",
    )(serve_t, packed, x_parts, *recv)

    if direct:
        rest, entity_grad = lax.optimization_barrier((rest, entity_grad))
        base = jnp.concatenate([chunk, rest], axis=0)
        swapped = jnp.concatenate([sibling, swap(rest, 0, 1)], axis=0)
        sizes = (workers, narrow, block, nrel)
        result = jax.ShapeDtypeStruct((dim, nrel), F32)
        bands = pltpu.VMEM((narrow // 8 * 16, nrel), F32)
        own_half = pl.pallas_call(
            functools.partial(spread_own_kernel, sizes),
            out_shape=result,
            in_specs=[VMEM],
            out_specs=HBM,
            scratch_shapes=[bands, pltpu.SemaphoreType.DMA((2,))],
            compiler_params=params(),
            cost_estimate=cost(10**6, 4 * dim * nrel),
            name="spread_own",
        )(base)
        relation_t = pl.pallas_call(
            functools.partial(spread_rest_kernel, sizes),
            out_shape=result,
            in_specs=[VMEM, VMEM, HBM],
            out_specs=HBM,
            scratch_shapes=[bands, pltpu.VMEM((16, nrel), F32), pltpu.SemaphoreType.DMA((4,))],
            input_output_aliases={2: 0},
            compiler_params=params(),
            name="spread_rest",
        )(base, swapped, own_half)
    else:
        whole = lax.all_gather(chunk[0, :, :block], ("dom", "rep"), axis=0)
        whole = decode(whole[:, :narrow], whole[:, narrow : narrow + 1])
        whole = whole.reshape(workers, replicas, narrow, block).transpose(1, 2, 0, 3)
        relation_t = whole.reshape(dim, workers * block)[:, :nrel]
    return (entity_grad.T, relation_t.T)


def solution(mesh):
    placed = (
        P("dom", None),
        P(),
        P("dom", None, None),
        P("dom", "rep", None),
        P("dom", "rep", None),
        P("dom", "rep", None),
        P("dom", "rep", None, None),
        P("dom", "rep"),
    )
    return jax.shard_map(
        shards, mesh=mesh, in_specs=placed, out_specs=(P("dom", "rep"), P()), check_vma=False
    )
```
